32 devices in a mesh: dp: 8 (over y, x, core), tensor: 4 (over z).
Axes of the slice: x: 2, y: 2, z: 4, core: 2. Of those that a mesh axis runs over, the one named last changes fastest.
Arguments:
- x_in: bfloat16 [8192, 1024], P(('dp', 'tensor')), may hold values from -6 to 6
- cotangent: bfloat16 [8192, 1024], P(('dp', 'tensor')), may hold values from -6 to 6
- segments: int32 [8, 1024], P('dp'), may hold values from 0 to 3, as said below
- norm_one: bfloat16 [1024], P('dp'), may hold values from 0.5 to 1.5
- w_query: bfloat16 [1024, 512], P('dp', 'tensor'), may hold values from -0.1875 to 0.1875
- w_keyval: bfloat16 [1024, 256], P('dp'), may hold values from -0.1875 to 0.1875
- w_attn_out: bfloat16 [512, 1024], P('tensor', 'dp'), may hold values from -1 to 1
- w_zgate: bfloat16 [1024, 1536], P('dp', 'tensor'), may hold values from -0.1875 to 0.1875
- w_xin: bfloat16 [1024, 1536], P('dp', 'tensor'), may hold values from -0.1875 to 0.1875
- w_bcin: bfloat16 [1024, 256], P('dp'), may hold values from -0.1875 to 0.1875
- w_dtin: bfloat16 [1024, 24], P('dp', 'tensor'), may hold values from -0.1875 to 0.1875
- conv_x: float32 [4, 1536], P(None, 'tensor'), may hold values from -0.7 to 0.7
- conv_bc: float32 [4, 256], replicated, may hold values from -0.7 to 0.7
- bias_x: float32 [1536], P('tensor'), may hold values from -0.5 to 0.5
- bias_bc: float32 [256], replicated, may hold values from -0.5 to 0.5
- dt_bias: float32 [24], P('tensor'), may hold values from -6.9 to -2.3
- a_log: float32 [24], P('tensor'), may hold values from 0 to 2.77
- d_skip: float32 [24], P('tensor'), may hold values from 0.5 to 1.5
- ssm_gain: float32 [1536], P('tensor'), may hold values from 0.5 to 1.5
- w_mix_out: bfloat16 [1536, 1024], P('tensor', 'dp'), may hold values from -0.15625 to 0.15625
- norm_two: bfloat16 [1024], P('dp'), may hold values from 0.5 to 1.5
- w_gate: bfloat16 [1024, 2048], P('dp', 'tensor'), may hold values from -0.1875 to 0.1875
- w_up: bfloat16 [1024, 2048], P('dp', 'tensor'), may hold values from -0.1875 to 0.1875
- w_down: bfloat16 [2048, 1024], P('tensor', 'dp'), may hold values from -0.125 to 0.125
Outputs:
- block_out: bfloat16 [8192, 1024], P(('dp', 'tensor'))
- grad_input: float32 [8192, 1024], P(('dp', 'tensor'))
- grad_norm_one: float32 [1024], P('dp')
- grad_w_query: float32 [1024, 512], P('dp', 'tensor')
- grad_w_keyval: float32 [1024, 256], P('dp')
- grad_w_attn_out: float32 [512, 1024], P('tensor', 'dp')
- grad_w_zgate: float32 [1024, 1536], P('dp', 'tensor')
- grad_w_xin: float32 [1024, 1536], P('dp', 'tensor')
- grad_w_bcin: float32 [1024, 256], P('dp')
- grad_w_dtin: float32 [1024, 24], P('dp', 'tensor')
- grad_conv_x: float32 [4, 1536], P(None, 'tensor')
- grad_conv_bc: float32 [4, 256], replicated
- grad_bias_x: float32 [1536], P('tensor')
- grad_bias_bc: float32 [256], replicated
- grad_dt_bias: float32 [24], P('tensor')
- grad_a_log: float32 [24], P('tensor')
- grad_d_skip: float32 [24], P('tensor')
- grad_ssm_gain: float32 [1536], P('tensor')
- grad_w_mix_out: float32 [1536, 1024], P('tensor', 'dp')
- grad_norm_two: float32 [1024], P('dp')
- grad_w_gate: float32 [1024, 2048], P('dp', 'tensor')
- grad_w_up: float32 [1024, 2048], P('dp', 'tensor')
- grad_w_down: float32 [2048, 1024], P('tensor', 'dp')
The draws below stay inside these ranges and needn't reach their ends.
Inputs may be any that keep to these rules, and one draw needn't show every extreme that they name: `segments`: document numbers never fall along a sequence; every sequence holds exactly 4 documents, one of exactly 800 tokens and three of at least 60 tokens each.
All inputs are finite; a program needn't handle non-finite values.
Results may differ from the reference program's by a relative error of at most 0.024.
Values may be sent and summed in bfloat16 or wider, within the bound.
No kernel may reach another device: no remote copies, remote signals or barrier semaphores. Data moves between devices by JAX's collectives and lax.ppermute only.
A program may use at most 128 MiB of HBM per device.

```python
import math
import jax
import jax.numpy as jnp
from jax import lax

D = 1024
QH = 8
KVH = 2
HD = 64
MH = 24
PD = 64
NS = 128
KW = 4
FF = 2048
SEQLEN = 1024
BLOCK = 128
NSEQ = 8
ROWS = 8192


def draw_segments(key, part):
    key = jax.random.fold_in(key, 7)
    first_key, second_key, place_key = jax.random.split(key, 3)
    longest = SEQLEN * 25 // 32
    floor_len = SEQLEN * 15 // 256
    spare = SEQLEN - longest - 3 * floor_len
    cut_one = jax.random.randint(first_key, (NSEQ,), 0, spare + 1)
    cut_two = jax.random.randint(second_key, (NSEQ,), 0, spare + 1)
    lower = jnp.minimum(cut_one, cut_two)
    upper = jnp.maximum(cut_one, cut_two)
    shorts = jnp.stack([lower, upper - lower, spare - upper], axis=1) + floor_len
    place = jax.random.randint(place_key, (NSEQ,), 0, 4)
    slots = jnp.arange(4, dtype=jnp.int32)[None, :]
    short_index = jnp.clip(slots - (slots > place[:, None]).astype(jnp.int32), 0, 2)
    picked = jnp.take_along_axis(shorts, short_index, axis=1)
    lengths = jnp.where(slots == place[:, None], longest, picked).astype(jnp.int32)
    ends = jnp.cumsum(lengths, axis=1)
    positions = jnp.arange(SEQLEN, dtype=jnp.int32)
    numbers = jnp.sum((positions[None, :, None] >= ends[:, None, :3]).astype(jnp.int32), axis=2)
    return numbers.astype(jnp.int32)


def block_scale(stream_key, dims, cuts, smallest, high):
    factor_of, own = 1.0, jax.random.fold_in(stream_key, 6)
    for dim, blocks in cuts:
        heights = jnp.exp(jax.random.uniform(jax.random.fold_in(own, dim), (blocks,), jnp.float32, smallest / len(cuts), high / len(cuts)))
        factor_of = factor_of * jnp.repeat(heights, dims[dim] // blocks).reshape([-1 if axis == dim else 1 for axis in range(len(dims))])
    return factor_of


def centred(own_key, shape, width, limit, shards=(), held_as=jnp.bfloat16):
    drawn = width * jax.random.normal(own_key, shape, jnp.float32)
    if shards:
        drawn = drawn * block_scale(own_key, shape, shards, -0.22, 0.18)
    return jnp.clip(drawn, -limit, limit).astype(held_as)


def setup_inputs(seed: int = 0) -> dict:
    key_list = jax.random.split(jax.random.key(seed), 25)
    return {
        "x_in": centred(key_list[0], (ROWS, D), 1.0, 6.0, ((0, 32),)),
        "cotangent": centred(key_list[1], (ROWS, D), 1.0, 6.0, ((0, 32),)),
        "segments": draw_segments(jax.random.fold_in(key_list[24], 71), 0),
        "norm_one": jnp.clip(1.0 + 0.1 * jax.random.normal(key_list[3], (D,), jnp.float32), 0.5, 1.5).astype(jnp.bfloat16),
        "w_query": centred(key_list[4], (D, QH * HD), D ** -0.5, 0.1875, ((0, 8), (1, 4))),
        "w_keyval": centred(key_list[5], (D, 2 * KVH * HD), D ** -0.5, 0.1875, ((0, 8),)),
        "w_attn_out": centred(key_list[6], (QH * HD, D), (QH * HD // 16) ** -0.5, 1.0, ((0, 4), (1, 8))),
        "w_zgate": centred(key_list[7], (D, MH * PD), D ** -0.5, 0.1875, ((0, 8), (1, 4))),
        "w_xin": centred(key_list[8], (D, MH * PD), D ** -0.5, 0.1875, ((0, 8), (1, 4))),
        "w_bcin": centred(key_list[9], (D, 2 * NS), D ** -0.5, 0.1875, ((0, 8),)),
        "w_dtin": centred(key_list[10], (D, MH), D ** -0.5, 0.1875, ((0, 8), (1, 4))),
        "conv_x": jnp.clip(jax.random.uniform(key_list[11], (KW, MH * PD), jnp.float32, -0.7, 0.7) * block_scale(key_list[11], (KW, MH * PD), ((1, 4),), -0.4, 0.0), -0.7, 0.7),
        "conv_bc": jnp.clip(jax.random.uniform(key_list[12], (KW, 2 * NS), jnp.float32, -0.7, 0.7), -0.7, 0.7),
        "bias_x": jnp.clip(jax.random.uniform(key_list[13], (MH * PD,), jnp.float32, -0.5, 0.5) * block_scale(key_list[13], (MH * PD,), ((0, 4),), -0.4, 0.0), -0.5, 0.5),
        "bias_bc": jnp.clip(jax.random.uniform(key_list[14], (2 * NS,), jnp.float32, -0.5, 0.5), -0.5, 0.5),
        "dt_bias": jnp.clip(-6.9 + 4.6000001430511475 * jax.random.uniform(key_list[15], (MH,), jnp.float32) ** block_scale(key_list[15], (MH,), ((0, 4),), -0.2, 0.2), -6.9, -2.3),
        "a_log": jnp.clip(2.77 * jax.random.uniform(key_list[16], (MH,), jnp.float32) ** block_scale(key_list[16], (MH,), ((0, 4),), -0.2, 0.2), 0.0, 2.77),
        "d_skip": jnp.clip(0.5 + 1.0 * jax.random.uniform(key_list[17], (MH,), jnp.float32) ** block_scale(key_list[17], (MH,), ((0, 4),), -0.2, 0.2), 0.5, 1.5),
        "ssm_gain": jnp.clip(1.0 + 0.1 * jax.random.normal(key_list[18], (MH * PD,), jnp.float32), 0.5, 1.5),
        "w_mix_out": centred(key_list[19], (MH * PD, D), (MH * PD) ** -0.5, 0.15625, ((0, 4), (1, 8))),
        "norm_two": jnp.clip(1.0 + 0.1 * jax.random.normal(key_list[20], (D,), jnp.float32), 0.5, 1.5).astype(jnp.bfloat16),
        "w_gate": centred(key_list[21], (D, FF), D ** -0.5, 0.1875, ((0, 8), (1, 4))),
        "w_up": centred(key_list[22], (D, FF), D ** -0.5, 0.1875, ((0, 8), (1, 4))),
        "w_down": centred(key_list[23], (FF, D), FF ** -0.5, 0.125, ((0, 4), (1, 8))),
    }


EPSILON = 1e-05
ROPE_BASE = 100000000000.0

@jax.custom_vjp
def low(v):
    return lax.optimization_barrier(v.astype(jnp.bfloat16)).astype(jnp.float32)

@jax.custom_vjp
def low_back(v):
    return v

def low_keep(v):
    return (low(v), None)

def low_pass(kept, grad):
    return (grad,)

def back_keep(v):
    return (v, None)

def back_low(kept, grad):
    return (low(grad),)
low.defvjp(low_keep, low_pass)
low_back.defvjp(back_keep, back_low)

def matmul_high(lhs_mat, rhs_mat):
    return jnp.dot(lhs_mat, rhs_mat, precision=lax.Precision.HIGHEST, preferred_element_type=jnp.float32)

def rms_scale(values):
    return lax.rsqrt(lax.optimization_barrier(jnp.mean(values * values, axis=-1, keepdims=True)) + EPSILON)

def rotate(tensor, length, direction):
    half_dim = HD // 2
    places = jnp.arange(length, dtype=jnp.float32)
    freqs = ROPE_BASE ** (-(jnp.arange(half_dim, dtype=jnp.float32) * (2.0 / HD)))
    angles = places[:, None] * freqs[None, :]
    cosine = jnp.cos(angles)[:, None, :]
    sine_part = direction * jnp.sin(angles)[:, None, :]
    first_half = tensor[..., :half_dim]
    second = tensor[..., half_dim:]
    return jnp.concatenate([first_half * cosine - second * sine_part, second * cosine + first_half * sine_part], axis=-1)

def attention_core(queries, keyvals, segment, head_map):
    length = queries.shape[0]
    head_count = head_map.shape[0]
    query_heads = queries.reshape(length, head_count, HD)
    key_heads = keyvals[:, :KVH * HD].reshape(length, KVH, HD)
    value_heads = keyvals[:, KVH * HD:].reshape(length, KVH, HD)
    key_sel = jnp.einsum('lkd,hk->lhd', key_heads, head_map, precision=lax.Precision.HIGHEST)
    value_sel = jnp.einsum('lkd,hk->lhd', value_heads, head_map, precision=lax.Precision.HIGHEST)
    low_query = low(rotate(query_heads, length, 1.0))
    low_key = low(rotate(key_sel, length, 1.0))
    low_value = low(value_sel)
    scores = low_back(jnp.einsum('ihd,jhd->hij', low_query, low_key, precision=lax.Precision.HIGHEST) / math.sqrt(HD))
    positions = jnp.arange(length)
    allowed = (positions[:, None] >= positions[None, :]) & (segment[:, None] == segment[None, :])
    masked = jnp.where(allowed[None, :, :], scores, -1000000000.0)
    probability = low(jax.nn.softmax(masked, axis=-1))
    attended = jnp.einsum('hij,jhd->ihd', probability, low_value, precision=lax.Precision.HIGHEST)
    return attended.reshape(length, head_count * HD)

def conv_silu(values, weight, bias_vec, segment):
    length = values.shape[1]
    accumulated = bias_vec[None, None, :] + weight[KW - 1][None, None, :] * values
    for offset in range(1, KW):
        shifted = jnp.pad(values, ((0, 0), (offset, 0), (0, 0)))[:, :length]
        linked = jnp.pad(segment, ((0, 0), (offset, 0)), constant_values=-1)[:, :length] == segment
        accumulated = accumulated + weight[KW - 1 - offset][None, None, :] * shifted * linked[:, :, None].astype(jnp.float32)
    return jax.nn.silu(accumulated)

def ssd_core(x_conv, bc_conv, dt_raw, gate_z, segment, dt_bias, a_log, d_skip):
    length, channels = x_conv.shape
    head_num = dt_raw.shape[1]
    block_num = length // BLOCK
    steps_all = jax.nn.softplus(dt_raw + dt_bias[None, :])
    logdecay = -steps_all * jnp.exp(a_log)[None, :]
    pieces = (x_conv.reshape(block_num, BLOCK, head_num, PD), bc_conv[:, :NS].reshape(block_num, BLOCK, NS), bc_conv[:, NS:].reshape(block_num, BLOCK, NS), steps_all.reshape(block_num, BLOCK, head_num), logdecay.reshape(block_num, BLOCK, head_num), segment.reshape(block_num, BLOCK))

    def one_block(carry, blocks):
        carried_state, last_segment = carry
        x_blk, b_blk, c_blk, step_blk, logdecay_blk, seg_blk = blocks
        cumlog = jnp.cumsum(logdecay_blk, axis=0)
        positions = jnp.arange(BLOCK)
        linked = (positions[:, None] >= positions[None, :]) & (seg_blk[:, None] == seg_blk[None, :])
        gaps = jnp.where(linked[:, :, None], cumlog[:, None, :] - cumlog[None, :, :], 0.0)
        decays = jnp.exp(gaps) * linked[:, :, None].astype(jnp.float32)
        contact = jnp.dot(c_blk, b_blk.T, precision=lax.Precision.HIGHEST, preferred_element_type=jnp.float32)
        mixing = decays * contact[:, :, None] * step_blk[None, :, :]
        within = jnp.einsum('ijh,jhp->ihp', mixing, x_blk, precision=lax.Precision.HIGHEST)
        entering = jnp.exp(cumlog) * (seg_blk == last_segment).astype(jnp.float32)[:, None]
        from_state = jnp.einsum('in,hpn->ihp', c_blk, carried_state, precision=lax.Precision.HIGHEST) * entering[:, :, None]
        outputs = within + from_state + d_skip[None, :, None] * x_blk
        tailing = (seg_blk == seg_blk[BLOCK - 1]).astype(jnp.float32)
        weights_tail = jnp.exp(cumlog[BLOCK - 1][None, :] - cumlog) * tailing[:, None] * step_blk
        kept_share = jnp.exp(cumlog[BLOCK - 1]) * (seg_blk[BLOCK - 1] == last_segment).astype(jnp.float32)
        next_state = jnp.einsum('jh,jhp,jn->hpn', weights_tail, x_blk, b_blk, precision=lax.Precision.HIGHEST) + carried_state * kept_share[:, None, None]
        return ((next_state, seg_blk[BLOCK - 1]), outputs)
    initial = (jnp.zeros((head_num, PD, NS), jnp.float32), jnp.int32(-1))
    unused, outputs = lax.scan(jax.checkpoint(one_block), initial, pieces)
    return outputs.reshape(length, channels) * jax.nn.silu(gate_z)

def forward(x_in, norm_one, w_query, w_keyval, w_attn_out, w_zgate, w_xin, w_bcin, w_dtin, conv_x, conv_bc, bias_x, bias_bc, dt_bias, a_log, d_skip, ssm_gain, w_mix_out, norm_two, w_gate, w_up, w_down, segments):
    seq_count = segments.shape[0]
    length = segments.shape[1]
    low_one = low(x_in * rms_scale(x_in) * norm_one[None, :])
    queries = low_back(matmul_high(low_one, w_query))
    keyvals = matmul_high(low_one, w_keyval)
    zgate = low_back(matmul_high(low_one, w_zgate))
    xin_raw = low_back(matmul_high(low_one, w_xin))
    bc_raw = matmul_high(low_one, w_bcin)
    dt_raw = low_back(matmul_high(low_one, w_dtin))
    head_map = ((jnp.arange(QH) // (QH // KVH))[:, None] == jnp.arange(KVH)[None, :]).astype(jnp.float32)

    def attend_one(pieces):
        return attention_core(pieces[0], pieces[1], pieces[2], head_map)
    attended = lax.map(jax.checkpoint(attend_one), (queries.reshape(seq_count, length, -1), keyvals.reshape(seq_count, length, -1), segments))
    attended = low(low_back(attended.reshape(-1, QH * HD)))
    x_conv = low(conv_silu(xin_raw.reshape(seq_count, length, -1), conv_x, bias_x, segments))
    bc_conv = low(conv_silu(bc_raw.reshape(seq_count, length, -1), conv_bc, bias_bc, segments))

    def scan_one(pieces):
        return ssd_core(pieces[0], pieces[1], pieces[2], pieces[3], pieces[4], dt_bias, a_log, d_skip)
    gated = lax.map(jax.checkpoint(scan_one), (x_conv, bc_conv, dt_raw.reshape(seq_count, length, -1), zgate.reshape(seq_count, length, -1), segments))
    gated = gated.reshape(-1, MH * PD)
    mixed = low(gated * rms_scale(gated) * ssm_gain[None, :])
    branch = low_back(matmul_high(attended, w_attn_out) + matmul_high(mixed, w_mix_out))
    middle = x_in + branch
    low_two = low(middle * rms_scale(middle) * norm_two[None, :])
    gate_pre = low_back(matmul_high(low_two, w_gate))
    up_pre = low_back(matmul_high(low_two, w_up))
    hidden = low(jax.nn.silu(gate_pre) * up_pre)
    return middle + low_back(matmul_high(hidden, w_down))

def reference(x_in, cotangent, segments, norm_one, w_query, w_keyval, w_attn_out, w_zgate, w_xin, w_bcin, w_dtin, conv_x, conv_bc, bias_x, bias_bc, dt_bias, a_log, d_skip, ssm_gain, w_mix_out, norm_two, w_gate, w_up, w_down):
    floats = [arr.astype(jnp.float32) for arr in (x_in, norm_one, w_query, w_keyval, w_attn_out, w_zgate, w_xin, w_bcin, w_dtin, conv_x, conv_bc, bias_x, bias_bc, dt_bias, a_log, d_skip, ssm_gain, w_mix_out, norm_two, w_gate, w_up, w_down)]

    def layer(*params):
        return forward(*params, segments)
    result, backward = jax.vjp(layer, *floats)
    grads = backward(cotangent.astype(jnp.float32))
    return (result.astype(jnp.bfloat16), grads[0], grads[1], grads[2], grads[3], grads[4], grads[5], grads[6], grads[7], grads[8], grads[9], grads[10], grads[11], grads[12], grads[13], grads[14], grads[15], grads[16], grads[17], grads[18], grads[19], grads[20], grads[21])
```

```python
import math

import jax
import jax.numpy as jnp
import numpy as np
from jax import lax
from jax.experimental import pallas as pl
from jax.experimental.pallas import tpu as pltpu
from jax.sharding import PartitionSpec as P

QH = 8
KVH = 2
HD = 64
MH = 24
PD = 64
NS = 128
KW = 4
BLOCK = 128
LANES = 128

EPSILON = 1e-05
ROPE_BASE = 100000000000.0
NEG = -1e9
F32 = jnp.float32
BF16 = jnp.bfloat16
VMEM_LIMIT = 48 * 1024 * 1024


def mm(lhs, rhs):
    return lax.dot_general(lhs, rhs, (((1,), (0,)), ((), ())), preferred_element_type=F32)


def mm_nt(lhs, rhs):
    return lax.dot_general(lhs, rhs, (((1,), (1,)), ((), ())), preferred_element_type=F32)


def mm_tn(lhs, rhs):
    return lax.dot_general(lhs, rhs, (((0,), (0,)), ((), ())), preferred_element_type=F32)


def rms_scale(values):
    return lax.rsqrt(jnp.mean(values * values, axis=-1, keepdims=True) + EPSILON)


def norm_back(grad_normed, normed, scale):
    return scale * (grad_normed - normed * jnp.mean(grad_normed * normed, axis=-1, keepdims=True))


def sigmoid(v):
    return 1.0 / (1.0 + jnp.exp(-v))


def iota(shape, dim):
    return lax.broadcasted_iota(jnp.int32, shape, dim)


def rope_tables(length):
    half = HD // 2
    freqs = np.float32(ROPE_BASE) ** (-(np.arange(half, dtype=np.float32) * np.float32(2.0 / HD)))
    angles = np.arange(length, dtype=np.float32)[:, None] * freqs.astype(np.float32)[None, :]
    cosine, sine = np.cos(angles).astype(np.float32), np.sin(angles).astype(np.float32)
    cos_lanes = np.concatenate([cosine] * 4, axis=1)
    sin_lanes = np.concatenate([-sine, sine, -sine, sine], axis=1)
    return jnp.asarray(cos_lanes), jnp.asarray(sin_lanes)


def swap_halves(values):
    lane = iota(values.shape, 1)
    ahead = pltpu.roll(values, LANES - HD // 2, 1)
    behind = pltpu.roll(values, HD // 2, 1)
    return jnp.where((lane & (HD - 1)) < HD // 2, ahead, behind)


def pair_rows(block):
    low = iota(block.shape, 1) < HD
    zero = jnp.zeros_like(block)
    return jnp.concatenate([jnp.where(low, block, zero), jnp.where(low, zero, block)], axis=0)


def attn_fwd_kernel(q_ref, kv_ref, cos_ref, sin_ref, start_ref, out_ref, lse_ref, lq_ref, lkv_ref):
    length = q_ref.shape[0]
    rows = 256
    cosine, sine = cos_ref[...], sin_ref[...]
    low = iota((length, LANES), 1) < HD
    queries = q_ref[...]
    lq_ref[...] = (queries * cosine + swap_halves(queries) * sine).astype(BF16)
    kv = kv_ref[...]
    kv = jnp.where(low, kv * cosine + swap_halves(kv) * sine, kv)
    lkv_ref[...] = kv.astype(BF16)
    other = pltpu.roll(kv, HD, 1)
    keys = jnp.where(low, kv, other).astype(BF16)
    vals = jnp.where(low, other, kv).astype(BF16)
    half = iota((rows, LANES), 1) < HD
    for step in range(length // rows):
        end = (step + 1) * rows
        span = slice(step * rows, end)
        stacked = pair_rows(lq_ref[span, :].astype(F32)).astype(BF16)
        scores = mm_nt(stacked, keys[:end]) * (1.0 / math.sqrt(HD))
        first = start_ref[span, :][:, :1]
        col = iota((rows, end), 1)
        row = iota((rows, end), 0) + step * rows
        allowed = (col <= row) & (col >= first)
        allowed = jnp.concatenate([allowed.astype(jnp.int32)] * 2, axis=0) > 0
        scores = jnp.where(allowed, scores, NEG)
        top = jnp.max(scores, axis=1, keepdims=True)
        expo = jnp.exp(scores - top)
        total = jnp.sum(expo, axis=1, keepdims=True)
        probs = (expo * (1.0 / total)).astype(BF16)
        result = mm(probs, vals[:end])
        out_ref[span, :] = jnp.where(half, result[:rows], result[rows:]).astype(BF16)
        lse = top + jnp.log(total)
        lse_ref[span, :] = jnp.where(half, lse[:rows], lse[rows:])


def attn_bwd_kernel(
    lq_ref, lkv_ref, lse_ref, out_ref, go_ref, cos_ref, sin_ref, start_ref, gq_ref, gkv_ref, dk_ref, dv_ref
):
    length = lq_ref.shape[0]
    rows = 256
    cosine, sine = cos_ref[...], sin_ref[...]
    low = iota((length, LANES), 1) < HD
    kv = lkv_ref[...].astype(F32)
    other = pltpu.roll(kv, HD, 1)
    keys = jnp.where(low, kv, other).astype(BF16)
    vals = jnp.where(low, other, kv).astype(BF16)
    half = iota((rows, LANES), 1) < HD
    dk_ref[...] = jnp.zeros_like(dk_ref)
    dv_ref[...] = jnp.zeros_like(dv_ref)
    inv = 1.0 / math.sqrt(HD)
    for step in range(length // rows):
        end = (step + 1) * rows
        span = slice(step * rows, end)
        stacked = pair_rows(lq_ref[span, :].astype(F32)).astype(BF16)
        grads = pair_rows(go_ref[span, :].astype(F32))
        outs = out_ref[span, :].astype(F32)
        inner = jnp.sum(grads * jnp.concatenate([outs, outs], axis=0), axis=1, keepdims=True)
        grads = grads.astype(BF16)
        lse = lse_ref[span, :]
        lse = jnp.concatenate([lse[:, :1], lse[:, HD : HD + 1]], axis=0)
        scores = mm_nt(stacked, keys[:end]) * inv
        first = start_ref[span, :][:, :1]
        col = iota((rows, end), 1)
        row = iota((rows, end), 0) + step * rows
        allowed = (col <= row) & (col >= first)
        allowed = jnp.concatenate([allowed.astype(jnp.int32)] * 2, axis=0) > 0
        probs = jnp.exp(jnp.where(allowed, scores, NEG) - lse)
        grad_probs = mm_nt(grads, vals[:end])
        grad_scores = (probs * (grad_probs - inner)).astype(BF16)
        gq = mm(grad_scores, keys[:end]) * inv
        gq = jnp.where(half, gq[:rows], gq[rows:])
        gq_ref[span, :] = (gq * cosine[span] - swap_halves(gq) * sine[span]).astype(BF16)
        dk_ref[:end, :] += mm_tn(grad_scores, stacked)
        dv_ref[:end, :] += mm_tn(probs.astype(BF16), grads)
    dk = dk_ref[...] * inv
    dk = dk + pltpu.roll(dk, HD, 1)
    dk = dk * cosine - swap_halves(dk) * sine
    dv = dv_ref[...]
    dv = dv + pltpu.roll(dv, HD, 1)
    gkv_ref[...] = jnp.where(low, dk, dv).astype(BF16)


def attn_forward(proj, cosine, sine, start_col):
    length = proj.shape[0]
    wide = pl.BlockSpec((length, LANES), lambda i: (0, 0))
    return pl.pallas_call(
        attn_fwd_kernel,
        grid=(1,),
        in_specs=[wide, pl.BlockSpec((length, LANES), lambda i: (0, 1)), wide, wide, wide],
        out_specs=[wide] * 4,
        out_shape=[
            jax.ShapeDtypeStruct((length, LANES), BF16),
            jax.ShapeDtypeStruct((length, LANES), F32),
            jax.ShapeDtypeStruct((length, LANES), BF16),
            jax.ShapeDtypeStruct((length, LANES), BF16),
        ],
        compiler_params=pltpu.CompilerParams(vmem_limit_bytes=VMEM_LIMIT),
        cost_estimate=pl.CostEstimate(flops=10**9, bytes_accessed=6 * 10**6, transcendentals=2 * 10**6),
        name="attn_fwd",
    )(proj, proj, cosine, sine, start_col)


def attn_backward(low_q, low_kv, lse, out, grad_out, cosine, sine, start_col):
    length = low_q.shape[0]
    wide = pl.BlockSpec((length, LANES), lambda i: (0, 0))
    return pl.pallas_call(
        attn_bwd_kernel,
        grid=(1,),
        in_specs=[wide] * 8,
        out_specs=[wide] * 2,
        out_shape=[jax.ShapeDtypeStruct((length, LANES), BF16)] * 2,
        scratch_shapes=[pltpu.VMEM((length, LANES), F32)] * 2,
        compiler_params=pltpu.CompilerParams(vmem_limit_bytes=VMEM_LIMIT),
        cost_estimate=pl.CostEstimate(flops=3 * 10**9, bytes_accessed=6 * 10**6, transcendentals=2 * 10**6),
        name="attn_bwd",
    )(low_q, low_kv, lse, out, grad_out, cosine, sine, start_col)


def split3(values):
    high = values.astype(BF16).astype(F32)
    rest = values - high
    mid = rest.astype(BF16).astype(F32)
    tail = rest - mid
    return jnp.concatenate([high, mid, tail, jnp.zeros_like(values)], axis=0).astype(BF16)


def spread(rows, width, lanes_each):
    pick = (iota((32, width), 1) // lanes_each) == (iota((32, width), 0) & 7)
    return mm_tn(split3(rows), pick.astype(F32).astype(BF16))


def decay_terms(dt_block, dt_bias, rate, start_row, start_col, base):
    dt_rows = jnp.transpose(dt_block)[:8] + dt_bias
    step = jnp.maximum(dt_rows, 0.0) + jnp.log1p(jnp.exp(-jnp.abs(dt_rows)))
    log_decay = -step * rate
    row = iota((BLOCK, BLOCK), 0) + base
    col = iota((BLOCK, BLOCK), 1) + base
    linked = (col <= row) & (col >= start_col)
    linked_low = jnp.where(linked, 1.0, 0.0).astype(BF16)
    cum = mm_nt(split3(log_decay), linked_low)
    cum = cum[0:8] + cum[8:16] + cum[16:24]
    enter = jnp.exp(jnp.where(start_row < base, cum, NEG))
    last = cum[:, BLOCK - 1 :]
    position = iota((8, BLOCK), 1) + base
    tail = jnp.exp(jnp.where(position >= start_row[:, BLOCK - 1 :], last - cum, NEG))
    return dt_rows, step, log_decay, linked, linked_low, cum, enter, tail


def conv_sum(ext_ref, taps, bias, place):
    total = bias + taps[KW - 1 : KW] * ext_ref[pl.ds(8, BLOCK), :]
    for offset in range(1, KW):
        shifted = ext_ref[pl.ds(8 - offset, BLOCK), :]
        total = total + jnp.where(place >= offset, taps[KW - 1 - offset : KW - offset] * shifted, 0.0)
    return total


def wide_place(start_col, base, width):
    place = iota((BLOCK, BLOCK), 0) + base - start_col
    return jnp.concatenate([place] * (width // LANES), axis=1)


def scan_fwd_kernel(
    cols,
    proj_ref,
    startc_ref,
    startr_ref,
    taps_ref,
    bias_ref,
    dtb_ref,
    rate_ref,
    skip_ref,
    y_ref,
    gated_ref,
    state_out_ref,
    ssq_ref,
    state_ref,
    ext_ref,
):
    zat, xat, dat, width = cols
    channels = xat - zat
    heads = channels // PD
    block = pl.program_id(0)
    base = block * BLOCK

    @pl.when(block == 0)
    def _():
        state_ref[...] = jnp.zeros_like(state_ref)
        ext_ref[0:8, :] = jnp.zeros((8, ext_ref.shape[1]), F32)

    start_col = startc_ref[...]
    start_row = startr_ref[...]
    ext_ref[pl.ds(8, BLOCK), :] = proj_ref[:, xat:dat]
    place = wide_place(start_col, base, dat - xat)
    pre = conv_sum(ext_ref, taps_ref[...], bias_ref[...], place)
    ext_ref[0:8, :] = ext_ref[pl.ds(BLOCK, 8), :]
    conv = (pre * sigmoid(pre)).astype(BF16)
    x_low, b_low, c_low = conv[:, :channels], conv[:, channels : channels + NS], conv[:, channels + NS :]
    x_val = x_low.astype(F32)
    _, step, _, linked, _, cum, enter, tail = decay_terms(
        proj_ref[:, dat:width], dtb_ref[...], rate_ref[...], start_row, start_col, base
    )
    contact = mm_nt(c_low, b_low)
    cum_cols = spread(cum, heads * LANES, LANES)
    enter_x = spread(enter, channels, PD)
    weight_x = spread(tail * step, channels, PD)
    low = iota((BLOCK, LANES), 1) < PD
    zero = jnp.zeros((BLOCK, LANES), F32)
    within = []
    for pair in range(heads // 2):
        mixes = []
        for head in (2 * pair, 2 * pair + 1):
            gap = cum_cols[:, head * LANES : (head + 1) * LANES] - cum[head : head + 1]
            decay = jnp.exp(jnp.where(linked, gap, NEG))
            mixes.append((decay * (contact * step[head : head + 1])).astype(BF16))
        x_pair = x_val[:, pair * LANES : (pair + 1) * LANES]
        both = jnp.concatenate([jnp.where(low, x_pair, zero), jnp.where(low, zero, x_pair)], axis=0).astype(BF16)
        within.append(mm(jnp.concatenate(mixes, axis=1), both))
    state = state_ref[...]
    state_low = state.astype(BF16)
    state_out_ref[0] = state_low
    y = jnp.concatenate(within, axis=1) + enter_x * mm(c_low, state_low) + skip_ref[...] * x_val
    y_ref[...] = y
    state_ref[...] = mm_tn(b_low, (weight_x * x_val).astype(BF16)) + enter_x[BLOCK - 1 :] * state
    z = proj_ref[:, zat:xat]
    gated = y * (z * sigmoid(z))
    gated_ref[...] = gated
    square = gated * gated
    high = square.astype(BF16)
    rest = (square - high.astype(F32)).astype(BF16)
    ones = jnp.ones((16, channels), BF16)
    ssq_ref[...] = (mm_nt(ones, high) + mm_nt(ones, rest))[:8]


def scan_bwd_kernel(
    cols,
    proj_ref,
    prev_ref,
    startc_ref,
    startr_ref,
    taps_ref,
    bias_ref,
    dtb_ref,
    rate_ref,
    skip_ref,
    y_ref,
    state_in_ref,
    grad_ref,
    out_ref,
    conv_acc_ref,
    head_acc_ref,
    skip_acc_ref,
    dstate_ref,
    ext_ref,
    dext_ref,
    pext_ref,
):
    zat, xat, dat, width = cols
    channels = xat - zat
    heads = channels // PD
    turn = pl.program_id(0)
    block = pl.num_programs(0) - 1 - turn
    base = block * BLOCK

    @pl.when(turn == 0)
    def _():
        dstate_ref[...] = jnp.zeros_like(dstate_ref)
        conv_acc_ref[...] = jnp.zeros_like(conv_acc_ref)
        head_acc_ref[...] = jnp.zeros_like(head_acc_ref)
        skip_acc_ref[...] = jnp.zeros_like(skip_acc_ref)
        dext_ref[pl.ds(BLOCK, 8), :] = jnp.zeros((8, dext_ref.shape[1]), F32)
        pext_ref[pl.ds(BLOCK, 8), :] = jnp.zeros((8, LANES), jnp.int32)

    start_col = startc_ref[...]
    start_row = startr_ref[...]
    taps = taps_ref[...]
    ext_ref[0:8, :] = prev_ref[:, xat:dat]
    ext_ref[pl.ds(8, BLOCK), :] = proj_ref[:, xat:dat]
    place = wide_place(start_col, base, dat - xat)
    pre = conv_sum(ext_ref, taps, bias_ref[...], place)
    pre_sig = sigmoid(pre)
    conv = (pre * pre_sig).astype(BF16)
    x_low, b_low, c_low = conv[:, :channels], conv[:, channels : channels + NS], conv[:, channels + NS :]
    x_val = x_low.astype(F32)
    rate = rate_ref[...]
    dt_rows, step, log_decay, linked, linked_low, cum, enter, tail = decay_terms(
        proj_ref[:, dat:width], dtb_ref[...], rate, start_row, start_col, base
    )
    contact = mm_nt(c_low, b_low)
    cum_cols = spread(cum, heads * LANES, LANES)
    enter_x = spread(enter, channels, PD)
    weight = tail * step
    weight_x = spread(weight, channels, PD)

    z = proj_ref[:, zat:xat]
    z_sig = sigmoid(z)
    grad = grad_ref[...]
    dy = grad * (z * z_sig)
    out_ref[:, : channels] = (grad * y_ref[...] * (z_sig * (1.0 + z * (1.0 - z_sig)))).astype(BF16)

    low = iota((BLOCK, LANES), 1) < PD
    strict = linked & (iota((BLOCK, BLOCK), 0) > iota((BLOCK, BLOCK), 1))
    zero = jnp.zeros((BLOCK, LANES), F32)
    dcontact = zero
    dx_parts, w_parts, step_rows = [], [], []
    for pair in range(heads // 2):
        lanes = slice(pair * LANES, (pair + 1) * LANES)
        dy_pair = dy[:, lanes]
        dy_both = jnp.concatenate([jnp.where(low, dy_pair, zero), jnp.where(low, zero, dy_pair)], axis=0).astype(BF16)
        outer = mm_nt(dy_both, x_low[:, lanes])
        mixes = []
        for slot in range(2):
            head = 2 * pair + slot
            gap = cum_cols[:, head * LANES : (head + 1) * LANES] - cum[head : head + 1]
            decay = jnp.exp(jnp.where(linked, gap, NEG))
            step_row = step[head : head + 1]
            share = outer[slot * BLOCK : (slot + 1) * BLOCK] * decay
            dcontact = dcontact + share * step_row
            flow = share * contact
            step_rows.append(jnp.sum(flow, axis=0, keepdims=True))
            w_parts.append(jnp.where(strict, flow * step_row, 0.0).astype(BF16))
            mixes.append((decay * (contact * step_row)).astype(BF16))
        dx_parts.append(mm_tn(jnp.concatenate(mixes, axis=0), dy_both))
    pad = [jnp.zeros((8 - heads, BLOCK), F32)] if heads < 8 else []
    dstep = jnp.concatenate(step_rows + pad, axis=0)
    pick_rows = (iota((16, heads * BLOCK), 1) // BLOCK) == iota((16, heads * BLOCK), 0)
    pick_rows = jnp.where(pick_rows, 1.0, 0.0).astype(BF16)
    dcum = mm_nt(pick_rows, jnp.concatenate(w_parts, axis=1))[:8]
    dcum = dcum - mm(pick_rows, jnp.concatenate(w_parts, axis=0))[:8]

    state_low = state_in_ref[0]
    dstate = dstate_ref[...]
    dstate_low = dstate.astype(BF16)
    pick_x = (iota((16, channels), 1) // PD) == iota((16, channels), 0)
    pick_f = jnp.where(pick_x, 1.0, 0.0)
    pick_x = pick_f.astype(BF16)
    from_state = enter_x * mm(c_low, state_low)
    dcum = dcum + mm_nt(pick_x, (dy * from_state).astype(BF16))[:8]
    dye = (enter_x * dy).astype(BF16)
    through = mm(b_low, dstate_low)
    dweight = mm_nt(pick_x, (x_val * through).astype(BF16))[:8]
    wx = (weight_x * x_val).astype(BF16)
    kept_x = enter_x[BLOCK - 1 :]
    dkept = jnp.sum(dstate * state_low.astype(F32), axis=0, keepdims=True) * kept_x
    dkept = jnp.sum(pick_f[:8] * dkept, axis=1, keepdims=True)
    moved = dweight * weight
    lane = iota((8, BLOCK), 1)
    dlast = jnp.sum(moved, axis=1, keepdims=True) + dkept
    dcum = dcum - moved + jnp.where(lane == BLOCK - 1, dlast, 0.0)
    dstep = dstep + dweight * tail
    dc = mm_nt(dye, state_low)
    db = mm_nt(wx, dstate_low)
    dstate_ref[...] = mm_tn(c_low, dye) + kept_x * dstate
    dcontact_low = dcontact.astype(BF16)
    dc = dc + mm(dcontact_low, b_low)
    db = db + mm_tn(dcontact_low, c_low)
    dx = jnp.concatenate(dx_parts, axis=1) + weight_x * through + skip_ref[...] * dy

    dlog = mm(split3(dcum), linked_low)
    dlog = dlog[0:8] + dlog[8:16] + dlog[16:24]
    dstep = dstep - dlog * rate
    ddt = dstep * sigmoid(dt_rows)
    head_acc_ref[0:8, :] += ddt
    head_acc_ref[8:16, :] += dlog * log_decay
    skip_acc_ref[0:1, :] += jnp.sum(dy * x_val, axis=0, keepdims=True)
    ddt_cols = jnp.transpose(jnp.concatenate([ddt, jnp.zeros((BLOCK - 8, BLOCK), F32)], axis=0))
    out_ref[:, dat - zat : width - zat] = ddt_cols.astype(BF16)

    dpre = jnp.concatenate([dx, db, dc], axis=1) * (pre_sig * (1.0 + pre * (1.0 - pre_sig)))
    conv_acc_ref[KW : KW + 1, :] += jnp.sum(dpre, axis=0, keepdims=True)
    dext_ref[0:BLOCK, :] = dpre
    pext_ref[0:BLOCK, :] = iota((BLOCK, BLOCK), 0) + base - start_col
    draw = taps[KW - 1 : KW] * dpre
    conv_acc_ref[KW - 1 : KW, :] += jnp.sum(dpre * ext_ref[pl.ds(8, BLOCK), :], axis=0, keepdims=True)
    for offset in range(1, KW):
        tap = KW - 1 - offset
        kept = jnp.where(place >= offset, dpre * ext_ref[pl.ds(8 - offset, BLOCK), :], 0.0)
        conv_acc_ref[tap : tap + 1, :] += jnp.sum(kept, axis=0, keepdims=True)
        later = pext_ref[pl.ds(offset, BLOCK), :]
        later = jnp.concatenate([later] * ((dat - xat) // LANES), axis=1)
        draw = draw + jnp.where(later >= offset, taps[tap : tap + 1] * dext_ref[pl.ds(offset, BLOCK), :], 0.0)
    dext_ref[pl.ds(BLOCK, 8), :] = dext_ref[0:8, :]
    pext_ref[pl.ds(BLOCK, 8), :] = pext_ref[0:8, :]
    out_ref[:, xat - zat : dat - zat] = draw.astype(BF16)


def scan_specs(cols, turn):
    zat, xat, dat, width = cols
    channels = xat - zat
    conv_width = dat - xat
    fixed = lambda shape: pl.BlockSpec(shape, lambda c: (0,) * len(shape))
    params = [
        fixed((8, conv_width)),
        fixed((1, conv_width)),
        fixed((8, LANES)),
        fixed((8, LANES)),
        fixed((1, channels)),
    ]
    starts = [
        pl.BlockSpec((BLOCK, LANES), lambda c: (turn(c), 0)),
        pl.BlockSpec((8, BLOCK), lambda c: (0, turn(c))),
    ]
    return starts, params


def scan_forward(cols, proj, start_col, start_row, params):
    zat, xat, dat, width = cols
    channels = xat - zat
    length = proj.shape[0]
    blocks = length // BLOCK
    starts, param_specs = scan_specs(cols, lambda c: c)
    body = lambda *refs: scan_fwd_kernel(cols, *refs)
    return pl.pallas_call(
        body,
        grid=(blocks,),
        in_specs=[pl.BlockSpec((BLOCK, width), lambda c: (c, 0))] + starts + param_specs,
        out_specs=[
            pl.BlockSpec((BLOCK, channels), lambda c: (c, 0)),
            pl.BlockSpec((BLOCK, channels), lambda c: (c, 0)),
            pl.BlockSpec((1, NS, channels), lambda c: (c, 0, 0)),
            pl.BlockSpec((8, BLOCK), lambda c: (0, c)),
        ],
        out_shape=[
            jax.ShapeDtypeStruct((length, channels), F32),
            jax.ShapeDtypeStruct((length, channels), F32),
            jax.ShapeDtypeStruct((blocks, NS, channels), BF16),
            jax.ShapeDtypeStruct((8, length), F32),
        ],
        scratch_shapes=[
            pltpu.VMEM((NS, channels), F32),
            pltpu.VMEM((BLOCK + 8, dat - xat), F32),
        ],
        compiler_params=pltpu.CompilerParams(vmem_limit_bytes=VMEM_LIMIT),
        cost_estimate=pl.CostEstimate(flops=2 * 10**9, bytes_accessed=10**7, transcendentals=2 * 10**6),
        name="scan_fwd",
    )(proj, start_col, start_row, *params)


def scan_backward(cols, proj, start_col, start_row, params, y, states, grad):
    zat, xat, dat, width = cols
    channels = xat - zat
    length = proj.shape[0]
    blocks = length // BLOCK
    turn = lambda c: blocks - 1 - c
    starts, param_specs = scan_specs(cols, turn)
    body = lambda *refs: scan_bwd_kernel(cols, *refs)
    tall = BLOCK // 8
    return pl.pallas_call(
        body,
        grid=(blocks,),
        in_specs=[
            pl.BlockSpec((BLOCK, width), lambda c: (turn(c), 0)),
            pl.BlockSpec((8, width), lambda c: (jnp.maximum(turn(c) * tall - 1, 0), 0)),
        ]
        + starts
        + param_specs
        + [
            pl.BlockSpec((BLOCK, channels), lambda c: (turn(c), 0)),
            pl.BlockSpec((1, NS, channels), lambda c: (turn(c), 0, 0)),
            pl.BlockSpec((BLOCK, channels), lambda c: (turn(c), 0)),
        ],
        out_specs=[
            pl.BlockSpec((BLOCK, width - zat), lambda c: (turn(c), 0)),
            pl.BlockSpec((8, dat - xat), lambda c: (0, 0)),
            pl.BlockSpec((16, LANES), lambda c: (0, 0)),
            pl.BlockSpec((8, channels), lambda c: (0, 0)),
        ],
        out_shape=[
            jax.ShapeDtypeStruct((length, width - zat), BF16),
            jax.ShapeDtypeStruct((8, dat - xat), F32),
            jax.ShapeDtypeStruct((16, LANES), F32),
            jax.ShapeDtypeStruct((8, channels), F32),
        ],
        scratch_shapes=[
            pltpu.VMEM((NS, channels), F32),
            pltpu.VMEM((BLOCK + 8, dat - xat), F32),
            pltpu.VMEM((BLOCK + 8, dat - xat), F32),
            pltpu.VMEM((BLOCK + 8, LANES), jnp.int32),
        ],
        compiler_params=pltpu.CompilerParams(vmem_limit_bytes=VMEM_LIMIT),
        cost_estimate=pl.CostEstimate(flops=6 * 10**9, bytes_accessed=2 * 10**7, transcendentals=3 * 10**6),
        name="scan_bwd",
    )(proj, proj, start_col, start_row, *params, y, states, grad)


def pack_kernel(cols, place_ref, q_ref, kv_ref, z_ref, x_ref, bc_ref, dt_ref, norms_ref, att_ref, mix_ref, gate_ref, up_ref, down_ref, mixer_ref, ffn_ref):
    zat, xat, dat, width = cols
    own = q_ref.shape[0]
    qwidth = q_ref.shape[1]
    channels = xat - zat
    hidden = gate_ref.shape[1]
    eye = jnp.where(iota((own, own), 0) == iota((own, own), 1), 1.0, 0.0).astype(BF16)
    turned = lambda ref: mm_nt(eye, ref[...]).astype(BF16)
    mixer_ref[:, :qwidth] = q_ref[...]
    kv = kv_ref[...].astype(F32)
    keys, vals = kv[:, :LANES], kv[:, LANES:]
    first = place_ref[0] == 0
    keys = jnp.where(first, keys, pltpu.roll(keys, HD, 1))
    vals = jnp.where(first, pltpu.roll(vals, HD, 1), vals)
    mixer_ref[:, qwidth:zat] = jnp.where(iota((own, LANES), 1) < HD, keys, vals).astype(BF16)
    mixer_ref[:, zat:xat] = z_ref[...]
    mixer_ref[:, xat : xat + channels] = x_ref[...]
    mixer_ref[:, xat + channels : dat] = bc_ref[...]
    mixer_ref[:, dat:width] = turned(norms_ref)
    mixer_ref[:, dat : dat + dt_ref.shape[1]] = dt_ref[...]
    mixer_ref[:, width : width + qwidth] = turned(att_ref)
    mixer_ref[:, width + qwidth :] = turned(mix_ref)
    ffn_ref[:, :hidden] = gate_ref[...]
    ffn_ref[:, hidden : 2 * hidden] = up_ref[...]
    ffn_ref[:, 2 * hidden :] = turned(down_ref)


def pack_weights(cols, kv_head, *shards):
    own = shards[0].shape[0]
    zat, xat, dat, width = cols
    body = lambda *refs: pack_kernel(cols, *refs)
    whole = pl.BlockSpec(memory_space=pltpu.VMEM)
    return pl.pallas_call(
        body,
        in_specs=[pl.BlockSpec(memory_space=pltpu.SMEM)] + [whole] * len(shards),
        out_specs=[whole] * 2,
        out_shape=[
            jax.ShapeDtypeStruct((own, width + shards[0].shape[1] + xat - zat), BF16),
            jax.ShapeDtypeStruct((own, 3 * shards[-1].shape[0]), BF16),
        ],
        compiler_params=pltpu.CompilerParams(vmem_limit_bytes=VMEM_LIMIT),
        cost_estimate=pl.CostEstimate(flops=10**7, bytes_accessed=2 * 10**6, transcendentals=0),
        name="pack_weights",
    )(kv_head, *shards)


def norm_kernel(parts, rank_ref, *refs):
    gain_ref, out_ref = refs[parts], refs[parts + 1]
    rows = refs[0].shape[0]
    gain = gain_ref[...]
    for shift in range(parts):
        values = refs[shift][...].astype(F32)
        spot = lax.rem(rank_ref[0] + (parts - shift), parts) * rows
        out_ref[pl.ds(pl.multiple_of(spot, rows), rows), :] = (values * rms_scale(values) * gain).astype(BF16)


def norm_rows(rank, pieces, gain):
    parts = len(pieces)
    rows, model = pieces[0].shape
    body = lambda *refs: norm_kernel(parts, *refs)
    whole = pl.BlockSpec(memory_space=pltpu.VMEM)
    return pl.pallas_call(
        body,
        in_specs=[pl.BlockSpec(memory_space=pltpu.SMEM)] + [whole] * (parts + 1),
        out_specs=whole,
        out_shape=jax.ShapeDtypeStruct((parts * rows, model), BF16),
        compiler_params=pltpu.CompilerParams(vmem_limit_bytes=VMEM_LIMIT),
        cost_estimate=pl.CostEstimate(flops=10**7, bytes_accessed=4 * 10**6, transcendentals=0),
        name="norm_rows",
    )(rank, *pieces, gain)


def ffn_kernel(middle_ref, cot_ref, gain_ref, w_ref, out_ref, gmid_ref, ggain_ref, gw_ref, low_ref, sum_ref, gsum_ref):
    step = pl.program_id(0)
    hidden = w_ref.shape[1] // 3

    @pl.when(step == 0)
    def _():
        middle = middle_ref[...]
        low_ref[...] = (middle * rms_scale(middle) * gain_ref[...]).astype(BF16)
        sum_ref[...] = jnp.zeros_like(sum_ref)
        gsum_ref[...] = jnp.zeros_like(gsum_ref)

    low = low_ref[...]
    cot = cot_ref[...]
    gate_pre = mm(low, w_ref[:, :hidden])
    up_pre = mm(low, w_ref[:, hidden : 2 * hidden])
    sig = sigmoid(gate_pre)
    silu_gate = gate_pre * sig
    act = (silu_gate * up_pre).astype(BF16)
    sum_ref[...] += mm_nt(act, w_ref[:, 2 * hidden :])
    gw_ref[:, 2 * hidden :] = mm_tn(cot, act).astype(BF16)
    grad_hidden = mm(cot, w_ref[:, 2 * hidden :])
    grad_gate = (grad_hidden * up_pre * sig * (1.0 + gate_pre * (1.0 - sig))).astype(BF16)
    grad_up = (grad_hidden * silu_gate).astype(BF16)
    gw_ref[:, :hidden] = mm_tn(low, grad_gate).astype(BF16)
    gw_ref[:, hidden : 2 * hidden] = mm_tn(low, grad_up).astype(BF16)
    gsum_ref[...] += mm_nt(grad_gate, w_ref[:, :hidden]) + mm_nt(grad_up, w_ref[:, hidden : 2 * hidden])

    @pl.when(step == pl.num_programs(0) - 1)
    def _():
        middle = middle_ref[...]
        out_ref[...] = (middle + sum_ref[...]).astype(BF16)
        scale = rms_scale(middle)
        normed = middle * scale
        grad_two = gsum_ref[...]
        ggain_ref[...] = jnp.broadcast_to(jnp.sum(grad_two * normed, axis=0, keepdims=True), ggain_ref.shape)
        gmid_ref[...] = cot_ref[...].astype(F32) + norm_back(grad_two * gain_ref[...], normed, scale)


def ffn_both(middle, cotangent, gain, ffn_w, parts):
    rows, model = middle.shape
    piece = ffn_w.shape[1] // parts
    rowspec = pl.BlockSpec((rows, model), lambda s: (0, 0))
    wspec = pl.BlockSpec((model, piece), lambda s: (0, s))
    return pl.pallas_call(
        ffn_kernel,
        grid=(parts,),
        in_specs=[rowspec, rowspec, pl.BlockSpec((1, model), lambda s: (0, 0)), wspec],
        out_specs=[rowspec, rowspec, pl.BlockSpec((8, model), lambda s: (0, 0)), wspec],
        out_shape=[
            jax.ShapeDtypeStruct((rows, model), BF16),
            jax.ShapeDtypeStruct((rows, model), F32),
            jax.ShapeDtypeStruct((8, model), F32),
            jax.ShapeDtypeStruct(ffn_w.shape, BF16),
        ],
        scratch_shapes=[
            pltpu.VMEM((rows, model), BF16),
            pltpu.VMEM((rows, model), F32),
            pltpu.VMEM((rows, model), F32),
        ],
        compiler_params=pltpu.CompilerParams(vmem_limit_bytes=VMEM_LIMIT),
        cost_estimate=pl.CostEstimate(flops=10**10, bytes_accessed=3 * 10**7, transcendentals=10**6),
        name="ffn_both",
    )(middle, cotangent, gain, ffn_w)


def lane_rows(values, rows):
    padded = jnp.pad(values, (0, rows - values.shape[0]))
    return jnp.broadcast_to(padded[:, None], (rows, LANES))


def shifted(values, axis, size, shift):
    return lax.ppermute(values, axis, [(i, (i + shift) % size) for i in range(size)])


def pieces_of_group(values, parts):
    return [values] + [shifted(values, "tensor", parts, shift) for shift in range(1, parts)]


def in_order(pieces, rank):
    parts, rows = len(pieces), pieces[0].shape[0]
    line = jnp.concatenate(pieces[:0:-1] + pieces[:1] + pieces[:0:-1], axis=0)
    return lax.dynamic_slice(line, ((parts - 1 - rank) * rows, 0), (parts * rows, line.shape[1]))


def rows_of(values, rank, shift, parts):
    rows = values.shape[0] // parts
    return lax.dynamic_slice(values, (lax.rem(rank + shift, parts) * rows, 0), (rows, values.shape[1]))


def group_total(values, parts):
    total = values.astype(F32)
    for shift in range(1, parts):
        total = total + shifted(values, "tensor", parts, shift).astype(F32)
    return total


def butterfly(values, axis, size):
    if size & (size - 1):
        return lax.psum(values, axis)
    step = 1
    while step < size:
        values = values + lax.ppermute(values, axis, [(i, i ^ step) for i in range(size)])
        step *= 2
    return values


def local(
    x_in,
    cotangent,
    segments,
    norm_one,
    w_query,
    w_keyval,
    w_attn_out,
    w_zgate,
    w_xin,
    w_bcin,
    w_dtin,
    conv_x,
    conv_bc,
    bias_x,
    bias_bc,
    dt_bias,
    a_log,
    d_skip,
    ssm_gain,
    w_mix_out,
    norm_two,
    w_gate,
    w_up,
    w_down,
):
    parts = lax.axis_size("tensor")
    rank = lax.axis_index("tensor")
    own = w_query.shape[0]
    length = segments.shape[1]
    qwidth = w_query.shape[1]
    channels = w_zgate.shape[1]
    heads = w_dtin.shape[1]
    hidden_own = w_gate.shape[1]
    width_ssm = MH * PD
    kv_head = (rank * (qwidth // HD)) // (QH // KVH)
    zat = 2 * qwidth
    xat = zat + channels
    bat = xat + channels
    dat = bat + 2 * NS
    width = dat + LANES
    cols = (zat, xat, dat, width)

    norms = jnp.zeros((LANES, own), BF16).at[HD].set(norm_one).at[HD + 1].set(norm_two)
    x_pieces = pieces_of_group(x_in, parts)
    mixer_own, ffn_own = pack_weights(
        cols,
        kv_head.astype(jnp.int32)[None],
        w_query,
        w_keyval,
        w_zgate,
        w_xin,
        w_bcin,
        w_dtin,
        norms,
        w_attn_out,
        w_mix_out,
        w_gate,
        w_up,
        w_down,
    )
    mixer_w = lax.all_gather(mixer_own, "dp", axis=0, tiled=True)
    proj_w = mixer_w[:, :width]
    out_w = mixer_w[:, width:]
    gain_one = mixer_w[:, dat + HD].astype(F32)[None, :]
    gain_two = mixer_w[:, dat + HD + 1].astype(F32)[None, :]
    ffn_own = jnp.concatenate(pieces_of_group(ffn_own, parts), axis=1)
    ffn_w = lax.all_gather(ffn_own, "dp", axis=0, tiled=True)

    seg = segments[0]
    start = jnp.sum((seg[None, :] < seg[:, None]).astype(jnp.int32), axis=1)
    start_col = jnp.broadcast_to(start[:, None], (length, LANES))
    start_row = jnp.broadcast_to(start[None, :], (8, length))
    cosine, sine = rope_tables(length)
    taps = jnp.pad(jnp.concatenate([conv_x, conv_bc], axis=1), ((0, 8 - KW), (0, 0)))
    bias = jnp.concatenate([bias_x, bias_bc])[None, :]
    params = (taps, bias, lane_rows(dt_bias, 8), lane_rows(jnp.exp(a_log), 8), jnp.repeat(d_skip, PD)[None, :])

    residual = x_in.astype(F32)
    scale_one = rms_scale(residual)
    normed_one = residual * scale_one
    rows_one = norm_rows(rank.astype(jnp.int32)[None], x_pieces, gain_one)
    proj = mm(rows_one, proj_w)
    y, gated, states, squares = scan_forward(cols, proj, start_col, start_row, params)
    attended, lse, low_q, low_kv = attn_forward(proj, cosine, sine, start_col)
    scale_ssm = lax.rsqrt(group_total(squares[:1], parts)[0] / width_ssm + EPSILON)[:, None]
    normed_ssm = gated * scale_ssm
    mixed = (normed_ssm * ssm_gain[None, :]).astype(BF16)
    att_mixed = jnp.concatenate([attended, mixed], axis=1)
    middle = residual
    for shift in range(parts):
        term = mm_nt(rows_of(att_mixed, rank, shift, parts), out_w)
        middle = middle + (shifted(term.astype(BF16), "tensor", parts, shift).astype(F32) if shift else term)
    block_out, grad_middle, grad_gain_two, grad_ffn_w = ffn_both(middle, cotangent, gain_two, ffn_w, parts)

    grad_branch = in_order(pieces_of_group(grad_middle.astype(BF16), parts), rank)
    grad_ffn_own = lax.psum_scatter(grad_ffn_w, "dp", scatter_dimension=0, tiled=True)
    piece = grad_ffn_own.shape[1] // parts
    grad_ffn = 0.0
    for shift in range(parts):
        term = grad_ffn_own[:, shift * piece : (shift + 1) * piece]
        grad_ffn = grad_ffn + (shifted(term, "tensor", parts, -shift) if shift else term).astype(F32)
    grad_am = mm(grad_branch, out_w)
    grad_att = grad_am[:, :qwidth].astype(BF16)
    grad_mixed = grad_am[:, qwidth:]
    grad_out_w = mm_tn(grad_branch, att_mixed)
    grad_gain_ssm = jnp.sum(grad_mixed * normed_ssm, axis=0)
    grad_normed = grad_mixed * ssm_gain[None, :]
    row_inner = group_total(jnp.sum(grad_normed * normed_ssm, axis=-1)[None, :], parts)[0]
    grad_gated = scale_ssm * (grad_normed - normed_ssm * (row_inner / width_ssm)[:, None])
    grad_q, grad_kv = attn_backward(low_q, low_kv, lse, attended, grad_att, cosine, sine, start_col)
    grad_rest, conv_acc, head_acc, skip_acc = scan_backward(
        cols, proj, start_col, start_row, params, y, states, grad_gated
    )
    grad_proj = jnp.concatenate([grad_q, grad_kv, grad_rest], axis=1)
    grad_one, grad_gain_one = 0.0, 0.0
    for shift in range(parts):
        term = mm_nt(rows_of(grad_proj, rank, shift, parts), proj_w)
        grad_gain_one = grad_gain_one + jnp.sum(
            term * rows_of(rows_one, rank, shift, parts).astype(F32), axis=0, keepdims=True
        )
        grad_one = grad_one + (shifted(term.astype(BF16), "tensor", parts, shift).astype(F32) if shift else term)
    grad_gain_one = grad_gain_one / gain_one
    grad_input = grad_middle + norm_back(grad_one * gain_one, normed_one, scale_one)
    grad_mixer_w = jnp.concatenate([mm_tn(rows_one, grad_proj), grad_out_w], axis=1).astype(BF16)
    grad_w = lax.psum_scatter(grad_mixer_w, "dp", scatter_dimension=0, tiled=True).astype(F32)

    model = x_in.shape[1]
    wide = lambda rows: jnp.pad(rows, ((0, 0), (0, model - rows.shape[1])))
    head_sums = jnp.sum(head_acc, axis=1)[None, :]
    small = jnp.concatenate(
        [
            wide(conv_acc),
            grad_gain_one,
            grad_gain_two[:1],
            wide(grad_gain_ssm[None, :]),
            wide(skip_acc[:1]),
            wide(head_sums),
            jnp.zeros((3, model), F32),
        ],
        axis=0,
    )
    small = butterfly(small, "dp", lax.axis_size("dp"))
    shared_small = butterfly(small, "tensor", parts)
    grad_conv_x = small[:KW, :channels]
    grad_bias_x = small[KW, :channels]
    grad_ssm_gain = small[10, :channels]
    grad_d_skip = jnp.sum(small[11, :channels].reshape(heads, PD), axis=1)
    grad_dt_bias = small[12, :heads]
    grad_a_log = small[12, 8 : 8 + heads]
    grad_conv_bc = shared_small[:KW, channels : channels + 2 * NS]
    grad_bias_bc = shared_small[KW, channels : channels + 2 * NS]
    place = lax.axis_index("dp") * own
    norm_grads = lax.dynamic_slice(shared_small, (8, place), (2, own))
    grad_norm_one, grad_norm_two = norm_grads[0], norm_grads[1]

    grad_keyval = jnp.zeros((own, 2 * KVH * HD), F32)
    grad_keyval = lax.dynamic_update_slice(grad_keyval, grad_w[:, qwidth : qwidth + HD], (0, kv_head * HD))
    grad_keyval = lax.dynamic_update_slice(
        grad_keyval, grad_w[:, qwidth + HD : zat], (0, (KVH + kv_head) * HD)
    )
    shared = jnp.concatenate([grad_keyval, grad_w[:, bat:dat]], axis=1)
    shared = group_total(shared.astype(BF16), parts)

    return (
        block_out,
        grad_input,
        grad_norm_one,
        grad_w[:, :qwidth],
        shared[:, : 2 * KVH * HD],
        grad_w[:, width : width + qwidth].T,
        grad_w[:, zat:xat],
        grad_w[:, xat:bat],
        shared[:, 2 * KVH * HD :],
        grad_w[:, dat : dat + heads],
        grad_conv_x,
        grad_conv_bc,
        grad_bias_x,
        grad_bias_bc,
        grad_dt_bias,
        grad_a_log,
        grad_d_skip,
        grad_ssm_gain,
        grad_w[:, width + qwidth :].T,
        grad_norm_two,
        grad_ffn[:, :hidden_own],
        grad_ffn[:, hidden_own : 2 * hidden_own],
        grad_ffn[:, 2 * hidden_own :].T,
    )


def solution(mesh):
    return jax.shard_map(
        local,
        mesh=mesh,
        in_specs=(
            P(("dp", "tensor"), None),
            P(("dp", "tensor"), None),
            P("dp", None),
            P("dp"),
            P("dp", "tensor"),
            P("dp", None),
            P("tensor", "dp"),
            P("dp", "tensor"),
            P("dp", "tensor"),
            P("dp", None),
            P("dp", "tensor"),
            P(None, "tensor"),
            P(),
            P("tensor"),
            P(),
            P("tensor"),
            P("tensor"),
            P("tensor"),
            P("tensor"),
            P("tensor", "dp"),
            P("dp"),
            P("dp", "tensor"),
            P("dp", "tensor"),
            P("tensor", "dp"),
        ),
        out_specs=(
            P(("dp", "tensor"), None),
            P(("dp", "tensor"), None),
            P("dp"),
            P("dp", "tensor"),
            P("dp", None),
            P("tensor", "dp"),
            P("dp", "tensor"),
            P("dp", "tensor"),
            P("dp", None),
            P("dp", "tensor"),
            P(None, "tensor"),
            P(),
            P("tensor"),
            P(),
            P("tensor"),
            P("tensor"),
            P("tensor"),
            P("tensor"),
            P("tensor", "dp"),
            P("dp"),
            P("dp", "tensor"),
            P("dp", "tensor"),
            P("tensor", "dp"),
        ),
        check_vma=False,
    )
```

```python
import math

import jax
import jax.numpy as jnp
import numpy as np
from jax import lax
from jax.experimental import pallas as pl
from jax.experimental.pallas import tpu as pltpu
from jax.sharding import PartitionSpec as P

QH = 8
KVH = 2
HD = 64
MH = 24
PD = 64
NS = 128
KW = 4
BLOCK = 128
LANES = 128

EPSILON = 1e-05
ROPE_BASE = 100000000000.0
NEG = -1e9
F32 = jnp.float32
BF16 = jnp.bfloat16
VMEM_LIMIT = 48 * 1024 * 1024


def mm(lhs, rhs):
    return lax.dot_general(lhs, rhs, (((1,), (0,)), ((), ())), preferred_element_type=F32)


def mm_nt(lhs, rhs):
    return lax.dot_general(lhs, rhs, (((1,), (1,)), ((), ())), preferred_element_type=F32)


def mm_tn(lhs, rhs):
    return lax.dot_general(lhs, rhs, (((0,), (0,)), ((), ())), preferred_element_type=F32)


def rms_scale(values):
    return lax.rsqrt(jnp.mean(values * values, axis=-1, keepdims=True) + EPSILON)


def norm_back(grad_normed, normed, scale):
    return scale * (grad_normed - normed * jnp.mean(grad_normed * normed, axis=-1, keepdims=True))


def sigmoid(v):
    return 1.0 / (1.0 + jnp.exp(-v))


def iota(shape, dim):
    return lax.broadcasted_iota(jnp.int32, shape, dim)


def rope_tables(length):
    half = HD // 2
    freqs = np.float32(ROPE_BASE) ** (-(np.arange(half, dtype=np.float32) * np.float32(2.0 / HD)))
    angles = np.arange(length, dtype=np.float32)[:, None] * freqs.astype(np.float32)[None, :]
    cosine, sine = np.cos(angles).astype(np.float32), np.sin(angles).astype(np.float32)
    cos_lanes = np.concatenate([cosine] * 4, axis=1)
    sin_lanes = np.concatenate([-sine, sine, -sine, sine], axis=1)
    return jnp.asarray(cos_lanes), jnp.asarray(sin_lanes)


def swap_halves(values):
    lane = iota(values.shape, 1)
    ahead = pltpu.roll(values, LANES - HD // 2, 1)
    behind = pltpu.roll(values, HD // 2, 1)
    return jnp.where((lane & (HD - 1)) < HD // 2, ahead, behind)


def pair_rows(block):
    low = iota(block.shape, 1) < HD
    zero = jnp.zeros_like(block)
    return jnp.concatenate([jnp.where(low, block, zero), jnp.where(low, zero, block)], axis=0)


def attn_fwd_kernel(q_ref, kv_ref, cos_ref, sin_ref, start_ref, out_ref, lse_ref, lq_ref, lkv_ref):
    length = q_ref.shape[0]
    rows = 256
    cosine, sine = cos_ref[...], sin_ref[...]
    low = iota((length, LANES), 1) < HD
    queries = q_ref[...]
    lq_ref[...] = (queries * cosine + swap_halves(queries) * sine).astype(BF16)
    kv = kv_ref[...]
    kv = jnp.where(low, kv * cosine + swap_halves(kv) * sine, kv)
    lkv_ref[...] = kv.astype(BF16)
    other = pltpu.roll(kv, HD, 1)
    keys = jnp.where(low, kv, other).astype(BF16)
    vals = jnp.where(low, other, kv).astype(BF16)
    half = iota((rows, LANES), 1) < HD
    for step in range(length // rows):
        end = (step + 1) * rows
        span = slice(step * rows, end)
        stacked = pair_rows(lq_ref[span, :].astype(F32)).astype(BF16)
        scores = mm_nt(stacked, keys[:end]) * (1.0 / math.sqrt(HD))
        first = start_ref[span, :][:, :1]
        col = iota((rows, end), 1)
        row = iota((rows, end), 0) + step * rows
        allowed = (col <= row) & (col >= first)
        allowed = jnp.concatenate([allowed.astype(jnp.int32)] * 2, axis=0) > 0
        scores = jnp.where(allowed, scores, NEG)
        top = jnp.max(scores, axis=1, keepdims=True)
        expo = jnp.exp(scores - top)
        total = jnp.sum(expo, axis=1, keepdims=True)
        probs = (expo * (1.0 / total)).astype(BF16)
        result = mm(probs, vals[:end])
        out_ref[span, :] = jnp.where(half, result[:rows], result[rows:]).astype(BF16)
        lse = top + jnp.log(total)
        lse_ref[span, :] = jnp.where(half, lse[:rows], lse[rows:])


def attn_bwd_kernel(
    lq_ref, lkv_ref, lse_ref, out_ref, go_ref, cos_ref, sin_ref, start_ref, gq_ref, gkv_ref, dk_ref, dv_ref
):
    length = lq_ref.shape[0]
    rows = 256
    cosine, sine = cos_ref[...], sin_ref[...]
    low = iota((length, LANES), 1) < HD
    kv = lkv_ref[...].astype(F32)
    other = pltpu.roll(kv, HD, 1)
    keys = jnp.where(low, kv, other).astype(BF16)
    vals = jnp.where(low, other, kv).astype(BF16)
    half = iota((rows, LANES), 1) < HD
    dk_ref[...] = jnp.zeros_like(dk_ref)
    dv_ref[...] = jnp.zeros_like(dv_ref)
    inv = 1.0 / math.sqrt(HD)
    for step in range(length // rows):
        end = (step + 1) * rows
        span = slice(step * rows, end)
        stacked = pair_rows(lq_ref[span, :].astype(F32)).astype(BF16)
        grads = pair_rows(go_ref[span, :].astype(F32))
        outs = out_ref[span, :].astype(F32)
        inner = jnp.sum(grads * jnp.concatenate([outs, outs], axis=0), axis=1, keepdims=True)
        grads = grads.astype(BF16)
        lse = lse_ref[span, :]
        lse = jnp.concatenate([lse[:, :1], lse[:, HD : HD + 1]], axis=0)
        scores = mm_nt(stacked, keys[:end]) * inv
        first = start_ref[span, :][:, :1]
        col = iota((rows, end), 1)
        row = iota((rows, end), 0) + step * rows
        allowed = (col <= row) & (col >= first)
        allowed = jnp.concatenate([allowed.astype(jnp.int32)] * 2, axis=0) > 0
        probs = jnp.exp(jnp.where(allowed, scores, NEG) - lse)
        grad_probs = mm_nt(grads, vals[:end])
        grad_scores = (probs * (grad_probs - inner)).astype(BF16)
        gq = mm(grad_scores, keys[:end]) * inv
        gq = jnp.where(half, gq[:rows], gq[rows:])
        gq_ref[span, :] = (gq * cosine[span] - swap_halves(gq) * sine[span]).astype(BF16)
        dk_ref[:end, :] += mm_tn(grad_scores, stacked)
        dv_ref[:end, :] += mm_tn(probs.astype(BF16), grads)
    dk = dk_ref[...] * inv
    dk = dk + pltpu.roll(dk, HD, 1)
    dk = dk * cosine - swap_halves(dk) * sine
    dv = dv_ref[...]
    dv = dv + pltpu.roll(dv, HD, 1)
    gkv_ref[...] = jnp.where(low, dk, dv).astype(BF16)


def attn_forward(proj, cosine, sine, start_col):
    length = proj.shape[0]
    wide = pl.BlockSpec((length, LANES), lambda i: (0, 0))
    return pl.pallas_call(
        attn_fwd_kernel,
        grid=(1,),
        in_specs=[wide, pl.BlockSpec((length, LANES), lambda i: (0, 1)), wide, wide, wide],
        out_specs=[wide] * 4,
        out_shape=[
            jax.ShapeDtypeStruct((length, LANES), BF16),
            jax.ShapeDtypeStruct((length, LANES), F32),
            jax.ShapeDtypeStruct((length, LANES), BF16),
            jax.ShapeDtypeStruct((length, LANES), BF16),
        ],
        compiler_params=pltpu.CompilerParams(vmem_limit_bytes=VMEM_LIMIT),
        cost_estimate=pl.CostEstimate(flops=10**9, bytes_accessed=6 * 10**6, transcendentals=2 * 10**6),
        name="attn_fwd",
    )(proj, proj, cosine, sine, start_col)


def attn_backward(low_q, low_kv, lse, out, grad_out, cosine, sine, start_col):
    length = low_q.shape[0]
    wide = pl.BlockSpec((length, LANES), lambda i: (0, 0))
    return pl.pallas_call(
        attn_bwd_kernel,
        grid=(1,),
        in_specs=[wide] * 8,
        out_specs=[wide] * 2,
        out_shape=[jax.ShapeDtypeStruct((length, LANES), BF16)] * 2,
        scratch_shapes=[pltpu.VMEM((length, LANES), F32)] * 2,
        compiler_params=pltpu.CompilerParams(vmem_limit_bytes=VMEM_LIMIT),
        cost_estimate=pl.CostEstimate(flops=3 * 10**9, bytes_accessed=6 * 10**6, transcendentals=2 * 10**6),
        name="attn_bwd",
    )(low_q, low_kv, lse, out, grad_out, cosine, sine, start_col)


def split3(values):
    high = values.astype(BF16).astype(F32)
    rest = values - high
    mid = rest.astype(BF16).astype(F32)
    tail = rest - mid
    return jnp.concatenate([high, mid, tail, jnp.zeros_like(values)], axis=0).astype(BF16)


def spread(rows, width, lanes_each):
    pick = (iota((32, width), 1) // lanes_each) == (iota((32, width), 0) & 7)
    return mm_tn(split3(rows), pick.astype(F32).astype(BF16))


def decay_terms(dt_block, dt_bias, rate, start_row, start_col, base):
    dt_rows = jnp.transpose(dt_block)[:8] + dt_bias
    step = jnp.maximum(dt_rows, 0.0) + jnp.log1p(jnp.exp(-jnp.abs(dt_rows)))
    log_decay = -step * rate
    row = iota((BLOCK, BLOCK), 0) + base
    col = iota((BLOCK, BLOCK), 1) + base
    linked = (col <= row) & (col >= start_col)
    linked_low = jnp.where(linked, 1.0, 0.0).astype(BF16)
    cum = mm_nt(split3(log_decay), linked_low)
    cum = cum[0:8] + cum[8:16] + cum[16:24]
    enter = jnp.exp(jnp.where(start_row < base, cum, NEG))
    last = cum[:, BLOCK - 1 :]
    position = iota((8, BLOCK), 1) + base
    tail = jnp.exp(jnp.where(position >= start_row[:, BLOCK - 1 :], last - cum, NEG))
    return dt_rows, step, log_decay, linked, linked_low, cum, enter, tail


def conv_sum(ext_ref, taps, bias, place):
    total = bias + taps[KW - 1 : KW] * ext_ref[pl.ds(8, BLOCK), :]
    for offset in range(1, KW):
        shifted = ext_ref[pl.ds(8 - offset, BLOCK), :]
        total = total + jnp.where(place >= offset, taps[KW - 1 - offset : KW - offset] * shifted, 0.0)
    return total


def wide_place(start_col, base, width):
    place = iota((BLOCK, BLOCK), 0) + base - start_col
    return jnp.concatenate([place] * (width // LANES), axis=1)


def scan_fwd_kernel(
    cols,
    proj_ref,
    startc_ref,
    startr_ref,
    taps_ref,
    bias_ref,
    dtb_ref,
    rate_ref,
    skip_ref,
    y_ref,
    gated_ref,
    state_out_ref,
    ssq_ref,
    state_ref,
    ext_ref,
):
    zat, xat, dat, width = cols
    channels = xat - zat
    heads = channels // PD
    block = pl.program_id(0)
    base = block * BLOCK

    @pl.when(block == 0)
    def _():
        state_ref[...] = jnp.zeros_like(state_ref)
        ext_ref[0:8, :] = jnp.zeros((8, ext_ref.shape[1]), F32)

    start_col = startc_ref[...]
    start_row = startr_ref[...]
    ext_ref[pl.ds(8, BLOCK), :] = proj_ref[:, xat:dat]
    place = wide_place(start_col, base, dat - xat)
    pre = conv_sum(ext_ref, taps_ref[...], bias_ref[...], place)
    ext_ref[0:8, :] = ext_ref[pl.ds(BLOCK, 8), :]
    conv = (pre * sigmoid(pre)).astype(BF16)
    x_low, b_low, c_low = conv[:, :channels], conv[:, channels : channels + NS], conv[:, channels + NS :]
    x_val = x_low.astype(F32)
    _, step, _, linked, _, cum, enter, tail = decay_terms(
        proj_ref[:, dat:width], dtb_ref[...], rate_ref[...], start_row, start_col, base
    )
    contact = mm_nt(c_low, b_low)
    cum_cols = spread(cum, heads * LANES, LANES)
    enter_x = spread(enter, channels, PD)
    weight_x = spread(tail * step, channels, PD)
    low = iota((BLOCK, LANES), 1) < PD
    zero = jnp.zeros((BLOCK, LANES), F32)
    within = []
    for pair in range(heads // 2):
        mixes = []
        for head in (2 * pair, 2 * pair + 1):
            gap = cum_cols[:, head * LANES : (head + 1) * LANES] - cum[head : head + 1]
            decay = jnp.exp(jnp.where(linked, gap, NEG))
            mixes.append((decay * (contact * step[head : head + 1])).astype(BF16))
        x_pair = x_val[:, pair * LANES : (pair + 1) * LANES]
        both = jnp.concatenate([jnp.where(low, x_pair, zero), jnp.where(low, zero, x_pair)], axis=0).astype(BF16)
        within.append(mm(jnp.concatenate(mixes, axis=1), both))
    state = state_ref[...]
    state_low = state.astype(BF16)
    state_out_ref[0] = state_low
    y = jnp.concatenate(within, axis=1) + enter_x * mm(c_low, state_low) + skip_ref[...] * x_val
    y_ref[...] = y
    state_ref[...] = mm_tn(b_low, (weight_x * x_val).astype(BF16)) + enter_x[BLOCK - 1 :] * state
    z = proj_ref[:, zat:xat]
    gated = y * (z * sigmoid(z))
    gated_ref[...] = gated
    square = gated * gated
    high = square.astype(BF16)
    rest = (square - high.astype(F32)).astype(BF16)
    ones = jnp.ones((16, channels), BF16)
    ssq_ref[...] = (mm_nt(ones, high) + mm_nt(ones, rest))[:8]


def scan_bwd_kernel(
    cols,
    proj_ref,
    prev_ref,
    startc_ref,
    startr_ref,
    taps_ref,
    bias_ref,
    dtb_ref,
    rate_ref,
    skip_ref,
    y_ref,
    state_in_ref,
    grad_ref,
    stats_ref,
    gain_ref,
    out_ref,
    conv_acc_ref,
    head_acc_ref,
    skip_acc_ref,
    dstate_ref,
    ext_ref,
    dext_ref,
    pext_ref,
):
    zat, xat, dat, width = cols
    channels = xat - zat
    heads = channels // PD
    turn = pl.program_id(0)
    block = pl.num_programs(0) - 1 - turn
    base = block * BLOCK

    @pl.when(turn == 0)
    def _():
        dstate_ref[...] = jnp.zeros_like(dstate_ref)
        conv_acc_ref[...] = jnp.zeros_like(conv_acc_ref)
        head_acc_ref[...] = jnp.zeros_like(head_acc_ref)
        skip_acc_ref[...] = jnp.zeros_like(skip_acc_ref)
        dext_ref[pl.ds(BLOCK, 8), :] = jnp.zeros((8, dext_ref.shape[1]), F32)
        pext_ref[pl.ds(BLOCK, 8), :] = jnp.zeros((8, LANES), jnp.int32)

    start_col = startc_ref[...]
    start_row = startr_ref[...]
    taps = taps_ref[...]
    ext_ref[0:8, :] = prev_ref[:, xat:dat]
    ext_ref[pl.ds(8, BLOCK), :] = proj_ref[:, xat:dat]
    place = wide_place(start_col, base, dat - xat)
    pre = conv_sum(ext_ref, taps, bias_ref[...], place)
    pre_sig = sigmoid(pre)
    conv = (pre * pre_sig).astype(BF16)
    x_low, b_low, c_low = conv[:, :channels], conv[:, channels : channels + NS], conv[:, channels + NS :]
    x_val = x_low.astype(F32)
    rate = rate_ref[...]
    dt_rows, step, log_decay, linked, linked_low, cum, enter, tail = decay_terms(
        proj_ref[:, dat:width], dtb_ref[...], rate, start_row, start_col, base
    )
    contact = mm_nt(c_low, b_low)
    cum_cols = spread(cum, heads * LANES, LANES)
    enter_x = spread(enter, channels, PD)
    weight = tail * step
    weight_x = spread(weight, channels, PD)

    z = proj_ref[:, zat:xat]
    z_sig = sigmoid(z)
    z_silu = z * z_sig
    y_val = y_ref[...]
    stats = spread(stats_ref[...], 2 * channels, channels)
    scale_x, inner_x = stats[:, :channels], stats[:, channels:]
    grad = scale_x * (grad_ref[...] * gain_ref[...] - y_val * z_silu * scale_x * inner_x)
    dy = grad * z_silu
    out_ref[:, :channels] = (grad * y_val * (z_sig * (1.0 + z * (1.0 - z_sig)))).astype(BF16)

    low = iota((BLOCK, LANES), 1) < PD
    strict = linked & (iota((BLOCK, BLOCK), 0) > iota((BLOCK, BLOCK), 1))
    zero = jnp.zeros((BLOCK, LANES), F32)
    dcontact = zero
    dx_parts, w_parts, step_rows = [], [], []
    for pair in range(heads // 2):
        lanes = slice(pair * LANES, (pair + 1) * LANES)
        dy_pair = dy[:, lanes]
        dy_both = jnp.concatenate([jnp.where(low, dy_pair, zero), jnp.where(low, zero, dy_pair)], axis=0).astype(BF16)
        outer = mm_nt(dy_both, x_low[:, lanes])
        mixes = []
        for slot in range(2):
            head = 2 * pair + slot
            gap = cum_cols[:, head * LANES : (head + 1) * LANES] - cum[head : head + 1]
            decay = jnp.exp(jnp.where(linked, gap, NEG))
            step_row = step[head : head + 1]
            share = outer[slot * BLOCK : (slot + 1) * BLOCK] * decay
            dcontact = dcontact + share * step_row
            flow = share * contact
            step_rows.append(jnp.sum(flow, axis=0, keepdims=True))
            w_parts.append(jnp.where(strict, flow * step_row, 0.0).astype(BF16))
            mixes.append((decay * (contact * step_row)).astype(BF16))
        dx_parts.append(mm_tn(jnp.concatenate(mixes, axis=0), dy_both))
    pad = [jnp.zeros((8 - heads, BLOCK), F32)] if heads < 8 else []
    dstep = jnp.concatenate(step_rows + pad, axis=0)
    pick_rows = (iota((16, heads * BLOCK), 1) // BLOCK) == iota((16, heads * BLOCK), 0)
    pick_rows = jnp.where(pick_rows, 1.0, 0.0).astype(BF16)
    dcum = mm_nt(pick_rows, jnp.concatenate(w_parts, axis=1))[:8]
    dcum = dcum - mm(pick_rows, jnp.concatenate(w_parts, axis=0))[:8]

    state_low = state_in_ref[0]
    dstate = dstate_ref[...]
    dstate_low = dstate.astype(BF16)
    pick_x = (iota((16, channels), 1) // PD) == iota((16, channels), 0)
    pick_f = jnp.where(pick_x, 1.0, 0.0)
    pick_x = pick_f.astype(BF16)
    from_state = enter_x * mm(c_low, state_low)
    dcum = dcum + mm_nt(pick_x, (dy * from_state).astype(BF16))[:8]
    dye = (enter_x * dy).astype(BF16)
    through = mm(b_low, dstate_low)
    dweight = mm_nt(pick_x, (x_val * through).astype(BF16))[:8]
    wx = (weight_x * x_val).astype(BF16)
    kept_x = enter_x[BLOCK - 1 :]
    dkept = jnp.sum(dstate * state_low.astype(F32), axis=0, keepdims=True) * kept_x
    dkept = jnp.sum(pick_f[:8] * dkept, axis=1, keepdims=True)
    moved = dweight * weight
    lane = iota((8, BLOCK), 1)
    dlast = jnp.sum(moved, axis=1, keepdims=True) + dkept
    dcum = dcum - moved + jnp.where(lane == BLOCK - 1, dlast, 0.0)
    dstep = dstep + dweight * tail
    dc = mm_nt(dye, state_low)
    db = mm_nt(wx, dstate_low)
    dstate_ref[...] = mm_tn(c_low, dye) + kept_x * dstate
    dcontact_low = dcontact.astype(BF16)
    dc = dc + mm(dcontact_low, b_low)
    db = db + mm_tn(dcontact_low, c_low)
    dx = jnp.concatenate(dx_parts, axis=1) + weight_x * through + skip_ref[...] * dy

    dlog = mm(split3(dcum), linked_low)
    dlog = dlog[0:8] + dlog[8:16] + dlog[16:24]
    dstep = dstep - dlog * rate
    ddt = dstep * sigmoid(dt_rows)
    head_acc_ref[0:8, :] += ddt
    head_acc_ref[8:16, :] += dlog * log_decay
    skip_acc_ref[0:1, :] += jnp.sum(dy * x_val, axis=0, keepdims=True)
    ddt_cols = jnp.transpose(jnp.concatenate([ddt, jnp.zeros((BLOCK - 8, BLOCK), F32)], axis=0))
    out_ref[:, dat - zat : width - zat] = ddt_cols.astype(BF16)

    dpre = jnp.concatenate([dx, db, dc], axis=1) * (pre_sig * (1.0 + pre * (1.0 - pre_sig)))
    conv_acc_ref[KW : KW + 1, :] += jnp.sum(dpre, axis=0, keepdims=True)
    dext_ref[0:BLOCK, :] = dpre
    pext_ref[0:BLOCK, :] = iota((BLOCK, BLOCK), 0) + base - start_col
    draw = taps[KW - 1 : KW] * dpre
    conv_acc_ref[KW - 1 : KW, :] += jnp.sum(dpre * ext_ref[pl.ds(8, BLOCK), :], axis=0, keepdims=True)
    for offset in range(1, KW):
        tap = KW - 1 - offset
        kept = jnp.where(place >= offset, dpre * ext_ref[pl.ds(8 - offset, BLOCK), :], 0.0)
        conv_acc_ref[tap : tap + 1, :] += jnp.sum(kept, axis=0, keepdims=True)
        later = pext_ref[pl.ds(offset, BLOCK), :]
        later = jnp.concatenate([later] * ((dat - xat) // LANES), axis=1)
        draw = draw + jnp.where(later >= offset, taps[tap : tap + 1] * dext_ref[pl.ds(offset, BLOCK), :], 0.0)
    dext_ref[pl.ds(BLOCK, 8), :] = dext_ref[0:8, :]
    pext_ref[pl.ds(BLOCK, 8), :] = pext_ref[0:8, :]
    out_ref[:, xat - zat : dat - zat] = draw.astype(BF16)


def scan_specs(cols, turn):
    zat, xat, dat, width = cols
    channels = xat - zat
    conv_width = dat - xat
    fixed = lambda shape: pl.BlockSpec(shape, lambda c: (0,) * len(shape))
    params = [
        fixed((8, conv_width)),
        fixed((1, conv_width)),
        fixed((8, LANES)),
        fixed((8, LANES)),
        fixed((1, channels)),
    ]
    starts = [
        pl.BlockSpec((BLOCK, LANES), lambda c: (turn(c), 0)),
        pl.BlockSpec((8, BLOCK), lambda c: (0, turn(c))),
    ]
    return starts, params


def scan_forward(cols, proj, start_col, start_row, params):
    zat, xat, dat, width = cols
    channels = xat - zat
    length = proj.shape[0]
    blocks = length // BLOCK
    starts, param_specs = scan_specs(cols, lambda c: c)
    body = lambda *refs: scan_fwd_kernel(cols, *refs)
    return pl.pallas_call(
        body,
        grid=(blocks,),
        in_specs=[pl.BlockSpec((BLOCK, width), lambda c: (c, 0))] + starts + param_specs,
        out_specs=[
            pl.BlockSpec((BLOCK, channels), lambda c: (c, 0)),
            pl.BlockSpec((BLOCK, channels), lambda c: (c, 0)),
            pl.BlockSpec((1, NS, channels), lambda c: (c, 0, 0)),
            pl.BlockSpec((8, BLOCK), lambda c: (0, c)),
        ],
        out_shape=[
            jax.ShapeDtypeStruct((length, channels), F32),
            jax.ShapeDtypeStruct((length, channels), F32),
            jax.ShapeDtypeStruct((blocks, NS, channels), BF16),
            jax.ShapeDtypeStruct((8, length), F32),
        ],
        scratch_shapes=[
            pltpu.VMEM((NS, channels), F32),
            pltpu.VMEM((BLOCK + 8, dat - xat), F32),
        ],
        compiler_params=pltpu.CompilerParams(vmem_limit_bytes=VMEM_LIMIT),
        cost_estimate=pl.CostEstimate(flops=2 * 10**9, bytes_accessed=10**7, transcendentals=2 * 10**6),
        name="scan_fwd",
    )(proj, start_col, start_row, *params)


def scan_backward(cols, proj, start_col, start_row, params, y, states, grad, stats, gain):
    zat, xat, dat, width = cols
    channels = xat - zat
    length = proj.shape[0]
    blocks = length // BLOCK
    turn = lambda c: blocks - 1 - c
    starts, param_specs = scan_specs(cols, turn)
    body = lambda *refs: scan_bwd_kernel(cols, *refs)
    tall = BLOCK // 8
    return pl.pallas_call(
        body,
        grid=(blocks,),
        in_specs=[
            pl.BlockSpec((BLOCK, width), lambda c: (turn(c), 0)),
            pl.BlockSpec((8, width), lambda c: (jnp.maximum(turn(c) * tall - 1, 0), 0)),
        ]
        + starts
        + param_specs
        + [
            pl.BlockSpec((BLOCK, channels), lambda c: (turn(c), 0)),
            pl.BlockSpec((1, NS, channels), lambda c: (turn(c), 0, 0)),
            pl.BlockSpec((BLOCK, channels), lambda c: (turn(c), 0)),
            pl.BlockSpec((8, BLOCK), lambda c: (0, turn(c))),
            pl.BlockSpec((1, channels), lambda c: (0, 0)),
        ],
        out_specs=[
            pl.BlockSpec((BLOCK, width - zat), lambda c: (turn(c), 0)),
            pl.BlockSpec((8, dat - xat), lambda c: (0, 0)),
            pl.BlockSpec((16, LANES), lambda c: (0, 0)),
            pl.BlockSpec((8, channels), lambda c: (0, 0)),
        ],
        out_shape=[
            jax.ShapeDtypeStruct((length, width - zat), BF16),
            jax.ShapeDtypeStruct((8, dat - xat), F32),
            jax.ShapeDtypeStruct((16, LANES), F32),
            jax.ShapeDtypeStruct((8, channels), F32),
        ],
        scratch_shapes=[
            pltpu.VMEM((NS, channels), F32),
            pltpu.VMEM((BLOCK + 8, dat - xat), F32),
            pltpu.VMEM((BLOCK + 8, dat - xat), F32),
            pltpu.VMEM((BLOCK + 8, LANES), jnp.int32),
        ],
        compiler_params=pltpu.CompilerParams(vmem_limit_bytes=VMEM_LIMIT),
        cost_estimate=pl.CostEstimate(flops=6 * 10**9, bytes_accessed=2 * 10**7, transcendentals=3 * 10**6),
        name="scan_bwd",
    )(proj, proj, start_col, start_row, *params, y, states, grad, stats, gain)


def pack_kernel(cols, place_ref, q_ref, kv_ref, z_ref, x_ref, bc_ref, dt_ref, one_ref, two_ref, att_ref, mix_ref, gate_ref, up_ref, down_ref, mixer_ref, ffn_ref):
    zat, xat, dat, width = cols
    own = q_ref.shape[0]
    qwidth = q_ref.shape[1]
    channels = xat - zat
    hidden = gate_ref.shape[1]
    eye = jnp.where(iota((own, own), 0) == iota((own, own), 1), 1.0, 0.0).astype(BF16)
    turned = lambda ref: mm_nt(eye, ref[...]).astype(BF16)
    mixer_ref[:, :qwidth] = q_ref[...]
    kv = kv_ref[...].astype(F32)
    keys, vals = kv[:, :LANES], kv[:, LANES:]
    first = place_ref[0] == 0
    keys = jnp.where(first, keys, pltpu.roll(keys, HD, 1))
    vals = jnp.where(first, pltpu.roll(vals, HD, 1), vals)
    mixer_ref[:, qwidth:zat] = jnp.where(iota((own, LANES), 1) < HD, keys, vals).astype(BF16)
    mixer_ref[:, zat:xat] = z_ref[...]
    mixer_ref[:, xat : xat + channels] = x_ref[...]
    mixer_ref[:, xat + channels : dat] = bc_ref[...]
    row, lane = iota((16, LANES), 0), iota((16, LANES), 1)
    pick = jnp.where((lane == row + HD) & (row < 2), 1.0, 0.0).astype(BF16)
    gains = iota((16, own), 0)
    gains = jnp.where(gains == 0, one_ref[...].astype(F32), jnp.where(gains == 1, two_ref[...].astype(F32), 0.0))
    mixer_ref[:, dat:width] = mm_tn(gains.astype(BF16), pick).astype(BF16)
    mixer_ref[:, dat : dat + dt_ref.shape[1]] = dt_ref[...]
    mixer_ref[:, width : width + qwidth] = turned(att_ref)
    mixer_ref[:, width + qwidth :] = turned(mix_ref)
    ffn_ref[:, :hidden] = gate_ref[...]
    ffn_ref[:, hidden : 2 * hidden] = up_ref[...]
    ffn_ref[:, 2 * hidden :] = turned(down_ref)


def pack_weights(cols, kv_head, *shards):
    own = shards[0].shape[0]
    zat, xat, dat, width = cols
    body = lambda *refs: pack_kernel(cols, *refs)
    whole = lambda shape: pl.BlockSpec(shape, lambda i: (0, 0))
    shapes = [(own, width + shards[0].shape[1] + xat - zat), (own, 3 * shards[-1].shape[0])]
    return pl.pallas_call(
        body,
        grid=(1,),
        in_specs=[pl.BlockSpec(memory_space=pltpu.SMEM)] + [whole(shard.shape) for shard in shards],
        out_specs=[whole(shape) for shape in shapes],
        out_shape=[jax.ShapeDtypeStruct(shape, BF16) for shape in shapes],
        compiler_params=pltpu.CompilerParams(vmem_limit_bytes=VMEM_LIMIT),
        cost_estimate=pl.CostEstimate(flops=10**7, bytes_accessed=2 * 10**6, transcendentals=0),
        name="pack_weights",
    )(kv_head, *shards)


def piece_at(rank_ref, refs, shift):
    if shift == 0:
        return refs[0][...]
    below, above = refs[2 * shift - 1][...], refs[2 * shift][...]
    return jnp.where(rank_ref[0] >= shift, below, above)


def norm_kernel(parts, rank_ref, *refs):
    gain_ref, out_ref = refs[2 * parts - 1], refs[2 * parts]
    rows = refs[0].shape[0]
    gain = gain_ref[...]
    for shift in range(parts):
        values = piece_at(rank_ref, refs, shift).astype(F32)
        spot = lax.rem(rank_ref[0] + (parts - shift), parts) * rows
        out_ref[pl.ds(pl.multiple_of(spot, rows), rows), :] = (values * rms_scale(values) * gain).astype(BF16)


def norm_rows(rank, parts, pieces, gain):
    rows, model = pieces[0].shape
    body = lambda *refs: norm_kernel(parts, *refs)
    whole = lambda shape: pl.BlockSpec(shape, lambda i: (0, 0))
    return pl.pallas_call(
        body,
        grid=(1,),
        in_specs=[pl.BlockSpec(memory_space=pltpu.SMEM)]
        + [whole((rows, model))] * len(pieces)
        + [whole((1, model))],
        out_specs=whole((parts * rows, model)),
        out_shape=jax.ShapeDtypeStruct((parts * rows, model), BF16),
        compiler_params=pltpu.CompilerParams(vmem_limit_bytes=VMEM_LIMIT),
        cost_estimate=pl.CostEstimate(flops=10**7, bytes_accessed=5 * 10**6, transcendentals=0),
        name="norm_rows",
    )(rank, *pieces, gain)


def branch_back_kernel(parts, rank_ref, *refs):
    count = 2 * parts - 1
    out_w_ref, am_ref, gain_ref, gatt_ref, gmix_ref, gow_ref, inner_ref, ggain_ref, sum_ref = refs[count:]
    rows = refs[0].shape[0]
    qwidth = gatt_ref.shape[1]
    sum_ref[...] = jnp.zeros_like(sum_ref)
    total = jnp.zeros((1, gmix_ref.shape[1]), F32)
    ones = jnp.ones((16, gmix_ref.shape[1]), BF16)
    for shift in range(parts):
        grads = piece_at(rank_ref, refs, shift)
        spot = pl.multiple_of(lax.rem(rank_ref[0] + (parts - shift), parts) * rows, rows)
        here = pl.ds(spot, rows)
        both = am_ref[here, :]
        grad_am = mm(grads, out_w_ref[...])
        gatt_ref[here, :] = grad_am[:, :qwidth].astype(BF16)
        grad_mixed = grad_am[:, qwidth:]
        gmix_ref[here, :] = grad_mixed
        product = grad_mixed * both[:, qwidth:].astype(F32)
        total = total + jnp.sum(product, axis=0, keepdims=True)
        high = product.astype(BF16)
        rest = (product - high.astype(F32)).astype(BF16)
        inner_ref[:, here] = (mm_nt(ones, high) + mm_nt(ones, rest))[:8]
        sum_ref[...] += mm_tn(grads, both)
    gow_ref[...] = sum_ref[...].astype(BF16)
    ggain_ref[...] = jnp.broadcast_to(total / gain_ref[...], ggain_ref.shape)


def branch_back(rank, parts, pieces, out_w, att_mixed, gain):
    rows, model = pieces[0].shape
    length, width = att_mixed.shape
    channels = gain.shape[1]
    body = lambda *refs: branch_back_kernel(parts, *refs)
    whole = lambda shape: pl.BlockSpec(shape, lambda i: (0, 0))
    shapes = [
        ((length, width - channels), BF16),
        ((length, channels), F32),
        ((model, width), BF16),
        ((8, length), F32),
        ((8, channels), F32),
    ]
    return pl.pallas_call(
        body,
        grid=(1,),
        in_specs=[pl.BlockSpec(memory_space=pltpu.SMEM)]
        + [whole((rows, model))] * len(pieces)
        + [whole((model, width)), whole((length, width)), whole((1, channels))],
        out_specs=[whole(shape) for shape, _ in shapes],
        out_shape=[jax.ShapeDtypeStruct(shape, dtype) for shape, dtype in shapes],
        scratch_shapes=[pltpu.VMEM((model, width), F32)],
        compiler_params=pltpu.CompilerParams(vmem_limit_bytes=VMEM_LIMIT),
        cost_estimate=pl.CostEstimate(flops=2 * 10**9, bytes_accessed=10**7, transcendentals=0),
        name="branch_back",
    )(rank, *pieces, out_w, att_mixed, gain)


def wgrad_kernel(rows_ref, gq_ref, gkv_ref, grest_ref, gow_ref, later_ref, out_ref):
    rows = rows_ref[...]
    at = 0
    for ref in (gq_ref, gkv_ref, grest_ref):
        for col in range(0, ref.shape[1], LANES * 3):
            end = min(col + LANES * 3, ref.shape[1])
            out_ref[:, at + col : at + end] = mm_tn(rows, ref[:, col:end]).astype(BF16)
        at += ref.shape[1]
    out_ref[:, at:] = gow_ref[...]


def mixer_wgrad(rows_one, grad_q, grad_kv, grad_rest, grad_out_w, later):
    length, model = rows_one.shape
    width = grad_q.shape[1] + grad_kv.shape[1] + grad_rest.shape[1] + grad_out_w.shape[1]
    whole = lambda shape: pl.BlockSpec(shape, lambda i: (0, 0))
    args = (rows_one, grad_q, grad_kv, grad_rest, grad_out_w)
    return pl.pallas_call(
        wgrad_kernel,
        grid=(1,),
        in_specs=[whole(arg.shape) for arg in args] + [pl.BlockSpec(memory_space=pl.ANY)],
        out_specs=whole((model, width)),
        out_shape=jax.ShapeDtypeStruct((model, width), BF16),
        compiler_params=pltpu.CompilerParams(vmem_limit_bytes=VMEM_LIMIT),
        cost_estimate=pl.CostEstimate(flops=3 * 10**9, bytes_accessed=10**7, transcendentals=0),
        name="mixer_wgrad",
    )(*args, later)


def ffn_kernel(middle_ref, cot_ref, gain_ref, w_ref, out_ref, gmid_ref, ggain_ref, gw_ref, low_ref, sum_ref, gsum_ref):
    step = pl.program_id(0)
    hidden = w_ref.shape[1] // 3

    @pl.when(step == 0)
    def _():
        middle = middle_ref[...]
        low_ref[...] = (middle * rms_scale(middle) * gain_ref[...]).astype(BF16)
        sum_ref[...] = jnp.zeros_like(sum_ref)
        gsum_ref[...] = jnp.zeros_like(gsum_ref)

    low = low_ref[...]
    cot = cot_ref[...]
    gate_pre = mm(low, w_ref[:, :hidden])
    up_pre = mm(low, w_ref[:, hidden : 2 * hidden])
    sig = sigmoid(gate_pre)
    silu_gate = gate_pre * sig
    act = (silu_gate * up_pre).astype(BF16)
    sum_ref[...] += mm_nt(act, w_ref[:, 2 * hidden :])
    gw_ref[:, 2 * hidden :] = mm_tn(cot, act).astype(BF16)
    grad_hidden = mm(cot, w_ref[:, 2 * hidden :])
    grad_gate = (grad_hidden * up_pre * sig * (1.0 + gate_pre * (1.0 - sig))).astype(BF16)
    grad_up = (grad_hidden * silu_gate).astype(BF16)
    gw_ref[:, :hidden] = mm_tn(low, grad_gate).astype(BF16)
    gw_ref[:, hidden : 2 * hidden] = mm_tn(low, grad_up).astype(BF16)
    gsum_ref[...] += mm_nt(grad_gate, w_ref[:, :hidden]) + mm_nt(grad_up, w_ref[:, hidden : 2 * hidden])

    @pl.when(step == pl.num_programs(0) - 1)
    def _():
        middle = middle_ref[...]
        out_ref[...] = (middle + sum_ref[...]).astype(BF16)
        scale = rms_scale(middle)
        normed = middle * scale
        grad_two = gsum_ref[...]
        ggain_ref[...] = jnp.broadcast_to(jnp.sum(grad_two * normed, axis=0, keepdims=True), ggain_ref.shape)
        gmid_ref[...] = cot_ref[...].astype(F32) + norm_back(grad_two * gain_ref[...], normed, scale)


def ffn_both(middle, cotangent, gain, ffn_w, parts):
    rows, model = middle.shape
    piece = ffn_w.shape[1] // parts
    rowspec = pl.BlockSpec((rows, model), lambda s: (0, 0))
    wspec = pl.BlockSpec((model, piece), lambda s: (0, s))
    return pl.pallas_call(
        ffn_kernel,
        grid=(parts,),
        in_specs=[rowspec, rowspec, pl.BlockSpec((1, model), lambda s: (0, 0)), wspec],
        out_specs=[rowspec, rowspec, pl.BlockSpec((8, model), lambda s: (0, 0)), wspec],
        out_shape=[
            jax.ShapeDtypeStruct((rows, model), BF16),
            jax.ShapeDtypeStruct((rows, model), F32),
            jax.ShapeDtypeStruct((8, model), F32),
            jax.ShapeDtypeStruct(ffn_w.shape, BF16),
        ],
        scratch_shapes=[
            pltpu.VMEM((rows, model), BF16),
            pltpu.VMEM((rows, model), F32),
            pltpu.VMEM((rows, model), F32),
        ],
        compiler_params=pltpu.CompilerParams(vmem_limit_bytes=VMEM_LIMIT),
        cost_estimate=pl.CostEstimate(flops=10**10, bytes_accessed=3 * 10**7, transcendentals=10**6),
        name="ffn_both",
    )(middle, cotangent, gain, ffn_w)


def lane_rows(values, rows):
    padded = jnp.pad(values, (0, rows - values.shape[0]))
    return jnp.broadcast_to(padded[:, None], (rows, LANES))


def shifted(values, axis, size, shift):
    return lax.ppermute(values, axis, [(i, (i + shift) % size) for i in range(size)])


def sent(values, pairs):
    return lax.ppermute(values, "tensor", pairs)


def pieces_of_group(values, parts):
    up = lambda shift: [(i, i + shift) for i in range(parts - shift)]
    down = lambda shift: [(i + shift, i) for i in range(parts - shift)]
    if parts != 4:
        below = [sent(values, up(shift)) for shift in range(1, parts)]
        above = [sent(values, down(shift)) for shift in range(1, parts)]
    else:
        first_up, first_down = sent(values, up(1)), sent(values, down(1))
        below = [first_up, sent(first_up, [(1, 2), (2, 3)]), sent(first_up, [(1, 3)])]
        above = [first_down, sent(first_down, [(2, 1), (1, 0)]), sent(first_down, [(2, 0)])]
    pieces = [values]
    for shift in range(1, parts):
        pieces += [below[shift - 1], above[parts - shift - 1]]
    return pieces


def sum_to_owner(terms, parts):
    if parts != 4:
        total = terms[0]
        for shift in range(1, parts):
            total = total + shifted(terms[shift].astype(BF16), "tensor", parts, shift).astype(F32)
        return total
    low = lambda value: value.astype(BF16)
    up = [sent(low(terms[2]), [(0, 1), (1, 2)]), sent(low(terms[3]), [(0, 2)])]
    down = [sent(low(terms[2]), [(3, 2), (2, 1)]), sent(low(terms[1]), [(3, 1)])]
    up = terms[1] + up[0].astype(F32) + up[1].astype(F32)
    down = terms[3] + down[0].astype(F32) + down[1].astype(F32)
    up = sent(low(up), [(0, 1), (1, 2), (2, 3)])
    down = sent(low(down), [(3, 2), (2, 1), (1, 0)])
    return terms[0] + up.astype(F32) + down.astype(F32)


def rows_of(values, rank, shift, parts):
    rows = values.shape[0] // parts
    return lax.dynamic_slice(values, (lax.rem(rank + shift, parts) * rows, 0), (rows, values.shape[1]))


def group_total(values, parts):
    total = values.astype(F32)
    for shift in range(1, parts):
        total = total + shifted(values, "tensor", parts, shift).astype(F32)
    return total


def butterfly(values, axis, size):
    if size & (size - 1):
        return lax.psum(values, axis)
    step = 1
    while step < size:
        values = values + lax.ppermute(values, axis, [(i, i ^ step) for i in range(size)])
        step *= 2
    return values


def local(
    x_in,
    cotangent,
    segments,
    norm_one,
    w_query,
    w_keyval,
    w_attn_out,
    w_zgate,
    w_xin,
    w_bcin,
    w_dtin,
    conv_x,
    conv_bc,
    bias_x,
    bias_bc,
    dt_bias,
    a_log,
    d_skip,
    ssm_gain,
    w_mix_out,
    norm_two,
    w_gate,
    w_up,
    w_down,
):
    parts = lax.axis_size("tensor")
    rank = lax.axis_index("tensor")
    own = w_query.shape[0]
    length = segments.shape[1]
    qwidth = w_query.shape[1]
    channels = w_zgate.shape[1]
    heads = w_dtin.shape[1]
    hidden_own = w_gate.shape[1]
    width_ssm = MH * PD
    kv_head = (rank * (qwidth // HD)) // (QH // KVH)
    zat = 2 * qwidth
    xat = zat + channels
    bat = xat + channels
    dat = bat + 2 * NS
    width = dat + LANES
    cols = (zat, xat, dat, width)

    x_pieces = pieces_of_group(x_in, parts)
    mixer_own, ffn_own = pack_weights(
        cols,
        kv_head.astype(jnp.int32)[None],
        w_query,
        w_keyval,
        w_zgate,
        w_xin,
        w_bcin,
        w_dtin,
        norm_one[None, :],
        norm_two[None, :],
        w_attn_out,
        w_mix_out,
        w_gate,
        w_up,
        w_down,
    )
    mixer_w = lax.all_gather(mixer_own, "dp", axis=0, tiled=True)
    proj_w = mixer_w[:, :width]
    out_w = mixer_w[:, width:]
    gain_one = mixer_w[:, dat + HD].astype(F32)[None, :]
    gain_two = mixer_w[:, dat + HD + 1].astype(F32)[None, :]
    ffn_pieces = pieces_of_group(ffn_own, parts)
    ffn_own = jnp.concatenate(
        ffn_pieces[:1]
        + [jnp.where(rank >= k, ffn_pieces[2 * k - 1], ffn_pieces[2 * k]) for k in range(1, parts)],
        axis=1,
    )
    ffn_w = lax.all_gather(ffn_own, "dp", axis=0, tiled=True)

    seg = segments[0]
    start = jnp.sum((seg[None, :] < seg[:, None]).astype(jnp.int32), axis=1)
    start_col = jnp.broadcast_to(start[:, None], (length, LANES))
    start_row = jnp.broadcast_to(start[None, :], (8, length))
    cosine, sine = rope_tables(length)
    taps = jnp.pad(jnp.concatenate([conv_x, conv_bc], axis=1), ((0, 8 - KW), (0, 0)))
    bias = jnp.concatenate([bias_x, bias_bc])[None, :]
    params = (taps, bias, lane_rows(dt_bias, 8), lane_rows(jnp.exp(a_log), 8), jnp.repeat(d_skip, PD)[None, :])

    residual = x_in.astype(F32)
    scale_one = rms_scale(residual)
    normed_one = residual * scale_one
    rank_arg = rank.astype(jnp.int32)[None]
    rows_one = norm_rows(rank_arg, parts, x_pieces, gain_one)
    proj = mm(rows_one, proj_w)
    y, gated, states, squares = scan_forward(cols, proj, start_col, start_row, params)
    attended, lse, low_q, low_kv = attn_forward(proj, cosine, sine, start_col)
    scale_ssm = lax.rsqrt(group_total(squares[:1], parts) / width_ssm + EPSILON)
    mixed = (gated * scale_ssm[0][:, None] * ssm_gain[None, :]).astype(BF16)
    att_mixed = jnp.concatenate([attended, mixed], axis=1)
    terms = [mm_nt(rows_of(att_mixed, rank, shift, parts), out_w) for shift in range(parts)]
    middle = residual + sum_to_owner(terms, parts)
    block_out, grad_middle, grad_gain_two, grad_ffn_w = ffn_both(middle, cotangent, gain_two, ffn_w, parts)

    branch_pieces = pieces_of_group(grad_middle.astype(BF16), parts)
    grad_ffn_own = lax.psum_scatter(grad_ffn_w, "dp", scatter_dimension=0, tiled=True)
    piece = grad_ffn_own.shape[1] // parts
    terms = [grad_ffn_own[:, k * piece : (k + 1) * piece].astype(F32) for k in range(parts)]
    grad_ffn = sum_to_owner(terms[:1] + terms[:0:-1], parts)

    grad_att, grad_mixed, grad_out_w, inner, grad_gain_ssm = branch_back(
        rank_arg, parts, branch_pieces, out_w, att_mixed, ssm_gain[None, :]
    )
    inner = group_total(inner[:1], parts) / width_ssm
    stats = jnp.concatenate([scale_ssm, inner, jnp.zeros((6, length), F32)], axis=0)
    grad_q, grad_kv = attn_backward(low_q, low_kv, lse, attended, grad_att, cosine, sine, start_col)
    grad_rest, conv_acc, head_acc, skip_acc = scan_backward(
        cols, proj, start_col, start_row, params, y, states, grad_mixed, stats, ssm_gain[None, :]
    )
    grad_proj = jnp.concatenate([grad_q, grad_kv, grad_rest], axis=1)
    terms = [mm_nt(rows_of(grad_proj, rank, shift, parts), proj_w) for shift in range(parts)]
    grad_gain_one = sum(
        jnp.sum(terms[k] * rows_of(rows_one, rank, k, parts).astype(F32), axis=0, keepdims=True) for k in range(parts)
    )
    grad_gain_one = grad_gain_one / gain_one
    grad_one = sum_to_owner(terms, parts)
    grad_input = grad_middle + norm_back(grad_one * gain_one, normed_one, scale_one)
    grad_mixer_w = mixer_wgrad(rows_one, grad_q, grad_kv, grad_rest, grad_out_w, grad_ffn_own)
    grad_w = lax.psum_scatter(grad_mixer_w, "dp", scatter_dimension=0, tiled=True).astype(F32)

    model = x_in.shape[1]
    wide = lambda rows: jnp.pad(rows, ((0, 0), (0, model - rows.shape[1])))
    head_sums = jnp.sum(head_acc, axis=1)[None, :]
    small = jnp.concatenate(
        [
            wide(conv_acc),
            grad_gain_one,
            grad_gain_two[:1],
            wide(grad_gain_ssm[:1]),
            wide(skip_acc[:1]),
            wide(head_sums),
            jnp.zeros((3, model), F32),
        ],
        axis=0,
    )
    small = butterfly(small, "dp", lax.axis_size("dp"))
    shared_small = butterfly(small, "tensor", parts)
    grad_conv_x = small[:KW, :channels]
    grad_bias_x = small[KW, :channels]
    grad_ssm_gain = small[10, :channels]
    grad_d_skip = jnp.sum(small[11, :channels].reshape(heads, PD), axis=1)
    grad_dt_bias = small[12, :heads]
    grad_a_log = small[12, 8 : 8 + heads]
    grad_conv_bc = shared_small[:KW, channels : channels + 2 * NS]
    grad_bias_bc = shared_small[KW, channels : channels + 2 * NS]
    place = lax.axis_index("dp") * own
    norm_grads = lax.dynamic_slice(shared_small, (8, place), (2, own))
    grad_norm_one, grad_norm_two = norm_grads[0], norm_grads[1]

    grad_keyval = jnp.zeros((own, 2 * KVH * HD), F32)
    grad_keyval = lax.dynamic_update_slice(grad_keyval, grad_w[:, qwidth : qwidth + HD], (0, kv_head * HD))
    grad_keyval = lax.dynamic_update_slice(
        grad_keyval, grad_w[:, qwidth + HD : zat], (0, (KVH + kv_head) * HD)
    )
    shared = jnp.concatenate([grad_keyval, grad_w[:, bat:dat]], axis=1)
    shared = group_total(shared.astype(BF16), parts)

    return (
        block_out,
        grad_input,
        grad_norm_one,
        grad_w[:, :qwidth],
        shared[:, : 2 * KVH * HD],
        grad_w[:, width : width + qwidth].T,
        grad_w[:, zat:xat],
        grad_w[:, xat:bat],
        shared[:, 2 * KVH * HD :],
        grad_w[:, dat : dat + heads],
        grad_conv_x,
        grad_conv_bc,
        grad_bias_x,
        grad_bias_bc,
        grad_dt_bias,
        grad_a_log,
        grad_d_skip,
        grad_ssm_gain,
        grad_w[:, width + qwidth :].T,
        grad_norm_two,
        grad_ffn[:, :hidden_own],
        grad_ffn[:, hidden_own : 2 * hidden_own],
        grad_ffn[:, 2 * hidden_own :].T,
    )


def solution(mesh):
    return jax.shard_map(
        local,
        mesh=mesh,
        in_specs=(
            P(("dp", "tensor"), None),
            P(("dp", "tensor"), None),
            P("dp", None),
            P("dp"),
            P("dp", "tensor"),
            P("dp", None),
            P("tensor", "dp"),
            P("dp", "tensor"),
            P("dp", "tensor"),
            P("dp", None),
            P("dp", "tensor"),
            P(None, "tensor"),
            P(),
            P("tensor"),
            P(),
            P("tensor"),
            P("tensor"),
            P("tensor"),
            P("tensor"),
            P("tensor", "dp"),
            P("dp"),
            P("dp", "tensor"),
            P("dp", "tensor"),
            P("tensor", "dp"),
        ),
        out_specs=(
            P(("dp", "tensor"), None),
            P(("dp", "tensor"), None),
            P("dp"),
            P("dp", "tensor"),
            P("dp", None),
            P("tensor", "dp"),
            P("dp", "tensor"),
            P("dp", "tensor"),
            P("dp", None),
            P("dp", "tensor"),
            P(None, "tensor"),
            P(),
            P("tensor"),
            P(),
            P("tensor"),
            P("tensor"),
            P("tensor"),
            P("tensor"),
            P("tensor", "dp"),
            P("dp"),
            P("dp", "tensor"),
            P("dp", "tensor"),
            P("tensor", "dp"),
        ),
        check_vma=False,
    )
```

```python
import math

import jax
import jax.numpy as jnp
import numpy as np
from jax import lax
from jax.experimental import pallas as pl
from jax.experimental.pallas import tpu as pltpu
from jax.sharding import PartitionSpec as P

QH = 8
KVH = 2
HD = 64
MH = 24
PD = 64
NS = 128
KW = 4
BLOCK = 128
LANES = 128

EPSILON = 1e-05
ROPE_BASE = 100000000000.0
NEG = -1e9
F32 = jnp.float32
BF16 = jnp.bfloat16
MIB = 1024 * 1024


def mm(lhs, rhs):
    return lax.dot_general(lhs, rhs, (((1,), (0,)), ((), ())), preferred_element_type=F32)


def mm_nt(lhs, rhs):
    return lax.dot_general(lhs, rhs, (((1,), (1,)), ((), ())), preferred_element_type=F32)


def mm_tn(lhs, rhs):
    return lax.dot_general(lhs, rhs, (((0,), (0,)), ((), ())), preferred_element_type=F32)


def rms_scale(values):
    return lax.rsqrt(jnp.mean(values * values, axis=-1, keepdims=True) + EPSILON)


def norm_back(grad_normed, normed, scale):
    return scale * (grad_normed - normed * jnp.mean(grad_normed * normed, axis=-1, keepdims=True))


def sigmoid(v):
    return 1.0 / (1.0 + jnp.exp(-v))


def iota(shape, dim):
    return lax.broadcasted_iota(jnp.int32, shape, dim)


def rope_tables(length):
    half = HD // 2
    freqs = np.float32(ROPE_BASE) ** (-(np.arange(half, dtype=np.float32) * np.float32(2.0 / HD)))
    angles = np.arange(length, dtype=np.float32)[:, None] * freqs.astype(np.float32)[None, :]
    cosine, sine = np.cos(angles).astype(np.float32), np.sin(angles).astype(np.float32)
    cos_lanes = np.concatenate([cosine] * 4, axis=1)
    sin_lanes = np.concatenate([-sine, sine, -sine, sine], axis=1)
    return jnp.asarray(cos_lanes), jnp.asarray(sin_lanes)


def swap_halves(values):
    lane = iota(values.shape, 1)
    ahead = pltpu.roll(values, LANES - HD // 2, 1)
    behind = pltpu.roll(values, HD // 2, 1)
    return jnp.where((lane & (HD - 1)) < HD // 2, ahead, behind)


def pair_rows(block):
    low = iota(block.shape, 1) < HD
    zero = jnp.zeros_like(block)
    return jnp.concatenate([jnp.where(low, block, zero), jnp.where(low, zero, block)], axis=0)


def attn_fwd_kernel(q_ref, kv_ref, cos_ref, sin_ref, start_ref, out_ref, lse_ref, lq_ref, lkv_ref):
    length = q_ref.shape[0]
    rows = 256
    cosine, sine = cos_ref[...], sin_ref[...]
    low = iota((length, LANES), 1) < HD
    queries = q_ref[...]
    lq_ref[...] = (queries * cosine + swap_halves(queries) * sine).astype(BF16)
    kv = kv_ref[...]
    kv = jnp.where(low, kv * cosine + swap_halves(kv) * sine, kv)
    lkv_ref[...] = kv.astype(BF16)
    other = pltpu.roll(kv, HD, 1)
    keys = jnp.where(low, kv, other).astype(BF16)
    vals = jnp.where(low, other, kv).astype(BF16)
    half = iota((rows, LANES), 1) < HD
    for step in range(length // rows):
        end = (step + 1) * rows
        span = slice(step * rows, end)
        stacked = pair_rows(lq_ref[span, :].astype(F32)).astype(BF16)
        scores = mm_nt(stacked, keys[:end]) * (1.0 / math.sqrt(HD))
        first = start_ref[span, :][:, :1]
        col = iota((rows, end), 1)
        row = iota((rows, end), 0) + step * rows
        allowed = (col <= row) & (col >= first)
        allowed = jnp.concatenate([allowed.astype(jnp.int32)] * 2, axis=0) > 0
        scores = jnp.where(allowed, scores, NEG)
        top = jnp.max(scores, axis=1, keepdims=True)
        expo = jnp.exp(scores - top)
        total = jnp.sum(expo, axis=1, keepdims=True)
        probs = (expo * (1.0 / total)).astype(BF16)
        result = mm(probs, vals[:end])
        out_ref[span, :] = jnp.where(half, result[:rows], result[rows:]).astype(BF16)
        lse = top + jnp.log(total)
        lse_ref[span, :] = jnp.where(half, lse[:rows], lse[rows:])


def attn_bwd_kernel(
    lq_ref, lkv_ref, lse_ref, out_ref, go_ref, cos_ref, sin_ref, start_ref, gq_ref, gkv_ref, dk_ref, dv_ref
):
    length = lq_ref.shape[0]
    rows = 256
    cosine, sine = cos_ref[...], sin_ref[...]
    low = iota((length, LANES), 1) < HD
    kv = lkv_ref[...].astype(F32)
    other = pltpu.roll(kv, HD, 1)
    keys = jnp.where(low, kv, other).astype(BF16)
    vals = jnp.where(low, other, kv).astype(BF16)
    half = iota((rows, LANES), 1) < HD
    dk_ref[...] = jnp.zeros_like(dk_ref)
    dv_ref[...] = jnp.zeros_like(dv_ref)
    inv = 1.0 / math.sqrt(HD)
    for step in range(length // rows):
        end = (step + 1) * rows
        span = slice(step * rows, end)
        stacked = pair_rows(lq_ref[span, :].astype(F32)).astype(BF16)
        grads = pair_rows(go_ref[span, :].astype(F32))
        outs = out_ref[span, :].astype(F32)
        inner = jnp.sum(grads * jnp.concatenate([outs, outs], axis=0), axis=1, keepdims=True)
        grads = grads.astype(BF16)
        lse = lse_ref[span, :]
        lse = jnp.concatenate([lse[:, :1], lse[:, HD : HD + 1]], axis=0)
        scores = mm_nt(stacked, keys[:end]) * inv
        first = start_ref[span, :][:, :1]
        col = iota((rows, end), 1)
        row = iota((rows, end), 0) + step * rows
        allowed = (col <= row) & (col >= first)
        allowed = jnp.concatenate([allowed.astype(jnp.int32)] * 2, axis=0) > 0
        probs = jnp.exp(jnp.where(allowed, scores, NEG) - lse)
        grad_probs = mm_nt(grads, vals[:end])
        grad_scores = (probs * (grad_probs - inner)).astype(BF16)
        gq = mm(grad_scores, keys[:end]) * inv
        gq = jnp.where(half, gq[:rows], gq[rows:])
        gq_ref[span, :] = (gq * cosine[span] - swap_halves(gq) * sine[span]).astype(BF16)
        dk_ref[:end, :] += mm_tn(grad_scores, stacked)
        dv_ref[:end, :] += mm_tn(probs.astype(BF16), grads)
    dk = dk_ref[...] * inv
    dk = dk + pltpu.roll(dk, HD, 1)
    dk = dk * cosine - swap_halves(dk) * sine
    dv = dv_ref[...]
    dv = dv + pltpu.roll(dv, HD, 1)
    gkv_ref[...] = jnp.where(low, dk, dv).astype(BF16)


def attn_forward(proj, cosine, sine, start_col):
    length = proj.shape[0]
    wide = pl.BlockSpec((length, LANES), lambda i: (0, 0))
    return pl.pallas_call(
        attn_fwd_kernel,
        grid=(1,),
        in_specs=[wide, pl.BlockSpec((length, LANES), lambda i: (0, 1)), wide, wide, wide],
        out_specs=[wide] * 4,
        out_shape=[
            jax.ShapeDtypeStruct((length, LANES), BF16),
            jax.ShapeDtypeStruct((length, LANES), F32),
            jax.ShapeDtypeStruct((length, LANES), BF16),
            jax.ShapeDtypeStruct((length, LANES), BF16),
        ],
        compiler_params=pltpu.CompilerParams(vmem_limit_bytes=32 * MIB),
        cost_estimate=pl.CostEstimate(flops=10**9, bytes_accessed=6 * 10**6, transcendentals=2 * 10**6),
        name="attn_fwd",
    )(proj, proj, cosine, sine, start_col)


def attn_backward(low_q, low_kv, lse, out, grad_out, cosine, sine, start_col):
    length = low_q.shape[0]
    wide = pl.BlockSpec((length, LANES), lambda i: (0, 0))
    return pl.pallas_call(
        attn_bwd_kernel,
        grid=(1,),
        in_specs=[wide] * 8,
        out_specs=[wide] * 2,
        out_shape=[jax.ShapeDtypeStruct((length, LANES), BF16)] * 2,
        scratch_shapes=[pltpu.VMEM((length, LANES), F32)] * 2,
        compiler_params=pltpu.CompilerParams(vmem_limit_bytes=32 * MIB),
        cost_estimate=pl.CostEstimate(flops=3 * 10**9, bytes_accessed=6 * 10**6, transcendentals=2 * 10**6),
        name="attn_bwd",
    )(low_q, low_kv, lse, out, grad_out, cosine, sine, start_col)


def split3(values):
    high = values.astype(BF16).astype(F32)
    rest = values - high
    mid = rest.astype(BF16).astype(F32)
    tail = rest - mid
    return jnp.concatenate([high, mid, tail, jnp.zeros_like(values)], axis=0).astype(BF16)


def spread(rows, width, lanes_each):
    pick = (iota((32, width), 1) // lanes_each) == (iota((32, width), 0) & 7)
    return mm_tn(split3(rows), pick.astype(F32).astype(BF16))


def decay_terms(dt_block, dt_bias, rate, start_row, start_col, base):
    dt_rows = jnp.transpose(dt_block)[:8] + dt_bias
    step = jnp.maximum(dt_rows, 0.0) + jnp.log1p(jnp.exp(-jnp.abs(dt_rows)))
    log_decay = -step * rate
    row = iota((BLOCK, BLOCK), 0) + base
    col = iota((BLOCK, BLOCK), 1) + base
    linked = (col <= row) & (col >= start_col)
    linked_low = jnp.where(linked, 1.0, 0.0).astype(BF16)
    cum = mm_nt(split3(log_decay), linked_low)
    cum = cum[0:8] + cum[8:16] + cum[16:24]
    enter = jnp.exp(jnp.where(start_row < base, cum, NEG))
    last = cum[:, BLOCK - 1 :]
    position = iota((8, BLOCK), 1) + base
    tail = jnp.exp(jnp.where(position >= start_row[:, BLOCK - 1 :], last - cum, NEG))
    return dt_rows, step, log_decay, linked, linked_low, cum, enter, tail


def conv_sum(ext_ref, taps, bias, place):
    total = bias + taps[KW - 1 : KW] * ext_ref[pl.ds(8, BLOCK), :]
    for offset in range(1, KW):
        shifted = ext_ref[pl.ds(8 - offset, BLOCK), :]
        total = total + jnp.where(place >= offset, taps[KW - 1 - offset : KW - offset] * shifted, 0.0)
    return total


def wide_place(start_col, base, width):
    place = iota((BLOCK, BLOCK), 0) + base - start_col
    return jnp.concatenate([place] * (width // LANES), axis=1)


def scan_fwd_kernel(
    cols,
    proj_ref,
    startc_ref,
    startr_ref,
    taps_ref,
    bias_ref,
    dtb_ref,
    rate_ref,
    skip_ref,
    y_ref,
    gated_ref,
    state_out_ref,
    ssq_ref,
    state_ref,
    ext_ref,
):
    zat, xat, dat, width = cols
    channels = xat - zat
    heads = channels // PD
    block = pl.program_id(0)
    base = block * BLOCK

    @pl.when(block == 0)
    def _():
        state_ref[...] = jnp.zeros_like(state_ref)
        ext_ref[0:8, :] = jnp.zeros((8, ext_ref.shape[1]), F32)

    start_col = startc_ref[...]
    start_row = startr_ref[...]
    ext_ref[pl.ds(8, BLOCK), :] = proj_ref[:, xat:dat]
    place = wide_place(start_col, base, dat - xat)
    pre = conv_sum(ext_ref, taps_ref[...], bias_ref[...], place)
    ext_ref[0:8, :] = ext_ref[pl.ds(BLOCK, 8), :]
    conv = (pre * sigmoid(pre)).astype(BF16)
    x_low, b_low, c_low = conv[:, :channels], conv[:, channels : channels + NS], conv[:, channels + NS :]
    x_val = x_low.astype(F32)
    _, step, _, linked, _, cum, enter, tail = decay_terms(
        proj_ref[:, dat:width], dtb_ref[...], rate_ref[...], start_row, start_col, base
    )
    contact = mm_nt(c_low, b_low)
    cum_cols = spread(cum, heads * LANES, LANES)
    enter_x = spread(enter, channels, PD)
    weight_x = spread(tail * step, channels, PD)
    low = iota((BLOCK, LANES), 1) < PD
    zero = jnp.zeros((BLOCK, LANES), F32)
    within = []
    for pair in range(heads // 2):
        mixes = []
        for head in (2 * pair, 2 * pair + 1):
            gap = cum_cols[:, head * LANES : (head + 1) * LANES] - cum[head : head + 1]
            decay = jnp.exp(jnp.where(linked, gap, NEG))
            mixes.append((decay * (contact * step[head : head + 1])).astype(BF16))
        x_pair = x_val[:, pair * LANES : (pair + 1) * LANES]
        both = jnp.concatenate([jnp.where(low, x_pair, zero), jnp.where(low, zero, x_pair)], axis=0).astype(BF16)
        within.append(mm(jnp.concatenate(mixes, axis=1), both))
    state = state_ref[...]
    state_low = state.astype(BF16)
    state_out_ref[0] = state_low
    y = jnp.concatenate(within, axis=1) + enter_x * mm(c_low, state_low) + skip_ref[...] * x_val
    y_ref[...] = y
    state_ref[...] = mm_tn(b_low, (weight_x * x_val).astype(BF16)) + enter_x[BLOCK - 1 :] * state
    z = proj_ref[:, zat:xat]
    gated = y * (z * sigmoid(z))
    gated_ref[...] = gated
    square = gated * gated
    high = square.astype(BF16)
    rest = (square - high.astype(F32)).astype(BF16)
    ones = jnp.ones((16, channels), BF16)
    ssq_ref[...] = (mm_nt(ones, high) + mm_nt(ones, rest))[:8]


def scan_bwd_kernel(
    cols,
    proj_ref,
    prev_ref,
    startc_ref,
    startr_ref,
    taps_ref,
    bias_ref,
    dtb_ref,
    rate_ref,
    skip_ref,
    y_ref,
    state_in_ref,
    grad_ref,
    stats_ref,
    gain_ref,
    out_ref,
    conv_acc_ref,
    head_acc_ref,
    skip_acc_ref,
    dstate_ref,
    ext_ref,
    dext_ref,
    pext_ref,
):
    zat, xat, dat, width = cols
    channels = xat - zat
    heads = channels // PD
    turn = pl.program_id(0)
    block = pl.num_programs(0) - 1 - turn
    base = block * BLOCK

    @pl.when(turn == 0)
    def _():
        dstate_ref[...] = jnp.zeros_like(dstate_ref)
        conv_acc_ref[...] = jnp.zeros_like(conv_acc_ref)
        head_acc_ref[...] = jnp.zeros_like(head_acc_ref)
        skip_acc_ref[...] = jnp.zeros_like(skip_acc_ref)
        dext_ref[pl.ds(BLOCK, 8), :] = jnp.zeros((8, dext_ref.shape[1]), F32)
        pext_ref[pl.ds(BLOCK, 8), :] = jnp.zeros((8, LANES), jnp.int32)

    start_col = startc_ref[...]
    start_row = startr_ref[...]
    taps = taps_ref[...]
    ext_ref[0:8, :] = prev_ref[:, xat:dat]
    ext_ref[pl.ds(8, BLOCK), :] = proj_ref[:, xat:dat]
    place = wide_place(start_col, base, dat - xat)
    pre = conv_sum(ext_ref, taps, bias_ref[...], place)
    pre_sig = sigmoid(pre)
    conv = (pre * pre_sig).astype(BF16)
    x_low, b_low, c_low = conv[:, :channels], conv[:, channels : channels + NS], conv[:, channels + NS :]
    x_val = x_low.astype(F32)
    rate = rate_ref[...]
    dt_rows, step, log_decay, linked, linked_low, cum, enter, tail = decay_terms(
        proj_ref[:, dat:width], dtb_ref[...], rate, start_row, start_col, base
    )
    contact = mm_nt(c_low, b_low)
    cum_cols = spread(cum, heads * LANES, LANES)
    enter_x = spread(enter, channels, PD)
    weight = tail * step
    weight_x = spread(weight, channels, PD)

    z = proj_ref[:, zat:xat]
    z_sig = sigmoid(z)
    z_silu = z * z_sig
    y_val = y_ref[...]
    stats = spread(stats_ref[...], 2 * channels, channels)
    scale_x, inner_x = stats[:, :channels], stats[:, channels:]
    grad = scale_x * (grad_ref[...] * gain_ref[...] - y_val * z_silu * scale_x * inner_x)
    dy = grad * z_silu
    out_ref[:, :channels] = (grad * y_val * (z_sig * (1.0 + z * (1.0 - z_sig)))).astype(BF16)

    low = iota((BLOCK, LANES), 1) < PD
    strict = linked & (iota((BLOCK, BLOCK), 0) > iota((BLOCK, BLOCK), 1))
    zero = jnp.zeros((BLOCK, LANES), F32)
    dcontact = zero
    dx_parts, w_parts, step_rows = [], [], []
    for pair in range(heads // 2):
        lanes = slice(pair * LANES, (pair + 1) * LANES)
        dy_pair = dy[:, lanes]
        dy_both = jnp.concatenate([jnp.where(low, dy_pair, zero), jnp.where(low, zero, dy_pair)], axis=0).astype(BF16)
        outer = mm_nt(dy_both, x_low[:, lanes])
        mixes = []
        for slot in range(2):
            head = 2 * pair + slot
            gap = cum_cols[:, head * LANES : (head + 1) * LANES] - cum[head : head + 1]
            decay = jnp.exp(jnp.where(linked, gap, NEG))
            step_row = step[head : head + 1]
            share = outer[slot * BLOCK : (slot + 1) * BLOCK] * decay
            dcontact = dcontact + share * step_row
            flow = share * contact
            step_rows.append(jnp.sum(flow, axis=0, keepdims=True))
            w_parts.append(jnp.where(strict, flow * step_row, 0.0).astype(BF16))
            mixes.append((decay * (contact * step_row)).astype(BF16))
        dx_parts.append(mm_tn(jnp.concatenate(mixes, axis=0), dy_both))
    pad = [jnp.zeros((8 - heads, BLOCK), F32)] if heads < 8 else []
    dstep = jnp.concatenate(step_rows + pad, axis=0)
    pick_rows = (iota((16, heads * BLOCK), 1) // BLOCK) == iota((16, heads * BLOCK), 0)
    pick_rows = jnp.where(pick_rows, 1.0, 0.0).astype(BF16)
    dcum = mm_nt(pick_rows, jnp.concatenate(w_parts, axis=1))[:8]
    dcum = dcum - mm(pick_rows, jnp.concatenate(w_parts, axis=0))[:8]

    state_low = state_in_ref[0]
    dstate = dstate_ref[...]
    dstate_low = dstate.astype(BF16)
    pick_x = (iota((16, channels), 1) // PD) == iota((16, channels), 0)
    pick_f = jnp.where(pick_x, 1.0, 0.0)
    pick_x = pick_f.astype(BF16)
    from_state = enter_x * mm(c_low, state_low)
    dcum = dcum + mm_nt(pick_x, (dy * from_state).astype(BF16))[:8]
    dye = (enter_x * dy).astype(BF16)
    through = mm(b_low, dstate_low)
    dweight = mm_nt(pick_x, (x_val * through).astype(BF16))[:8]
    wx = (weight_x * x_val).astype(BF16)
    kept_x = enter_x[BLOCK - 1 :]
    dkept = jnp.sum(dstate * state_low.astype(F32), axis=0, keepdims=True) * kept_x
    dkept = jnp.sum(pick_f[:8] * dkept, axis=1, keepdims=True)
    moved = dweight * weight
    lane = iota((8, BLOCK), 1)
    dlast = jnp.sum(moved, axis=1, keepdims=True) + dkept
    dcum = dcum - moved + jnp.where(lane == BLOCK - 1, dlast, 0.0)
    dstep = dstep + dweight * tail
    dc = mm_nt(dye, state_low)
    db = mm_nt(wx, dstate_low)
    dstate_ref[...] = mm_tn(c_low, dye) + kept_x * dstate
    dcontact_low = dcontact.astype(BF16)
    dc = dc + mm(dcontact_low, b_low)
    db = db + mm_tn(dcontact_low, c_low)
    dx = jnp.concatenate(dx_parts, axis=1) + weight_x * through + skip_ref[...] * dy

    dlog = mm(split3(dcum), linked_low)
    dlog = dlog[0:8] + dlog[8:16] + dlog[16:24]
    dstep = dstep - dlog * rate
    ddt = dstep * sigmoid(dt_rows)
    head_acc_ref[0:8, :] += ddt
    head_acc_ref[8:16, :] += dlog * log_decay
    skip_acc_ref[0:1, :] += jnp.sum(dy * x_val, axis=0, keepdims=True)
    ddt_cols = jnp.transpose(jnp.concatenate([ddt, jnp.zeros((BLOCK - 8, BLOCK), F32)], axis=0))
    out_ref[:, dat - zat : width - zat] = ddt_cols.astype(BF16)

    dpre = jnp.concatenate([dx, db, dc], axis=1) * (pre_sig * (1.0 + pre * (1.0 - pre_sig)))
    conv_acc_ref[KW : KW + 1, :] += jnp.sum(dpre, axis=0, keepdims=True)
    dext_ref[0:BLOCK, :] = dpre
    pext_ref[0:BLOCK, :] = iota((BLOCK, BLOCK), 0) + base - start_col
    draw = taps[KW - 1 : KW] * dpre
    conv_acc_ref[KW - 1 : KW, :] += jnp.sum(dpre * ext_ref[pl.ds(8, BLOCK), :], axis=0, keepdims=True)
    for offset in range(1, KW):
        tap = KW - 1 - offset
        kept = jnp.where(place >= offset, dpre * ext_ref[pl.ds(8 - offset, BLOCK), :], 0.0)
        conv_acc_ref[tap : tap + 1, :] += jnp.sum(kept, axis=0, keepdims=True)
        later = pext_ref[pl.ds(offset, BLOCK), :]
        later = jnp.concatenate([later] * ((dat - xat) // LANES), axis=1)
        draw = draw + jnp.where(later >= offset, taps[tap : tap + 1] * dext_ref[pl.ds(offset, BLOCK), :], 0.0)
    dext_ref[pl.ds(BLOCK, 8), :] = dext_ref[0:8, :]
    pext_ref[pl.ds(BLOCK, 8), :] = pext_ref[0:8, :]
    out_ref[:, xat - zat : dat - zat] = draw.astype(BF16)


def scan_specs(cols, turn):
    zat, xat, dat, width = cols
    channels = xat - zat
    conv_width = dat - xat
    fixed = lambda shape: pl.BlockSpec(shape, lambda c: (0,) * len(shape))
    params = [
        fixed((8, conv_width)),
        fixed((1, conv_width)),
        fixed((8, LANES)),
        fixed((8, LANES)),
        fixed((1, channels)),
    ]
    starts = [
        pl.BlockSpec((BLOCK, LANES), lambda c: (turn(c), 0)),
        pl.BlockSpec((8, BLOCK), lambda c: (0, turn(c))),
    ]
    return starts, params


def scan_forward(cols, proj, start_col, start_row, params):
    zat, xat, dat, width = cols
    channels = xat - zat
    length = proj.shape[0]
    blocks = length // BLOCK
    starts, param_specs = scan_specs(cols, lambda c: c)
    body = lambda *refs: scan_fwd_kernel(cols, *refs)
    return pl.pallas_call(
        body,
        grid=(blocks,),
        in_specs=[pl.BlockSpec((BLOCK, width), lambda c: (c, 0))] + starts + param_specs,
        out_specs=[
            pl.BlockSpec((BLOCK, channels), lambda c: (c, 0)),
            pl.BlockSpec((BLOCK, channels), lambda c: (c, 0)),
            pl.BlockSpec((1, NS, channels), lambda c: (c, 0, 0)),
            pl.BlockSpec((8, BLOCK), lambda c: (0, c)),
        ],
        out_shape=[
            jax.ShapeDtypeStruct((length, channels), F32),
            jax.ShapeDtypeStruct((length, channels), F32),
            jax.ShapeDtypeStruct((blocks, NS, channels), BF16),
            jax.ShapeDtypeStruct((8, length), F32),
        ],
        scratch_shapes=[
            pltpu.VMEM((NS, channels), F32),
            pltpu.VMEM((BLOCK + 8, dat - xat), F32),
        ],
        compiler_params=pltpu.CompilerParams(vmem_limit_bytes=24 * MIB),
        cost_estimate=pl.CostEstimate(flops=2 * 10**9, bytes_accessed=10**7, transcendentals=2 * 10**6),
        name="scan_fwd",
    )(proj, start_col, start_row, *params)


def scan_backward(cols, proj, start_col, start_row, params, y, states, grad, stats, gain):
    zat, xat, dat, width = cols
    channels = xat - zat
    length = proj.shape[0]
    blocks = length // BLOCK
    turn = lambda c: blocks - 1 - c
    starts, param_specs = scan_specs(cols, turn)
    body = lambda *refs: scan_bwd_kernel(cols, *refs)
    tall = BLOCK // 8
    return pl.pallas_call(
        body,
        grid=(blocks,),
        in_specs=[
            pl.BlockSpec((BLOCK, width), lambda c: (turn(c), 0)),
            pl.BlockSpec((8, width), lambda c: (jnp.maximum(turn(c) * tall - 1, 0), 0)),
        ]
        + starts
        + param_specs
        + [
            pl.BlockSpec((BLOCK, channels), lambda c: (turn(c), 0)),
            pl.BlockSpec((1, NS, channels), lambda c: (turn(c), 0, 0)),
            pl.BlockSpec((BLOCK, channels), lambda c: (turn(c), 0)),
            pl.BlockSpec((8, BLOCK), lambda c: (0, turn(c))),
            pl.BlockSpec((1, channels), lambda c: (0, 0)),
        ],
        out_specs=[
            pl.BlockSpec((BLOCK, width - zat), lambda c: (turn(c), 0)),
            pl.BlockSpec((8, dat - xat), lambda c: (0, 0)),
            pl.BlockSpec((16, LANES), lambda c: (0, 0)),
            pl.BlockSpec((8, channels), lambda c: (0, 0)),
        ],
        out_shape=[
            jax.ShapeDtypeStruct((length, width - zat), BF16),
            jax.ShapeDtypeStruct((8, dat - xat), F32),
            jax.ShapeDtypeStruct((16, LANES), F32),
            jax.ShapeDtypeStruct((8, channels), F32),
        ],
        scratch_shapes=[
            pltpu.VMEM((NS, channels), F32),
            pltpu.VMEM((BLOCK + 8, dat - xat), F32),
            pltpu.VMEM((BLOCK + 8, dat - xat), F32),
            pltpu.VMEM((BLOCK + 8, LANES), jnp.int32),
        ],
        compiler_params=pltpu.CompilerParams(vmem_limit_bytes=24 * MIB),
        cost_estimate=pl.CostEstimate(flops=6 * 10**9, bytes_accessed=2 * 10**7, transcendentals=3 * 10**6),
        name="scan_bwd",
    )(proj, proj, start_col, start_row, *params, y, states, grad, stats, gain)


def turned(ref, own):
    eye = jnp.where(iota((own, own), 0) == iota((own, own), 1), 1.0, 0.0).astype(BF16)
    return mm_nt(eye, ref[...]).astype(BF16)


def pack_mixer_kernel(cols, place_ref, q_ref, kv_ref, z_ref, x_ref, bc_ref, dt_ref, one_ref, two_ref, att_ref, mix_ref, out_ref):
    zat, xat, dat, width = cols
    own, qwidth = q_ref.shape
    channels = xat - zat
    out_ref[:, :qwidth] = q_ref[...]
    kv = kv_ref[...].astype(F32)
    keys, vals = kv[:, :LANES], kv[:, LANES:]
    first = place_ref[0] == 0
    keys = jnp.where(first, keys, pltpu.roll(keys, HD, 1))
    vals = jnp.where(first, pltpu.roll(vals, HD, 1), vals)
    out_ref[:, qwidth:zat] = jnp.where(iota((own, LANES), 1) < HD, keys, vals).astype(BF16)
    out_ref[:, zat:xat] = z_ref[...]
    out_ref[:, xat : xat + channels] = x_ref[...]
    out_ref[:, xat + channels : dat] = bc_ref[...]
    row, lane = iota((16, LANES), 0), iota((16, LANES), 1)
    pick = jnp.where((lane == row + HD) & (row < 2), 1.0, 0.0).astype(BF16)
    gains = iota((16, own), 0)
    gains = jnp.where(gains == 0, one_ref[...].astype(F32), jnp.where(gains == 1, two_ref[...].astype(F32), 0.0))
    out_ref[:, dat:width] = mm_tn(gains.astype(BF16), pick).astype(BF16)
    out_ref[:, dat : dat + dt_ref.shape[1]] = dt_ref[...]
    out_ref[:, width : width + qwidth] = turned(att_ref, own)
    out_ref[:, width + qwidth :] = turned(mix_ref, own)


def pack_mixer(cols, kv_head, *shards):
    own, qwidth = shards[0].shape
    zat, xat, dat, width = cols
    body = lambda *refs: pack_mixer_kernel(cols, *refs)
    whole = lambda shape: pl.BlockSpec(shape, lambda i: (0, 0))
    shape = (own, width + qwidth + xat - zat)
    return pl.pallas_call(
        body,
        grid=(1,),
        in_specs=[pl.BlockSpec(memory_space=pltpu.SMEM)] + [whole(shard.shape) for shard in shards],
        out_specs=whole(shape),
        out_shape=jax.ShapeDtypeStruct(shape, BF16),
        compiler_params=pltpu.CompilerParams(vmem_limit_bytes=60 * MIB),
        cost_estimate=pl.CostEstimate(flops=10**7, bytes_accessed=10**6, transcendentals=0),
        name="pack_mixer",
    )(kv_head, *shards)


def pack_ffn_kernel(gate_ref, up_ref, down_ref, *refs):
    out_ref = refs[-1]
    own, hidden = gate_ref.shape
    out_ref[:, :hidden] = gate_ref[...]
    out_ref[:, hidden : 2 * hidden] = up_ref[...]
    out_ref[:, 2 * hidden :] = turned(down_ref, own)


def pack_ffn(gate, up, down, earlier):
    own, hidden = gate.shape
    whole = lambda shape: pl.BlockSpec(shape, lambda i: (0, 0))
    shape = (own, 3 * hidden)
    return pl.pallas_call(
        pack_ffn_kernel,
        grid=(1,),
        in_specs=[whole(gate.shape), whole(up.shape), whole(down.shape)]
        + [pl.BlockSpec(memory_space=pl.ANY)] * len(earlier),
        out_specs=whole(shape),
        out_shape=jax.ShapeDtypeStruct(shape, BF16),
        compiler_params=pltpu.CompilerParams(vmem_limit_bytes=24 * MIB),
        cost_estimate=pl.CostEstimate(flops=10**7, bytes_accessed=10**6, transcendentals=0),
        name="pack_ffn",
    )(gate, up, down, *earlier)


def piece_at(rank_ref, refs, shift):
    if shift == 0:
        return refs[0][...]
    below, above = refs[2 * shift - 1][...], refs[2 * shift][...]
    return jnp.where(rank_ref[0] >= shift, below, above)


def norm_kernel(parts, rank_ref, *refs):
    gain_ref, out_ref = refs[2 * parts - 1], refs[2 * parts]
    rows = refs[0].shape[0]
    gain = gain_ref[...]
    for shift in range(parts):
        values = piece_at(rank_ref, refs, shift).astype(F32)
        spot = lax.rem(rank_ref[0] + (parts - shift), parts) * rows
        out_ref[pl.ds(pl.multiple_of(spot, rows), rows), :] = (values * rms_scale(values) * gain).astype(BF16)


def norm_rows(rank, parts, pieces, gain):
    rows, model = pieces[0].shape
    body = lambda *refs: norm_kernel(parts, *refs)
    whole = lambda shape: pl.BlockSpec(shape, lambda i: (0, 0))
    return pl.pallas_call(
        body,
        grid=(1,),
        in_specs=[pl.BlockSpec(memory_space=pltpu.SMEM)]
        + [whole((rows, model))] * len(pieces)
        + [whole((1, model))],
        out_specs=whole((parts * rows, model)),
        out_shape=jax.ShapeDtypeStruct((parts * rows, model), BF16),
        compiler_params=pltpu.CompilerParams(vmem_limit_bytes=24 * MIB),
        cost_estimate=pl.CostEstimate(flops=10**7, bytes_accessed=5 * 10**6, transcendentals=0),
        name="norm_rows",
    )(rank, *pieces, gain)


def branch_back_kernel(parts, rank_ref, *refs):
    count = 2 * parts - 1
    out_w_ref, am_ref, gain_ref, gatt_ref, gmix_ref, gow_ref, inner_ref, ggain_ref, sum_ref = refs[count:]
    rows = refs[0].shape[0]
    qwidth = gatt_ref.shape[1]
    sum_ref[...] = jnp.zeros_like(sum_ref)
    total = jnp.zeros((1, gmix_ref.shape[1]), F32)
    ones = jnp.ones((16, gmix_ref.shape[1]), BF16)
    for shift in range(parts):
        grads = piece_at(rank_ref, refs, shift)
        spot = pl.multiple_of(lax.rem(rank_ref[0] + (parts - shift), parts) * rows, rows)
        here = pl.ds(spot, rows)
        both = am_ref[here, :]
        grad_am = mm(grads, out_w_ref[...])
        gatt_ref[here, :] = grad_am[:, :qwidth].astype(BF16)
        grad_mixed = grad_am[:, qwidth:]
        gmix_ref[here, :] = grad_mixed
        product = grad_mixed * both[:, qwidth:].astype(F32)
        total = total + jnp.sum(product, axis=0, keepdims=True)
        high = product.astype(BF16)
        rest = (product - high.astype(F32)).astype(BF16)
        inner_ref[:, here] = (mm_nt(ones, high) + mm_nt(ones, rest))[:8]
        sum_ref[...] += mm_tn(grads, both)
    gow_ref[...] = sum_ref[...].astype(BF16)
    ggain_ref[...] = jnp.broadcast_to(total / gain_ref[...], ggain_ref.shape)


def branch_back(rank, parts, pieces, out_w, att_mixed, gain):
    rows, model = pieces[0].shape
    length, width = att_mixed.shape
    channels = gain.shape[1]
    body = lambda *refs: branch_back_kernel(parts, *refs)
    whole = lambda shape: pl.BlockSpec(shape, lambda i: (0, 0))
    shapes = [
        ((length, width - channels), BF16),
        ((length, channels), F32),
        ((model, width), BF16),
        ((8, length), F32),
        ((8, channels), F32),
    ]
    return pl.pallas_call(
        body,
        grid=(1,),
        in_specs=[pl.BlockSpec(memory_space=pltpu.SMEM)]
        + [whole((rows, model))] * len(pieces)
        + [whole((model, width)), whole((length, width)), whole((1, channels))],
        out_specs=[whole(shape) for shape, _ in shapes],
        out_shape=[jax.ShapeDtypeStruct(shape, dtype) for shape, dtype in shapes],
        scratch_shapes=[pltpu.VMEM((model, width), F32)],
        compiler_params=pltpu.CompilerParams(vmem_limit_bytes=32 * MIB),
        cost_estimate=pl.CostEstimate(flops=2 * 10**9, bytes_accessed=10**7, transcendentals=0),
        name="branch_back",
    )(rank, *pieces, out_w, att_mixed, gain)


def wgrad_kernel(step, rows_ref, gq_ref, gkv_ref, grest_ref, gow_ref, out_ref):
    turn = pl.program_id(0)
    sources = []
    for ref in (gq_ref, gkv_ref, grest_ref, gow_ref):
        sources += [(ref, lane) for lane in range(0, ref.shape[1], LANES)]
    for index in range(len(sources) // step):

        @pl.when(turn == index)
        def _(index=index):
            lanes = sources[index * step : (index + 1) * step]
            at = 0
            while at < step:
                ref, lane = lanes[at]
                count = 1
                while at + count < step and lanes[at + count][0] is ref:
                    count += 1
                span = slice(lane, lane + count * LANES)
                value = ref[:, span] if ref is gow_ref else mm_tn(rows_ref[...], ref[:, span]).astype(BF16)
                out_ref[:, at * LANES : (at + count) * LANES] = value
                at += count


def mixer_wgrad(rows_one, grad_q, grad_kv, grad_rest, grad_out_w):
    length, model = rows_one.shape
    width = grad_q.shape[1] + grad_kv.shape[1] + grad_rest.shape[1] + grad_out_w.shape[1]
    step = 3
    whole = lambda shape: pl.BlockSpec(shape, lambda i: (0, 0))
    args = (rows_one, grad_q, grad_kv, grad_rest, grad_out_w)
    return pl.pallas_call(
        lambda *refs: wgrad_kernel(step, *refs),
        grid=(width // (step * LANES),),
        in_specs=[whole(arg.shape) for arg in args],
        out_specs=pl.BlockSpec((model, step * LANES), lambda i: (0, i)),
        out_shape=jax.ShapeDtypeStruct((model, width), BF16),
        compiler_params=pltpu.CompilerParams(vmem_limit_bytes=32 * MIB),
        cost_estimate=pl.CostEstimate(flops=3 * 10**9, bytes_accessed=10**7, transcendentals=0),
        name="mixer_wgrad",
    )(*args)


def back_proj_kernel(zat, rank_ref, gq_ref, gkv_ref, grest_ref, w_ref, rows_ref, gain_ref, *outs):
    turn = pl.program_id(0)
    ggain_ref = outs[-1]
    qwidth = gq_ref.shape[1]
    term = mm_nt(gq_ref[...], w_ref[:, :qwidth]) + mm_nt(gkv_ref[...], w_ref[:, qwidth:zat])
    term = term + mm_nt(grest_ref[...], w_ref[:, zat:])
    share = jnp.sum(term * rows_ref[...].astype(F32), axis=0, keepdims=True) / gain_ref[...]

    @pl.when(turn == 0)
    def _():
        ggain_ref[...] = jnp.zeros_like(ggain_ref)

    ggain_ref[0:1, :] += share
    for index in range(len(outs) - 1):

        @pl.when(turn == index)
        def _(index=index):
            outs[index][...] = term.astype(outs[index].dtype)


def back_proj(rank, parts, zat, width, grad_q, grad_kv, grad_rest, mixer_w, rows_one, gain):
    length, model = rows_one.shape
    rows = length // parts
    at = lambda s, rank_ref: (lax.rem(rank_ref[0] + s, parts), 0)
    fixed = lambda s, rank_ref: (0, 0)
    spec = pltpu.PrefetchScalarGridSpec(
        num_scalar_prefetch=1,
        grid=(parts,),
        in_specs=[
            pl.BlockSpec((rows, grad_q.shape[1]), at),
            pl.BlockSpec((rows, grad_kv.shape[1]), at),
            pl.BlockSpec((rows, grad_rest.shape[1]), at),
            pl.BlockSpec((model, width), fixed),
            pl.BlockSpec((rows, model), at),
            pl.BlockSpec((1, model), fixed),
        ],
        out_specs=[pl.BlockSpec((rows, model), fixed)] * parts + [pl.BlockSpec((8, model), fixed)],
    )
    return pl.pallas_call(
        lambda *refs: back_proj_kernel(zat, *refs),
        grid_spec=spec,
        out_shape=[jax.ShapeDtypeStruct((rows, model), F32)]
        + [jax.ShapeDtypeStruct((rows, model), BF16)] * (parts - 1)
        + [jax.ShapeDtypeStruct((8, model), F32)],
        compiler_params=pltpu.CompilerParams(vmem_limit_bytes=32 * MIB),
        cost_estimate=pl.CostEstimate(flops=3 * 10**9, bytes_accessed=10**7, transcendentals=0),
        name="back_proj",
    )(rank, grad_q, grad_kv, grad_rest, mixer_w, rows_one, gain)


def ffn_kernel(middle_ref, cot_ref, gain_ref, w_ref, out_ref, gmid_ref, glow_ref, ggain_ref, gw_ref, low_ref, sum_ref, gsum_ref):
    step = pl.program_id(0)
    hidden = w_ref.shape[1] // 3

    @pl.when(step == 0)
    def _():
        middle = middle_ref[...]
        low_ref[...] = (middle * rms_scale(middle) * gain_ref[...]).astype(BF16)
        sum_ref[...] = jnp.zeros_like(sum_ref)
        gsum_ref[...] = jnp.zeros_like(gsum_ref)

    low = low_ref[...]
    cot = cot_ref[...]
    gate_pre = mm(low, w_ref[:, :hidden])
    up_pre = mm(low, w_ref[:, hidden : 2 * hidden])
    sig = sigmoid(gate_pre)
    silu_gate = gate_pre * sig
    act = (silu_gate * up_pre).astype(BF16)
    sum_ref[...] += mm_nt(act, w_ref[:, 2 * hidden :])
    gw_ref[:, 2 * hidden :] = mm_tn(cot, act).astype(BF16)
    grad_hidden = mm(cot, w_ref[:, 2 * hidden :])
    grad_gate = (grad_hidden * up_pre * sig * (1.0 + gate_pre * (1.0 - sig))).astype(BF16)
    grad_up = (grad_hidden * silu_gate).astype(BF16)
    gw_ref[:, :hidden] = mm_tn(low, grad_gate).astype(BF16)
    gw_ref[:, hidden : 2 * hidden] = mm_tn(low, grad_up).astype(BF16)
    gsum_ref[...] += mm_nt(grad_gate, w_ref[:, :hidden]) + mm_nt(grad_up, w_ref[:, hidden : 2 * hidden])

    @pl.when(step == pl.num_programs(0) - 1)
    def _():
        middle = middle_ref[...]
        out_ref[...] = (middle + sum_ref[...]).astype(BF16)
        scale = rms_scale(middle)
        normed = middle * scale
        grad_two = gsum_ref[...]
        ggain_ref[...] = jnp.broadcast_to(jnp.sum(grad_two * normed, axis=0, keepdims=True), ggain_ref.shape)
        grad_middle = cot_ref[...].astype(F32) + norm_back(grad_two * gain_ref[...], normed, scale)
        gmid_ref[...] = grad_middle
        glow_ref[...] = grad_middle.astype(BF16)


def ffn_both(middle, cotangent, gain, ffn_w, parts):
    rows, model = middle.shape
    piece = ffn_w.shape[1] // parts
    rowspec = pl.BlockSpec((rows, model), lambda s: (0, 0))
    wspec = pl.BlockSpec((model, piece), lambda s: (0, s))
    return pl.pallas_call(
        ffn_kernel,
        grid=(parts,),
        in_specs=[rowspec, rowspec, pl.BlockSpec((1, model), lambda s: (0, 0)), wspec],
        out_specs=[rowspec, rowspec, rowspec, pl.BlockSpec((8, model), lambda s: (0, 0)), wspec],
        out_shape=[
            jax.ShapeDtypeStruct((rows, model), BF16),
            jax.ShapeDtypeStruct((rows, model), F32),
            jax.ShapeDtypeStruct((rows, model), BF16),
            jax.ShapeDtypeStruct((8, model), F32),
            jax.ShapeDtypeStruct(ffn_w.shape, BF16),
        ],
        scratch_shapes=[
            pltpu.VMEM((rows, model), BF16),
            pltpu.VMEM((rows, model), F32),
            pltpu.VMEM((rows, model), F32),
        ],
        compiler_params=pltpu.CompilerParams(vmem_limit_bytes=40 * MIB),
        cost_estimate=pl.CostEstimate(flops=10**10, bytes_accessed=3 * 10**7, transcendentals=10**6),
        name="ffn_both",
    )(middle, cotangent, gain, ffn_w)


def lane_rows(values, rows):
    padded = jnp.pad(values, (0, rows - values.shape[0]))
    return jnp.broadcast_to(padded[:, None], (rows, LANES))


def shifted(values, axis, size, shift):
    return lax.ppermute(values, axis, [(i, (i + shift) % size) for i in range(size)])


def sent(values, pairs):
    return lax.ppermute(values, "tensor", pairs)


def pieces_of_group(values, parts):
    up = lambda shift: [(i, i + shift) for i in range(parts - shift)]
    down = lambda shift: [(i + shift, i) for i in range(parts - shift)]
    if parts != 4:
        below = [sent(values, up(shift)) for shift in range(1, parts)]
        above = [sent(values, down(shift)) for shift in range(1, parts)]
    else:
        first_up, first_down = sent(values, up(1)), sent(values, down(1))
        below = [first_up, sent(first_up, [(1, 2), (2, 3)]), sent(first_up, [(1, 3)])]
        above = [first_down, sent(first_down, [(2, 1), (1, 0)]), sent(first_down, [(2, 0)])]
    pieces = [values]
    for shift in range(1, parts):
        pieces += [below[shift - 1], above[parts - shift - 1]]
    return pieces


def sum_to_owner(terms, parts):
    total = terms[0].astype(F32)
    for shift in range(1, parts):
        total = total + shifted(terms[shift].astype(BF16), "tensor", parts, shift).astype(F32)
    return total


def chip_sum(values, own):
    size = lax.axis_size("dp")
    me = lax.axis_index("dp")
    chips = size // 2
    if size & (size - 1):
        return lax.psum_scatter(values, "dp", scatter_dimension=0, tiled=True).astype(F32)
    blocks = values.reshape(chips, 2, own, values.shape[1])
    core = lax.rem(me, 2)
    theirs = lax.dynamic_index_in_dim(blocks, 1 - core, 1, keepdims=False)
    ours = lax.dynamic_index_in_dim(blocks, core, 1, keepdims=False)
    theirs = lax.ppermute(theirs, "dp", [(i, i ^ 1) for i in range(size)])
    total = 0.0
    for mask in range(chips):
        chip = lax.bitwise_xor(me // 2, mask)
        term = lax.dynamic_index_in_dim(ours, chip, 0, keepdims=False).astype(F32)
        term = term + lax.dynamic_index_in_dim(theirs, chip, 0, keepdims=False).astype(F32)
        if mask:
            term = lax.ppermute(term.astype(BF16), "dp", [(i, i ^ (2 * mask)) for i in range(size)]).astype(F32)
        total = total + term
    return total


def rows_of(values, rank, shift, parts):
    rows = values.shape[0] // parts
    return lax.dynamic_slice(values, (lax.rem(rank + shift, parts) * rows, 0), (rows, values.shape[1]))


def group_total(values, parts):
    total = values.astype(F32)
    for shift in range(1, parts):
        total = total + shifted(values, "tensor", parts, shift).astype(F32)
    return total


def butterfly(values, axis, size):
    if size & (size - 1):
        return lax.psum(values, axis)
    step = 1
    while step < size:
        values = values + lax.ppermute(values, axis, [(i, i ^ step) for i in range(size)])
        step *= 2
    return values


def local(
    x_in,
    cotangent,
    segments,
    norm_one,
    w_query,
    w_keyval,
    w_attn_out,
    w_zgate,
    w_xin,
    w_bcin,
    w_dtin,
    conv_x,
    conv_bc,
    bias_x,
    bias_bc,
    dt_bias,
    a_log,
    d_skip,
    ssm_gain,
    w_mix_out,
    norm_two,
    w_gate,
    w_up,
    w_down,
):
    parts = lax.axis_size("tensor")
    rank = lax.axis_index("tensor")
    own = w_query.shape[0]
    length = segments.shape[1]
    qwidth = w_query.shape[1]
    channels = w_zgate.shape[1]
    heads = w_dtin.shape[1]
    hidden_own = w_gate.shape[1]
    width_ssm = MH * PD
    kv_head = (rank * (qwidth // HD)) // (QH // KVH)
    zat = 2 * qwidth
    xat = zat + channels
    bat = xat + channels
    dat = bat + 2 * NS
    width = dat + LANES
    cols = (zat, xat, dat, width)

    x_pieces = pieces_of_group(x_in, parts)
    mixer_own = pack_mixer(
        cols,
        kv_head.astype(jnp.int32)[None],
        w_query,
        w_keyval,
        w_zgate,
        w_xin,
        w_bcin,
        w_dtin,
        norm_one[None, :],
        norm_two[None, :],
        w_attn_out,
        w_mix_out,
    )
    mixer_w = lax.all_gather(mixer_own, "dp", axis=0, tiled=True)
    proj_w = mixer_w[:, :width]
    out_w = mixer_w[:, width:]
    gain_one = mixer_w[:, dat + HD].astype(F32)[None, :]
    gain_two = mixer_w[:, dat + HD + 1].astype(F32)[None, :]
    ffn_own = pack_ffn(w_gate, w_up, w_down, x_pieces[1:])
    ffn_own = jnp.concatenate(
        [ffn_own] + [shifted(ffn_own, "tensor", parts, shift) for shift in range(1, parts)], axis=1
    )
    ffn_w = lax.all_gather(ffn_own, "dp", axis=0, tiled=True)

    seg = segments[0]
    start = jnp.sum((seg[None, :] < seg[:, None]).astype(jnp.int32), axis=1)
    start_col = jnp.broadcast_to(start[:, None], (length, LANES))
    start_row = jnp.broadcast_to(start[None, :], (8, length))
    cosine, sine = rope_tables(length)
    taps = jnp.pad(jnp.concatenate([conv_x, conv_bc], axis=1), ((0, 8 - KW), (0, 0)))
    bias = jnp.concatenate([bias_x, bias_bc])[None, :]
    params = (taps, bias, lane_rows(dt_bias, 8), lane_rows(jnp.exp(a_log), 8), jnp.repeat(d_skip, PD)[None, :])

    residual = x_in.astype(F32)
    scale_one = rms_scale(residual)
    normed_one = residual * scale_one
    rank_arg = rank.astype(jnp.int32)[None]
    rows_one = norm_rows(rank_arg, parts, x_pieces, gain_one)
    proj = mm(rows_one, proj_w)
    y, gated, states, squares = scan_forward(cols, proj, start_col, start_row, params)
    attended, lse, low_q, low_kv = attn_forward(proj, cosine, sine, start_col)
    scale_ssm = lax.rsqrt(group_total(squares[:1], parts) / width_ssm + EPSILON)
    mixed = (gated * scale_ssm[0][:, None] * ssm_gain[None, :]).astype(BF16)
    att_mixed = jnp.concatenate([attended, mixed], axis=1)
    terms = [mm_nt(rows_of(att_mixed, rank, shift, parts), out_w) for shift in range(parts)]
    middle = residual + sum_to_owner(terms, parts)
    block_out, grad_middle, grad_low, grad_gain_two, grad_ffn_w = ffn_both(middle, cotangent, gain_two, ffn_w, parts)

    branch_pieces = pieces_of_group(grad_low, parts)
    grad_ffn_own = lax.psum_scatter(grad_ffn_w, "dp", scatter_dimension=0, tiled=True)
    piece = grad_ffn_own.shape[1] // parts
    terms = [grad_ffn_own[:, k * piece : (k + 1) * piece] for k in range(parts)]
    grad_ffn = sum_to_owner(terms[:1] + terms[:0:-1], parts)

    grad_att, grad_mixed, grad_out_w, inner, grad_gain_ssm = branch_back(
        rank_arg, parts, branch_pieces, out_w, att_mixed, ssm_gain[None, :]
    )
    inner = group_total(inner[:1], parts) / width_ssm
    stats = jnp.concatenate([scale_ssm, inner, jnp.zeros((6, length), F32)], axis=0)
    grad_q, grad_kv = attn_backward(low_q, low_kv, lse, attended, grad_att, cosine, sine, start_col)
    grad_rest, conv_acc, head_acc, skip_acc = scan_backward(
        cols, proj, start_col, start_row, params, y, states, grad_mixed, stats, ssm_gain[None, :]
    )
    *terms, grad_gain_one = back_proj(
        rank_arg, parts, zat, width, grad_q, grad_kv, grad_rest, mixer_w, rows_one, gain_one
    )
    grad_one = sum_to_owner(terms, parts)
    grad_input = grad_middle + norm_back(grad_one * gain_one, normed_one, scale_one)
    grad_mixer_w = mixer_wgrad(rows_one, grad_q, grad_kv, grad_rest, grad_out_w)
    grad_w = chip_sum(grad_mixer_w, own)

    model = x_in.shape[1]
    wide = lambda rows: jnp.pad(rows, ((0, 0), (0, model - rows.shape[1])))
    head_sums = jnp.sum(head_acc, axis=1)[None, :]
    small = jnp.concatenate(
        [
            wide(conv_acc),
            grad_gain_one[:1],
            grad_gain_two[:1],
            wide(grad_gain_ssm[:1]),
            wide(skip_acc[:1]),
            wide(head_sums),
            jnp.zeros((3, model), F32),
        ],
        axis=0,
    )
    small = butterfly(small, "dp", lax.axis_size("dp"))
    shared_small = butterfly(small, "tensor", parts)
    grad_conv_x = small[:KW, :channels]
    grad_bias_x = small[KW, :channels]
    grad_ssm_gain = small[10, :channels]
    grad_d_skip = jnp.sum(small[11, :channels].reshape(heads, PD), axis=1)
    grad_dt_bias = small[12, :heads]
    grad_a_log = small[12, 8 : 8 + heads]
    grad_conv_bc = shared_small[:KW, channels : channels + 2 * NS]
    grad_bias_bc = shared_small[KW, channels : channels + 2 * NS]
    place = lax.axis_index("dp") * own
    norm_grads = lax.dynamic_slice(shared_small, (8, place), (2, own))
    grad_norm_one, grad_norm_two = norm_grads[0], norm_grads[1]

    grad_keyval = jnp.zeros((own, 2 * KVH * HD), F32)
    grad_keyval = lax.dynamic_update_slice(grad_keyval, grad_w[:, qwidth : qwidth + HD], (0, kv_head * HD))
    grad_keyval = lax.dynamic_update_slice(
        grad_keyval, grad_w[:, qwidth + HD : zat], (0, (KVH + kv_head) * HD)
    )
    shared = jnp.concatenate([grad_keyval, grad_w[:, bat:dat]], axis=1)
    shared = group_total(shared.astype(BF16), parts)

    return (
        block_out,
        grad_input,
        grad_norm_one,
        grad_w[:, :qwidth],
        shared[:, : 2 * KVH * HD],
        grad_w[:, width : width + qwidth].T,
        grad_w[:, zat:xat],
        grad_w[:, xat:bat],
        shared[:, 2 * KVH * HD :],
        grad_w[:, dat : dat + heads],
        grad_conv_x,
        grad_conv_bc,
        grad_bias_x,
        grad_bias_bc,
        grad_dt_bias,
        grad_a_log,
        grad_d_skip,
        grad_ssm_gain,
        grad_w[:, width + qwidth :].T,
        grad_norm_two,
        grad_ffn[:, :hidden_own],
        grad_ffn[:, hidden_own : 2 * hidden_own],
        grad_ffn[:, 2 * hidden_own :].T,
    )


def solution(mesh):
    return jax.shard_map(
        local,
        mesh=mesh,
        in_specs=(
            P(("dp", "tensor"), None),
            P(("dp", "tensor"), None),
            P("dp", None),
            P("dp"),
            P("dp", "tensor"),
            P("dp", None),
            P("tensor", "dp"),
            P("dp", "tensor"),
            P("dp", "tensor"),
            P("dp", None),
            P("dp", "tensor"),
            P(None, "tensor"),
            P(),
            P("tensor"),
            P(),
            P("tensor"),
            P("tensor"),
            P("tensor"),
            P("tensor"),
            P("tensor", "dp"),
            P("dp"),
            P("dp", "tensor"),
            P("dp", "tensor"),
            P("tensor", "dp"),
        ),
        out_specs=(
            P(("dp", "tensor"), None),
            P(("dp", "tensor"), None),
            P("dp"),
            P("dp", "tensor"),
            P("dp", None),
            P("tensor", "dp"),
            P("dp", "tensor"),
            P("dp", "tensor"),
            P("dp", None),
            P("dp", "tensor"),
            P(None, "tensor"),
            P(),
            P("tensor"),
            P(),
            P("tensor"),
            P("tensor"),
            P("tensor"),
            P("tensor"),
            P("tensor", "dp"),
            P("dp"),
            P("dp", "tensor"),
            P("dp", "tensor"),
            P("tensor", "dp"),
        ),
        check_vma=False,
    )
```

```python
import math

import jax
import jax.numpy as jnp
import numpy as np
from jax import lax
from jax.experimental import pallas as pl
from jax.experimental.pallas import tpu as pltpu
from jax.sharding import PartitionSpec as P

QH = 8
KVH = 2
HD = 64
MH = 24
PD = 64
NS = 128
KW = 4
BLOCK = 128
LANES = 128

EPSILON = 1e-05
ROPE_BASE = 100000000000.0
NEG = -1e9
F32 = jnp.float32
BF16 = jnp.bfloat16
MIB = 1024 * 1024


def mm(lhs, rhs):
    return lax.dot_general(lhs, rhs, (((1,), (0,)), ((), ())), preferred_element_type=F32)


def mm_nt(lhs, rhs):
    return lax.dot_general(lhs, rhs, (((1,), (1,)), ((), ())), preferred_element_type=F32)


def mm_tn(lhs, rhs):
    return lax.dot_general(lhs, rhs, (((0,), (0,)), ((), ())), preferred_element_type=F32)


def rms_scale(values):
    return lax.rsqrt(jnp.mean(values * values, axis=-1, keepdims=True) + EPSILON)


def norm_back(grad_normed, normed, scale):
    return scale * (grad_normed - normed * jnp.mean(grad_normed * normed, axis=-1, keepdims=True))


def sigmoid(v):
    return 1.0 / (1.0 + jnp.exp(-v))


def iota(shape, dim):
    return lax.broadcasted_iota(jnp.int32, shape, dim)


def rope_tables(length):
    half = HD // 2
    freqs = np.float32(ROPE_BASE) ** (-(np.arange(half, dtype=np.float32) * np.float32(2.0 / HD)))
    angles = np.arange(length, dtype=np.float32)[:, None] * freqs.astype(np.float32)[None, :]
    cosine, sine = np.cos(angles).astype(np.float32), np.sin(angles).astype(np.float32)
    cos_lanes = np.concatenate([cosine] * 4, axis=1)
    sin_lanes = np.concatenate([-sine, sine, -sine, sine], axis=1)
    return jnp.asarray(cos_lanes), jnp.asarray(sin_lanes)


def swap_halves(values):
    lane = iota(values.shape, 1)
    ahead = pltpu.roll(values, LANES - HD // 2, 1)
    behind = pltpu.roll(values, HD // 2, 1)
    return jnp.where((lane & (HD - 1)) < HD // 2, ahead, behind)


def pair_rows(block):
    low = iota(block.shape, 1) < HD
    zero = jnp.zeros_like(block)
    return jnp.concatenate([jnp.where(low, block, zero), jnp.where(low, zero, block)], axis=0)


def attn_fwd_kernel(q_ref, kv_ref, cos_ref, sin_ref, start_ref, out_ref, lse_ref, lq_ref, lkv_ref):
    length = q_ref.shape[0]
    rows = 256
    cosine, sine = cos_ref[...], sin_ref[...]
    low = iota((length, LANES), 1) < HD
    queries = q_ref[...]
    lq_ref[...] = (queries * cosine + swap_halves(queries) * sine).astype(BF16)
    kv = kv_ref[...]
    kv = jnp.where(low, kv * cosine + swap_halves(kv) * sine, kv)
    lkv_ref[...] = kv.astype(BF16)
    other = pltpu.roll(kv, HD, 1)
    keys = jnp.where(low, kv, other).astype(BF16)
    vals = jnp.where(low, other, kv).astype(BF16)
    half = iota((rows, LANES), 1) < HD
    for step in range(length // rows):
        end = (step + 1) * rows
        span = slice(step * rows, end)
        stacked = pair_rows(lq_ref[span, :].astype(F32)).astype(BF16)
        scores = mm_nt(stacked, keys[:end]) * (1.0 / math.sqrt(HD))
        first = start_ref[span, :][:, :1]
        col = iota((rows, end), 1)
        row = iota((rows, end), 0) + step * rows
        allowed = (col <= row) & (col >= first)
        allowed = jnp.concatenate([allowed.astype(jnp.int32)] * 2, axis=0) > 0
        scores = jnp.where(allowed, scores, NEG)
        top = jnp.max(scores, axis=1, keepdims=True)
        expo = jnp.exp(scores - top)
        total = jnp.sum(expo, axis=1, keepdims=True)
        probs = (expo * (1.0 / total)).astype(BF16)
        result = mm(probs, vals[:end])
        out_ref[span, :] = jnp.where(half, result[:rows], result[rows:]).astype(BF16)
        lse = top + jnp.log(total)
        lse_ref[span, :] = jnp.where(half, lse[:rows], lse[rows:])


def attn_bwd_kernel(
    lq_ref, lkv_ref, lse_ref, out_ref, go_ref, cos_ref, sin_ref, start_ref, gq_ref, gkv_ref, dk_ref, dv_ref
):
    length = lq_ref.shape[0]
    rows = 256
    cosine, sine = cos_ref[...], sin_ref[...]
    low = iota((length, LANES), 1) < HD
    kv = lkv_ref[...].astype(F32)
    other = pltpu.roll(kv, HD, 1)
    keys = jnp.where(low, kv, other).astype(BF16)
    vals = jnp.where(low, other, kv).astype(BF16)
    half = iota((rows, LANES), 1) < HD
    dk_ref[...] = jnp.zeros_like(dk_ref)
    dv_ref[...] = jnp.zeros_like(dv_ref)
    inv = 1.0 / math.sqrt(HD)
    for step in range(length // rows):
        end = (step + 1) * rows
        span = slice(step * rows, end)
        stacked = pair_rows(lq_ref[span, :].astype(F32)).astype(BF16)
        grads = pair_rows(go_ref[span, :].astype(F32))
        outs = out_ref[span, :].astype(F32)
        inner = jnp.sum(grads * jnp.concatenate([outs, outs], axis=0), axis=1, keepdims=True)
        grads = grads.astype(BF16)
        lse = lse_ref[span, :]
        lse = jnp.concatenate([lse[:, :1], lse[:, HD : HD + 1]], axis=0)
        scores = mm_nt(stacked, keys[:end]) * inv
        first = start_ref[span, :][:, :1]
        col = iota((rows, end), 1)
        row = iota((rows, end), 0) + step * rows
        allowed = (col <= row) & (col >= first)
        allowed = jnp.concatenate([allowed.astype(jnp.int32)] * 2, axis=0) > 0
        probs = jnp.exp(jnp.where(allowed, scores, NEG) - lse)
        grad_probs = mm_nt(grads, vals[:end])
        grad_scores = (probs * (grad_probs - inner)).astype(BF16)
        gq = mm(grad_scores, keys[:end]) * inv
        gq = jnp.where(half, gq[:rows], gq[rows:])
        gq_ref[span, :] = (gq * cosine[span] - swap_halves(gq) * sine[span]).astype(BF16)
        dk_ref[:end, :] += mm_tn(grad_scores, stacked)
        dv_ref[:end, :] += mm_tn(probs.astype(BF16), grads)
    dk = dk_ref[...] * inv
    dk = dk + pltpu.roll(dk, HD, 1)
    dk = dk * cosine - swap_halves(dk) * sine
    dv = dv_ref[...]
    dv = dv + pltpu.roll(dv, HD, 1)
    gkv_ref[...] = jnp.where(low, dk, dv).astype(BF16)


def attn_forward(proj, cosine, sine, start_col):
    length = proj.shape[0]
    wide = pl.BlockSpec((length, LANES), lambda i: (0, 0))
    return pl.pallas_call(
        attn_fwd_kernel,
        grid=(1,),
        in_specs=[wide, pl.BlockSpec((length, LANES), lambda i: (0, 1)), wide, wide, wide],
        out_specs=[wide] * 4,
        out_shape=[
            jax.ShapeDtypeStruct((length, LANES), BF16),
            jax.ShapeDtypeStruct((length, LANES), F32),
            jax.ShapeDtypeStruct((length, LANES), BF16),
            jax.ShapeDtypeStruct((length, LANES), BF16),
        ],
        compiler_params=pltpu.CompilerParams(vmem_limit_bytes=32 * MIB),
        cost_estimate=pl.CostEstimate(flops=10**9, bytes_accessed=6 * 10**6, transcendentals=2 * 10**6),
        name="attn_fwd",
    )(proj, proj, cosine, sine, start_col)


def attn_backward(low_q, low_kv, lse, out, grad_out, cosine, sine, start_col):
    length = low_q.shape[0]
    wide = pl.BlockSpec((length, LANES), lambda i: (0, 0))
    return pl.pallas_call(
        attn_bwd_kernel,
        grid=(1,),
        in_specs=[wide] * 8,
        out_specs=[wide] * 2,
        out_shape=[jax.ShapeDtypeStruct((length, LANES), BF16)] * 2,
        scratch_shapes=[pltpu.VMEM((length, LANES), F32)] * 2,
        compiler_params=pltpu.CompilerParams(vmem_limit_bytes=32 * MIB),
        cost_estimate=pl.CostEstimate(flops=3 * 10**9, bytes_accessed=6 * 10**6, transcendentals=2 * 10**6),
        name="attn_bwd",
    )(low_q, low_kv, lse, out, grad_out, cosine, sine, start_col)


def split3(values):
    high = values.astype(BF16).astype(F32)
    rest = values - high
    mid = rest.astype(BF16).astype(F32)
    tail = rest - mid
    return jnp.concatenate([high, mid, tail, jnp.zeros_like(values)], axis=0).astype(BF16)


def spread(rows, width, lanes_each):
    pick = (iota((32, width), 1) // lanes_each) == (iota((32, width), 0) & 7)
    return mm_tn(split3(rows), pick.astype(F32).astype(BF16))


def decay_terms(dt_block, dt_bias, rate, start_row, start_col, base):
    dt_rows = jnp.transpose(dt_block)[:8] + dt_bias
    step = jnp.maximum(dt_rows, 0.0) + jnp.log1p(jnp.exp(-jnp.abs(dt_rows)))
    log_decay = -step * rate
    row = iota((BLOCK, BLOCK), 0) + base
    col = iota((BLOCK, BLOCK), 1) + base
    linked = (col <= row) & (col >= start_col)
    linked_low = jnp.where(linked, 1.0, 0.0).astype(BF16)
    cum = mm_nt(split3(log_decay), linked_low)
    cum = cum[0:8] + cum[8:16] + cum[16:24]
    enter = jnp.exp(jnp.where(start_row < base, cum, NEG))
    last = cum[:, BLOCK - 1 :]
    position = iota((8, BLOCK), 1) + base
    tail = jnp.exp(jnp.where(position >= start_row[:, BLOCK - 1 :], last - cum, NEG))
    return dt_rows, step, log_decay, linked, linked_low, cum, enter, tail


def conv_sum(ext_ref, taps, bias, place):
    total = bias + taps[KW - 1 : KW] * ext_ref[pl.ds(8, BLOCK), :]
    for offset in range(1, KW):
        shifted = ext_ref[pl.ds(8 - offset, BLOCK), :]
        total = total + jnp.where(place >= offset, taps[KW - 1 - offset : KW - offset] * shifted, 0.0)
    return total


def wide_place(start_col, base, width):
    place = iota((BLOCK, BLOCK), 0) + base - start_col
    return jnp.concatenate([place] * (width // LANES), axis=1)


def scan_fwd_kernel(
    cols,
    proj_ref,
    startc_ref,
    startr_ref,
    taps_ref,
    bias_ref,
    dtb_ref,
    rate_ref,
    skip_ref,
    y_ref,
    gated_ref,
    state_out_ref,
    ssq_ref,
    state_ref,
    ext_ref,
):
    zat, xat, dat, width = cols
    channels = xat - zat
    heads = channels // PD
    block = pl.program_id(0)
    base = block * BLOCK

    @pl.when(block == 0)
    def _():
        state_ref[...] = jnp.zeros_like(state_ref)
        ext_ref[0:8, :] = jnp.zeros((8, ext_ref.shape[1]), F32)

    start_col = startc_ref[...]
    start_row = startr_ref[...]
    ext_ref[pl.ds(8, BLOCK), :] = proj_ref[:, xat:dat]
    place = wide_place(start_col, base, dat - xat)
    pre = conv_sum(ext_ref, taps_ref[...], bias_ref[...], place)
    ext_ref[0:8, :] = ext_ref[pl.ds(BLOCK, 8), :]
    conv = (pre * sigmoid(pre)).astype(BF16)
    x_low, b_low, c_low = conv[:, :channels], conv[:, channels : channels + NS], conv[:, channels + NS :]
    x_val = x_low.astype(F32)
    _, step, _, linked, _, cum, enter, tail = decay_terms(
        proj_ref[:, dat:width], dtb_ref[...], rate_ref[...], start_row, start_col, base
    )
    contact = mm_nt(c_low, b_low)
    cum_cols = spread(cum, heads * LANES, LANES)
    enter_x = spread(enter, channels, PD)
    weight_x = spread(tail * step, channels, PD)
    low = iota((BLOCK, LANES), 1) < PD
    zero = jnp.zeros((BLOCK, LANES), F32)
    within = []
    for pair in range(heads // 2):
        mixes = []
        for head in (2 * pair, 2 * pair + 1):
            gap = cum_cols[:, head * LANES : (head + 1) * LANES] - cum[head : head + 1]
            decay = jnp.exp(jnp.where(linked, gap, NEG))
            mixes.append((decay * (contact * step[head : head + 1])).astype(BF16))
        x_pair = x_val[:, pair * LANES : (pair + 1) * LANES]
        both = jnp.concatenate([jnp.where(low, x_pair, zero), jnp.where(low, zero, x_pair)], axis=0).astype(BF16)
        within.append(mm(jnp.concatenate(mixes, axis=1), both))
    state = state_ref[...]
    state_low = state.astype(BF16)
    state_out_ref[0] = state_low
    y = jnp.concatenate(within, axis=1) + enter_x * mm(c_low, state_low) + skip_ref[...] * x_val
    y_ref[...] = y
    state_ref[...] = mm_tn(b_low, (weight_x * x_val).astype(BF16)) + enter_x[BLOCK - 1 :] * state
    z = proj_ref[:, zat:xat]
    gated = y * (z * sigmoid(z))
    gated_ref[...] = gated
    square = gated * gated
    high = square.astype(BF16)
    rest = (square - high.astype(F32)).astype(BF16)
    ones = jnp.ones((16, channels), BF16)
    ssq_ref[...] = (mm_nt(ones, high) + mm_nt(ones, rest))[:8]


def scan_bwd_kernel(
    cols,
    proj_ref,
    prev_ref,
    startc_ref,
    startr_ref,
    taps_ref,
    bias_ref,
    dtb_ref,
    rate_ref,
    skip_ref,
    y_ref,
    state_in_ref,
    grad_ref,
    stats_ref,
    gain_ref,
    out_ref,
    conv_acc_ref,
    head_acc_ref,
    skip_acc_ref,
    dstate_ref,
    ext_ref,
    dext_ref,
    pext_ref,
):
    zat, xat, dat, width = cols
    channels = xat - zat
    heads = channels // PD
    turn = pl.program_id(0)
    block = pl.num_programs(0) - 1 - turn
    base = block * BLOCK

    @pl.when(turn == 0)
    def _():
        dstate_ref[...] = jnp.zeros_like(dstate_ref)
        conv_acc_ref[...] = jnp.zeros_like(conv_acc_ref)
        head_acc_ref[...] = jnp.zeros_like(head_acc_ref)
        skip_acc_ref[...] = jnp.zeros_like(skip_acc_ref)
        dext_ref[pl.ds(BLOCK, 8), :] = jnp.zeros((8, dext_ref.shape[1]), F32)
        pext_ref[pl.ds(BLOCK, 8), :] = jnp.zeros((8, LANES), jnp.int32)

    start_col = startc_ref[...]
    start_row = startr_ref[...]
    taps = taps_ref[...]
    ext_ref[0:8, :] = prev_ref[:, xat:dat]
    ext_ref[pl.ds(8, BLOCK), :] = proj_ref[:, xat:dat]
    place = wide_place(start_col, base, dat - xat)
    pre = conv_sum(ext_ref, taps, bias_ref[...], place)
    pre_sig = sigmoid(pre)
    conv = (pre * pre_sig).astype(BF16)
    x_low, b_low, c_low = conv[:, :channels], conv[:, channels : channels + NS], conv[:, channels + NS :]
    x_val = x_low.astype(F32)
    rate = rate_ref[...]
    dt_rows, step, log_decay, linked, linked_low, cum, enter, tail = decay_terms(
        proj_ref[:, dat:width], dtb_ref[...], rate, start_row, start_col, base
    )
    contact = mm_nt(c_low, b_low)
    cum_cols = spread(cum, heads * LANES, LANES)
    enter_x = spread(enter, channels, PD)
    weight = tail * step
    weight_x = spread(weight, channels, PD)

    z = proj_ref[:, zat:xat]
    z_sig = sigmoid(z)
    z_silu = z * z_sig
    y_val = y_ref[...]
    stats = spread(stats_ref[...], 2 * channels, channels)
    scale_x, inner_x = stats[:, :channels], stats[:, channels:]
    grad = scale_x * (grad_ref[...] * gain_ref[...] - y_val * z_silu * scale_x * inner_x)
    dy = grad * z_silu
    out_ref[:, :channels] = (grad * y_val * (z_sig * (1.0 + z * (1.0 - z_sig)))).astype(BF16)

    low = iota((BLOCK, LANES), 1) < PD
    strict = linked & (iota((BLOCK, BLOCK), 0) > iota((BLOCK, BLOCK), 1))
    zero = jnp.zeros((BLOCK, LANES), F32)
    dcontact = zero
    dx_parts, w_parts, step_rows = [], [], []
    for pair in range(heads // 2):
        lanes = slice(pair * LANES, (pair + 1) * LANES)
        dy_pair = dy[:, lanes]
        dy_both = jnp.concatenate([jnp.where(low, dy_pair, zero), jnp.where(low, zero, dy_pair)], axis=0).astype(BF16)
        outer = mm_nt(dy_both, x_low[:, lanes])
        mixes = []
        for slot in range(2):
            head = 2 * pair + slot
            gap = cum_cols[:, head * LANES : (head + 1) * LANES] - cum[head : head + 1]
            decay = jnp.exp(jnp.where(linked, gap, NEG))
            step_row = step[head : head + 1]
            share = outer[slot * BLOCK : (slot + 1) * BLOCK] * decay
            dcontact = dcontact + share * step_row
            flow = share * contact
            step_rows.append(jnp.sum(flow, axis=0, keepdims=True))
            w_parts.append(jnp.where(strict, flow * step_row, 0.0).astype(BF16))
            mixes.append((decay * (contact * step_row)).astype(BF16))
        dx_parts.append(mm_tn(jnp.concatenate(mixes, axis=0), dy_both))
    pad = [jnp.zeros((8 - heads, BLOCK), F32)] if heads < 8 else []
    dstep = jnp.concatenate(step_rows + pad, axis=0)
    pick_rows = (iota((16, heads * BLOCK), 1) // BLOCK) == iota((16, heads * BLOCK), 0)
    pick_rows = jnp.where(pick_rows, 1.0, 0.0).astype(BF16)
    dcum = mm_nt(pick_rows, jnp.concatenate(w_parts, axis=1))[:8]
    dcum = dcum - mm(pick_rows, jnp.concatenate(w_parts, axis=0))[:8]

    state_low = state_in_ref[0]
    dstate = dstate_ref[...]
    dstate_low = dstate.astype(BF16)
    pick_x = (iota((16, channels), 1) // PD) == iota((16, channels), 0)
    pick_f = jnp.where(pick_x, 1.0, 0.0)
    pick_x = pick_f.astype(BF16)
    from_state = enter_x * mm(c_low, state_low)
    dcum = dcum + mm_nt(pick_x, (dy * from_state).astype(BF16))[:8]
    dye = (enter_x * dy).astype(BF16)
    through = mm(b_low, dstate_low)
    dweight = mm_nt(pick_x, (x_val * through).astype(BF16))[:8]
    wx = (weight_x * x_val).astype(BF16)
    kept_x = enter_x[BLOCK - 1 :]
    dkept = jnp.sum(dstate * state_low.astype(F32), axis=0, keepdims=True) * kept_x
    dkept = jnp.sum(pick_f[:8] * dkept, axis=1, keepdims=True)
    moved = dweight * weight
    lane = iota((8, BLOCK), 1)
    dlast = jnp.sum(moved, axis=1, keepdims=True) + dkept
    dcum = dcum - moved + jnp.where(lane == BLOCK - 1, dlast, 0.0)
    dstep = dstep + dweight * tail
    dc = mm_nt(dye, state_low)
    db = mm_nt(wx, dstate_low)
    dstate_ref[...] = mm_tn(c_low, dye) + kept_x * dstate
    dcontact_low = dcontact.astype(BF16)
    dc = dc + mm(dcontact_low, b_low)
    db = db + mm_tn(dcontact_low, c_low)
    dx = jnp.concatenate(dx_parts, axis=1) + weight_x * through + skip_ref[...] * dy

    dlog = mm(split3(dcum), linked_low)
    dlog = dlog[0:8] + dlog[8:16] + dlog[16:24]
    dstep = dstep - dlog * rate
    ddt = dstep * sigmoid(dt_rows)
    head_acc_ref[0:8, :] += ddt
    head_acc_ref[8:16, :] += dlog * log_decay
    skip_acc_ref[0:1, :] += jnp.sum(dy * x_val, axis=0, keepdims=True)
    ddt_cols = jnp.transpose(jnp.concatenate([ddt, jnp.zeros((BLOCK - 8, BLOCK), F32)], axis=0))
    out_ref[:, dat - zat : width - zat] = ddt_cols.astype(BF16)

    dpre = jnp.concatenate([dx, db, dc], axis=1) * (pre_sig * (1.0 + pre * (1.0 - pre_sig)))
    conv_acc_ref[KW : KW + 1, :] += jnp.sum(dpre, axis=0, keepdims=True)
    dext_ref[0:BLOCK, :] = dpre
    pext_ref[0:BLOCK, :] = iota((BLOCK, BLOCK), 0) + base - start_col
    draw = taps[KW - 1 : KW] * dpre
    conv_acc_ref[KW - 1 : KW, :] += jnp.sum(dpre * ext_ref[pl.ds(8, BLOCK), :], axis=0, keepdims=True)
    for offset in range(1, KW):
        tap = KW - 1 - offset
        kept = jnp.where(place >= offset, dpre * ext_ref[pl.ds(8 - offset, BLOCK), :], 0.0)
        conv_acc_ref[tap : tap + 1, :] += jnp.sum(kept, axis=0, keepdims=True)
        later = pext_ref[pl.ds(offset, BLOCK), :]
        later = jnp.concatenate([later] * ((dat - xat) // LANES), axis=1)
        draw = draw + jnp.where(later >= offset, taps[tap : tap + 1] * dext_ref[pl.ds(offset, BLOCK), :], 0.0)
    dext_ref[pl.ds(BLOCK, 8), :] = dext_ref[0:8, :]
    pext_ref[pl.ds(BLOCK, 8), :] = pext_ref[0:8, :]
    out_ref[:, xat - zat : dat - zat] = draw.astype(BF16)


def scan_specs(cols, turn):
    zat, xat, dat, width = cols
    channels = xat - zat
    conv_width = dat - xat
    fixed = lambda shape: pl.BlockSpec(shape, lambda c: (0,) * len(shape))
    params = [
        fixed((8, conv_width)),
        fixed((1, conv_width)),
        fixed((8, LANES)),
        fixed((8, LANES)),
        fixed((1, channels)),
    ]
    starts = [
        pl.BlockSpec((BLOCK, LANES), lambda c: (turn(c), 0)),
        pl.BlockSpec((8, BLOCK), lambda c: (0, turn(c))),
    ]
    return starts, params


def scan_forward(cols, proj, start_col, start_row, params):
    zat, xat, dat, width = cols
    channels = xat - zat
    length = proj.shape[0]
    blocks = length // BLOCK
    starts, param_specs = scan_specs(cols, lambda c: c)
    body = lambda *refs: scan_fwd_kernel(cols, *refs)
    return pl.pallas_call(
        body,
        grid=(blocks,),
        in_specs=[pl.BlockSpec((BLOCK, width), lambda c: (c, 0))] + starts + param_specs,
        out_specs=[
            pl.BlockSpec((BLOCK, channels), lambda c: (c, 0)),
            pl.BlockSpec((BLOCK, channels), lambda c: (c, 0)),
            pl.BlockSpec((1, NS, channels), lambda c: (c, 0, 0)),
            pl.BlockSpec((8, BLOCK), lambda c: (0, c)),
        ],
        out_shape=[
            jax.ShapeDtypeStruct((length, channels), F32),
            jax.ShapeDtypeStruct((length, channels), F32),
            jax.ShapeDtypeStruct((blocks, NS, channels), BF16),
            jax.ShapeDtypeStruct((8, length), F32),
        ],
        scratch_shapes=[
            pltpu.VMEM((NS, channels), F32),
            pltpu.VMEM((BLOCK + 8, dat - xat), F32),
        ],
        compiler_params=pltpu.CompilerParams(vmem_limit_bytes=24 * MIB),
        cost_estimate=pl.CostEstimate(flops=2 * 10**9, bytes_accessed=10**7, transcendentals=2 * 10**6),
        name="scan_fwd",
    )(proj, start_col, start_row, *params)


def scan_backward(cols, proj, start_col, start_row, params, y, states, grad, stats, gain):
    zat, xat, dat, width = cols
    channels = xat - zat
    length = proj.shape[0]
    blocks = length // BLOCK
    turn = lambda c: blocks - 1 - c
    starts, param_specs = scan_specs(cols, turn)
    body = lambda *refs: scan_bwd_kernel(cols, *refs)
    tall = BLOCK // 8
    return pl.pallas_call(
        body,
        grid=(blocks,),
        in_specs=[
            pl.BlockSpec((BLOCK, width), lambda c: (turn(c), 0)),
            pl.BlockSpec((8, width), lambda c: (jnp.maximum(turn(c) * tall - 1, 0), 0)),
        ]
        + starts
        + param_specs
        + [
            pl.BlockSpec((BLOCK, channels), lambda c: (turn(c), 0)),
            pl.BlockSpec((1, NS, channels), lambda c: (turn(c), 0, 0)),
            pl.BlockSpec((BLOCK, channels), lambda c: (turn(c), 0)),
            pl.BlockSpec((8, BLOCK), lambda c: (0, turn(c))),
            pl.BlockSpec((1, channels), lambda c: (0, 0)),
        ],
        out_specs=[
            pl.BlockSpec((BLOCK, width - zat), lambda c: (turn(c), 0)),
            pl.BlockSpec((8, dat - xat), lambda c: (0, 0)),
            pl.BlockSpec((16, LANES), lambda c: (0, 0)),
            pl.BlockSpec((8, channels), lambda c: (0, 0)),
        ],
        out_shape=[
            jax.ShapeDtypeStruct((length, width - zat), BF16),
            jax.ShapeDtypeStruct((8, dat - xat), F32),
            jax.ShapeDtypeStruct((16, LANES), F32),
            jax.ShapeDtypeStruct((8, channels), F32),
        ],
        scratch_shapes=[
            pltpu.VMEM((NS, channels), F32),
            pltpu.VMEM((BLOCK + 8, dat - xat), F32),
            pltpu.VMEM((BLOCK + 8, dat - xat), F32),
            pltpu.VMEM((BLOCK + 8, LANES), jnp.int32),
        ],
        compiler_params=pltpu.CompilerParams(vmem_limit_bytes=24 * MIB),
        cost_estimate=pl.CostEstimate(flops=6 * 10**9, bytes_accessed=2 * 10**7, transcendentals=3 * 10**6),
        name="scan_bwd",
    )(proj, proj, start_col, start_row, *params, y, states, grad, stats, gain)


def turned(ref, own):
    eye = jnp.where(iota((own, own), 0) == iota((own, own), 1), 1.0, 0.0).astype(BF16)
    return mm_nt(eye, ref[...]).astype(BF16)


def pack_mixer_kernel(cols, place_ref, q_ref, kv_ref, z_ref, x_ref, bc_ref, dt_ref, one_ref, two_ref, att_ref, mix_ref, out_ref):
    zat, xat, dat, width = cols
    own, qwidth = q_ref.shape
    channels = xat - zat
    out_ref[:, :qwidth] = q_ref[...]
    kv = kv_ref[...].astype(F32)
    keys, vals = kv[:, :LANES], kv[:, LANES:]
    first = place_ref[0] == 0
    keys = jnp.where(first, keys, pltpu.roll(keys, HD, 1))
    vals = jnp.where(first, pltpu.roll(vals, HD, 1), vals)
    out_ref[:, qwidth:zat] = jnp.where(iota((own, LANES), 1) < HD, keys, vals).astype(BF16)
    out_ref[:, zat:xat] = z_ref[...]
    out_ref[:, xat : xat + channels] = x_ref[...]
    out_ref[:, xat + channels : dat] = bc_ref[...]
    row, lane = iota((16, LANES), 0), iota((16, LANES), 1)
    pick = jnp.where((lane == row + HD) & (row < 2), 1.0, 0.0).astype(BF16)
    gains = iota((16, own), 0)
    gains = jnp.where(gains == 0, one_ref[...].astype(F32), jnp.where(gains == 1, two_ref[...].astype(F32), 0.0))
    out_ref[:, dat:width] = mm_tn(gains.astype(BF16), pick).astype(BF16)
    out_ref[:, dat : dat + dt_ref.shape[1]] = dt_ref[...]
    out_ref[:, width : width + qwidth] = turned(att_ref, own)
    out_ref[:, width + qwidth :] = turned(mix_ref, own)


def pack_mixer(cols, kv_head, *shards):
    own, qwidth = shards[0].shape
    zat, xat, dat, width = cols
    body = lambda *refs: pack_mixer_kernel(cols, *refs)
    whole = lambda shape: pl.BlockSpec(shape, lambda i: (0, 0))
    shape = (own, width + qwidth + xat - zat)
    return pl.pallas_call(
        body,
        grid=(1,),
        in_specs=[pl.BlockSpec(memory_space=pltpu.SMEM)] + [whole(shard.shape) for shard in shards],
        out_specs=whole(shape),
        out_shape=jax.ShapeDtypeStruct(shape, BF16),
        compiler_params=pltpu.CompilerParams(vmem_limit_bytes=60 * MIB),
        cost_estimate=pl.CostEstimate(flops=10**7, bytes_accessed=10**6, transcendentals=0),
        name="pack_mixer",
    )(kv_head, *shards)


def pack_ffn_kernel(gate_ref, up_ref, down_ref, out_ref):
    own, hidden = gate_ref.shape
    out_ref[:, :hidden] = gate_ref[...]
    out_ref[:, hidden : 2 * hidden] = up_ref[...]
    out_ref[:, 2 * hidden :] = turned(down_ref, own)


def pack_ffn(gate, up, down):
    own, hidden = gate.shape
    whole = lambda shape: pl.BlockSpec(shape, lambda i: (0, 0))
    shape = (own, 3 * hidden)
    return pl.pallas_call(
        pack_ffn_kernel,
        grid=(1,),
        in_specs=[whole(gate.shape), whole(up.shape), whole(down.shape)],
        out_specs=whole(shape),
        out_shape=jax.ShapeDtypeStruct(shape, BF16),
        compiler_params=pltpu.CompilerParams(vmem_limit_bytes=60 * MIB),
        cost_estimate=pl.CostEstimate(flops=10**7, bytes_accessed=10**6, transcendentals=0),
        name="pack_ffn",
    )(gate, up, down)


def piece_at(rank_ref, refs, shift):
    if shift == 0:
        return refs[0][...]
    below, above = refs[2 * shift - 1][...], refs[2 * shift][...]
    return jnp.where(rank_ref[0] >= shift, below, above)


def norm_kernel(parts, rank_ref, *refs):
    gain_ref, out_ref = refs[2 * parts - 1], refs[2 * parts]
    rows = refs[0].shape[0]
    gain = gain_ref[...]
    for shift in range(parts):
        values = piece_at(rank_ref, refs, shift).astype(F32)
        spot = lax.rem(rank_ref[0] + (parts - shift), parts) * rows
        out_ref[pl.ds(pl.multiple_of(spot, rows), rows), :] = (values * rms_scale(values) * gain).astype(BF16)


def norm_rows(rank, parts, pieces, gain):
    rows, model = pieces[0].shape
    body = lambda *refs: norm_kernel(parts, *refs)
    whole = lambda shape: pl.BlockSpec(shape, lambda i: (0, 0))
    return pl.pallas_call(
        body,
        grid=(1,),
        in_specs=[pl.BlockSpec(memory_space=pltpu.SMEM)]
        + [whole((rows, model))] * len(pieces)
        + [whole((1, model))],
        out_specs=whole((parts * rows, model)),
        out_shape=jax.ShapeDtypeStruct((parts * rows, model), BF16),
        compiler_params=pltpu.CompilerParams(vmem_limit_bytes=24 * MIB),
        cost_estimate=pl.CostEstimate(flops=10**7, bytes_accessed=5 * 10**6, transcendentals=0),
        name="norm_rows",
    )(rank, *pieces, gain)


def branch_back_kernel(parts, rank_ref, *refs):
    count = 2 * parts - 1
    out_w_ref, am_ref, gain_ref, gatt_ref, gmix_ref, gow_ref, inner_ref, ggain_ref, sum_ref = refs[count:]
    rows = refs[0].shape[0]
    qwidth = gatt_ref.shape[1]
    sum_ref[...] = jnp.zeros_like(sum_ref)
    total = jnp.zeros((1, gmix_ref.shape[1]), F32)
    ones = jnp.ones((16, gmix_ref.shape[1]), BF16)
    for shift in range(parts):
        grads = piece_at(rank_ref, refs, shift)
        spot = pl.multiple_of(lax.rem(rank_ref[0] + (parts - shift), parts) * rows, rows)
        here = pl.ds(spot, rows)
        both = am_ref[here, :]
        grad_am = mm(grads, out_w_ref[...])
        gatt_ref[here, :] = grad_am[:, :qwidth].astype(BF16)
        grad_mixed = grad_am[:, qwidth:]
        gmix_ref[here, :] = grad_mixed
        product = grad_mixed * both[:, qwidth:].astype(F32)
        total = total + jnp.sum(product, axis=0, keepdims=True)
        high = product.astype(BF16)
        rest = (product - high.astype(F32)).astype(BF16)
        inner_ref[:, here] = (mm_nt(ones, high) + mm_nt(ones, rest))[:8]
        sum_ref[...] += mm_tn(grads, both)
    gow_ref[...] = sum_ref[...].astype(BF16)
    ggain_ref[...] = jnp.broadcast_to(total / gain_ref[...], ggain_ref.shape)


def branch_back(rank, parts, pieces, out_w, att_mixed, gain):
    rows, model = pieces[0].shape
    length, width = att_mixed.shape
    channels = gain.shape[1]
    body = lambda *refs: branch_back_kernel(parts, *refs)
    whole = lambda shape: pl.BlockSpec(shape, lambda i: (0, 0))
    shapes = [
        ((length, width - channels), BF16),
        ((length, channels), F32),
        ((model, width), BF16),
        ((8, length), F32),
        ((8, channels), F32),
    ]
    return pl.pallas_call(
        body,
        grid=(1,),
        in_specs=[pl.BlockSpec(memory_space=pltpu.SMEM)]
        + [whole((rows, model))] * len(pieces)
        + [whole((model, width)), whole((length, width)), whole((1, channels))],
        out_specs=[whole(shape) for shape, _ in shapes],
        out_shape=[jax.ShapeDtypeStruct(shape, dtype) for shape, dtype in shapes],
        scratch_shapes=[pltpu.VMEM((model, width), F32)],
        compiler_params=pltpu.CompilerParams(vmem_limit_bytes=32 * MIB),
        cost_estimate=pl.CostEstimate(flops=2 * 10**9, bytes_accessed=10**7, transcendentals=0),
        name="branch_back",
    )(rank, *pieces, out_w, att_mixed, gain)


def wgrad_kernel(step, own, core_ref, rows_ref, gq_ref, gkv_ref, grest_ref, gow_ref, theirs_ref, ours_ref):
    turn = pl.program_id(0)
    first = core_ref[0] == 0
    sources = []
    for ref in (gq_ref, gkv_ref, grest_ref, gow_ref):
        sources += [(ref, lane) for lane in range(0, ref.shape[1], LANES)]
    for index in range(len(sources) // step):

        @pl.when(turn == index)
        def _(index=index):
            lanes = sources[index * step : (index + 1) * step]
            at = 0
            while at < step:
                ref, lane = lanes[at]
                count = 1
                while at + count < step and lanes[at + count][0] is ref:
                    count += 1
                span = slice(lane, lane + count * LANES)
                to = slice(at * LANES, (at + count) * LANES)
                value = ref[:, span].astype(F32) if ref is gow_ref else mm_tn(rows_ref[...], ref[:, span])
                for chip in range(value.shape[0] // (2 * own)):
                    even = value[2 * chip * own : (2 * chip + 1) * own]
                    odd = value[(2 * chip + 1) * own : (2 * chip + 2) * own]
                    rows = slice(chip * own, (chip + 1) * own)
                    ours_ref[rows, to] = jnp.where(first, even, odd).astype(BF16)
                    theirs_ref[rows, to] = jnp.where(first, odd, even).astype(BF16)
                at += count


def mixer_wgrad(core, own, rows_one, grad_q, grad_kv, grad_rest, grad_out_w):
    length, model = rows_one.shape
    width = grad_q.shape[1] + grad_kv.shape[1] + grad_rest.shape[1] + grad_out_w.shape[1]
    step = 3
    whole = lambda shape: pl.BlockSpec(shape, lambda i: (0, 0))
    args = (rows_one, grad_q, grad_kv, grad_rest, grad_out_w)
    return pl.pallas_call(
        lambda *refs: wgrad_kernel(step, own, *refs),
        grid=(width // (step * LANES),),
        in_specs=[pl.BlockSpec(memory_space=pltpu.SMEM)] + [whole(arg.shape) for arg in args],
        out_specs=[pl.BlockSpec((model // 2, step * LANES), lambda i: (0, i))] * 2,
        out_shape=[jax.ShapeDtypeStruct((model // 2, width), BF16)] * 2,
        compiler_params=pltpu.CompilerParams(vmem_limit_bytes=32 * MIB),
        cost_estimate=pl.CostEstimate(flops=3 * 10**9, bytes_accessed=10**7, transcendentals=0),
        name="mixer_wgrad",
    )(core, *args)


EXTRA = 16


def back_proj_kernel(zat, rank_ref, gq_ref, gkv_ref, grest_ref, w_ref, rows_ref, gain_ref, two_ref, conv_ref, *refs):
    turn = pl.program_id(0)
    outs, share_ref = refs[:-1], refs[-1]
    qwidth = gq_ref.shape[1]
    rows = gq_ref.shape[0]
    term = mm_nt(gq_ref[...], w_ref[:, :qwidth]) + mm_nt(gkv_ref[...], w_ref[:, qwidth:zat])
    term = term + mm_nt(grest_ref[...], w_ref[:, zat:])
    share = jnp.sum(term * rows_ref[...].astype(F32), axis=0, keepdims=True) / gain_ref[...]

    @pl.when(turn == 0)
    def _():
        share_ref[...] = jnp.zeros_like(share_ref)
        share_ref[1:2, :] = two_ref[0:1, :]
        share_ref[8:16, 0 : 2 * NS] = conv_ref[:, conv_ref.shape[1] - 2 * NS :]

    share_ref[0:1, :] += share
    for index in range(len(outs)):

        @pl.when(turn == index)
        def _(index=index):
            outs[index][0:rows, :] = term.astype(outs[index].dtype)

    @pl.when(turn == pl.num_programs(0) - 1)
    def _():
        for out in outs:
            out[rows : rows + EXTRA, :] = share_ref[...].astype(out.dtype)


def back_proj(rank, parts, zat, width, grad_q, grad_kv, grad_rest, mixer_w, rows_one, gain, gain_two, conv_acc):
    length, model = rows_one.shape
    rows = length // parts
    at = lambda s, rank_ref: (lax.rem(rank_ref[0] + s, parts), 0)
    fixed = lambda s, rank_ref: (0, 0)
    spec = pltpu.PrefetchScalarGridSpec(
        num_scalar_prefetch=1,
        grid=(parts,),
        in_specs=[
            pl.BlockSpec((rows, grad_q.shape[1]), at),
            pl.BlockSpec((rows, grad_kv.shape[1]), at),
            pl.BlockSpec((rows, grad_rest.shape[1]), at),
            pl.BlockSpec((model, width), fixed),
            pl.BlockSpec((rows, model), at),
            pl.BlockSpec((1, model), fixed),
            pl.BlockSpec(gain_two.shape, fixed),
            pl.BlockSpec(conv_acc.shape, fixed),
        ],
        out_specs=[pl.BlockSpec((rows + EXTRA, model), fixed)] * parts,
        scratch_shapes=[pltpu.VMEM((EXTRA, model), F32)],
    )
    return pl.pallas_call(
        lambda *refs: back_proj_kernel(zat, *refs),
        grid_spec=spec,
        out_shape=[jax.ShapeDtypeStruct((rows + EXTRA, model), F32)]
        + [jax.ShapeDtypeStruct((rows + EXTRA, model), BF16)] * (parts - 1),
        compiler_params=pltpu.CompilerParams(vmem_limit_bytes=32 * MIB),
        cost_estimate=pl.CostEstimate(flops=3 * 10**9, bytes_accessed=10**7, transcendentals=0),
        name="back_proj",
    )(rank, grad_q, grad_kv, grad_rest, mixer_w, rows_one, gain, gain_two, conv_acc)


def ffn_kernel(middle_ref, cot_ref, gain_ref, w_ref, out_ref, gmid_ref, glow_ref, ggain_ref, gw_ref, low_ref, sum_ref, gsum_ref):
    step = pl.program_id(0)
    hidden = w_ref.shape[1] // 3

    @pl.when(step == 0)
    def _():
        middle = middle_ref[...]
        low_ref[...] = (middle * rms_scale(middle) * gain_ref[...]).astype(BF16)
        sum_ref[...] = jnp.zeros_like(sum_ref)
        gsum_ref[...] = jnp.zeros_like(gsum_ref)

    low = low_ref[...]
    cot = cot_ref[...]
    gate_pre = mm(low, w_ref[:, :hidden])
    up_pre = mm(low, w_ref[:, hidden : 2 * hidden])
    sig = sigmoid(gate_pre)
    silu_gate = gate_pre * sig
    act = (silu_gate * up_pre).astype(BF16)
    sum_ref[...] += mm_nt(act, w_ref[:, 2 * hidden :])
    gw_ref[:, 2 * hidden :] = mm_tn(cot, act).astype(BF16)
    grad_hidden = mm(cot, w_ref[:, 2 * hidden :])
    grad_gate = (grad_hidden * up_pre * sig * (1.0 + gate_pre * (1.0 - sig))).astype(BF16)
    grad_up = (grad_hidden * silu_gate).astype(BF16)
    gw_ref[:, :hidden] = mm_tn(low, grad_gate).astype(BF16)
    gw_ref[:, hidden : 2 * hidden] = mm_tn(low, grad_up).astype(BF16)
    gsum_ref[...] += mm_nt(grad_gate, w_ref[:, :hidden]) + mm_nt(grad_up, w_ref[:, hidden : 2 * hidden])

    @pl.when(step == pl.num_programs(0) - 1)
    def _():
        middle = middle_ref[...]
        out_ref[...] = (middle + sum_ref[...]).astype(BF16)
        scale = rms_scale(middle)
        normed = middle * scale
        grad_two = gsum_ref[...]
        ggain_ref[...] = jnp.broadcast_to(jnp.sum(grad_two * normed, axis=0, keepdims=True), ggain_ref.shape)
        grad_middle = cot_ref[...].astype(F32) + norm_back(grad_two * gain_ref[...], normed, scale)
        gmid_ref[...] = grad_middle
        glow_ref[...] = grad_middle.astype(BF16)


def ffn_both(middle, cotangent, gain, ffn_w, parts):
    rows, model = middle.shape
    piece = ffn_w.shape[1] // parts
    rowspec = pl.BlockSpec((rows, model), lambda s: (0, 0))
    wspec = pl.BlockSpec((model, piece), lambda s: (0, s))
    return pl.pallas_call(
        ffn_kernel,
        grid=(parts,),
        in_specs=[rowspec, rowspec, pl.BlockSpec((1, model), lambda s: (0, 0)), wspec],
        out_specs=[rowspec, rowspec, rowspec, pl.BlockSpec((8, model), lambda s: (0, 0)), wspec],
        out_shape=[
            jax.ShapeDtypeStruct((rows, model), BF16),
            jax.ShapeDtypeStruct((rows, model), F32),
            jax.ShapeDtypeStruct((rows, model), BF16),
            jax.ShapeDtypeStruct((8, model), F32),
            jax.ShapeDtypeStruct(ffn_w.shape, BF16),
        ],
        scratch_shapes=[
            pltpu.VMEM((rows, model), BF16),
            pltpu.VMEM((rows, model), F32),
            pltpu.VMEM((rows, model), F32),
        ],
        compiler_params=pltpu.CompilerParams(vmem_limit_bytes=60 * MIB),
        cost_estimate=pl.CostEstimate(flops=10**10, bytes_accessed=3 * 10**7, transcendentals=10**6),
        name="ffn_both",
    )(middle, cotangent, gain, ffn_w)


def lane_rows(values, rows):
    padded = jnp.pad(values, (0, rows - values.shape[0]))
    return jnp.broadcast_to(padded[:, None], (rows, LANES))


def shifted(values, axis, size, shift):
    return lax.ppermute(values, axis, [(i, (i + shift) % size) for i in range(size)])


def sent(values, pairs):
    return lax.ppermute(values, "tensor", pairs)


def after(values, *earlier):
    return lax.optimization_barrier((values, earlier))[0]


def first_phase(values, parts):
    up = [(i, i + 1) for i in range(parts - 1)]
    return sent(values, up), sent(values, [(j, i) for i, j in up])


def second_phase(values, firsts, parts):
    first_up, first_down = firsts
    if parts == 4:
        below = [first_up, sent(first_up, [(1, 2), (2, 3)]), sent(first_up, [(1, 3)])]
        above = [first_down, sent(first_down, [(2, 1), (1, 0)]), sent(first_down, [(2, 0)])]
    else:
        up = lambda shift: [(i, i + shift) for i in range(parts - shift)]
        below = [first_up] + [sent(values, up(shift)) for shift in range(2, parts)]
        above = [first_down] + [sent(values, [(j, i) for i, j in up(shift)]) for shift in range(2, parts)]
    pieces = [values]
    for shift in range(1, parts):
        pieces += [below[shift - 1], above[parts - shift - 1]]
    return pieces


def sum_first(terms, parts):
    if parts != 4:
        return [shifted(terms[shift].astype(BF16), "tensor", parts, shift) for shift in range(1, parts)]
    low = lambda value: value.astype(BF16)
    up = [sent(low(terms[2]), [(0, 1), (1, 2)]), sent(low(terms[3]), [(0, 2)])]
    return up + [sent(low(terms[2]), [(3, 2), (2, 1)]), sent(low(terms[1]), [(3, 1)])]


def sum_second(terms, firsts, parts):
    if parts != 4:
        return firsts
    firsts = [first.astype(F32) for first in firsts]
    up = terms[1].astype(F32) + firsts[0] + firsts[1]
    down = terms[3].astype(F32) + firsts[2] + firsts[3]
    return [
        sent(up.astype(BF16), [(0, 1), (1, 2), (2, 3)]),
        sent(down.astype(BF16), [(3, 2), (2, 1), (1, 0)]),
    ]


def sum_last(terms, seconds):
    total = terms[0].astype(F32)
    for second in seconds:
        total = total + second.astype(F32)
    return total


def chip_total(theirs, ours, earlier):
    size = lax.axis_size("dp")
    theirs = after(lax.ppermute(theirs, "dp", [(i, i ^ 1) for i in range(size)]), earlier)
    return (ours.astype(F32) + theirs.astype(F32)).astype(BF16)


def sum_over_chips(values):
    size = lax.axis_size("dp")
    groups = [list(range(core, size, 2)) for core in range(2)]
    return lax.psum_scatter(values, "dp", scatter_dimension=0, axis_index_groups=groups, tiled=True)


def rows_of(values, rank, shift, parts):
    rows = values.shape[0] // parts
    return lax.dynamic_slice(values, (lax.rem(rank + shift, parts) * rows, 0), (rows, values.shape[1]))


def group_total(values, parts):
    total = values.astype(F32)
    for shift in range(1, parts):
        total = total + shifted(values, "tensor", parts, shift).astype(F32)
    return total


def butterfly(values, axis, size):
    if size & (size - 1):
        return lax.psum(values, axis)
    step = 1
    while step < size:
        values = values + lax.ppermute(values, axis, [(i, i ^ step) for i in range(size)])
        step *= 2
    return values


def local(
    x_in,
    cotangent,
    segments,
    norm_one,
    w_query,
    w_keyval,
    w_attn_out,
    w_zgate,
    w_xin,
    w_bcin,
    w_dtin,
    conv_x,
    conv_bc,
    bias_x,
    bias_bc,
    dt_bias,
    a_log,
    d_skip,
    ssm_gain,
    w_mix_out,
    norm_two,
    w_gate,
    w_up,
    w_down,
):
    parts = lax.axis_size("tensor")
    rank = lax.axis_index("tensor")
    own = w_query.shape[0]
    length = segments.shape[1]
    qwidth = w_query.shape[1]
    channels = w_zgate.shape[1]
    heads = w_dtin.shape[1]
    hidden_own = w_gate.shape[1]
    width_ssm = MH * PD
    kv_head = (rank * (qwidth // HD)) // (QH // KVH)
    zat = 2 * qwidth
    xat = zat + channels
    bat = xat + channels
    dat = bat + 2 * NS
    width = dat + LANES
    cols = (zat, xat, dat, width)

    mixer_own = pack_mixer(
        cols,
        kv_head.astype(jnp.int32)[None],
        w_query,
        w_keyval,
        w_zgate,
        w_xin,
        w_bcin,
        w_dtin,
        norm_one[None, :],
        norm_two[None, :],
        w_attn_out,
        w_mix_out,
    )
    mixer_w = lax.all_gather(mixer_own, "dp", axis=0, tiled=True)
    proj_w = mixer_w[:, :width]
    out_w = mixer_w[:, width:]
    gain_one = mixer_w[:, dat + HD].astype(F32)[None, :]
    gain_two = mixer_w[:, dat + HD + 1].astype(F32)[None, :]
    ffn_own = pack_ffn(w_gate, w_up, w_down)
    ffn_first, x_first = lax.optimization_barrier((first_phase(ffn_own, parts), first_phase(x_in, parts)))
    ffn_pieces = second_phase(ffn_own, ffn_first, parts)
    x_pieces = second_phase(x_in, x_first, parts)
    ffn_own = jnp.concatenate(
        ffn_pieces[:1]
        + [jnp.where(rank >= k, ffn_pieces[2 * k - 1], ffn_pieces[2 * k]) for k in range(1, parts)],
        axis=1,
    )
    ffn_w = lax.all_gather(ffn_own, "dp", axis=0, tiled=True)

    seg = segments[0]
    start = jnp.sum((seg[None, :] < seg[:, None]).astype(jnp.int32), axis=1)
    start_col = jnp.broadcast_to(start[:, None], (length, LANES))
    start_row = jnp.broadcast_to(start[None, :], (8, length))
    cosine, sine = rope_tables(length)
    taps = jnp.pad(jnp.concatenate([conv_x, conv_bc], axis=1), ((0, 8 - KW), (0, 0)))
    bias = jnp.concatenate([bias_x, bias_bc])[None, :]
    params = (taps, bias, lane_rows(dt_bias, 8), lane_rows(jnp.exp(a_log), 8), jnp.repeat(d_skip, PD)[None, :])

    residual = x_in.astype(F32)
    scale_one = rms_scale(residual)
    normed_one = residual * scale_one
    rank_arg = rank.astype(jnp.int32)[None]
    rows_one = norm_rows(rank_arg, parts, x_pieces, gain_one)
    proj = mm(rows_one, proj_w)
    y, gated, states, squares = scan_forward(cols, proj, start_col, start_row, params)
    attended, lse, low_q, low_kv = attn_forward(proj, cosine, sine, start_col)
    scale_ssm = lax.rsqrt(group_total(squares[:1], parts) / width_ssm + EPSILON)
    mixed = (gated * scale_ssm[0][:, None] * ssm_gain[None, :]).astype(BF16)
    att_mixed = jnp.concatenate([attended, mixed], axis=1)
    terms = [mm_nt(rows_of(att_mixed, rank, shift, parts), out_w) for shift in range(parts)]
    middle = residual + sum_last(terms, sum_second(terms, sum_first(terms, parts), parts))
    block_out, grad_middle, grad_low, grad_gain_two, grad_ffn_w = ffn_both(middle, cotangent, gain_two, ffn_w, parts)

    branch_pieces = second_phase(grad_low, first_phase(grad_low, parts), parts)
    grad_ffn_own = lax.psum_scatter(grad_ffn_w, "dp", scatter_dimension=0, tiled=True)
    piece = grad_ffn_own.shape[1] // parts
    ffn_terms = [grad_ffn_own[:, k * piece : (k + 1) * piece] for k in range(parts)]
    ffn_terms = ffn_terms[:1] + ffn_terms[:0:-1]

    grad_att, grad_mixed, grad_out_w, inner, grad_gain_ssm = branch_back(
        rank_arg, parts, branch_pieces, out_w, att_mixed, ssm_gain[None, :]
    )
    inner = group_total(inner[:1], parts) / width_ssm
    stats = jnp.concatenate([scale_ssm, inner, jnp.zeros((6, length), F32)], axis=0)
    grad_q, grad_kv = attn_backward(low_q, low_kv, lse, attended, grad_att, cosine, sine, start_col)
    grad_rest, conv_acc, head_acc, skip_acc = scan_backward(
        cols, proj, start_col, start_row, params, y, states, grad_mixed, stats, ssm_gain[None, :]
    )
    core = lax.rem(lax.axis_index("dp"), 2).astype(jnp.int32)[None]
    theirs, ours = mixer_wgrad(core, own, rows_one, grad_q, grad_kv, grad_rest, grad_out_w)
    terms = back_proj(
        rank_arg, parts, zat, width, grad_q, grad_kv, after(grad_rest, theirs), mixer_w, rows_one, gain_one, grad_gain_two, conv_acc
    )
    chip_share = chip_total(theirs, ours, terms)
    firsts = after(sum_first(terms, parts), chip_share, grad_ffn_own)
    seconds = sum_second(terms, firsts, parts)
    seconds, ffn_firsts = lax.optimization_barrier((seconds, sum_first(ffn_terms, parts)))
    grad_ffn = sum_last(ffn_terms, sum_second(ffn_terms, ffn_firsts, parts))
    summed = sum_last(terms, seconds)
    grad_one, shared_small = summed[:-EXTRA], summed[-EXTRA:]
    grad_input = grad_middle + norm_back(grad_one * gain_one, normed_one, scale_one)
    grad_w = after(sum_over_chips(chip_share), seconds).astype(F32)

    model = x_in.shape[1]
    wide = lambda rows: jnp.pad(rows, ((0, 0), (0, model - rows.shape[1])))
    head_sums = jnp.sum(head_acc, axis=1)[None, :]
    small = jnp.concatenate(
        [
            shared_small,
            wide(conv_acc),
            wide(grad_gain_ssm[:1]),
            wide(skip_acc[:1]),
            wide(head_sums),
            jnp.zeros((5, model), F32),
        ],
        axis=0,
    )
    small = butterfly(small, "dp", lax.axis_size("dp"))
    at = EXTRA
    grad_conv_x = small[at : at + KW, :channels]
    grad_bias_x = small[at + KW, :channels]
    grad_ssm_gain = small[at + 8, :channels]
    grad_d_skip = jnp.sum(small[at + 9, :channels].reshape(heads, PD), axis=1)
    grad_dt_bias = small[at + 10, :heads]
    grad_a_log = small[at + 10, 8 : 8 + heads]
    grad_conv_bc = small[8 : 8 + KW, : 2 * NS]
    grad_bias_bc = small[8 + KW, : 2 * NS]
    place = lax.axis_index("dp") * own
    norm_grads = lax.dynamic_slice(small, (0, place), (2, own))
    grad_norm_one, grad_norm_two = norm_grads[0], norm_grads[1]

    grad_keyval = jnp.zeros((own, 2 * KVH * HD), F32)
    grad_keyval = lax.dynamic_update_slice(grad_keyval, grad_w[:, qwidth : qwidth + HD], (0, kv_head * HD))
    grad_keyval = lax.dynamic_update_slice(
        grad_keyval, grad_w[:, qwidth + HD : zat], (0, (KVH + kv_head) * HD)
    )
    shared = jnp.concatenate([grad_keyval, grad_w[:, bat:dat]], axis=1)
    shared = group_total(shared.astype(BF16), parts)

    return (
        block_out,
        grad_input,
        grad_norm_one,
        grad_w[:, :qwidth],
        shared[:, : 2 * KVH * HD],
        grad_w[:, width : width + qwidth].T,
        grad_w[:, zat:xat],
        grad_w[:, xat:bat],
        shared[:, 2 * KVH * HD :],
        grad_w[:, dat : dat + heads],
        grad_conv_x,
        grad_conv_bc,
        grad_bias_x,
        grad_bias_bc,
        grad_dt_bias,
        grad_a_log,
        grad_d_skip,
        grad_ssm_gain,
        grad_w[:, width + qwidth :].T,
        grad_norm_two,
        grad_ffn[:, :hidden_own],
        grad_ffn[:, hidden_own : 2 * hidden_own],
        grad_ffn[:, 2 * hidden_own :].T,
    )


def solution(mesh):
    return jax.shard_map(
        local,
        mesh=mesh,
        in_specs=(
            P(("dp", "tensor"), None),
            P(("dp", "tensor"), None),
            P("dp", None),
            P("dp"),
            P("dp", "tensor"),
            P("dp", None),
            P("tensor", "dp"),
            P("dp", "tensor"),
            P("dp", "tensor"),
            P("dp", None),
            P("dp", "tensor"),
            P(None, "tensor"),
            P(),
            P("tensor"),
            P(),
            P("tensor"),
            P("tensor"),
            P("tensor"),
            P("tensor"),
            P("tensor", "dp"),
            P("dp"),
            P("dp", "tensor"),
            P("dp", "tensor"),
            P("tensor", "dp"),
        ),
        out_specs=(
            P(("dp", "tensor"), None),
            P(("dp", "tensor"), None),
            P("dp"),
            P("dp", "tensor"),
            P("dp", None),
            P("tensor", "dp"),
            P("dp", "tensor"),
            P("dp", "tensor"),
            P("dp", None),
            P("dp", "tensor"),
            P(None, "tensor"),
            P(),
            P("tensor"),
            P(),
            P("tensor"),
            P("tensor"),
            P("tensor"),
            P("tensor"),
            P("tensor", "dp"),
            P("dp"),
            P("dp", "tensor"),
            P("dp", "tensor"),
            P("tensor", "dp"),
        ),
        check_vma=False,
    )
```

```python
import math

import jax
import jax.numpy as jnp
import numpy as np
from jax import lax
from jax.experimental import pallas as pl
from jax.experimental.pallas import tpu as pltpu
from jax.sharding import PartitionSpec as P

QH = 8
KVH = 2
HD = 64
MH = 24
PD = 64
NS = 128
KW = 4
BLOCK = 128
LANES = 128

EPSILON = 1e-05
ROPE_BASE = 100000000000.0
NEG = -1e9
F32 = jnp.float32
BF16 = jnp.bfloat16
MIB = 1024 * 1024


def mm(lhs, rhs):
    return lax.dot_general(lhs, rhs, (((1,), (0,)), ((), ())), preferred_element_type=F32)


def mm_nt(lhs, rhs):
    return lax.dot_general(lhs, rhs, (((1,), (1,)), ((), ())), preferred_element_type=F32)


def mm_tn(lhs, rhs):
    return lax.dot_general(lhs, rhs, (((0,), (0,)), ((), ())), preferred_element_type=F32)


def rms_scale(values):
    return lax.rsqrt(jnp.mean(values * values, axis=-1, keepdims=True) + EPSILON)


def norm_back(grad_normed, normed, scale):
    return scale * (grad_normed - normed * jnp.mean(grad_normed * normed, axis=-1, keepdims=True))


def sigmoid(v):
    return 1.0 / (1.0 + jnp.exp(-v))


def iota(shape, dim):
    return lax.broadcasted_iota(jnp.int32, shape, dim)


def rope_tables(length):
    half = HD // 2
    freqs = np.float32(ROPE_BASE) ** (-(np.arange(half, dtype=np.float32) * np.float32(2.0 / HD)))
    angles = np.arange(length, dtype=np.float32)[:, None] * freqs.astype(np.float32)[None, :]
    cosine, sine = np.cos(angles).astype(np.float32), np.sin(angles).astype(np.float32)
    cos_lanes = np.concatenate([cosine] * 4, axis=1)
    sin_lanes = np.concatenate([-sine, sine, -sine, sine], axis=1)
    return jnp.asarray(cos_lanes), jnp.asarray(sin_lanes)


def swap_halves(values):
    lane = iota(values.shape, 1)
    ahead = pltpu.roll(values, LANES - HD // 2, 1)
    behind = pltpu.roll(values, HD // 2, 1)
    return jnp.where((lane & (HD - 1)) < HD // 2, ahead, behind)


def pair_rows(block):
    low = iota(block.shape, 1) < HD
    zero = jnp.zeros_like(block)
    return jnp.concatenate([jnp.where(low, block, zero), jnp.where(low, zero, block)], axis=0)


def attn_fwd_kernel(q_ref, kv_ref, cos_ref, sin_ref, start_ref, out_ref, lse_ref, lq_ref, lkv_ref):
    length = q_ref.shape[0]
    rows = 256
    cosine, sine = cos_ref[...], sin_ref[...]
    low = iota((length, LANES), 1) < HD
    queries = q_ref[...]
    lq_ref[...] = (queries * cosine + swap_halves(queries) * sine).astype(BF16)
    kv = kv_ref[...]
    kv = jnp.where(low, kv * cosine + swap_halves(kv) * sine, kv)
    lkv_ref[...] = kv.astype(BF16)
    other = pltpu.roll(kv, HD, 1)
    keys = jnp.where(low, kv, other).astype(BF16)
    vals = jnp.where(low, other, kv).astype(BF16)
    half = iota((rows, LANES), 1) < HD
    for step in range(length // rows):
        end = (step + 1) * rows
        span = slice(step * rows, end)
        stacked = pair_rows(lq_ref[span, :].astype(F32)).astype(BF16)
        scores = mm_nt(stacked, keys[:end]) * (1.0 / math.sqrt(HD))
        first = start_ref[span, :][:, :1]
        col = iota((rows, end), 1)
        row = iota((rows, end), 0) + step * rows
        allowed = (col <= row) & (col >= first)
        allowed = jnp.concatenate([allowed.astype(jnp.int32)] * 2, axis=0) > 0
        scores = jnp.where(allowed, scores, NEG)
        top = jnp.max(scores, axis=1, keepdims=True)
        expo = jnp.exp(scores - top)
        total = jnp.sum(expo, axis=1, keepdims=True)
        probs = (expo * (1.0 / total)).astype(BF16)
        result = mm(probs, vals[:end])
        out_ref[span, :] = jnp.where(half, result[:rows], result[rows:]).astype(BF16)
        lse = top + jnp.log(total)
        lse_ref[span, :] = jnp.where(half, lse[:rows], lse[rows:])


def attn_bwd_kernel(
    lq_ref, lkv_ref, lse_ref, out_ref, go_ref, cos_ref, sin_ref, start_ref, gq_ref, gkv_ref, dk_ref, dv_ref
):
    length = lq_ref.shape[0]
    rows = 256
    cosine, sine = cos_ref[...], sin_ref[...]
    low = iota((length, LANES), 1) < HD
    kv = lkv_ref[...].astype(F32)
    other = pltpu.roll(kv, HD, 1)
    keys = jnp.where(low, kv, other).astype(BF16)
    vals = jnp.where(low, other, kv).astype(BF16)
    half = iota((rows, LANES), 1) < HD
    dk_ref[...] = jnp.zeros_like(dk_ref)
    dv_ref[...] = jnp.zeros_like(dv_ref)
    inv = 1.0 / math.sqrt(HD)
    for step in range(length // rows):
        end = (step + 1) * rows
        span = slice(step * rows, end)
        stacked = pair_rows(lq_ref[span, :].astype(F32)).astype(BF16)
        grads = pair_rows(go_ref[span, :].astype(F32))
        outs = out_ref[span, :].astype(F32)
        inner = jnp.sum(grads * jnp.concatenate([outs, outs], axis=0), axis=1, keepdims=True)
        grads = grads.astype(BF16)
        lse = lse_ref[span, :]
        lse = jnp.concatenate([lse[:, :1], lse[:, HD : HD + 1]], axis=0)
        scores = mm_nt(stacked, keys[:end]) * inv
        first = start_ref[span, :][:, :1]
        col = iota((rows, end), 1)
        row = iota((rows, end), 0) + step * rows
        allowed = (col <= row) & (col >= first)
        allowed = jnp.concatenate([allowed.astype(jnp.int32)] * 2, axis=0) > 0
        probs = jnp.exp(jnp.where(allowed, scores, NEG) - lse)
        grad_probs = mm_nt(grads, vals[:end])
        grad_scores = (probs * (grad_probs - inner)).astype(BF16)
        gq = mm(grad_scores, keys[:end]) * inv
        gq = jnp.where(half, gq[:rows], gq[rows:])
        gq_ref[span, :] = (gq * cosine[span] - swap_halves(gq) * sine[span]).astype(BF16)
        dk_ref[:end, :] += mm_tn(grad_scores, stacked)
        dv_ref[:end, :] += mm_tn(probs.astype(BF16), grads)
    dk = dk_ref[...] * inv
    dk = dk + pltpu.roll(dk, HD, 1)
    dk = dk * cosine - swap_halves(dk) * sine
    dv = dv_ref[...]
    dv = dv + pltpu.roll(dv, HD, 1)
    gkv_ref[...] = jnp.where(low, dk, dv).astype(BF16)


def attn_forward(proj, cosine, sine, start_col):
    length = proj.shape[0]
    wide = pl.BlockSpec((length, LANES), lambda i: (0, 0))
    return pl.pallas_call(
        attn_fwd_kernel,
        grid=(1,),
        in_specs=[wide, pl.BlockSpec((length, LANES), lambda i: (0, 1)), wide, wide, wide],
        out_specs=[wide] * 4,
        out_shape=[
            jax.ShapeDtypeStruct((length, LANES), BF16),
            jax.ShapeDtypeStruct((length, LANES), F32),
            jax.ShapeDtypeStruct((length, LANES), BF16),
            jax.ShapeDtypeStruct((length, LANES), BF16),
        ],
        compiler_params=pltpu.CompilerParams(vmem_limit_bytes=32 * MIB),
        cost_estimate=pl.CostEstimate(flops=10**9, bytes_accessed=6 * 10**6, transcendentals=2 * 10**6),
        name="attn_fwd",
    )(proj, proj, cosine, sine, start_col)


def attn_backward(low_q, low_kv, lse, out, grad_out, cosine, sine, start_col):
    length = low_q.shape[0]
    wide = pl.BlockSpec((length, LANES), lambda i: (0, 0))
    return pl.pallas_call(
        attn_bwd_kernel,
        grid=(1,),
        in_specs=[wide] * 8,
        out_specs=[wide] * 2,
        out_shape=[jax.ShapeDtypeStruct((length, LANES), BF16)] * 2,
        scratch_shapes=[pltpu.VMEM((length, LANES), F32)] * 2,
        compiler_params=pltpu.CompilerParams(vmem_limit_bytes=32 * MIB),
        cost_estimate=pl.CostEstimate(flops=3 * 10**9, bytes_accessed=6 * 10**6, transcendentals=2 * 10**6),
        name="attn_bwd",
    )(low_q, low_kv, lse, out, grad_out, cosine, sine, start_col)


def split3(values):
    high = values.astype(BF16).astype(F32)
    rest = values - high
    mid = rest.astype(BF16).astype(F32)
    tail = rest - mid
    return jnp.concatenate([high, mid, tail, jnp.zeros_like(values)], axis=0).astype(BF16)


def spread(rows, width, lanes_each):
    pick = (iota((32, width), 1) // lanes_each) == (iota((32, width), 0) & 7)
    return mm_tn(split3(rows), pick.astype(F32).astype(BF16))


def decay_terms(dt_block, dt_bias, rate, start_row, start_col, base):
    dt_rows = jnp.transpose(dt_block)[:8] + dt_bias
    step = jnp.maximum(dt_rows, 0.0) + jnp.log1p(jnp.exp(-jnp.abs(dt_rows)))
    log_decay = -step * rate
    row = iota((BLOCK, BLOCK), 0) + base
    col = iota((BLOCK, BLOCK), 1) + base
    linked = (col <= row) & (col >= start_col)
    linked_low = jnp.where(linked, 1.0, 0.0).astype(BF16)
    cum = mm_nt(split3(log_decay), linked_low)
    cum = cum[0:8] + cum[8:16] + cum[16:24]
    enter = jnp.exp(jnp.where(start_row < base, cum, NEG))
    last = cum[:, BLOCK - 1 :]
    position = iota((8, BLOCK), 1) + base
    tail = jnp.exp(jnp.where(position >= start_row[:, BLOCK - 1 :], last - cum, NEG))
    return dt_rows, step, log_decay, linked, linked_low, cum, enter, tail


def conv_sum(ext_ref, taps, bias, place):
    total = bias + taps[KW - 1 : KW] * ext_ref[pl.ds(8, BLOCK), :]
    for offset in range(1, KW):
        shifted = ext_ref[pl.ds(8 - offset, BLOCK), :]
        total = total + jnp.where(place >= offset, taps[KW - 1 - offset : KW - offset] * shifted, 0.0)
    return total


def wide_place(start_col, base, width):
    place = iota((BLOCK, BLOCK), 0) + base - start_col
    return jnp.concatenate([place] * (width // LANES), axis=1)


def scan_fwd_kernel(
    cols,
    proj_ref,
    startc_ref,
    startr_ref,
    taps_ref,
    bias_ref,
    dtb_ref,
    rate_ref,
    skip_ref,
    y_ref,
    gated_ref,
    state_out_ref,
    ssq_ref,
    state_ref,
    ext_ref,
):
    zat, xat, dat, width = cols
    channels = xat - zat
    heads = channels // PD
    block = pl.program_id(0)
    base = block * BLOCK

    @pl.when(block == 0)
    def _():
        state_ref[...] = jnp.zeros_like(state_ref)
        ext_ref[0:8, :] = jnp.zeros((8, ext_ref.shape[1]), F32)

    start_col = startc_ref[...]
    start_row = startr_ref[...]
    ext_ref[pl.ds(8, BLOCK), :] = proj_ref[:, xat:dat]
    place = wide_place(start_col, base, dat - xat)
    pre = conv_sum(ext_ref, taps_ref[...], bias_ref[...], place)
    ext_ref[0:8, :] = ext_ref[pl.ds(BLOCK, 8), :]
    conv = (pre * sigmoid(pre)).astype(BF16)
    x_low, b_low, c_low = conv[:, :channels], conv[:, channels : channels + NS], conv[:, channels + NS :]
    x_val = x_low.astype(F32)
    _, step, _, linked, _, cum, enter, tail = decay_terms(
        proj_ref[:, dat:width], dtb_ref[...], rate_ref[...], start_row, start_col, base
    )
    contact = mm_nt(c_low, b_low)
    cum_cols = spread(cum, heads * LANES, LANES)
    enter_x = spread(enter, channels, PD)
    weight_x = spread(tail * step, channels, PD)
    low = iota((BLOCK, LANES), 1) < PD
    zero = jnp.zeros((BLOCK, LANES), F32)
    within = []
    for pair in range(heads // 2):
        mixes = []
        for head in (2 * pair, 2 * pair + 1):
            gap = cum_cols[:, head * LANES : (head + 1) * LANES] - cum[head : head + 1]
            decay = jnp.exp(jnp.where(linked, gap, NEG))
            mixes.append((decay * (contact * step[head : head + 1])).astype(BF16))
        x_pair = x_val[:, pair * LANES : (pair + 1) * LANES]
        both = jnp.concatenate([jnp.where(low, x_pair, zero), jnp.where(low, zero, x_pair)], axis=0).astype(BF16)
        within.append(mm(jnp.concatenate(mixes, axis=1), both))
    state = state_ref[...]
    state_low = state.astype(BF16)
    state_out_ref[0] = state_low
    y = jnp.concatenate(within, axis=1) + enter_x * mm(c_low, state_low) + skip_ref[...] * x_val
    y_ref[...] = y
    state_ref[...] = mm_tn(b_low, (weight_x * x_val).astype(BF16)) + enter_x[BLOCK - 1 :] * state
    z = proj_ref[:, zat:xat]
    gated = y * (z * sigmoid(z))
    gated_ref[...] = gated
    square = gated * gated
    high = square.astype(BF16)
    rest = (square - high.astype(F32)).astype(BF16)
    ones = jnp.ones((16, channels), BF16)
    ssq_ref[...] = (mm_nt(ones, high) + mm_nt(ones, rest))[:8]


def scan_bwd_kernel(
    cols,
    proj_ref,
    prev_ref,
    startc_ref,
    startr_ref,
    taps_ref,
    bias_ref,
    dtb_ref,
    rate_ref,
    skip_ref,
    y_ref,
    state_in_ref,
    grad_ref,
    stats_ref,
    gain_ref,
    out_ref,
    conv_acc_ref,
    head_acc_ref,
    skip_acc_ref,
    dstate_ref,
    ext_ref,
    dext_ref,
    pext_ref,
):
    zat, xat, dat, width = cols
    channels = xat - zat
    heads = channels // PD
    turn = pl.program_id(0)
    block = pl.num_programs(0) - 1 - turn
    base = block * BLOCK

    @pl.when(turn == 0)
    def _():
        dstate_ref[...] = jnp.zeros_like(dstate_ref)
        conv_acc_ref[...] = jnp.zeros_like(conv_acc_ref)
        head_acc_ref[...] = jnp.zeros_like(head_acc_ref)
        skip_acc_ref[...] = jnp.zeros_like(skip_acc_ref)
        dext_ref[pl.ds(BLOCK, 8), :] = jnp.zeros((8, dext_ref.shape[1]), F32)
        pext_ref[pl.ds(BLOCK, 8), :] = jnp.zeros((8, LANES), jnp.int32)

    start_col = startc_ref[...]
    start_row = startr_ref[...]
    taps = taps_ref[...]
    ext_ref[0:8, :] = prev_ref[:, xat:dat]
    ext_ref[pl.ds(8, BLOCK), :] = proj_ref[:, xat:dat]
    place = wide_place(start_col, base, dat - xat)
    pre = conv_sum(ext_ref, taps, bias_ref[...], place)
    pre_sig = sigmoid(pre)
    conv = (pre * pre_sig).astype(BF16)
    x_low, b_low, c_low = conv[:, :channels], conv[:, channels : channels + NS], conv[:, channels + NS :]
    x_val = x_low.astype(F32)
    rate = rate_ref[...]
    dt_rows, step, log_decay, linked, linked_low, cum, enter, tail = decay_terms(
        proj_ref[:, dat:width], dtb_ref[...], rate, start_row, start_col, base
    )
    contact = mm_nt(c_low, b_low)
    cum_cols = spread(cum, heads * LANES, LANES)
    enter_x = spread(enter, channels, PD)
    weight = tail * step
    weight_x = spread(weight, channels, PD)

    z = proj_ref[:, zat:xat]
    z_sig = sigmoid(z)
    z_silu = z * z_sig
    y_val = y_ref[...]
    stats = spread(stats_ref[...], 2 * channels, channels)
    scale_x, inner_x = stats[:, :channels], stats[:, channels:]
    grad = scale_x * (grad_ref[...] * gain_ref[...] - y_val * z_silu * scale_x * inner_x)
    dy = grad * z_silu
    out_ref[:, :channels] = (grad * y_val * (z_sig * (1.0 + z * (1.0 - z_sig)))).astype(BF16)

    low = iota((BLOCK, LANES), 1) < PD
    strict = linked & (iota((BLOCK, BLOCK), 0) > iota((BLOCK, BLOCK), 1))
    zero = jnp.zeros((BLOCK, LANES), F32)
    dcontact = zero
    dx_parts, w_parts, step_rows = [], [], []
    for pair in range(heads // 2):
        lanes = slice(pair * LANES, (pair + 1) * LANES)
        dy_pair = dy[:, lanes]
        dy_both = jnp.concatenate([jnp.where(low, dy_pair, zero), jnp.where(low, zero, dy_pair)], axis=0).astype(BF16)
        outer = mm_nt(dy_both, x_low[:, lanes])
        mixes = []
        for slot in range(2):
            head = 2 * pair + slot
            gap = cum_cols[:, head * LANES : (head + 1) * LANES] - cum[head : head + 1]
            decay = jnp.exp(jnp.where(linked, gap, NEG))
            step_row = step[head : head + 1]
            share = outer[slot * BLOCK : (slot + 1) * BLOCK] * decay
            dcontact = dcontact + share * step_row
            flow = share * contact
            step_rows.append(jnp.sum(flow, axis=0, keepdims=True))
            w_parts.append(jnp.where(strict, flow * step_row, 0.0).astype(BF16))
            mixes.append((decay * (contact * step_row)).astype(BF16))
        dx_parts.append(mm_tn(jnp.concatenate(mixes, axis=0), dy_both))
    pad = [jnp.zeros((8 - heads, BLOCK), F32)] if heads < 8 else []
    dstep = jnp.concatenate(step_rows + pad, axis=0)
    pick_rows = (iota((16, heads * BLOCK), 1) // BLOCK) == iota((16, heads * BLOCK), 0)
    pick_rows = jnp.where(pick_rows, 1.0, 0.0).astype(BF16)
    dcum = mm_nt(pick_rows, jnp.concatenate(w_parts, axis=1))[:8]
    dcum = dcum - mm(pick_rows, jnp.concatenate(w_parts, axis=0))[:8]

    state_low = state_in_ref[0]
    dstate = dstate_ref[...]
    dstate_low = dstate.astype(BF16)
    pick_x = (iota((16, channels), 1) // PD) == iota((16, channels), 0)
    pick_f = jnp.where(pick_x, 1.0, 0.0)
    pick_x = pick_f.astype(BF16)
    from_state = enter_x * mm(c_low, state_low)
    dcum = dcum + mm_nt(pick_x, (dy * from_state).astype(BF16))[:8]
    dye = (enter_x * dy).astype(BF16)
    through = mm(b_low, dstate_low)
    dweight = mm_nt(pick_x, (x_val * through).astype(BF16))[:8]
    wx = (weight_x * x_val).astype(BF16)
    kept_x = enter_x[BLOCK - 1 :]
    dkept = jnp.sum(dstate * state_low.astype(F32), axis=0, keepdims=True) * kept_x
    dkept = jnp.sum(pick_f[:8] * dkept, axis=1, keepdims=True)
    moved = dweight * weight
    lane = iota((8, BLOCK), 1)
    dlast = jnp.sum(moved, axis=1, keepdims=True) + dkept
    dcum = dcum - moved + jnp.where(lane == BLOCK - 1, dlast, 0.0)
    dstep = dstep + dweight * tail
    dc = mm_nt(dye, state_low)
    db = mm_nt(wx, dstate_low)
    dstate_ref[...] = mm_tn(c_low, dye) + kept_x * dstate
    dcontact_low = dcontact.astype(BF16)
    dc = dc + mm(dcontact_low, b_low)
    db = db + mm_tn(dcontact_low, c_low)
    dx = jnp.concatenate(dx_parts, axis=1) + weight_x * through + skip_ref[...] * dy

    dlog = mm(split3(dcum), linked_low)
    dlog = dlog[0:8] + dlog[8:16] + dlog[16:24]
    dstep = dstep - dlog * rate
    ddt = dstep * sigmoid(dt_rows)
    head_acc_ref[0:8, :] += ddt
    head_acc_ref[8:16, :] += dlog * log_decay
    skip_acc_ref[0:1, :] += jnp.sum(dy * x_val, axis=0, keepdims=True)
    ddt_cols = jnp.transpose(jnp.concatenate([ddt, jnp.zeros((BLOCK - 8, BLOCK), F32)], axis=0))
    out_ref[:, dat - zat : width - zat] = ddt_cols.astype(BF16)

    dpre = jnp.concatenate([dx, db, dc], axis=1) * (pre_sig * (1.0 + pre * (1.0 - pre_sig)))
    conv_acc_ref[KW : KW + 1, :] += jnp.sum(dpre, axis=0, keepdims=True)
    dext_ref[0:BLOCK, :] = dpre
    pext_ref[0:BLOCK, :] = iota((BLOCK, BLOCK), 0) + base - start_col
    draw = taps[KW - 1 : KW] * dpre
    conv_acc_ref[KW - 1 : KW, :] += jnp.sum(dpre * ext_ref[pl.ds(8, BLOCK), :], axis=0, keepdims=True)
    for offset in range(1, KW):
        tap = KW - 1 - offset
        kept = jnp.where(place >= offset, dpre * ext_ref[pl.ds(8 - offset, BLOCK), :], 0.0)
        conv_acc_ref[tap : tap + 1, :] += jnp.sum(kept, axis=0, keepdims=True)
        later = pext_ref[pl.ds(offset, BLOCK), :]
        later = jnp.concatenate([later] * ((dat - xat) // LANES), axis=1)
        draw = draw + jnp.where(later >= offset, taps[tap : tap + 1] * dext_ref[pl.ds(offset, BLOCK), :], 0.0)
    dext_ref[pl.ds(BLOCK, 8), :] = dext_ref[0:8, :]
    pext_ref[pl.ds(BLOCK, 8), :] = pext_ref[0:8, :]
    out_ref[:, xat - zat : dat - zat] = draw.astype(BF16)


def scan_specs(cols, turn):
    zat, xat, dat, width = cols
    channels = xat - zat
    conv_width = dat - xat
    fixed = lambda shape: pl.BlockSpec(shape, lambda c: (0,) * len(shape))
    params = [
        fixed((8, conv_width)),
        fixed((1, conv_width)),
        fixed((8, LANES)),
        fixed((8, LANES)),
        fixed((1, channels)),
    ]
    starts = [
        pl.BlockSpec((BLOCK, LANES), lambda c: (turn(c), 0)),
        pl.BlockSpec((8, BLOCK), lambda c: (0, turn(c))),
    ]
    return starts, params


def scan_forward(cols, proj, start_col, start_row, params):
    zat, xat, dat, width = cols
    channels = xat - zat
    length = proj.shape[0]
    blocks = length // BLOCK
    starts, param_specs = scan_specs(cols, lambda c: c)
    body = lambda *refs: scan_fwd_kernel(cols, *refs)
    return pl.pallas_call(
        body,
        grid=(blocks,),
        in_specs=[pl.BlockSpec((BLOCK, width), lambda c: (c, 0))] + starts + param_specs,
        out_specs=[
            pl.BlockSpec((BLOCK, channels), lambda c: (c, 0)),
            pl.BlockSpec((BLOCK, channels), lambda c: (c, 0)),
            pl.BlockSpec((1, NS, channels), lambda c: (c, 0, 0)),
            pl.BlockSpec((8, BLOCK), lambda c: (0, c)),
        ],
        out_shape=[
            jax.ShapeDtypeStruct((length, channels), F32),
            jax.ShapeDtypeStruct((length, channels), F32),
            jax.ShapeDtypeStruct((blocks, NS, channels), BF16),
            jax.ShapeDtypeStruct((8, length), F32),
        ],
        scratch_shapes=[
            pltpu.VMEM((NS, channels), F32),
            pltpu.VMEM((BLOCK + 8, dat - xat), F32),
        ],
        compiler_params=pltpu.CompilerParams(vmem_limit_bytes=24 * MIB),
        cost_estimate=pl.CostEstimate(flops=2 * 10**9, bytes_accessed=10**7, transcendentals=2 * 10**6),
        name="scan_fwd",
    )(proj, start_col, start_row, *params)


def scan_backward(cols, proj, start_col, start_row, params, y, states, grad, stats, gain):
    zat, xat, dat, width = cols
    channels = xat - zat
    length = proj.shape[0]
    blocks = length // BLOCK
    turn = lambda c: blocks - 1 - c
    starts, param_specs = scan_specs(cols, turn)
    body = lambda *refs: scan_bwd_kernel(cols, *refs)
    tall = BLOCK // 8
    return pl.pallas_call(
        body,
        grid=(blocks,),
        in_specs=[
            pl.BlockSpec((BLOCK, width), lambda c: (turn(c), 0)),
            pl.BlockSpec((8, width), lambda c: (jnp.maximum(turn(c) * tall - 1, 0), 0)),
        ]
        + starts
        + param_specs
        + [
            pl.BlockSpec((BLOCK, channels), lambda c: (turn(c), 0)),
            pl.BlockSpec((1, NS, channels), lambda c: (turn(c), 0, 0)),
            pl.BlockSpec((BLOCK, channels), lambda c: (turn(c), 0)),
            pl.BlockSpec((8, BLOCK), lambda c: (0, turn(c))),
            pl.BlockSpec((1, channels), lambda c: (0, 0)),
        ],
        out_specs=[
            pl.BlockSpec((BLOCK, width - zat), lambda c: (turn(c), 0)),
            pl.BlockSpec((8, dat - xat), lambda c: (0, 0)),
            pl.BlockSpec((16, LANES), lambda c: (0, 0)),
            pl.BlockSpec((8, channels), lambda c: (0, 0)),
        ],
        out_shape=[
            jax.ShapeDtypeStruct((length, width - zat), BF16),
            jax.ShapeDtypeStruct((8, dat - xat), F32),
            jax.ShapeDtypeStruct((16, LANES), F32),
            jax.ShapeDtypeStruct((8, channels), F32),
        ],
        scratch_shapes=[
            pltpu.VMEM((NS, channels), F32),
            pltpu.VMEM((BLOCK + 8, dat - xat), F32),
            pltpu.VMEM((BLOCK + 8, dat - xat), F32),
            pltpu.VMEM((BLOCK + 8, LANES), jnp.int32),
        ],
        compiler_params=pltpu.CompilerParams(vmem_limit_bytes=24 * MIB),
        cost_estimate=pl.CostEstimate(flops=6 * 10**9, bytes_accessed=2 * 10**7, transcendentals=3 * 10**6),
        name="scan_bwd",
    )(proj, proj, start_col, start_row, *params, y, states, grad, stats, gain)


def turned(ref, own):
    eye = jnp.where(iota((own, own), 0) == iota((own, own), 1), 1.0, 0.0).astype(BF16)
    return mm_nt(eye, ref[...]).astype(BF16)


def pack_mixer_kernel(cols, place_ref, q_ref, kv_ref, z_ref, x_ref, bc_ref, dt_ref, one_ref, two_ref, att_ref, mix_ref, out_ref):
    zat, xat, dat, width = cols
    own, qwidth = q_ref.shape
    channels = xat - zat
    out_ref[:, :qwidth] = q_ref[...]
    kv = kv_ref[...].astype(F32)
    keys, vals = kv[:, :LANES], kv[:, LANES:]
    first = place_ref[0] == 0
    keys = jnp.where(first, keys, pltpu.roll(keys, HD, 1))
    vals = jnp.where(first, pltpu.roll(vals, HD, 1), vals)
    out_ref[:, qwidth:zat] = jnp.where(iota((own, LANES), 1) < HD, keys, vals).astype(BF16)
    out_ref[:, zat:xat] = z_ref[...]
    out_ref[:, xat : xat + channels] = x_ref[...]
    out_ref[:, xat + channels : dat] = bc_ref[...]
    row, lane = iota((16, LANES), 0), iota((16, LANES), 1)
    pick = jnp.where((lane == row + HD) & (row < 2), 1.0, 0.0).astype(BF16)
    gains = iota((16, own), 0)
    gains = jnp.where(gains == 0, one_ref[...].astype(F32), jnp.where(gains == 1, two_ref[...].astype(F32), 0.0))
    out_ref[:, dat:width] = mm_tn(gains.astype(BF16), pick).astype(BF16)
    out_ref[:, dat : dat + dt_ref.shape[1]] = dt_ref[...]
    out_ref[:, width : width + qwidth] = turned(att_ref, own)
    out_ref[:, width + qwidth :] = turned(mix_ref, own)


def pack_mixer(cols, kv_head, *shards):
    own, qwidth = shards[0].shape
    zat, xat, dat, width = cols
    body = lambda *refs: pack_mixer_kernel(cols, *refs)
    whole = lambda shape: pl.BlockSpec(shape, lambda i: (0, 0))
    shape = (own, width + qwidth + xat - zat)
    return pl.pallas_call(
        body,
        grid=(1,),
        in_specs=[pl.BlockSpec(memory_space=pltpu.SMEM)] + [whole(shard.shape) for shard in shards],
        out_specs=whole(shape),
        out_shape=jax.ShapeDtypeStruct(shape, BF16),
        compiler_params=pltpu.CompilerParams(vmem_limit_bytes=60 * MIB),
        cost_estimate=pl.CostEstimate(flops=10**7, bytes_accessed=10**6, transcendentals=0),
        name="pack_mixer",
    )(kv_head, *shards)


def pack_ffn_kernel(gate_ref, up_ref, down_ref, out_ref):
    own, hidden = gate_ref.shape
    out_ref[:, :hidden] = gate_ref[...]
    out_ref[:, hidden : 2 * hidden] = up_ref[...]
    out_ref[:, 2 * hidden :] = turned(down_ref, own)


def pack_ffn(gate, up, down):
    own, hidden = gate.shape
    whole = lambda shape: pl.BlockSpec(shape, lambda i: (0, 0))
    shape = (own, 3 * hidden)
    return pl.pallas_call(
        pack_ffn_kernel,
        grid=(1,),
        in_specs=[whole(gate.shape), whole(up.shape), whole(down.shape)],
        out_specs=whole(shape),
        out_shape=jax.ShapeDtypeStruct(shape, BF16),
        compiler_params=pltpu.CompilerParams(vmem_limit_bytes=60 * MIB),
        cost_estimate=pl.CostEstimate(flops=10**7, bytes_accessed=10**6, transcendentals=0),
        name="pack_ffn",
    )(gate, up, down)


def piece_at(rank_ref, refs, shift):
    if shift == 0:
        return refs[0][...]
    below, above = refs[2 * shift - 1][...], refs[2 * shift][...]
    return jnp.where(rank_ref[0] >= shift, below, above)


def norm_kernel(parts, rank_ref, *refs):
    gain_ref, out_ref = refs[2 * parts - 1], refs[2 * parts]
    rows = refs[0].shape[0]
    gain = gain_ref[...]
    for shift in range(parts):
        values = piece_at(rank_ref, refs, shift).astype(F32)
        spot = lax.rem(rank_ref[0] + (parts - shift), parts) * rows
        out_ref[pl.ds(pl.multiple_of(spot, rows), rows), :] = (values * rms_scale(values) * gain).astype(BF16)


def norm_rows(rank, parts, pieces, gain):
    rows, model = pieces[0].shape
    body = lambda *refs: norm_kernel(parts, *refs)
    whole = lambda shape: pl.BlockSpec(shape, lambda i: (0, 0))
    return pl.pallas_call(
        body,
        grid=(1,),
        in_specs=[pl.BlockSpec(memory_space=pltpu.SMEM)]
        + [whole((rows, model))] * len(pieces)
        + [whole((1, model))],
        out_specs=whole((parts * rows, model)),
        out_shape=jax.ShapeDtypeStruct((parts * rows, model), BF16),
        compiler_params=pltpu.CompilerParams(vmem_limit_bytes=60 * MIB),
        cost_estimate=pl.CostEstimate(flops=10**7, bytes_accessed=5 * 10**6, transcendentals=0),
        name="norm_rows",
    )(rank, *pieces, gain)


def branch_back_kernel(parts, rank_ref, *refs):
    count = 2 * parts - 1
    out_w_ref, am_ref, gain_ref, gatt_ref, gmix_ref, gow_ref, inner_ref, ggain_ref, sum_ref = refs[count:]
    rows = refs[0].shape[0]
    qwidth = gatt_ref.shape[1]
    sum_ref[...] = jnp.zeros_like(sum_ref)
    total = jnp.zeros((1, gmix_ref.shape[1]), F32)
    ones = jnp.ones((16, gmix_ref.shape[1]), BF16)
    for shift in range(parts):
        grads = piece_at(rank_ref, refs, shift)
        spot = pl.multiple_of(lax.rem(rank_ref[0] + (parts - shift), parts) * rows, rows)
        here = pl.ds(spot, rows)
        both = am_ref[here, :]
        grad_am = mm(grads, out_w_ref[...])
        gatt_ref[here, :] = grad_am[:, :qwidth].astype(BF16)
        grad_mixed = grad_am[:, qwidth:]
        gmix_ref[here, :] = grad_mixed
        product = grad_mixed * both[:, qwidth:].astype(F32)
        total = total + jnp.sum(product, axis=0, keepdims=True)
        high = product.astype(BF16)
        rest = (product - high.astype(F32)).astype(BF16)
        inner_ref[:, here] = (mm_nt(ones, high) + mm_nt(ones, rest))[:8]
        sum_ref[...] += mm_tn(grads, both)
    gow_ref[...] = sum_ref[...].astype(BF16)
    ggain_ref[...] = jnp.broadcast_to(total / gain_ref[...], ggain_ref.shape)


def branch_back(rank, parts, pieces, out_w, att_mixed, gain):
    rows, model = pieces[0].shape
    length, width = att_mixed.shape
    channels = gain.shape[1]
    body = lambda *refs: branch_back_kernel(parts, *refs)
    whole = lambda shape: pl.BlockSpec(shape, lambda i: (0, 0))
    shapes = [
        ((length, width - channels), BF16),
        ((length, channels), F32),
        ((model, width), BF16),
        ((8, length), F32),
        ((8, channels), F32),
    ]
    return pl.pallas_call(
        body,
        grid=(1,),
        in_specs=[pl.BlockSpec(memory_space=pltpu.SMEM)]
        + [whole((rows, model))] * len(pieces)
        + [whole((model, width)), whole((length, width)), whole((1, channels))],
        out_specs=[whole(shape) for shape, _ in shapes],
        out_shape=[jax.ShapeDtypeStruct(shape, dtype) for shape, dtype in shapes],
        scratch_shapes=[pltpu.VMEM((model, width), F32)],
        compiler_params=pltpu.CompilerParams(vmem_limit_bytes=32 * MIB),
        cost_estimate=pl.CostEstimate(flops=2 * 10**9, bytes_accessed=10**7, transcendentals=0),
        name="branch_back",
    )(rank, *pieces, out_w, att_mixed, gain)


def wgrad_kernel(step, own, core_ref, rows_ref, gq_ref, gkv_ref, grest_ref, gow_ref, theirs_ref, ours_ref):
    turn = pl.program_id(0)
    first = core_ref[0] == 0
    sources = []
    for ref in (gq_ref, gkv_ref, grest_ref, gow_ref):
        sources += [(ref, lane) for lane in range(0, ref.shape[1], LANES)]
    for index in range(len(sources) // step):

        @pl.when(turn == index)
        def _(index=index):
            lanes = sources[index * step : (index + 1) * step]
            at = 0
            while at < step:
                ref, lane = lanes[at]
                count = 1
                while at + count < step and lanes[at + count][0] is ref:
                    count += 1
                span = slice(lane, lane + count * LANES)
                to = slice(at * LANES, (at + count) * LANES)
                value = ref[:, span].astype(F32) if ref is gow_ref else mm_tn(rows_ref[...], ref[:, span])
                for chip in range(value.shape[0] // (2 * own)):
                    even = value[2 * chip * own : (2 * chip + 1) * own]
                    odd = value[(2 * chip + 1) * own : (2 * chip + 2) * own]
                    rows = slice(chip * own, (chip + 1) * own)
                    ours_ref[rows, to] = jnp.where(first, even, odd).astype(BF16)
                    theirs_ref[rows, to] = jnp.where(first, odd, even).astype(BF16)
                at += count


def mixer_wgrad(core, own, rows_one, grad_q, grad_kv, grad_rest, grad_out_w):
    length, model = rows_one.shape
    width = grad_q.shape[1] + grad_kv.shape[1] + grad_rest.shape[1] + grad_out_w.shape[1]
    step = 3
    whole = lambda shape: pl.BlockSpec(shape, lambda i: (0, 0))
    args = (rows_one, grad_q, grad_kv, grad_rest, grad_out_w)
    return pl.pallas_call(
        lambda *refs: wgrad_kernel(step, own, *refs),
        grid=(width // (step * LANES),),
        in_specs=[pl.BlockSpec(memory_space=pltpu.SMEM)] + [whole(arg.shape) for arg in args],
        out_specs=[pl.BlockSpec((model // 2, step * LANES), lambda i: (0, i))] * 2,
        out_shape=[jax.ShapeDtypeStruct((model // 2, width), BF16)] * 2,
        compiler_params=pltpu.CompilerParams(vmem_limit_bytes=32 * MIB),
        cost_estimate=pl.CostEstimate(flops=3 * 10**9, bytes_accessed=10**7, transcendentals=0),
        name="mixer_wgrad",
    )(core, *args)


def back_proj_kernel(zat, rank_ref, gq_ref, gkv_ref, grest_ref, w_ref, rows_ref, gain_ref, two_ref, *refs):
    turn = pl.program_id(0)
    outs, share_ref = refs[:-1], refs[-1]
    qwidth = gq_ref.shape[1]
    term = mm_nt(gq_ref[...], w_ref[:, :qwidth]) + mm_nt(gkv_ref[...], w_ref[:, qwidth:zat])
    term = term + mm_nt(grest_ref[...], w_ref[:, zat:])
    share = jnp.sum(term * rows_ref[...].astype(F32), axis=0, keepdims=True) / gain_ref[...]

    @pl.when(turn == 0)
    def _():
        share_ref[...] = jnp.zeros_like(share_ref)
        share_ref[1:2, :] = two_ref[0:1, :]

    share_ref[0:1, :] += share
    for index in range(len(outs)):

        @pl.when(turn == index)
        def _(index=index):
            outs[index][...] = term.astype(outs[index].dtype)


def back_proj(rank, parts, zat, width, grad_q, grad_kv, grad_rest, mixer_w, rows_one, gain, gain_two):
    length, model = rows_one.shape
    rows = length // parts
    at = lambda s, rank_ref: (lax.rem(rank_ref[0] + s, parts), 0)
    fixed = lambda s, rank_ref: (0, 0)
    spec = pltpu.PrefetchScalarGridSpec(
        num_scalar_prefetch=1,
        grid=(parts,),
        in_specs=[
            pl.BlockSpec((rows, grad_q.shape[1]), at),
            pl.BlockSpec((rows, grad_kv.shape[1]), at),
            pl.BlockSpec((rows, grad_rest.shape[1]), at),
            pl.BlockSpec((model, width), fixed),
            pl.BlockSpec((rows, model), at),
            pl.BlockSpec((1, model), fixed),
            pl.BlockSpec(gain_two.shape, fixed),
        ],
        out_specs=[pl.BlockSpec((rows, model), fixed)] * parts + [pl.BlockSpec((8, model), fixed)],
    )
    return pl.pallas_call(
        lambda *refs: back_proj_kernel(zat, *refs),
        grid_spec=spec,
        out_shape=[jax.ShapeDtypeStruct((rows, model), F32)]
        + [jax.ShapeDtypeStruct((rows, model), BF16)] * (parts - 1)
        + [jax.ShapeDtypeStruct((8, model), F32)],
        compiler_params=pltpu.CompilerParams(vmem_limit_bytes=32 * MIB),
        cost_estimate=pl.CostEstimate(flops=3 * 10**9, bytes_accessed=10**7, transcendentals=0),
        name="back_proj",
    )(rank, grad_q, grad_kv, grad_rest, mixer_w, rows_one, gain, gain_two)


def ffn_kernel(middle_ref, cot_ref, gain_ref, w_ref, out_ref, gmid_ref, glow_ref, ggain_ref, gw_ref, low_ref, sum_ref, gsum_ref):
    step = pl.program_id(0)
    hidden = w_ref.shape[1] // 3

    @pl.when(step == 0)
    def _():
        middle = middle_ref[...]
        low_ref[...] = (middle * rms_scale(middle) * gain_ref[...]).astype(BF16)
        sum_ref[...] = jnp.zeros_like(sum_ref)
        gsum_ref[...] = jnp.zeros_like(gsum_ref)

    low = low_ref[...]
    cot = cot_ref[...]
    gate_pre = mm(low, w_ref[:, :hidden])
    up_pre = mm(low, w_ref[:, hidden : 2 * hidden])
    sig = sigmoid(gate_pre)
    silu_gate = gate_pre * sig
    act = (silu_gate * up_pre).astype(BF16)
    sum_ref[...] += mm_nt(act, w_ref[:, 2 * hidden :])
    gw_ref[:, 2 * hidden :] = mm_tn(cot, act).astype(BF16)
    grad_hidden = mm(cot, w_ref[:, 2 * hidden :])
    grad_gate = (grad_hidden * up_pre * sig * (1.0 + gate_pre * (1.0 - sig))).astype(BF16)
    grad_up = (grad_hidden * silu_gate).astype(BF16)
    gw_ref[:, :hidden] = mm_tn(low, grad_gate).astype(BF16)
    gw_ref[:, hidden : 2 * hidden] = mm_tn(low, grad_up).astype(BF16)
    gsum_ref[...] += mm_nt(grad_gate, w_ref[:, :hidden]) + mm_nt(grad_up, w_ref[:, hidden : 2 * hidden])

    @pl.when(step == pl.num_programs(0) - 1)
    def _():
        middle = middle_ref[...]
        out_ref[...] = (middle + sum_ref[...]).astype(BF16)
        scale = rms_scale(middle)
        normed = middle * scale
        grad_two = gsum_ref[...]
        ggain_ref[...] = jnp.broadcast_to(jnp.sum(grad_two * normed, axis=0, keepdims=True), ggain_ref.shape)
        grad_middle = cot_ref[...].astype(F32) + norm_back(grad_two * gain_ref[...], normed, scale)
        gmid_ref[...] = grad_middle
        glow_ref[...] = grad_middle.astype(BF16)


def ffn_both(middle, cotangent, gain, ffn_w, parts):
    rows, model = middle.shape
    piece = ffn_w.shape[1] // parts
    rowspec = pl.BlockSpec((rows, model), lambda s: (0, 0))
    wspec = pl.BlockSpec((model, piece), lambda s: (0, s))
    return pl.pallas_call(
        ffn_kernel,
        grid=(parts,),
        in_specs=[rowspec, rowspec, pl.BlockSpec((1, model), lambda s: (0, 0)), wspec],
        out_specs=[rowspec, rowspec, rowspec, pl.BlockSpec((8, model), lambda s: (0, 0)), wspec],
        out_shape=[
            jax.ShapeDtypeStruct((rows, model), BF16),
            jax.ShapeDtypeStruct((rows, model), F32),
            jax.ShapeDtypeStruct((rows, model), BF16),
            jax.ShapeDtypeStruct((8, model), F32),
            jax.ShapeDtypeStruct(ffn_w.shape, BF16),
        ],
        scratch_shapes=[
            pltpu.VMEM((rows, model), BF16),
            pltpu.VMEM((rows, model), F32),
            pltpu.VMEM((rows, model), F32),
        ],
        compiler_params=pltpu.CompilerParams(vmem_limit_bytes=60 * MIB),
        cost_estimate=pl.CostEstimate(flops=10**10, bytes_accessed=3 * 10**7, transcendentals=10**6),
        name="ffn_both",
    )(middle, cotangent, gain, ffn_w)


def lane_rows(values, rows):
    padded = jnp.pad(values, (0, rows - values.shape[0]))
    return jnp.broadcast_to(padded[:, None], (rows, LANES))


def shifted(values, axis, size, shift):
    return lax.ppermute(values, axis, [(i, (i + shift) % size) for i in range(size)])


def sent(values, pairs):
    return lax.ppermute(values, "tensor", pairs)


def after(values, *earlier):
    return lax.optimization_barrier((values, earlier))[0]


def first_phase(values, parts):
    up = [(i, i + 1) for i in range(parts - 1)]
    return sent(values, up), sent(values, [(j, i) for i, j in up])


def second_phase(values, firsts, parts):
    first_up, first_down = firsts
    if parts == 4:
        below = [first_up, sent(first_up, [(1, 2), (2, 3)]), sent(first_up, [(1, 3)])]
        above = [first_down, sent(first_down, [(2, 1), (1, 0)]), sent(first_down, [(2, 0)])]
    else:
        up = lambda shift: [(i, i + shift) for i in range(parts - shift)]
        below = [first_up] + [sent(values, up(shift)) for shift in range(2, parts)]
        above = [first_down] + [sent(values, [(j, i) for i, j in up(shift)]) for shift in range(2, parts)]
    pieces = [values]
    for shift in range(1, parts):
        pieces += [below[shift - 1], above[parts - shift - 1]]
    return pieces


def sum_first(terms, rank, parts):
    if parts != 4:
        return [shifted(terms[shift].astype(BF16), "tensor", parts, shift) for shift in range(1, parts)]
    far = jnp.where(rank == 0, terms[3], terms[1])
    return [
        sent(terms[2].astype(BF16), [(0, 1), (3, 2)]),
        sent(terms[2].astype(BF16), [(1, 2), (2, 1)]),
        sent(far.astype(BF16), [(0, 2), (3, 1)]),
    ]


def sum_second(terms, firsts, rank, parts):
    if parts != 4:
        return firsts
    near, cross = firsts[0].astype(F32), firsts[1].astype(F32) + firsts[2].astype(F32)
    up = terms[1].astype(F32) + jnp.where(rank == 1, near, cross)
    down = terms[3].astype(F32) + jnp.where(rank == 1, cross, near)
    return [
        sent(up.astype(BF16), [(0, 1), (1, 2), (2, 3)]),
        sent(down.astype(BF16), [(3, 2), (2, 1), (1, 0)]),
    ]


def sum_last(terms, seconds):
    total = terms[0].astype(F32)
    for second in seconds:
        total = total + second.astype(F32)
    return total


def chip_total(theirs, ours, earlier):
    size = lax.axis_size("dp")
    theirs = after(lax.ppermute(theirs, "dp", [(i, i ^ 1) for i in range(size)]), earlier)
    return (ours.astype(F32) + theirs.astype(F32)).astype(BF16)


def sum_over_chips(values):
    size = lax.axis_size("dp")
    groups = [list(range(core, size, 2)) for core in range(2)]
    return lax.psum_scatter(values, "dp", scatter_dimension=0, axis_index_groups=groups, tiled=True)


def rows_of(values, rank, shift, parts):
    rows = values.shape[0] // parts
    return lax.dynamic_slice(values, (lax.rem(rank + shift, parts) * rows, 0), (rows, values.shape[1]))


def group_total(values, parts):
    total = values.astype(F32)
    for shift in range(1, parts):
        total = total + shifted(values, "tensor", parts, shift).astype(F32)
    return total


def butterfly(values, axis, size, step):
    while step < size:
        values = values + lax.ppermute(values, axis, [(i, i ^ step) for i in range(size)])
        step *= 2
    return values


def local(
    x_in,
    cotangent,
    segments,
    norm_one,
    w_query,
    w_keyval,
    w_attn_out,
    w_zgate,
    w_xin,
    w_bcin,
    w_dtin,
    conv_x,
    conv_bc,
    bias_x,
    bias_bc,
    dt_bias,
    a_log,
    d_skip,
    ssm_gain,
    w_mix_out,
    norm_two,
    w_gate,
    w_up,
    w_down,
):
    parts = lax.axis_size("tensor")
    rank = lax.axis_index("tensor")
    own = w_query.shape[0]
    length = segments.shape[1]
    qwidth = w_query.shape[1]
    channels = w_zgate.shape[1]
    heads = w_dtin.shape[1]
    hidden_own = w_gate.shape[1]
    width_ssm = MH * PD
    kv_head = (rank * (qwidth // HD)) // (QH // KVH)
    zat = 2 * qwidth
    xat = zat + channels
    bat = xat + channels
    dat = bat + 2 * NS
    width = dat + LANES
    cols = (zat, xat, dat, width)

    mixer_own = pack_mixer(
        cols,
        kv_head.astype(jnp.int32)[None],
        w_query,
        w_keyval,
        w_zgate,
        w_xin,
        w_bcin,
        w_dtin,
        norm_one[None, :],
        norm_two[None, :],
        w_attn_out,
        w_mix_out,
    )
    mixer_w = lax.all_gather(mixer_own, "dp", axis=0, tiled=True)
    proj_w = mixer_w[:, :width]
    out_w = mixer_w[:, width:]
    gain_one = mixer_w[:, dat + HD].astype(F32)[None, :]
    gain_two = mixer_w[:, dat + HD + 1].astype(F32)[None, :]
    ffn_own = pack_ffn(w_gate, w_up, w_down)
    ffn_first, x_first = lax.optimization_barrier((first_phase(ffn_own, parts), first_phase(x_in, parts)))
    x_pieces = second_phase(x_in, x_first, parts)
    ffn_pieces = second_phase(ffn_own, after(ffn_first, x_pieces), parts)

    seg = segments[0]
    start = jnp.sum((seg[None, :] < seg[:, None]).astype(jnp.int32), axis=1)
    start_col = jnp.broadcast_to(start[:, None], (length, LANES))
    start_row = jnp.broadcast_to(start[None, :], (8, length))
    cosine, sine = rope_tables(length)
    taps = jnp.pad(jnp.concatenate([conv_x, conv_bc], axis=1), ((0, 8 - KW), (0, 0)))
    bias = jnp.concatenate([bias_x, bias_bc])[None, :]
    params = (taps, bias, lane_rows(dt_bias, 8), lane_rows(jnp.exp(a_log), 8), jnp.repeat(d_skip, PD)[None, :])

    residual = x_in.astype(F32)
    scale_one = rms_scale(residual)
    normed_one = residual * scale_one
    rank_arg = rank.astype(jnp.int32)[None]
    rows_one = norm_rows(rank_arg, parts, x_pieces, gain_one)
    proj = mm(rows_one, proj_w)
    y, gated, states, squares = scan_forward(cols, proj, start_col, start_row, params)
    ffn_pieces = after(ffn_pieces, squares)
    ffn_own = jnp.concatenate(
        ffn_pieces[:1]
        + [jnp.where(rank >= k, ffn_pieces[2 * k - 1], ffn_pieces[2 * k]) for k in range(1, parts)],
        axis=1,
    )
    ffn_w = lax.all_gather(ffn_own, "dp", axis=0, tiled=True)
    attended, lse, low_q, low_kv = attn_forward(proj, cosine, sine, start_col)
    scale_ssm = lax.rsqrt(group_total(squares[:1], parts) / width_ssm + EPSILON)
    mixed = (gated * scale_ssm[0][:, None] * ssm_gain[None, :]).astype(BF16)
    att_mixed = jnp.concatenate([attended, mixed], axis=1)
    terms = [mm_nt(rows_of(att_mixed, rank, shift, parts), out_w) for shift in range(parts)]
    middle = residual + sum_last(terms, sum_second(terms, sum_first(terms, rank, parts), rank, parts))
    block_out, grad_middle, grad_low, grad_gain_two, grad_ffn_w = ffn_both(middle, cotangent, gain_two, ffn_w, parts)

    branch_pieces = second_phase(grad_low, first_phase(grad_low, parts), parts)
    grad_ffn_own = lax.psum_scatter(grad_ffn_w, "dp", scatter_dimension=0, tiled=True)
    piece = grad_ffn_own.shape[1] // parts
    ffn_terms = [grad_ffn_own[:, k * piece : (k + 1) * piece] for k in range(parts)]
    ffn_terms = ffn_terms[:1] + ffn_terms[:0:-1]

    grad_att, grad_mixed, grad_out_w, inner, grad_gain_ssm = branch_back(
        rank_arg, parts, branch_pieces, out_w, att_mixed, ssm_gain[None, :]
    )
    inner = group_total(inner[:1], parts) / width_ssm
    stats = jnp.concatenate([scale_ssm, inner, jnp.zeros((6, length), F32)], axis=0)
    grad_q, grad_kv = attn_backward(low_q, low_kv, lse, attended, grad_att, cosine, sine, start_col)
    grad_rest, conv_acc, head_acc, skip_acc = scan_backward(
        cols, proj, start_col, start_row, params, y, states, grad_mixed, stats, ssm_gain[None, :]
    )
    core = lax.rem(lax.axis_index("dp"), 2).astype(jnp.int32)[None]
    theirs, ours = mixer_wgrad(core, own, rows_one, grad_q, grad_kv, grad_rest, grad_out_w)
    *terms, norm_shares = back_proj(
        rank_arg, parts, zat, width, grad_q, grad_kv, after(grad_rest, theirs), mixer_w, rows_one, gain_one, grad_gain_two
    )

    model = x_in.shape[1]
    wide = lambda rows: jnp.pad(rows, ((0, 0), (0, model - rows.shape[1])))
    head_sums = jnp.sum(head_acc, axis=1)[None, :]
    small = jnp.concatenate(
        [
            wide(conv_acc),
            norm_shares[:2],
            wide(grad_gain_ssm[:1]),
            wide(skip_acc[:1]),
            wide(head_sums),
            jnp.zeros((3, model), F32),
        ],
        axis=0,
    )
    size = lax.axis_size("dp")
    small = small + lax.ppermute(small, "dp", [(i, i ^ 1) for i in range(size)])

    chip_share = chip_total(theirs, ours, small)
    small = butterfly(after(small, chip_share), "dp", size, 2)
    firsts = after(sum_first(terms, rank, parts), small, grad_ffn_own)
    seconds = sum_second(terms, firsts, rank, parts)
    grad_w = sum_over_chips(chip_share)
    seconds, ffn_firsts, grad_w = lax.optimization_barrier((seconds, sum_first(ffn_terms, rank, parts), grad_w))
    ffn_seconds = sum_second(ffn_terms, ffn_firsts, rank, parts)
    grad_one = sum_last(terms, seconds)
    grad_input = grad_middle + norm_back(grad_one * gain_one, normed_one, scale_one)

    grad_conv_x = small[:KW, :channels]
    grad_bias_x = small[KW, :channels]
    grad_ssm_gain = small[10, :channels]
    grad_d_skip = jnp.sum(small[11, :channels].reshape(heads, PD), axis=1)
    grad_dt_bias = small[12, :heads]
    grad_a_log = small[12, 8 : 8 + heads]

    place = lax.axis_index("dp") * own
    norm_parts = lax.dynamic_slice(small, (8, place), (2, own))
    conv_parts = small[: KW + 1, channels : channels + 2 * NS]
    small_rows = jnp.concatenate(
        [
            jnp.pad(norm_parts, ((0, 0), (0, LANES - own))),
            conv_parts[:, :NS],
            conv_parts[:, NS:],
            jnp.zeros((own - 2 * KW - 4, LANES), F32),
        ],
        axis=0,
    )
    keyval = jnp.zeros((own, 2 * KVH * HD), BF16)
    keyval = lax.dynamic_update_slice(keyval, grad_w[:, qwidth : qwidth + HD], (0, kv_head * HD))
    keyval = lax.dynamic_update_slice(keyval, grad_w[:, qwidth + HD : zat], (0, (KVH + kv_head) * HD))
    shared = group_total(jnp.concatenate([keyval, grad_w[:, bat:dat], small_rows.astype(BF16)], axis=1), parts)
    grad_ffn = sum_last(ffn_terms, ffn_seconds)
    grad_w = grad_w.astype(F32)
    small_rows = shared[:, 2 * KVH * HD + 2 * NS :]
    grad_norm_one, grad_norm_two = small_rows[0, :own], small_rows[1, :own]
    conv_parts = jnp.concatenate([small_rows[2 : KW + 3], small_rows[KW + 3 : 2 * KW + 4]], axis=1)
    grad_conv_bc, grad_bias_bc = conv_parts[:KW], conv_parts[KW]

    return (
        block_out,
        grad_input,
        grad_norm_one,
        grad_w[:, :qwidth],
        shared[:, : 2 * KVH * HD],
        grad_w[:, width : width + qwidth].T,
        grad_w[:, zat:xat],
        grad_w[:, xat:bat],
        shared[:, 2 * KVH * HD : 2 * KVH * HD + 2 * NS],
        grad_w[:, dat : dat + heads],
        grad_conv_x,
        grad_conv_bc,
        grad_bias_x,
        grad_bias_bc,
        grad_dt_bias,
        grad_a_log,
        grad_d_skip,
        grad_ssm_gain,
        grad_w[:, width + qwidth :].T,
        grad_norm_two,
        grad_ffn[:, :hidden_own],
        grad_ffn[:, hidden_own : 2 * hidden_own],
        grad_ffn[:, 2 * hidden_own :].T,
    )


def solution(mesh):
    return jax.shard_map(
        local,
        mesh=mesh,
        in_specs=(
            P(("dp", "tensor"), None),
            P(("dp", "tensor"), None),
            P("dp", None),
            P("dp"),
            P("dp", "tensor"),
            P("dp", None),
            P("tensor", "dp"),
            P("dp", "tensor"),
            P("dp", "tensor"),
            P("dp", None),
            P("dp", "tensor"),
            P(None, "tensor"),
            P(),
            P("tensor"),
            P(),
            P("tensor"),
            P("tensor"),
            P("tensor"),
            P("tensor"),
            P("tensor", "dp"),
            P("dp"),
            P("dp", "tensor"),
            P("dp", "tensor"),
            P("tensor", "dp"),
        ),
        out_specs=(
            P(("dp", "tensor"), None),
            P(("dp", "tensor"), None),
            P("dp"),
            P("dp", "tensor"),
            P("dp", None),
            P("tensor", "dp"),
            P("dp", "tensor"),
            P("dp", "tensor"),
            P("dp", None),
            P("dp", "tensor"),
            P(None, "tensor"),
            P(),
            P("tensor"),
            P(),
            P("tensor"),
            P("tensor"),
            P("tensor"),
            P("tensor"),
            P("tensor", "dp"),
            P("dp"),
            P("dp", "tensor"),
            P("dp", "tensor"),
            P("tensor", "dp"),
        ),
        check_vma=False,
    )
```

```python
import math

import jax
import jax.numpy as jnp
import numpy as np
from jax import lax
from jax.experimental import pallas as pl
from jax.experimental.pallas import tpu as pltpu
from jax.sharding import PartitionSpec as P

QH = 8
KVH = 2
HD = 64
MH = 24
PD = 64
NS = 128
KW = 4
BLOCK = 128
LANES = 128

EPSILON = 1e-05
ROPE_BASE = 100000000000.0
NEG = -1e9
F32 = jnp.float32
BF16 = jnp.bfloat16
MIB = 1024 * 1024


def mm(lhs, rhs):
    return lax.dot_general(lhs, rhs, (((1,), (0,)), ((), ())), preferred_element_type=F32)


def mm_nt(lhs, rhs):
    return lax.dot_general(lhs, rhs, (((1,), (1,)), ((), ())), preferred_element_type=F32)


def mm_tn(lhs, rhs):
    return lax.dot_general(lhs, rhs, (((0,), (0,)), ((), ())), preferred_element_type=F32)


def rms_scale(values):
    return lax.rsqrt(jnp.mean(values * values, axis=-1, keepdims=True) + EPSILON)


def norm_back(grad_normed, normed, scale):
    return scale * (grad_normed - normed * jnp.mean(grad_normed * normed, axis=-1, keepdims=True))


def sigmoid(v):
    return 1.0 / (1.0 + jnp.exp(-v))


def iota(shape, dim):
    return lax.broadcasted_iota(jnp.int32, shape, dim)


def rope_tables(length):
    half = HD // 2
    freqs = np.float32(ROPE_BASE) ** (-(np.arange(half, dtype=np.float32) * np.float32(2.0 / HD)))
    angles = np.arange(length, dtype=np.float32)[:, None] * freqs.astype(np.float32)[None, :]
    cosine, sine = np.cos(angles).astype(np.float32), np.sin(angles).astype(np.float32)
    cos_lanes = np.concatenate([cosine] * 4, axis=1)
    sin_lanes = np.concatenate([-sine, sine, -sine, sine], axis=1)
    return jnp.asarray(cos_lanes), jnp.asarray(sin_lanes)


def swap_halves(values):
    lane = iota(values.shape, 1)
    ahead = pltpu.roll(values, LANES - HD // 2, 1)
    behind = pltpu.roll(values, HD // 2, 1)
    return jnp.where((lane & (HD - 1)) < HD // 2, ahead, behind)


def pair_rows(block):
    low = iota(block.shape, 1) < HD
    zero = jnp.zeros_like(block)
    return jnp.concatenate([jnp.where(low, block, zero), jnp.where(low, zero, block)], axis=0)


def attn_fwd_kernel(q_ref, kv_ref, cos_ref, sin_ref, start_ref, out_ref, lse_ref, lq_ref, lkv_ref):
    length = q_ref.shape[0]
    rows = 256
    cosine, sine = cos_ref[...], sin_ref[...]
    low = iota((length, LANES), 1) < HD
    queries = q_ref[...]
    lq_ref[...] = (queries * cosine + swap_halves(queries) * sine).astype(BF16)
    kv = kv_ref[...]
    kv = jnp.where(low, kv * cosine + swap_halves(kv) * sine, kv)
    lkv_ref[...] = kv.astype(BF16)
    other = pltpu.roll(kv, HD, 1)
    keys = jnp.where(low, kv, other).astype(BF16)
    vals = jnp.where(low, other, kv).astype(BF16)
    half = iota((rows, LANES), 1) < HD
    for step in range(length // rows):
        end = (step + 1) * rows
        span = slice(step * rows, end)
        stacked = pair_rows(lq_ref[span, :].astype(F32)).astype(BF16)
        scores = mm_nt(stacked, keys[:end]) * (1.0 / math.sqrt(HD))
        first = start_ref[span, :][:, :1]
        col = iota((rows, end), 1)
        row = iota((rows, end), 0) + step * rows
        allowed = (col <= row) & (col >= first)
        allowed = jnp.concatenate([allowed.astype(jnp.int32)] * 2, axis=0) > 0
        scores = jnp.where(allowed, scores, NEG)
        top = jnp.max(scores, axis=1, keepdims=True)
        expo = jnp.exp(scores - top)
        total = jnp.sum(expo, axis=1, keepdims=True)
        probs = (expo * (1.0 / total)).astype(BF16)
        result = mm(probs, vals[:end])
        out_ref[span, :] = jnp.where(half, result[:rows], result[rows:]).astype(BF16)
        lse = top + jnp.log(total)
        lse_ref[span, :] = jnp.where(half, lse[:rows], lse[rows:])


def attn_bwd_kernel(
    lq_ref, lkv_ref, lse_ref, out_ref, go_ref, cos_ref, sin_ref, start_ref, gq_ref, gkv_ref, dk_ref, dv_ref
):
    length = lq_ref.shape[0]
    rows = 256
    cosine, sine = cos_ref[...], sin_ref[...]
    low = iota((length, LANES), 1) < HD
    kv = lkv_ref[...].astype(F32)
    other = pltpu.roll(kv, HD, 1)
    keys = jnp.where(low, kv, other).astype(BF16)
    vals = jnp.where(low, other, kv).astype(BF16)
    half = iota((rows, LANES), 1) < HD
    dk_ref[...] = jnp.zeros_like(dk_ref)
    dv_ref[...] = jnp.zeros_like(dv_ref)
    inv = 1.0 / math.sqrt(HD)
    for step in range(length // rows):
        end = (step + 1) * rows
        span = slice(step * rows, end)
        stacked = pair_rows(lq_ref[span, :].astype(F32)).astype(BF16)
        grads = pair_rows(go_ref[span, :].astype(F32))
        outs = out_ref[span, :].astype(F32)
        inner = jnp.sum(grads * jnp.concatenate([outs, outs], axis=0), axis=1, keepdims=True)
        grads = grads.astype(BF16)
        lse = lse_ref[span, :]
        lse = jnp.concatenate([lse[:, :1], lse[:, HD : HD + 1]], axis=0)
        scores = mm_nt(stacked, keys[:end]) * inv
        first = start_ref[span, :][:, :1]
        col = iota((rows, end), 1)
        row = iota((rows, end), 0) + step * rows
        allowed = (col <= row) & (col >= first)
        allowed = jnp.concatenate([allowed.astype(jnp.int32)] * 2, axis=0) > 0
        probs = jnp.exp(jnp.where(allowed, scores, NEG) - lse)
        grad_probs = mm_nt(grads, vals[:end])
        grad_scores = (probs * (grad_probs - inner)).astype(BF16)
        gq = mm(grad_scores, keys[:end]) * inv
        gq = jnp.where(half, gq[:rows], gq[rows:])
        gq_ref[span, :] = (gq * cosine[span] - swap_halves(gq) * sine[span]).astype(BF16)
        dk_ref[:end, :] += mm_tn(grad_scores, stacked)
        dv_ref[:end, :] += mm_tn(probs.astype(BF16), grads)
    dk = dk_ref[...] * inv
    dk = dk + pltpu.roll(dk, HD, 1)
    dk = dk * cosine - swap_halves(dk) * sine
    dv = dv_ref[...]
    dv = dv + pltpu.roll(dv, HD, 1)
    gkv_ref[...] = jnp.where(low, dk, dv).astype(BF16)


def attn_forward(proj, cosine, sine, start_col):
    length = proj.shape[0]
    wide = pl.BlockSpec((length, LANES), lambda i: (0, 0))
    return pl.pallas_call(
        attn_fwd_kernel,
        grid=(1,),
        in_specs=[wide, pl.BlockSpec((length, LANES), lambda i: (0, 1)), wide, wide, wide],
        out_specs=[wide] * 4,
        out_shape=[
            jax.ShapeDtypeStruct((length, LANES), BF16),
            jax.ShapeDtypeStruct((length, LANES), F32),
            jax.ShapeDtypeStruct((length, LANES), BF16),
            jax.ShapeDtypeStruct((length, LANES), BF16),
        ],
        compiler_params=pltpu.CompilerParams(vmem_limit_bytes=32 * MIB),
        cost_estimate=pl.CostEstimate(flops=10**9, bytes_accessed=6 * 10**6, transcendentals=2 * 10**6),
        name="attn_fwd",
    )(proj, proj, cosine, sine, start_col)


def attn_backward(low_q, low_kv, lse, out, grad_out, cosine, sine, start_col):
    length = low_q.shape[0]
    wide = pl.BlockSpec((length, LANES), lambda i: (0, 0))
    return pl.pallas_call(
        attn_bwd_kernel,
        grid=(1,),
        in_specs=[wide] * 8,
        out_specs=[wide] * 2,
        out_shape=[jax.ShapeDtypeStruct((length, LANES), BF16)] * 2,
        scratch_shapes=[pltpu.VMEM((length, LANES), F32)] * 2,
        compiler_params=pltpu.CompilerParams(vmem_limit_bytes=32 * MIB),
        cost_estimate=pl.CostEstimate(flops=3 * 10**9, bytes_accessed=6 * 10**6, transcendentals=2 * 10**6),
        name="attn_bwd",
    )(low_q, low_kv, lse, out, grad_out, cosine, sine, start_col)


def split3(values):
    high = values.astype(BF16).astype(F32)
    rest = values - high
    mid = rest.astype(BF16).astype(F32)
    tail = rest - mid
    return jnp.concatenate([high, mid, tail, jnp.zeros_like(values)], axis=0).astype(BF16)


def spread(rows, width, lanes_each):
    pick = (iota((32, width), 1) // lanes_each) == (iota((32, width), 0) & 7)
    return mm_tn(split3(rows), pick.astype(F32).astype(BF16))


def decay_terms(dt_block, dt_bias, rate, start_row, start_col, base):
    dt_rows = jnp.transpose(dt_block)[:8] + dt_bias
    step = jnp.maximum(dt_rows, 0.0) + jnp.log1p(jnp.exp(-jnp.abs(dt_rows)))
    log_decay = -step * rate
    row = iota((BLOCK, BLOCK), 0) + base
    col = iota((BLOCK, BLOCK), 1) + base
    linked = (col <= row) & (col >= start_col)
    linked_low = jnp.where(linked, 1.0, 0.0).astype(BF16)
    cum = mm_nt(split3(log_decay), linked_low)
    cum = cum[0:8] + cum[8:16] + cum[16:24]
    enter = jnp.exp(jnp.where(start_row < base, cum, NEG))
    last = cum[:, BLOCK - 1 :]
    position = iota((8, BLOCK), 1) + base
    tail = jnp.exp(jnp.where(position >= start_row[:, BLOCK - 1 :], last - cum, NEG))
    return dt_rows, step, log_decay, linked, linked_low, cum, enter, tail


def conv_sum(ext_ref, taps, bias, place):
    total = bias + taps[KW - 1 : KW] * ext_ref[pl.ds(8, BLOCK), :]
    for offset in range(1, KW):
        shifted = ext_ref[pl.ds(8 - offset, BLOCK), :]
        total = total + jnp.where(place >= offset, taps[KW - 1 - offset : KW - offset] * shifted, 0.0)
    return total


def wide_place(start_col, base, width):
    place = iota((BLOCK, BLOCK), 0) + base - start_col
    return jnp.concatenate([place] * (width // LANES), axis=1)


def scan_fwd_kernel(
    cols,
    proj_ref,
    startc_ref,
    startr_ref,
    taps_ref,
    bias_ref,
    dtb_ref,
    rate_ref,
    skip_ref,
    y_ref,
    gated_ref,
    state_out_ref,
    ssq_ref,
    state_ref,
    ext_ref,
):
    zat, xat, dat, width = cols
    channels = xat - zat
    heads = channels // PD
    block = pl.program_id(0)
    base = block * BLOCK

    @pl.when(block == 0)
    def _():
        state_ref[...] = jnp.zeros_like(state_ref)
        ext_ref[0:8, :] = jnp.zeros((8, ext_ref.shape[1]), F32)

    start_col = startc_ref[...]
    start_row = startr_ref[...]
    ext_ref[pl.ds(8, BLOCK), :] = proj_ref[:, xat:dat]
    place = wide_place(start_col, base, dat - xat)
    pre = conv_sum(ext_ref, taps_ref[...], bias_ref[...], place)
    ext_ref[0:8, :] = ext_ref[pl.ds(BLOCK, 8), :]
    conv = (pre * sigmoid(pre)).astype(BF16)
    x_low, b_low, c_low = conv[:, :channels], conv[:, channels : channels + NS], conv[:, channels + NS :]
    x_val = x_low.astype(F32)
    _, step, _, linked, _, cum, enter, tail = decay_terms(
        proj_ref[:, dat:width], dtb_ref[...], rate_ref[...], start_row, start_col, base
    )
    contact = mm_nt(c_low, b_low)
    cum_cols = spread(cum, heads * LANES, LANES)
    enter_x = spread(enter, channels, PD)
    weight_x = spread(tail * step, channels, PD)
    low = iota((BLOCK, LANES), 1) < PD
    zero = jnp.zeros((BLOCK, LANES), F32)
    within = []
    for pair in range(heads // 2):
        mixes = []
        for head in (2 * pair, 2 * pair + 1):
            gap = cum_cols[:, head * LANES : (head + 1) * LANES] - cum[head : head + 1]
            decay = jnp.exp(jnp.where(linked, gap, NEG))
            mixes.append((decay * (contact * step[head : head + 1])).astype(BF16))
        x_pair = x_val[:, pair * LANES : (pair + 1) * LANES]
        both = jnp.concatenate([jnp.where(low, x_pair, zero), jnp.where(low, zero, x_pair)], axis=0).astype(BF16)
        within.append(mm(jnp.concatenate(mixes, axis=1), both))
    state = state_ref[...]
    state_low = state.astype(BF16)
    state_out_ref[0] = state_low
    y = jnp.concatenate(within, axis=1) + enter_x * mm(c_low, state_low) + skip_ref[...] * x_val
    y_ref[...] = y
    state_ref[...] = mm_tn(b_low, (weight_x * x_val).astype(BF16)) + enter_x[BLOCK - 1 :] * state
    z = proj_ref[:, zat:xat]
    gated = y * (z * sigmoid(z))
    gated_ref[...] = gated
    square = gated * gated
    high = square.astype(BF16)
    rest = (square - high.astype(F32)).astype(BF16)
    ones = jnp.ones((16, channels), BF16)
    ssq_ref[...] = (mm_nt(ones, high) + mm_nt(ones, rest))[:8]


def scan_bwd_kernel(
    cols,
    proj_ref,
    prev_ref,
    startc_ref,
    startr_ref,
    taps_ref,
    bias_ref,
    dtb_ref,
    rate_ref,
    skip_ref,
    y_ref,
    state_in_ref,
    grad_ref,
    stats_ref,
    gain_ref,
    out_ref,
    conv_acc_ref,
    head_acc_ref,
    skip_acc_ref,
    dstate_ref,
    ext_ref,
    dext_ref,
    pext_ref,
):
    zat, xat, dat, width = cols
    channels = xat - zat
    heads = channels // PD
    turn = pl.program_id(0)
    block = pl.num_programs(0) - 1 - turn
    base = block * BLOCK

    @pl.when(turn == 0)
    def _():
        dstate_ref[...] = jnp.zeros_like(dstate_ref)
        conv_acc_ref[...] = jnp.zeros_like(conv_acc_ref)
        head_acc_ref[...] = jnp.zeros_like(head_acc_ref)
        skip_acc_ref[...] = jnp.zeros_like(skip_acc_ref)
        dext_ref[pl.ds(BLOCK, 8), :] = jnp.zeros((8, dext_ref.shape[1]), F32)
        pext_ref[pl.ds(BLOCK, 8), :] = jnp.zeros((8, LANES), jnp.int32)

    start_col = startc_ref[...]
    start_row = startr_ref[...]
    taps = taps_ref[...]
    ext_ref[0:8, :] = prev_ref[:, xat:dat]
    ext_ref[pl.ds(8, BLOCK), :] = proj_ref[:, xat:dat]
    place = wide_place(start_col, base, dat - xat)
    pre = conv_sum(ext_ref, taps, bias_ref[...], place)
    pre_sig = sigmoid(pre)
    conv = (pre * pre_sig).astype(BF16)
    x_low, b_low, c_low = conv[:, :channels], conv[:, channels : channels + NS], conv[:, channels + NS :]
    x_val = x_low.astype(F32)
    rate = rate_ref[...]
    dt_rows, step, log_decay, linked, linked_low, cum, enter, tail = decay_terms(
        proj_ref[:, dat:width], dtb_ref[...], rate, start_row, start_col, base
    )
    contact = mm_nt(c_low, b_low)
    cum_cols = spread(cum, heads * LANES, LANES)
    enter_x = spread(enter, channels, PD)
    weight = tail * step
    weight_x = spread(weight, channels, PD)

    z = proj_ref[:, zat:xat]
    z_sig = sigmoid(z)
    z_silu = z * z_sig
    y_val = y_ref[...]
    stats = spread(stats_ref[...], 2 * channels, channels)
    scale_x, inner_x = stats[:, :channels], stats[:, channels:]
    grad = scale_x * (grad_ref[...] * gain_ref[...] - y_val * z_silu * scale_x * inner_x)
    dy = grad * z_silu
    out_ref[:, :channels] = (grad * y_val * (z_sig * (1.0 + z * (1.0 - z_sig)))).astype(BF16)

    low = iota((BLOCK, LANES), 1) < PD
    strict = linked & (iota((BLOCK, BLOCK), 0) > iota((BLOCK, BLOCK), 1))
    zero = jnp.zeros((BLOCK, LANES), F32)
    dcontact = zero
    dx_parts, w_parts, step_rows = [], [], []
    for pair in range(heads // 2):
        lanes = slice(pair * LANES, (pair + 1) * LANES)
        dy_pair = dy[:, lanes]
        dy_both = jnp.concatenate([jnp.where(low, dy_pair, zero), jnp.where(low, zero, dy_pair)], axis=0).astype(BF16)
        outer = mm_nt(dy_both, x_low[:, lanes])
        mixes = []
        for slot in range(2):
            head = 2 * pair + slot
            gap = cum_cols[:, head * LANES : (head + 1) * LANES] - cum[head : head + 1]
            decay = jnp.exp(jnp.where(linked, gap, NEG))
            step_row = step[head : head + 1]
            share = outer[slot * BLOCK : (slot + 1) * BLOCK] * decay
            dcontact = dcontact + share * step_row
            flow = share * contact
            step_rows.append(jnp.sum(flow, axis=0, keepdims=True))
            w_parts.append(jnp.where(strict, flow * step_row, 0.0).astype(BF16))
            mixes.append((decay * (contact * step_row)).astype(BF16))
        dx_parts.append(mm_tn(jnp.concatenate(mixes, axis=0), dy_both))
    pad = [jnp.zeros((8 - heads, BLOCK), F32)] if heads < 8 else []
    dstep = jnp.concatenate(step_rows + pad, axis=0)
    pick_rows = (iota((16, heads * BLOCK), 1) // BLOCK) == iota((16, heads * BLOCK), 0)
    pick_rows = jnp.where(pick_rows, 1.0, 0.0).astype(BF16)
    dcum = mm_nt(pick_rows, jnp.concatenate(w_parts, axis=1))[:8]
    dcum = dcum - mm(pick_rows, jnp.concatenate(w_parts, axis=0))[:8]

    state_low = state_in_ref[0]
    dstate = dstate_ref[...]
    dstate_low = dstate.astype(BF16)
    pick_x = (iota((16, channels), 1) // PD) == iota((16, channels), 0)
    pick_f = jnp.where(pick_x, 1.0, 0.0)
    pick_x = pick_f.astype(BF16)
    from_state = enter_x * mm(c_low, state_low)
    dcum = dcum + mm_nt(pick_x, (dy * from_state).astype(BF16))[:8]
    dye = (enter_x * dy).astype(BF16)
    through = mm(b_low, dstate_low)
    dweight = mm_nt(pick_x, (x_val * through).astype(BF16))[:8]
    wx = (weight_x * x_val).astype(BF16)
    kept_x = enter_x[BLOCK - 1 :]
    dkept = jnp.sum(dstate * state_low.astype(F32), axis=0, keepdims=True) * kept_x
    dkept = jnp.sum(pick_f[:8] * dkept, axis=1, keepdims=True)
    moved = dweight * weight
    lane = iota((8, BLOCK), 1)
    dlast = jnp.sum(moved, axis=1, keepdims=True) + dkept
    dcum = dcum - moved + jnp.where(lane == BLOCK - 1, dlast, 0.0)
    dstep = dstep + dweight * tail
    dc = mm_nt(dye, state_low)
    db = mm_nt(wx, dstate_low)
    dstate_ref[...] = mm_tn(c_low, dye) + kept_x * dstate
    dcontact_low = dcontact.astype(BF16)
    dc = dc + mm(dcontact_low, b_low)
    db = db + mm_tn(dcontact_low, c_low)
    dx = jnp.concatenate(dx_parts, axis=1) + weight_x * through + skip_ref[...] * dy

    dlog = mm(split3(dcum), linked_low)
    dlog = dlog[0:8] + dlog[8:16] + dlog[16:24]
    dstep = dstep - dlog * rate
    ddt = dstep * sigmoid(dt_rows)
    head_acc_ref[0:8, :] += ddt
    head_acc_ref[8:16, :] += dlog * log_decay
    skip_acc_ref[0:1, :] += jnp.sum(dy * x_val, axis=0, keepdims=True)
    ddt_cols = jnp.transpose(jnp.concatenate([ddt, jnp.zeros((BLOCK - 8, BLOCK), F32)], axis=0))
    out_ref[:, dat - zat : width - zat] = ddt_cols.astype(BF16)

    dpre = jnp.concatenate([dx, db, dc], axis=1) * (pre_sig * (1.0 + pre * (1.0 - pre_sig)))
    conv_acc_ref[KW : KW + 1, :] += jnp.sum(dpre, axis=0, keepdims=True)
    dext_ref[0:BLOCK, :] = dpre
    pext_ref[0:BLOCK, :] = iota((BLOCK, BLOCK), 0) + base - start_col
    draw = taps[KW - 1 : KW] * dpre
    conv_acc_ref[KW - 1 : KW, :] += jnp.sum(dpre * ext_ref[pl.ds(8, BLOCK), :], axis=0, keepdims=True)
    for offset in range(1, KW):
        tap = KW - 1 - offset
        kept = jnp.where(place >= offset, dpre * ext_ref[pl.ds(8 - offset, BLOCK), :], 0.0)
        conv_acc_ref[tap : tap + 1, :] += jnp.sum(kept, axis=0, keepdims=True)
        later = pext_ref[pl.ds(offset, BLOCK), :]
        later = jnp.concatenate([later] * ((dat - xat) // LANES), axis=1)
        draw = draw + jnp.where(later >= offset, taps[tap : tap + 1] * dext_ref[pl.ds(offset, BLOCK), :], 0.0)
    dext_ref[pl.ds(BLOCK, 8), :] = dext_ref[0:8, :]
    pext_ref[pl.ds(BLOCK, 8), :] = pext_ref[0:8, :]
    out_ref[:, xat - zat : dat - zat] = draw.astype(BF16)


def scan_specs(cols, turn):
    zat, xat, dat, width = cols
    channels = xat - zat
    conv_width = dat - xat
    fixed = lambda shape: pl.BlockSpec(shape, lambda c: (0,) * len(shape))
    params = [
        fixed((8, conv_width)),
        fixed((1, conv_width)),
        fixed((8, LANES)),
        fixed((8, LANES)),
        fixed((1, channels)),
    ]
    starts = [
        pl.BlockSpec((BLOCK, LANES), lambda c: (turn(c), 0)),
        pl.BlockSpec((8, BLOCK), lambda c: (0, turn(c))),
    ]
    return starts, params


def scan_forward(cols, proj, start_col, start_row, params):
    zat, xat, dat, width = cols
    channels = xat - zat
    length = proj.shape[0]
    blocks = length // BLOCK
    starts, param_specs = scan_specs(cols, lambda c: c)
    body = lambda *refs: scan_fwd_kernel(cols, *refs)
    return pl.pallas_call(
        body,
        grid=(blocks,),
        in_specs=[pl.BlockSpec((BLOCK, width), lambda c: (c, 0))] + starts + param_specs,
        out_specs=[
            pl.BlockSpec((BLOCK, channels), lambda c: (c, 0)),
            pl.BlockSpec((BLOCK, channels), lambda c: (c, 0)),
            pl.BlockSpec((1, NS, channels), lambda c: (c, 0, 0)),
            pl.BlockSpec((8, BLOCK), lambda c: (0, c)),
        ],
        out_shape=[
            jax.ShapeDtypeStruct((length, channels), F32),
            jax.ShapeDtypeStruct((length, channels), F32),
            jax.ShapeDtypeStruct((blocks, NS, channels), BF16),
            jax.ShapeDtypeStruct((8, length), F32),
        ],
        scratch_shapes=[
            pltpu.VMEM((NS, channels), F32),
            pltpu.VMEM((BLOCK + 8, dat - xat), F32),
        ],
        compiler_params=pltpu.CompilerParams(vmem_limit_bytes=24 * MIB),
        cost_estimate=pl.CostEstimate(flops=2 * 10**9, bytes_accessed=10**7, transcendentals=2 * 10**6),
        name="scan_fwd",
    )(proj, start_col, start_row, *params)


def scan_backward(cols, proj, start_col, start_row, params, y, states, grad, stats, gain):
    zat, xat, dat, width = cols
    channels = xat - zat
    length = proj.shape[0]
    blocks = length // BLOCK
    turn = lambda c: blocks - 1 - c
    starts, param_specs = scan_specs(cols, turn)
    body = lambda *refs: scan_bwd_kernel(cols, *refs)
    tall = BLOCK // 8
    return pl.pallas_call(
        body,
        grid=(blocks,),
        in_specs=[
            pl.BlockSpec((BLOCK, width), lambda c: (turn(c), 0)),
            pl.BlockSpec((8, width), lambda c: (jnp.maximum(turn(c) * tall - 1, 0), 0)),
        ]
        + starts
        + param_specs
        + [
            pl.BlockSpec((BLOCK, channels), lambda c: (turn(c), 0)),
            pl.BlockSpec((1, NS, channels), lambda c: (turn(c), 0, 0)),
            pl.BlockSpec((BLOCK, channels), lambda c: (turn(c), 0)),
            pl.BlockSpec((8, BLOCK), lambda c: (0, turn(c))),
            pl.BlockSpec((1, channels), lambda c: (0, 0)),
        ],
        out_specs=[
            pl.BlockSpec((BLOCK, width - zat), lambda c: (turn(c), 0)),
            pl.BlockSpec((8, dat - xat), lambda c: (0, 0)),
            pl.BlockSpec((16, LANES), lambda c: (0, 0)),
            pl.BlockSpec((8, channels), lambda c: (0, 0)),
        ],
        out_shape=[
            jax.ShapeDtypeStruct((length, width - zat), BF16),
            jax.ShapeDtypeStruct((8, dat - xat), F32),
            jax.ShapeDtypeStruct((16, LANES), F32),
            jax.ShapeDtypeStruct((8, channels), F32),
        ],
        scratch_shapes=[
            pltpu.VMEM((NS, channels), F32),
            pltpu.VMEM((BLOCK + 8, dat - xat), F32),
            pltpu.VMEM((BLOCK + 8, dat - xat), F32),
            pltpu.VMEM((BLOCK + 8, LANES), jnp.int32),
        ],
        compiler_params=pltpu.CompilerParams(vmem_limit_bytes=24 * MIB),
        cost_estimate=pl.CostEstimate(flops=6 * 10**9, bytes_accessed=2 * 10**7, transcendentals=3 * 10**6),
        name="scan_bwd",
    )(proj, proj, start_col, start_row, *params, y, states, grad, stats, gain)


def turned(ref, own):
    eye = jnp.where(iota((own, own), 0) == iota((own, own), 1), 1.0, 0.0).astype(BF16)
    return mm_nt(eye, ref[...]).astype(BF16)


def pack_mixer_kernel(cols, place_ref, q_ref, kv_ref, z_ref, x_ref, bc_ref, dt_ref, one_ref, two_ref, att_ref, mix_ref, out_ref):
    zat, xat, dat, width = cols
    own, qwidth = q_ref.shape
    channels = xat - zat
    out_ref[:, :qwidth] = q_ref[...]
    kv = kv_ref[...].astype(F32)
    keys, vals = kv[:, :LANES], kv[:, LANES:]
    first = place_ref[0] == 0
    keys = jnp.where(first, keys, pltpu.roll(keys, HD, 1))
    vals = jnp.where(first, pltpu.roll(vals, HD, 1), vals)
    out_ref[:, qwidth:zat] = jnp.where(iota((own, LANES), 1) < HD, keys, vals).astype(BF16)
    out_ref[:, zat:xat] = z_ref[...]
    out_ref[:, xat : xat + channels] = x_ref[...]
    out_ref[:, xat + channels : dat] = bc_ref[...]
    row, lane = iota((16, LANES), 0), iota((16, LANES), 1)
    pick = jnp.where((lane == row + HD) & (row < 2), 1.0, 0.0).astype(BF16)
    gains = iota((16, own), 0)
    gains = jnp.where(gains == 0, one_ref[...].astype(F32), jnp.where(gains == 1, two_ref[...].astype(F32), 0.0))
    out_ref[:, dat:width] = mm_tn(gains.astype(BF16), pick).astype(BF16)
    out_ref[:, dat : dat + dt_ref.shape[1]] = dt_ref[...]
    out_ref[:, width : width + qwidth] = turned(att_ref, own)
    out_ref[:, width + qwidth :] = turned(mix_ref, own)


def pack_mixer(cols, kv_head, *shards):
    own, qwidth = shards[0].shape
    zat, xat, dat, width = cols
    body = lambda *refs: pack_mixer_kernel(cols, *refs)
    whole = lambda shape: pl.BlockSpec(shape, lambda i: (0, 0))
    shape = (own, width + qwidth + xat - zat)
    return pl.pallas_call(
        body,
        grid=(1,),
        in_specs=[pl.BlockSpec(memory_space=pltpu.SMEM)] + [whole(shard.shape) for shard in shards],
        out_specs=whole(shape),
        out_shape=jax.ShapeDtypeStruct(shape, BF16),
        compiler_params=pltpu.CompilerParams(vmem_limit_bytes=60 * MIB),
        cost_estimate=pl.CostEstimate(flops=10**7, bytes_accessed=10**6, transcendentals=0),
        name="pack_mixer",
    )(kv_head, *shards)


def pack_ffn_kernel(gate_ref, up_ref, down_ref, out_ref):
    own, hidden = gate_ref.shape
    out_ref[:, :hidden] = gate_ref[...]
    out_ref[:, hidden : 2 * hidden] = up_ref[...]
    out_ref[:, 2 * hidden :] = turned(down_ref, own)


def pack_ffn(gate, up, down):
    own, hidden = gate.shape
    whole = lambda shape: pl.BlockSpec(shape, lambda i: (0, 0))
    shape = (own, 3 * hidden)
    return pl.pallas_call(
        pack_ffn_kernel,
        grid=(1,),
        in_specs=[whole(gate.shape), whole(up.shape), whole(down.shape)],
        out_specs=whole(shape),
        out_shape=jax.ShapeDtypeStruct(shape, BF16),
        compiler_params=pltpu.CompilerParams(vmem_limit_bytes=60 * MIB),
        cost_estimate=pl.CostEstimate(flops=10**7, bytes_accessed=10**6, transcendentals=0),
        name="pack_ffn",
    )(gate, up, down)


def piece_at(rank_ref, refs, shift):
    if shift == 0:
        return refs[0][...]
    below, above = refs[2 * shift - 1][...], refs[2 * shift][...]
    return jnp.where(rank_ref[0] >= shift, below, above)


def norm_kernel(parts, rank_ref, *refs):
    gain_ref, out_ref = refs[2 * parts - 1], refs[2 * parts]
    rows = refs[0].shape[0]
    gain = gain_ref[...]
    for shift in range(parts):
        values = piece_at(rank_ref, refs, shift).astype(F32)
        spot = lax.rem(rank_ref[0] + (parts - shift), parts) * rows
        out_ref[pl.ds(pl.multiple_of(spot, rows), rows), :] = (values * rms_scale(values) * gain).astype(BF16)


def norm_rows(rank, parts, pieces, gain):
    rows, model = pieces[0].shape
    body = lambda *refs: norm_kernel(parts, *refs)
    whole = lambda shape: pl.BlockSpec(shape, lambda i: (0, 0))
    return pl.pallas_call(
        body,
        grid=(1,),
        in_specs=[pl.BlockSpec(memory_space=pltpu.SMEM)]
        + [whole((rows, model))] * len(pieces)
        + [whole((1, model))],
        out_specs=whole((parts * rows, model)),
        out_shape=jax.ShapeDtypeStruct((parts * rows, model), BF16),
        compiler_params=pltpu.CompilerParams(vmem_limit_bytes=60 * MIB),
        cost_estimate=pl.CostEstimate(flops=10**7, bytes_accessed=5 * 10**6, transcendentals=0),
        name="norm_rows",
    )(rank, *pieces, gain)


def branch_back_kernel(parts, rank_ref, *refs):
    count = 2 * parts - 1
    out_w_ref, am_ref, gain_ref, gatt_ref, gmix_ref, gow_ref, inner_ref, ggain_ref, sum_ref = refs[count:]
    rows = refs[0].shape[0]
    qwidth = gatt_ref.shape[1]
    sum_ref[...] = jnp.zeros_like(sum_ref)
    total = jnp.zeros((1, gmix_ref.shape[1]), F32)
    ones = jnp.ones((16, gmix_ref.shape[1]), BF16)
    for shift in range(parts):
        grads = piece_at(rank_ref, refs, shift)
        spot = pl.multiple_of(lax.rem(rank_ref[0] + (parts - shift), parts) * rows, rows)
        here = pl.ds(spot, rows)
        both = am_ref[here, :]
        grad_am = mm(grads, out_w_ref[...])
        gatt_ref[here, :] = grad_am[:, :qwidth].astype(BF16)
        grad_mixed = grad_am[:, qwidth:]
        gmix_ref[here, :] = grad_mixed
        product = grad_mixed * both[:, qwidth:].astype(F32)
        total = total + jnp.sum(product, axis=0, keepdims=True)
        high = product.astype(BF16)
        rest = (product - high.astype(F32)).astype(BF16)
        inner_ref[:, here] = (mm_nt(ones, high) + mm_nt(ones, rest))[:8]
        sum_ref[...] += mm_tn(grads, both)
    gow_ref[...] = sum_ref[...].astype(BF16)
    ggain_ref[...] = jnp.broadcast_to(total / gain_ref[...], ggain_ref.shape)


def branch_back(rank, parts, pieces, out_w, att_mixed, gain):
    rows, model = pieces[0].shape
    length, width = att_mixed.shape
    channels = gain.shape[1]
    body = lambda *refs: branch_back_kernel(parts, *refs)
    whole = lambda shape: pl.BlockSpec(shape, lambda i: (0, 0))
    shapes = [
        ((length, width - channels), BF16),
        ((length, channels), F32),
        ((model, width), BF16),
        ((8, length), F32),
        ((8, channels), F32),
    ]
    return pl.pallas_call(
        body,
        grid=(1,),
        in_specs=[pl.BlockSpec(memory_space=pltpu.SMEM)]
        + [whole((rows, model))] * len(pieces)
        + [whole((model, width)), whole((length, width)), whole((1, channels))],
        out_specs=[whole(shape) for shape, _ in shapes],
        out_shape=[jax.ShapeDtypeStruct(shape, dtype) for shape, dtype in shapes],
        scratch_shapes=[pltpu.VMEM((model, width), F32)],
        compiler_params=pltpu.CompilerParams(vmem_limit_bytes=32 * MIB),
        cost_estimate=pl.CostEstimate(flops=2 * 10**9, bytes_accessed=10**7, transcendentals=0),
        name="branch_back",
    )(rank, *pieces, out_w, att_mixed, gain)


def wgrad_kernel(step, own, core_ref, rows_ref, gq_ref, gkv_ref, grest_ref, gow_ref, theirs_ref, ours_ref, turned_ref):
    turn = pl.program_id(0)

    @pl.when(turn == 0)
    def _():
        for row in range(0, rows_ref.shape[0], LANES):
            span = slice(row, row + LANES)
            turned_ref[:, span] = jnp.transpose(rows_ref[span, :].astype(F32)).astype(BF16)

    first = core_ref[0] == 0
    sources = []
    for ref in (gq_ref, gkv_ref, grest_ref, gow_ref):
        sources += [(ref, lane) for lane in range(0, ref.shape[1], LANES)]
    for index in range(len(sources) // step):

        @pl.when(turn == index)
        def _(index=index):
            lanes = sources[index * step : (index + 1) * step]
            at = 0
            while at < step:
                ref, lane = lanes[at]
                count = 1
                while at + count < step and lanes[at + count][0] is ref:
                    count += 1
                span = slice(lane, lane + count * LANES)
                to = slice(at * LANES, (at + count) * LANES)
                value = ref[:, span].astype(F32) if ref is gow_ref else mm(turned_ref[...], ref[:, span])
                for chip in range(value.shape[0] // (2 * own)):
                    even = value[2 * chip * own : (2 * chip + 1) * own]
                    odd = value[(2 * chip + 1) * own : (2 * chip + 2) * own]
                    rows = slice(chip * own, (chip + 1) * own)
                    ours_ref[rows, to] = jnp.where(first, even, odd).astype(BF16)
                    theirs_ref[rows, to] = jnp.where(first, odd, even).astype(BF16)
                at += count


def mixer_wgrad(core, own, rows_one, grad_q, grad_kv, grad_rest, grad_out_w):
    length, model = rows_one.shape
    width = grad_q.shape[1] + grad_kv.shape[1] + grad_rest.shape[1] + grad_out_w.shape[1]
    step = 3
    whole = lambda shape: pl.BlockSpec(shape, lambda i: (0, 0))
    args = (rows_one, grad_q, grad_kv, grad_rest, grad_out_w)
    return pl.pallas_call(
        lambda *refs: wgrad_kernel(step, own, *refs),
        grid=(width // (step * LANES),),
        in_specs=[pl.BlockSpec(memory_space=pltpu.SMEM)] + [whole(arg.shape) for arg in args],
        out_specs=[pl.BlockSpec((model // 2, step * LANES), lambda i: (0, i))] * 2,
        out_shape=[jax.ShapeDtypeStruct((model // 2, width), BF16)] * 2,
        scratch_shapes=[pltpu.VMEM((model, length), BF16)],
        compiler_params=pltpu.CompilerParams(vmem_limit_bytes=32 * MIB),
        cost_estimate=pl.CostEstimate(flops=3 * 10**9, bytes_accessed=10**7, transcendentals=0),
        name="mixer_wgrad",
    )(core, *args)


def back_proj_kernel(zat, rank_ref, gq_ref, gkv_ref, grest_ref, w_ref, rows_ref, gain_ref, two_ref, *refs):
    turn = pl.program_id(0)
    outs, share_ref = refs[:-1], refs[-1]
    qwidth = gq_ref.shape[1]
    term = mm_nt(gq_ref[...], w_ref[:, :qwidth]) + mm_nt(gkv_ref[...], w_ref[:, qwidth:zat])
    term = term + mm_nt(grest_ref[...], w_ref[:, zat:])
    share = jnp.sum(term * rows_ref[...].astype(F32), axis=0, keepdims=True) / gain_ref[...]

    @pl.when(turn == 0)
    def _():
        share_ref[...] = jnp.zeros_like(share_ref)
        share_ref[1:2, :] = two_ref[0:1, :]

    share_ref[0:1, :] += share
    for index in range(len(outs)):

        @pl.when(turn == index)
        def _(index=index):
            outs[index][...] = term.astype(outs[index].dtype)


def back_proj(rank, parts, zat, width, grad_q, grad_kv, grad_rest, mixer_w, rows_one, gain, gain_two):
    length, model = rows_one.shape
    rows = length // parts
    at = lambda s, rank_ref: (lax.rem(rank_ref[0] + s, parts), 0)
    fixed = lambda s, rank_ref: (0, 0)
    spec = pltpu.PrefetchScalarGridSpec(
        num_scalar_prefetch=1,
        grid=(parts,),
        in_specs=[
            pl.BlockSpec((rows, grad_q.shape[1]), at),
            pl.BlockSpec((rows, grad_kv.shape[1]), at),
            pl.BlockSpec((rows, grad_rest.shape[1]), at),
            pl.BlockSpec((model, width), fixed),
            pl.BlockSpec((rows, model), at),
            pl.BlockSpec((1, model), fixed),
            pl.BlockSpec(gain_two.shape, fixed),
        ],
        out_specs=[pl.BlockSpec((rows, model), fixed)] * parts + [pl.BlockSpec((8, model), fixed)],
    )
    return pl.pallas_call(
        lambda *refs: back_proj_kernel(zat, *refs),
        grid_spec=spec,
        out_shape=[jax.ShapeDtypeStruct((rows, model), F32)]
        + [jax.ShapeDtypeStruct((rows, model), BF16)] * (parts - 1)
        + [jax.ShapeDtypeStruct((8, model), F32)],
        compiler_params=pltpu.CompilerParams(vmem_limit_bytes=32 * MIB),
        cost_estimate=pl.CostEstimate(flops=3 * 10**9, bytes_accessed=10**7, transcendentals=0),
        name="back_proj",
    )(rank, grad_q, grad_kv, grad_rest, mixer_w, rows_one, gain, gain_two)


def ffn_kernel(middle_ref, cot_ref, gain_ref, w_ref, out_ref, gmid_ref, glow_ref, ggain_ref, gw_ref, low_ref, low_t_ref, cot_t_ref, sum_ref, gsum_ref):
    step = pl.program_id(0)
    hidden = w_ref.shape[1] // 3

    @pl.when(step == 0)
    def _():
        middle = middle_ref[...]
        low = middle * rms_scale(middle) * gain_ref[...]
        low_ref[...] = low.astype(BF16)
        low_t_ref[...] = jnp.transpose(low).astype(BF16)
        cot_t_ref[...] = jnp.transpose(cot_ref[...].astype(F32)).astype(BF16)
        sum_ref[...] = jnp.zeros_like(sum_ref)
        gsum_ref[...] = jnp.zeros_like(gsum_ref)

    low = low_ref[...]
    cot = cot_ref[...]
    gate_pre = mm(low, w_ref[:, :hidden])
    up_pre = mm(low, w_ref[:, hidden : 2 * hidden])
    sig = sigmoid(gate_pre)
    silu_gate = gate_pre * sig
    act = (silu_gate * up_pre).astype(BF16)
    sum_ref[...] += mm_nt(act, w_ref[:, 2 * hidden :])
    gw_ref[:, 2 * hidden :] = mm(cot_t_ref[...], act).astype(BF16)
    grad_hidden = mm(cot, w_ref[:, 2 * hidden :])
    grad_gate = (grad_hidden * up_pre * sig * (1.0 + gate_pre * (1.0 - sig))).astype(BF16)
    grad_up = (grad_hidden * silu_gate).astype(BF16)
    gw_ref[:, :hidden] = mm(low_t_ref[...], grad_gate).astype(BF16)
    gw_ref[:, hidden : 2 * hidden] = mm(low_t_ref[...], grad_up).astype(BF16)
    gsum_ref[...] += mm_nt(grad_gate, w_ref[:, :hidden]) + mm_nt(grad_up, w_ref[:, hidden : 2 * hidden])

    @pl.when(step == pl.num_programs(0) - 1)
    def _():
        middle = middle_ref[...]
        out_ref[...] = (middle + sum_ref[...]).astype(BF16)
        scale = rms_scale(middle)
        normed = middle * scale
        grad_two = gsum_ref[...]
        ggain_ref[...] = jnp.broadcast_to(jnp.sum(grad_two * normed, axis=0, keepdims=True), ggain_ref.shape)
        grad_middle = cot_ref[...].astype(F32) + norm_back(grad_two * gain_ref[...], normed, scale)
        gmid_ref[...] = grad_middle
        glow_ref[...] = grad_middle.astype(BF16)


def ffn_both(middle, cotangent, gain, ffn_w, parts):
    rows, model = middle.shape
    piece = ffn_w.shape[1] // parts
    rowspec = pl.BlockSpec((rows, model), lambda s: (0, 0))
    wspec = pl.BlockSpec((model, piece), lambda s: (0, s))
    return pl.pallas_call(
        ffn_kernel,
        grid=(parts,),
        in_specs=[rowspec, rowspec, pl.BlockSpec((1, model), lambda s: (0, 0)), wspec],
        out_specs=[rowspec, rowspec, rowspec, pl.BlockSpec((8, model), lambda s: (0, 0)), wspec],
        out_shape=[
            jax.ShapeDtypeStruct((rows, model), BF16),
            jax.ShapeDtypeStruct((rows, model), F32),
            jax.ShapeDtypeStruct((rows, model), BF16),
            jax.ShapeDtypeStruct((8, model), F32),
            jax.ShapeDtypeStruct(ffn_w.shape, BF16),
        ],
        scratch_shapes=[
            pltpu.VMEM((rows, model), BF16),
            pltpu.VMEM((model, rows), BF16),
            pltpu.VMEM((model, rows), BF16),
            pltpu.VMEM((rows, model), F32),
            pltpu.VMEM((rows, model), F32),
        ],
        compiler_params=pltpu.CompilerParams(vmem_limit_bytes=60 * MIB),
        cost_estimate=pl.CostEstimate(flops=10**10, bytes_accessed=3 * 10**7, transcendentals=10**6),
        name="ffn_both",
    )(middle, cotangent, gain, ffn_w)


def lane_rows(values, rows):
    padded = jnp.pad(values, (0, rows - values.shape[0]))
    return jnp.broadcast_to(padded[:, None], (rows, LANES))


def shifted(values, axis, size, shift):
    return lax.ppermute(values, axis, [(i, (i + shift) % size) for i in range(size)])


def sent(values, pairs):
    return lax.ppermute(values, "tensor", pairs)


def after(values, *earlier):
    return lax.optimization_barrier((values, earlier))[0]


def first_phase(values, parts):
    up = [(i, i + 1) for i in range(parts - 1)]
    return sent(values, up), sent(values, [(j, i) for i, j in up])


def second_phase(values, firsts, parts):
    first_up, first_down = firsts
    if parts == 4:
        below = [first_up, sent(first_up, [(1, 2), (2, 3)]), sent(first_up, [(1, 3)])]
        above = [first_down, sent(first_down, [(2, 1), (1, 0)]), sent(first_down, [(2, 0)])]
    else:
        up = lambda shift: [(i, i + shift) for i in range(parts - shift)]
        below = [first_up] + [sent(values, up(shift)) for shift in range(2, parts)]
        above = [first_down] + [sent(values, [(j, i) for i, j in up(shift)]) for shift in range(2, parts)]
    pieces = [values]
    for shift in range(1, parts):
        pieces += [below[shift - 1], above[parts - shift - 1]]
    return pieces


def sum_first(terms, rank, parts):
    if parts != 4:
        return [shifted(terms[shift].astype(BF16), "tensor", parts, shift) for shift in range(1, parts)]
    far = jnp.where(rank == 0, terms[3], terms[1])
    return [
        sent(terms[2].astype(BF16), [(0, 1), (3, 2)]),
        sent(terms[2].astype(BF16), [(1, 2), (2, 1)]),
        sent(far.astype(BF16), [(0, 2), (3, 1)]),
    ]


def sum_second(terms, firsts, rank, parts):
    if parts != 4:
        return firsts
    near, cross = firsts[0].astype(F32), firsts[1].astype(F32) + firsts[2].astype(F32)
    up = terms[1].astype(F32) + jnp.where(rank == 1, near, cross)
    down = terms[3].astype(F32) + jnp.where(rank == 1, cross, near)
    return [
        sent(up.astype(BF16), [(0, 1), (1, 2), (2, 3)]),
        sent(down.astype(BF16), [(3, 2), (2, 1), (1, 0)]),
    ]


def sum_last(terms, seconds):
    total = terms[0].astype(F32)
    for second in seconds:
        total = total + second.astype(F32)
    return total


def chip_total(theirs, ours, earlier):
    size = lax.axis_size("dp")
    theirs = after(lax.ppermute(theirs, "dp", [(i, i ^ 1) for i in range(size)]), earlier)
    return (ours.astype(F32) + theirs.astype(F32)).astype(BF16)


def sum_over_chips(values):
    size = lax.axis_size("dp")
    groups = [list(range(core, size, 2)) for core in range(2)]
    return lax.psum_scatter(values, "dp", scatter_dimension=0, axis_index_groups=groups, tiled=True)


def rows_of(values, rank, shift, parts):
    rows = values.shape[0] // parts
    return lax.dynamic_slice(values, (lax.rem(rank + shift, parts) * rows, 0), (rows, values.shape[1]))


def group_total(values, parts):
    total = values.astype(F32)
    for shift in range(1, parts):
        total = total + shifted(values, "tensor", parts, shift).astype(F32)
    return total


def butterfly(values, axis, size, step):
    while step < size:
        values = values + lax.ppermute(values, axis, [(i, i ^ step) for i in range(size)])
        step *= 2
    return values


def local(
    x_in,
    cotangent,
    segments,
    norm_one,
    w_query,
    w_keyval,
    w_attn_out,
    w_zgate,
    w_xin,
    w_bcin,
    w_dtin,
    conv_x,
    conv_bc,
    bias_x,
    bias_bc,
    dt_bias,
    a_log,
    d_skip,
    ssm_gain,
    w_mix_out,
    norm_two,
    w_gate,
    w_up,
    w_down,
):
    parts = lax.axis_size("tensor")
    rank = lax.axis_index("tensor")
    own = w_query.shape[0]
    length = segments.shape[1]
    qwidth = w_query.shape[1]
    channels = w_zgate.shape[1]
    heads = w_dtin.shape[1]
    hidden_own = w_gate.shape[1]
    width_ssm = MH * PD
    kv_head = (rank * (qwidth // HD)) // (QH // KVH)
    zat = 2 * qwidth
    xat = zat + channels
    bat = xat + channels
    dat = bat + 2 * NS
    width = dat + LANES
    cols = (zat, xat, dat, width)

    mixer_own = pack_mixer(
        cols,
        kv_head.astype(jnp.int32)[None],
        w_query,
        w_keyval,
        w_zgate,
        w_xin,
        w_bcin,
        w_dtin,
        norm_one[None, :],
        norm_two[None, :],
        w_attn_out,
        w_mix_out,
    )
    mixer_w = lax.all_gather(mixer_own, "dp", axis=0, tiled=True)
    proj_w = mixer_w[:, :width]
    out_w = mixer_w[:, width:]
    gain_one = mixer_w[:, dat + HD].astype(F32)[None, :]
    gain_two = mixer_w[:, dat + HD + 1].astype(F32)[None, :]
    ffn_own = pack_ffn(w_gate, w_up, w_down)
    ffn_first, x_first = lax.optimization_barrier((first_phase(ffn_own, parts), first_phase(x_in, parts)))
    x_pieces = after(second_phase(x_in, x_first, parts), gain_one, gain_two)
    ffn_pieces = second_phase(ffn_own, after(ffn_first, x_pieces), parts)

    seg = segments[0]
    start = jnp.sum((seg[None, :] < seg[:, None]).astype(jnp.int32), axis=1)
    start_col = jnp.broadcast_to(start[:, None], (length, LANES))
    start_row = jnp.broadcast_to(start[None, :], (8, length))
    cosine, sine = rope_tables(length)
    taps = jnp.pad(jnp.concatenate([conv_x, conv_bc], axis=1), ((0, 8 - KW), (0, 0)))
    bias = jnp.concatenate([bias_x, bias_bc])[None, :]
    params = (taps, bias, lane_rows(dt_bias, 8), lane_rows(jnp.exp(a_log), 8), jnp.repeat(d_skip, PD)[None, :])

    residual = x_in.astype(F32)
    scale_one = rms_scale(residual)
    normed_one = residual * scale_one
    rank_arg = rank.astype(jnp.int32)[None]
    rows_one = norm_rows(rank_arg, parts, x_pieces, gain_one)
    proj = mm(rows_one, proj_w)
    y, gated, states, squares = scan_forward(cols, proj, start_col, start_row, params)
    ffn_pieces = after(ffn_pieces, squares)
    ffn_own = jnp.concatenate(
        ffn_pieces[:1]
        + [jnp.where(rank >= k, ffn_pieces[2 * k - 1], ffn_pieces[2 * k]) for k in range(1, parts)],
        axis=1,
    )
    ffn_w = lax.all_gather(ffn_own, "dp", axis=0, tiled=True)
    attended, lse, low_q, low_kv = attn_forward(proj, cosine, sine, start_col)
    scale_ssm = lax.rsqrt(group_total(squares[:1], parts) / width_ssm + EPSILON)
    mixed = (gated * scale_ssm[0][:, None] * ssm_gain[None, :]).astype(BF16)
    att_mixed = jnp.concatenate([attended, mixed], axis=1)
    terms = [mm_nt(rows_of(att_mixed, rank, shift, parts), out_w) for shift in range(parts)]
    middle = residual + sum_last(terms, sum_second(terms, sum_first(terms, rank, parts), rank, parts))
    block_out, grad_middle, grad_low, grad_gain_two, grad_ffn_w = ffn_both(middle, cotangent, gain_two, ffn_w, parts)

    branch_pieces = second_phase(grad_low, first_phase(grad_low, parts), parts)
    grad_ffn_own = lax.psum_scatter(grad_ffn_w, "dp", scatter_dimension=0, tiled=True)
    piece = grad_ffn_own.shape[1] // parts
    ffn_terms = [grad_ffn_own[:, k * piece : (k + 1) * piece] for k in range(parts)]
    ffn_terms = ffn_terms[:1] + ffn_terms[:0:-1]

    grad_att, grad_mixed, grad_out_w, inner, grad_gain_ssm = branch_back(
        rank_arg, parts, branch_pieces, out_w, att_mixed, ssm_gain[None, :]
    )
    inner = group_total(inner[:1], parts) / width_ssm
    stats = jnp.concatenate([scale_ssm, inner, jnp.zeros((6, length), F32)], axis=0)
    grad_q, grad_kv = attn_backward(low_q, low_kv, lse, attended, grad_att, cosine, sine, start_col)
    grad_rest, conv_acc, head_acc, skip_acc = scan_backward(
        cols, proj, start_col, start_row, params, y, states, grad_mixed, stats, ssm_gain[None, :]
    )
    core = lax.rem(lax.axis_index("dp"), 2).astype(jnp.int32)[None]
    theirs, ours = mixer_wgrad(core, own, rows_one, grad_q, grad_kv, grad_rest, grad_out_w)
    *terms, norm_shares = back_proj(
        rank_arg, parts, zat, width, grad_q, grad_kv, after(grad_rest, theirs), mixer_w, rows_one, gain_one, grad_gain_two
    )

    model = x_in.shape[1]
    wide = lambda rows: jnp.pad(rows, ((0, 0), (0, model - rows.shape[1])))
    head_sums = jnp.sum(head_acc, axis=1)[None, :]
    small = jnp.concatenate(
        [
            wide(conv_acc),
            norm_shares[:2],
            wide(grad_gain_ssm[:1]),
            wide(skip_acc[:1]),
            wide(head_sums),
            jnp.zeros((3, model), F32),
        ],
        axis=0,
    )
    size = lax.axis_size("dp")
    small = small + lax.ppermute(small, "dp", [(i, i ^ 1) for i in range(size)])

    firsts = sum_first(terms, rank, parts)
    chip_share = chip_total(theirs, ours, firsts)
    firsts = after(firsts, grad_ffn_own)
    seconds = sum_second(terms, firsts, rank, parts)
    grad_w = sum_over_chips(chip_share)
    small = butterfly(after(small, seconds), "dp", size, 2)
    seconds, ffn_firsts, grad_w = lax.optimization_barrier((seconds, sum_first(ffn_terms, rank, parts), grad_w))
    ffn_seconds = sum_second(ffn_terms, ffn_firsts, rank, parts)
    grad_one = sum_last(terms, seconds)
    grad_input = grad_middle + norm_back(grad_one * gain_one, normed_one, scale_one)

    grad_conv_x = small[:KW, :channels]
    grad_bias_x = small[KW, :channels]
    grad_ssm_gain = small[10, :channels]
    grad_d_skip = jnp.sum(small[11, :channels].reshape(heads, PD), axis=1)
    grad_dt_bias = small[12, :heads]
    grad_a_log = small[12, 8 : 8 + heads]

    place = lax.axis_index("dp") * own
    norm_parts = lax.dynamic_slice(small, (8, place), (2, own))
    conv_parts = small[: KW + 1, channels : channels + 2 * NS]
    small_rows = jnp.concatenate(
        [
            jnp.pad(norm_parts, ((0, 0), (0, LANES - own))),
            conv_parts[:, :NS],
            conv_parts[:, NS:],
            jnp.zeros((own - 2 * KW - 4, LANES), F32),
        ],
        axis=0,
    )
    payload = jnp.concatenate([grad_w[:, qwidth:zat], grad_w[:, bat:dat], small_rows.astype(BF16)], axis=1)
    same, other, shared = 0.0, 0.0, 0.0
    for shift in range(parts):
        share = (shifted(payload, "tensor", parts, shift) if shift else payload).astype(F32)
        head = (lax.rem(rank + parts - shift, parts) * (qwidth // HD)) // (QH // KVH)
        shared = shared + share[:, 2 * HD :]
        same = same + jnp.where(head == kv_head, share[:, : 2 * HD], 0.0)
        other = other + jnp.where(head == kv_head, 0.0, share[:, : 2 * HD])
    first, second = jnp.where(kv_head == 0, same, other), jnp.where(kv_head == 0, other, same)
    grad_keyval = jnp.concatenate([first[:, :HD], second[:, :HD], first[:, HD:], second[:, HD:]], axis=1)
    grad_ffn = sum_last(ffn_terms, ffn_seconds)
    grad_w = grad_w.astype(F32)
    small_rows = shared[:, 2 * NS :]
    grad_norm_one, grad_norm_two = small_rows[0, :own], small_rows[1, :own]
    conv_parts = jnp.concatenate([small_rows[2 : KW + 3], small_rows[KW + 3 : 2 * KW + 4]], axis=1)
    grad_conv_bc, grad_bias_bc = conv_parts[:KW], conv_parts[KW]

    return (
        block_out,
        grad_input,
        grad_norm_one,
        grad_w[:, :qwidth],
        grad_keyval,
        grad_w[:, width : width + qwidth].T,
        grad_w[:, zat:xat],
        grad_w[:, xat:bat],
        shared[:, : 2 * NS],
        grad_w[:, dat : dat + heads],
        grad_conv_x,
        grad_conv_bc,
        grad_bias_x,
        grad_bias_bc,
        grad_dt_bias,
        grad_a_log,
        grad_d_skip,
        grad_ssm_gain,
        grad_w[:, width + qwidth :].T,
        grad_norm_two,
        grad_ffn[:, :hidden_own],
        grad_ffn[:, hidden_own : 2 * hidden_own],
        grad_ffn[:, 2 * hidden_own :].T,
    )


def solution(mesh):
    return jax.shard_map(
        local,
        mesh=mesh,
        in_specs=(
            P(("dp", "tensor"), None),
            P(("dp", "tensor"), None),
            P("dp", None),
            P("dp"),
            P("dp", "tensor"),
            P("dp", None),
            P("tensor", "dp"),
            P("dp", "tensor"),
            P("dp", "tensor"),
            P("dp", None),
            P("dp", "tensor"),
            P(None, "tensor"),
            P(),
            P("tensor"),
            P(),
            P("tensor"),
            P("tensor"),
            P("tensor"),
            P("tensor"),
            P("tensor", "dp"),
            P("dp"),
            P("dp", "tensor"),
            P("dp", "tensor"),
            P("tensor", "dp"),
        ),
        out_specs=(
            P(("dp", "tensor"), None),
            P(("dp", "tensor"), None),
            P("dp"),
            P("dp", "tensor"),
            P("dp", None),
            P("tensor", "dp"),
            P("dp", "tensor"),
            P("dp", "tensor"),
            P("dp", None),
            P("dp", "tensor"),
            P(None, "tensor"),
            P(),
            P("tensor"),
            P(),
            P("tensor"),
            P("tensor"),
            P("tensor"),
            P("tensor"),
            P("tensor", "dp"),
            P("dp"),
            P("dp", "tensor"),
            P("dp", "tensor"),
            P("tensor", "dp"),
        ),
        check_vma=False,
    )
```

```python
import math

import jax
import jax.numpy as jnp
import numpy as np
from jax import lax
from jax.experimental import pallas as pl
from jax.experimental.pallas import tpu as pltpu
from jax.sharding import PartitionSpec as P

QH = 8
KVH = 2
HD = 64
MH = 24
PD = 64
NS = 128
KW = 4
BLOCK = 128
LANES = 128

EPSILON = 1e-05
ROPE_BASE = 100000000000.0
NEG = -1e9
F32 = jnp.float32
BF16 = jnp.bfloat16
MIB = 1024 * 1024


def mm(lhs, rhs):
    return lax.dot_general(lhs, rhs, (((1,), (0,)), ((), ())), preferred_element_type=F32)


def mm_nt(lhs, rhs):
    return lax.dot_general(lhs, rhs, (((1,), (1,)), ((), ())), preferred_element_type=F32)


def mm_tn(lhs, rhs):
    return lax.dot_general(lhs, rhs, (((0,), (0,)), ((), ())), preferred_element_type=F32)


def rms_scale(values):
    return lax.rsqrt(jnp.mean(values * values, axis=-1, keepdims=True) + EPSILON)


def norm_back(grad_normed, normed, scale):
    return scale * (grad_normed - normed * jnp.mean(grad_normed * normed, axis=-1, keepdims=True))


def sigmoid(v):
    return 1.0 / (1.0 + jnp.exp(-v))


def iota(shape, dim):
    return lax.broadcasted_iota(jnp.int32, shape, dim)


def rope_tables(length):
    half = HD // 2
    freqs = np.float32(ROPE_BASE) ** (-(np.arange(half, dtype=np.float32) * np.float32(2.0 / HD)))
    angles = np.arange(length, dtype=np.float32)[:, None] * freqs.astype(np.float32)[None, :]
    cosine, sine = np.cos(angles).astype(np.float32), np.sin(angles).astype(np.float32)
    cos_lanes = np.concatenate([cosine] * 4, axis=1)
    sin_lanes = np.concatenate([-sine, sine, -sine, sine], axis=1)
    return jnp.asarray(cos_lanes), jnp.asarray(sin_lanes)


def swap_halves(values):
    lane = iota(values.shape, 1)
    ahead = pltpu.roll(values, LANES - HD // 2, 1)
    behind = pltpu.roll(values, HD // 2, 1)
    return jnp.where((lane & (HD - 1)) < HD // 2, ahead, behind)


def pair_rows(block):
    low = iota(block.shape, 1) < HD
    zero = jnp.zeros_like(block)
    return jnp.concatenate([jnp.where(low, block, zero), jnp.where(low, zero, block)], axis=0)


def attn_fwd_kernel(q_ref, kv_ref, cos_ref, sin_ref, start_ref, out_ref, lse_ref, lq_ref, lkv_ref):
    length = q_ref.shape[0]
    rows = 256
    cosine, sine = cos_ref[...], sin_ref[...]
    low = iota((length, LANES), 1) < HD
    queries = q_ref[...]
    lq_ref[...] = (queries * cosine + swap_halves(queries) * sine).astype(BF16)
    kv = kv_ref[...]
    kv = jnp.where(low, kv * cosine + swap_halves(kv) * sine, kv)
    lkv_ref[...] = kv.astype(BF16)
    other = pltpu.roll(kv, HD, 1)
    keys = jnp.where(low, kv, other).astype(BF16)
    vals = jnp.where(low, other, kv).astype(BF16)
    half = iota((rows, LANES), 1) < HD
    for step in range(length // rows):
        end = (step + 1) * rows
        span = slice(step * rows, end)
        stacked = pair_rows(lq_ref[span, :].astype(F32)).astype(BF16)
        scores = mm_nt(stacked, keys[:end]) * (1.0 / math.sqrt(HD))
        first = start_ref[span, :][:, :1]
        col = iota((rows, end), 1)
        row = iota((rows, end), 0) + step * rows
        allowed = (col <= row) & (col >= first)
        allowed = jnp.concatenate([allowed.astype(jnp.int32)] * 2, axis=0) > 0
        scores = jnp.where(allowed, scores, NEG)
        top = jnp.max(scores, axis=1, keepdims=True)
        expo = jnp.exp(scores - top)
        total = jnp.sum(expo, axis=1, keepdims=True)
        probs = (expo * (1.0 / total)).astype(BF16)
        result = mm(probs, vals[:end])
        out_ref[span, :] = jnp.where(half, result[:rows], result[rows:]).astype(BF16)
        lse = top + jnp.log(total)
        lse_ref[span, :] = jnp.where(half, lse[:rows], lse[rows:])


def attn_bwd_kernel(
    lq_ref, lkv_ref, lse_ref, out_ref, go_ref, cos_ref, sin_ref, start_ref, gq_ref, gkv_ref, dk_ref, dv_ref
):
    length = lq_ref.shape[0]
    rows = 256
    cosine, sine = cos_ref[...], sin_ref[...]
    low = iota((length, LANES), 1) < HD
    kv = lkv_ref[...].astype(F32)
    other = pltpu.roll(kv, HD, 1)
    keys = jnp.where(low, kv, other).astype(BF16)
    vals = jnp.where(low, other, kv).astype(BF16)
    half = iota((rows, LANES), 1) < HD
    dk_ref[...] = jnp.zeros_like(dk_ref)
    dv_ref[...] = jnp.zeros_like(dv_ref)
    inv = 1.0 / math.sqrt(HD)
    for step in range(length // rows):
        end = (step + 1) * rows
        span = slice(step * rows, end)
        stacked = pair_rows(lq_ref[span, :].astype(F32)).astype(BF16)
        grads = pair_rows(go_ref[span, :].astype(F32))
        outs = out_ref[span, :].astype(F32)
        inner = jnp.sum(grads * jnp.concatenate([outs, outs], axis=0), axis=1, keepdims=True)
        grads = grads.astype(BF16)
        lse = lse_ref[span, :]
        lse = jnp.concatenate([lse[:, :1], lse[:, HD : HD + 1]], axis=0)
        scores = mm_nt(stacked, keys[:end]) * inv
        first = start_ref[span, :][:, :1]
        col = iota((rows, end), 1)
        row = iota((rows, end), 0) + step * rows
        allowed = (col <= row) & (col >= first)
        allowed = jnp.concatenate([allowed.astype(jnp.int32)] * 2, axis=0) > 0
        probs = jnp.exp(jnp.where(allowed, scores, NEG) - lse)
        grad_probs = mm_nt(grads, vals[:end])
        grad_scores = (probs * (grad_probs - inner)).astype(BF16)
        gq = mm(grad_scores, keys[:end]) * inv
        gq = jnp.where(half, gq[:rows], gq[rows:])
        gq_ref[span, :] = (gq * cosine[span] - swap_halves(gq) * sine[span]).astype(BF16)
        dk_ref[:end, :] += mm_tn(grad_scores, stacked)
        dv_ref[:end, :] += mm_tn(probs.astype(BF16), grads)
    dk = dk_ref[...] * inv
    dk = dk + pltpu.roll(dk, HD, 1)
    dk = dk * cosine - swap_halves(dk) * sine
    dv = dv_ref[...]
    dv = dv + pltpu.roll(dv, HD, 1)
    gkv_ref[...] = jnp.where(low, dk, dv).astype(BF16)


def attn_forward(proj, cosine, sine, start_col):
    length = proj.shape[0]
    wide = pl.BlockSpec((length, LANES), lambda i: (0, 0))
    return pl.pallas_call(
        attn_fwd_kernel,
        grid=(1,),
        in_specs=[wide, pl.BlockSpec((length, LANES), lambda i: (0, 1)), wide, wide, wide],
        out_specs=[wide] * 4,
        out_shape=[
            jax.ShapeDtypeStruct((length, LANES), BF16),
            jax.ShapeDtypeStruct((length, LANES), F32),
            jax.ShapeDtypeStruct((length, LANES), BF16),
            jax.ShapeDtypeStruct((length, LANES), BF16),
        ],
        compiler_params=pltpu.CompilerParams(vmem_limit_bytes=32 * MIB),
        cost_estimate=pl.CostEstimate(flops=10**9, bytes_accessed=6 * 10**6, transcendentals=2 * 10**6),
        name="attn_fwd",
    )(proj, proj, cosine, sine, start_col)


def attn_backward(low_q, low_kv, lse, out, grad_out, cosine, sine, start_col):
    length = low_q.shape[0]
    wide = pl.BlockSpec((length, LANES), lambda i: (0, 0))
    return pl.pallas_call(
        attn_bwd_kernel,
        grid=(1,),
        in_specs=[wide] * 8,
        out_specs=[wide] * 2,
        out_shape=[jax.ShapeDtypeStruct((length, LANES), BF16)] * 2,
        scratch_shapes=[pltpu.VMEM((length, LANES), F32)] * 2,
        compiler_params=pltpu.CompilerParams(vmem_limit_bytes=32 * MIB),
        cost_estimate=pl.CostEstimate(flops=3 * 10**9, bytes_accessed=6 * 10**6, transcendentals=2 * 10**6),
        name="attn_bwd",
    )(low_q, low_kv, lse, out, grad_out, cosine, sine, start_col)


def split3(values):
    high = values.astype(BF16).astype(F32)
    rest = values - high
    mid = rest.astype(BF16).astype(F32)
    tail = rest - mid
    return jnp.concatenate([high, mid, tail, jnp.zeros_like(values)], axis=0).astype(BF16)


def spread(rows, width, lanes_each):
    pick = (iota((32, width), 1) // lanes_each) == (iota((32, width), 0) & 7)
    return mm_tn(split3(rows), pick.astype(F32).astype(BF16))


def decay_terms(dt_block, dt_bias, rate, start_row, start_col, base):
    dt_rows = jnp.transpose(dt_block)[:8] + dt_bias
    step = jnp.maximum(dt_rows, 0.0) + jnp.log1p(jnp.exp(-jnp.abs(dt_rows)))
    log_decay = -step * rate
    row = iota((BLOCK, BLOCK), 0) + base
    col = iota((BLOCK, BLOCK), 1) + base
    linked = (col <= row) & (col >= start_col)
    linked_low = jnp.where(linked, 1.0, 0.0).astype(BF16)
    cum = mm_nt(split3(log_decay), linked_low)
    cum = cum[0:8] + cum[8:16] + cum[16:24]
    enter = jnp.exp(jnp.where(start_row < base, cum, NEG))
    last = cum[:, BLOCK - 1 :]
    position = iota((8, BLOCK), 1) + base
    tail = jnp.exp(jnp.where(position >= start_row[:, BLOCK - 1 :], last - cum, NEG))
    return dt_rows, step, log_decay, linked, linked_low, cum, enter, tail


def conv_sum(ext_ref, taps, bias, place):
    total = bias + taps[KW - 1 : KW] * ext_ref[pl.ds(8, BLOCK), :]
    for offset in range(1, KW):
        shifted = ext_ref[pl.ds(8 - offset, BLOCK), :]
        total = total + jnp.where(place >= offset, taps[KW - 1 - offset : KW - offset] * shifted, 0.0)
    return total


def wide_place(start_col, base, width):
    place = iota((BLOCK, BLOCK), 0) + base - start_col
    return jnp.concatenate([place] * (width // LANES), axis=1)


def scan_fwd_kernel(
    cols,
    proj_ref,
    startc_ref,
    startr_ref,
    taps_ref,
    bias_ref,
    dtb_ref,
    rate_ref,
    skip_ref,
    y_ref,
    gated_ref,
    state_out_ref,
    ssq_ref,
    state_ref,
    ext_ref,
):
    zat, xat, dat, width = cols
    channels = xat - zat
    heads = channels // PD
    block = pl.program_id(0)
    base = block * BLOCK

    @pl.when(block == 0)
    def _():
        state_ref[...] = jnp.zeros_like(state_ref)
        ext_ref[0:8, :] = jnp.zeros((8, ext_ref.shape[1]), F32)

    start_col = startc_ref[...]
    start_row = startr_ref[...]
    ext_ref[pl.ds(8, BLOCK), :] = proj_ref[:, xat:dat]
    place = wide_place(start_col, base, dat - xat)
    pre = conv_sum(ext_ref, taps_ref[...], bias_ref[...], place)
    ext_ref[0:8, :] = ext_ref[pl.ds(BLOCK, 8), :]
    conv = (pre * sigmoid(pre)).astype(BF16)
    x_low, b_low, c_low = conv[:, :channels], conv[:, channels : channels + NS], conv[:, channels + NS :]
    x_val = x_low.astype(F32)
    _, step, _, linked, _, cum, enter, tail = decay_terms(
        proj_ref[:, dat:width], dtb_ref[...], rate_ref[...], start_row, start_col, base
    )
    contact = mm_nt(c_low, b_low)
    cum_cols = spread(cum, heads * LANES, LANES)
    enter_x = spread(enter, channels, PD)
    weight_x = spread(tail * step, channels, PD)
    low = iota((BLOCK, LANES), 1) < PD
    zero = jnp.zeros((BLOCK, LANES), F32)
    within = []
    for pair in range(heads // 2):
        mixes = []
        for head in (2 * pair, 2 * pair + 1):
            gap = cum_cols[:, head * LANES : (head + 1) * LANES] - cum[head : head + 1]
            decay = jnp.exp(jnp.where(linked, gap, NEG))
            mixes.append((decay * (contact * step[head : head + 1])).astype(BF16))
        x_pair = x_val[:, pair * LANES : (pair + 1) * LANES]
        both = jnp.concatenate([jnp.where(low, x_pair, zero), jnp.where(low, zero, x_pair)], axis=0).astype(BF16)
        within.append(mm(jnp.concatenate(mixes, axis=1), both))
    state = state_ref[...]
    state_low = state.astype(BF16)
    state_out_ref[0] = state_low
    y = jnp.concatenate(within, axis=1) + enter_x * mm(c_low, state_low) + skip_ref[...] * x_val
    y_ref[...] = y
    state_ref[...] = mm_tn(b_low, (weight_x * x_val).astype(BF16)) + enter_x[BLOCK - 1 :] * state
    z = proj_ref[:, zat:xat]
    gated = y * (z * sigmoid(z))
    gated_ref[...] = gated
    square = gated * gated
    high = square.astype(BF16)
    rest = (square - high.astype(F32)).astype(BF16)
    ones = jnp.ones((16, channels), BF16)
    ssq_ref[...] = (mm_nt(ones, high) + mm_nt(ones, rest))[:8]


def scan_bwd_kernel(
    cols,
    proj_ref,
    prev_ref,
    startc_ref,
    startr_ref,
    taps_ref,
    bias_ref,
    dtb_ref,
    rate_ref,
    skip_ref,
    y_ref,
    state_in_ref,
    grad_ref,
    stats_ref,
    gain_ref,
    out_ref,
    conv_acc_ref,
    head_acc_ref,
    skip_acc_ref,
    dstate_ref,
    ext_ref,
    dext_ref,
    pext_ref,
):
    zat, xat, dat, width = cols
    channels = xat - zat
    heads = channels // PD
    turn = pl.program_id(0)
    block = pl.num_programs(0) - 1 - turn
    base = block * BLOCK

    @pl.when(turn == 0)
    def _():
        dstate_ref[...] = jnp.zeros_like(dstate_ref)
        conv_acc_ref[...] = jnp.zeros_like(conv_acc_ref)
        head_acc_ref[...] = jnp.zeros_like(head_acc_ref)
        skip_acc_ref[...] = jnp.zeros_like(skip_acc_ref)
        dext_ref[pl.ds(BLOCK, 8), :] = jnp.zeros((8, dext_ref.shape[1]), F32)
        pext_ref[pl.ds(BLOCK, 8), :] = jnp.zeros((8, LANES), jnp.int32)

    start_col = startc_ref[...]
    start_row = startr_ref[...]
    taps = taps_ref[...]
    ext_ref[0:8, :] = prev_ref[:, xat:dat]
    ext_ref[pl.ds(8, BLOCK), :] = proj_ref[:, xat:dat]
    place = wide_place(start_col, base, dat - xat)
    pre = conv_sum(ext_ref, taps, bias_ref[...], place)
    pre_sig = sigmoid(pre)
    conv = (pre * pre_sig).astype(BF16)
    x_low, b_low, c_low = conv[:, :channels], conv[:, channels : channels + NS], conv[:, channels + NS :]
    x_val = x_low.astype(F32)
    rate = rate_ref[...]
    dt_rows, step, log_decay, linked, linked_low, cum, enter, tail = decay_terms(
        proj_ref[:, dat:width], dtb_ref[...], rate, start_row, start_col, base
    )
    contact = mm_nt(c_low, b_low)
    cum_cols = spread(cum, heads * LANES, LANES)
    enter_x = spread(enter, channels, PD)
    weight = tail * step
    weight_x = spread(weight, channels, PD)

    z = proj_ref[:, zat:xat]
    z_sig = sigmoid(z)
    z_silu = z * z_sig
    y_val = y_ref[...]
    stats = spread(stats_ref[...], 2 * channels, channels)
    scale_x, inner_x = stats[:, :channels], stats[:, channels:]
    grad = scale_x * (grad_ref[...] * gain_ref[...] - y_val * z_silu * scale_x * inner_x)
    dy = grad * z_silu
    out_ref[:, :channels] = (grad * y_val * (z_sig * (1.0 + z * (1.0 - z_sig)))).astype(BF16)

    low = iota((BLOCK, LANES), 1) < PD
    strict = linked & (iota((BLOCK, BLOCK), 0) > iota((BLOCK, BLOCK), 1))
    zero = jnp.zeros((BLOCK, LANES), F32)
    dcontact = zero
    dx_parts, w_parts, step_rows = [], [], []
    for pair in range(heads // 2):
        lanes = slice(pair * LANES, (pair + 1) * LANES)
        dy_pair = dy[:, lanes]
        dy_both = jnp.concatenate([jnp.where(low, dy_pair, zero), jnp.where(low, zero, dy_pair)], axis=0).astype(BF16)
        outer = mm_nt(dy_both, x_low[:, lanes])
        mixes = []
        for slot in range(2):
            head = 2 * pair + slot
            gap = cum_cols[:, head * LANES : (head + 1) * LANES] - cum[head : head + 1]
            decay = jnp.exp(jnp.where(linked, gap, NEG))
            step_row = step[head : head + 1]
            share = outer[slot * BLOCK : (slot + 1) * BLOCK] * decay
            dcontact = dcontact + share * step_row
            flow = share * contact
            step_rows.append(jnp.sum(flow, axis=0, keepdims=True))
            w_parts.append(jnp.where(strict, flow * step_row, 0.0).astype(BF16))
            mixes.append((decay * (contact * step_row)).astype(BF16))
        dx_parts.append(mm_tn(jnp.concatenate(mixes, axis=0), dy_both))
    pad = [jnp.zeros((8 - heads, BLOCK), F32)] if heads < 8 else []
    dstep = jnp.concatenate(step_rows + pad, axis=0)
    pick_rows = (iota((16, heads * BLOCK), 1) // BLOCK) == iota((16, heads * BLOCK), 0)
    pick_rows = jnp.where(pick_rows, 1.0, 0.0).astype(BF16)
    dcum = mm_nt(pick_rows, jnp.concatenate(w_parts, axis=1))[:8]
    dcum = dcum - mm(pick_rows, jnp.concatenate(w_parts, axis=0))[:8]

    state_low = state_in_ref[0]
    dstate = dstate_ref[...]
    dstate_low = dstate.astype(BF16)
    pick_x = (iota((16, channels), 1) // PD) == iota((16, channels), 0)
    pick_f = jnp.where(pick_x, 1.0, 0.0)
    pick_x = pick_f.astype(BF16)
    from_state = enter_x * mm(c_low, state_low)
    dcum = dcum + mm_nt(pick_x, (dy * from_state).astype(BF16))[:8]
    dye = (enter_x * dy).astype(BF16)
    through = mm(b_low, dstate_low)
    dweight = mm_nt(pick_x, (x_val * through).astype(BF16))[:8]
    wx = (weight_x * x_val).astype(BF16)
    kept_x = enter_x[BLOCK - 1 :]
    dkept = jnp.sum(dstate * state_low.astype(F32), axis=0, keepdims=True) * kept_x
    dkept = jnp.sum(pick_f[:8] * dkept, axis=1, keepdims=True)
    moved = dweight * weight
    lane = iota((8, BLOCK), 1)
    dlast = jnp.sum(moved, axis=1, keepdims=True) + dkept
    dcum = dcum - moved + jnp.where(lane == BLOCK - 1, dlast, 0.0)
    dstep = dstep + dweight * tail
    dc = mm_nt(dye, state_low)
    db = mm_nt(wx, dstate_low)
    dstate_ref[...] = mm_tn(c_low, dye) + kept_x * dstate
    dcontact_low = dcontact.astype(BF16)
    dc = dc + mm(dcontact_low, b_low)
    db = db + mm_tn(dcontact_low, c_low)
    dx = jnp.concatenate(dx_parts, axis=1) + weight_x * through + skip_ref[...] * dy

    dlog = mm(split3(dcum), linked_low)
    dlog = dlog[0:8] + dlog[8:16] + dlog[16:24]
    dstep = dstep - dlog * rate
    ddt = dstep * sigmoid(dt_rows)
    head_acc_ref[0:8, :] += ddt
    head_acc_ref[8:16, :] += dlog * log_decay
    skip_acc_ref[0:1, :] += jnp.sum(dy * x_val, axis=0, keepdims=True)
    ddt_cols = jnp.transpose(jnp.concatenate([ddt, jnp.zeros((BLOCK - 8, BLOCK), F32)], axis=0))
    out_ref[:, dat - zat : width - zat] = ddt_cols.astype(BF16)

    dpre = jnp.concatenate([dx, db, dc], axis=1) * (pre_sig * (1.0 + pre * (1.0 - pre_sig)))
    conv_acc_ref[KW : KW + 1, :] += jnp.sum(dpre, axis=0, keepdims=True)
    dext_ref[0:BLOCK, :] = dpre
    pext_ref[0:BLOCK, :] = iota((BLOCK, BLOCK), 0) + base - start_col
    draw = taps[KW - 1 : KW] * dpre
    conv_acc_ref[KW - 1 : KW, :] += jnp.sum(dpre * ext_ref[pl.ds(8, BLOCK), :], axis=0, keepdims=True)
    for offset in range(1, KW):
        tap = KW - 1 - offset
        kept = jnp.where(place >= offset, dpre * ext_ref[pl.ds(8 - offset, BLOCK), :], 0.0)
        conv_acc_ref[tap : tap + 1, :] += jnp.sum(kept, axis=0, keepdims=True)
        later = pext_ref[pl.ds(offset, BLOCK), :]
        later = jnp.concatenate([later] * ((dat - xat) // LANES), axis=1)
        draw = draw + jnp.where(later >= offset, taps[tap : tap + 1] * dext_ref[pl.ds(offset, BLOCK), :], 0.0)
    dext_ref[pl.ds(BLOCK, 8), :] = dext_ref[0:8, :]
    pext_ref[pl.ds(BLOCK, 8), :] = pext_ref[0:8, :]
    out_ref[:, xat - zat : dat - zat] = draw.astype(BF16)


def scan_specs(cols, turn):
    zat, xat, dat, width = cols
    channels = xat - zat
    conv_width = dat - xat
    fixed = lambda shape: pl.BlockSpec(shape, lambda c: (0,) * len(shape))
    params = [
        fixed((8, conv_width)),
        fixed((1, conv_width)),
        fixed((8, LANES)),
        fixed((8, LANES)),
        fixed((1, channels)),
    ]
    starts = [
        pl.BlockSpec((BLOCK, LANES), lambda c: (turn(c), 0)),
        pl.BlockSpec((8, BLOCK), lambda c: (0, turn(c))),
    ]
    return starts, params


def scan_forward(cols, proj, start_col, start_row, params):
    zat, xat, dat, width = cols
    channels = xat - zat
    length = proj.shape[0]
    blocks = length // BLOCK
    starts, param_specs = scan_specs(cols, lambda c: c)
    body = lambda *refs: scan_fwd_kernel(cols, *refs)
    return pl.pallas_call(
        body,
        grid=(blocks,),
        in_specs=[pl.BlockSpec((BLOCK, width), lambda c: (c, 0))] + starts + param_specs,
        out_specs=[
            pl.BlockSpec((BLOCK, channels), lambda c: (c, 0)),
            pl.BlockSpec((BLOCK, channels), lambda c: (c, 0)),
            pl.BlockSpec((1, NS, channels), lambda c: (c, 0, 0)),
            pl.BlockSpec((8, BLOCK), lambda c: (0, c)),
        ],
        out_shape=[
            jax.ShapeDtypeStruct((length, channels), F32),
            jax.ShapeDtypeStruct((length, channels), F32),
            jax.ShapeDtypeStruct((blocks, NS, channels), BF16),
            jax.ShapeDtypeStruct((8, length), F32),
        ],
        scratch_shapes=[
            pltpu.VMEM((NS, channels), F32),
            pltpu.VMEM((BLOCK + 8, dat - xat), F32),
        ],
        compiler_params=pltpu.CompilerParams(vmem_limit_bytes=24 * MIB),
        cost_estimate=pl.CostEstimate(flops=2 * 10**9, bytes_accessed=10**7, transcendentals=2 * 10**6),
        name="scan_fwd",
    )(proj, start_col, start_row, *params)


def scan_backward(cols, proj, start_col, start_row, params, y, states, grad, stats, gain):
    zat, xat, dat, width = cols
    channels = xat - zat
    length = proj.shape[0]
    blocks = length // BLOCK
    turn = lambda c: blocks - 1 - c
    starts, param_specs = scan_specs(cols, turn)
    body = lambda *refs: scan_bwd_kernel(cols, *refs)
    tall = BLOCK // 8
    return pl.pallas_call(
        body,
        grid=(blocks,),
        in_specs=[
            pl.BlockSpec((BLOCK, width), lambda c: (turn(c), 0)),
            pl.BlockSpec((8, width), lambda c: (jnp.maximum(turn(c) * tall - 1, 0), 0)),
        ]
        + starts
        + param_specs
        + [
            pl.BlockSpec((BLOCK, channels), lambda c: (turn(c), 0)),
            pl.BlockSpec((1, NS, channels), lambda c: (turn(c), 0, 0)),
            pl.BlockSpec((BLOCK, channels), lambda c: (turn(c), 0)),
            pl.BlockSpec((8, BLOCK), lambda c: (0, turn(c))),
            pl.BlockSpec((1, channels), lambda c: (0, 0)),
        ],
        out_specs=[
            pl.BlockSpec((BLOCK, width - zat), lambda c: (turn(c), 0)),
            pl.BlockSpec((8, dat - xat), lambda c: (0, 0)),
            pl.BlockSpec((16, LANES), lambda c: (0, 0)),
            pl.BlockSpec((8, channels), lambda c: (0, 0)),
        ],
        out_shape=[
            jax.ShapeDtypeStruct((length, width - zat), BF16),
            jax.ShapeDtypeStruct((8, dat - xat), F32),
            jax.ShapeDtypeStruct((16, LANES), F32),
            jax.ShapeDtypeStruct((8, channels), F32),
        ],
        scratch_shapes=[
            pltpu.VMEM((NS, channels), F32),
            pltpu.VMEM((BLOCK + 8, dat - xat), F32),
            pltpu.VMEM((BLOCK + 8, dat - xat), F32),
            pltpu.VMEM((BLOCK + 8, LANES), jnp.int32),
        ],
        compiler_params=pltpu.CompilerParams(vmem_limit_bytes=24 * MIB),
        cost_estimate=pl.CostEstimate(flops=6 * 10**9, bytes_accessed=2 * 10**7, transcendentals=3 * 10**6),
        name="scan_bwd",
    )(proj, proj, start_col, start_row, *params, y, states, grad, stats, gain)


def turned(ref, own):
    eye = jnp.where(iota((own, own), 0) == iota((own, own), 1), 1.0, 0.0).astype(BF16)
    return mm_nt(eye, ref[...]).astype(BF16)


def pack_mixer_kernel(cols, place_ref, q_ref, kv_ref, z_ref, x_ref, bc_ref, dt_ref, one_ref, two_ref, att_ref, mix_ref, out_ref):
    zat, xat, dat, width = cols
    own, qwidth = q_ref.shape
    channels = xat - zat
    out_ref[:, :qwidth] = q_ref[...]
    kv = kv_ref[...].astype(F32)
    keys, vals = kv[:, :LANES], kv[:, LANES:]
    first = place_ref[0] == 0
    keys = jnp.where(first, keys, pltpu.roll(keys, HD, 1))
    vals = jnp.where(first, pltpu.roll(vals, HD, 1), vals)
    out_ref[:, qwidth:zat] = jnp.where(iota((own, LANES), 1) < HD, keys, vals).astype(BF16)
    out_ref[:, zat:xat] = z_ref[...]
    out_ref[:, xat : xat + channels] = x_ref[...]
    out_ref[:, xat + channels : dat] = bc_ref[...]
    row, lane = iota((16, LANES), 0), iota((16, LANES), 1)
    pick = jnp.where((lane == row + HD) & (row < 2), 1.0, 0.0).astype(BF16)
    gains = iota((16, own), 0)
    gains = jnp.where(gains == 0, one_ref[...].astype(F32), jnp.where(gains == 1, two_ref[...].astype(F32), 0.0))
    out_ref[:, dat:width] = mm_tn(gains.astype(BF16), pick).astype(BF16)
    out_ref[:, dat : dat + dt_ref.shape[1]] = dt_ref[...]
    out_ref[:, width : width + qwidth] = turned(att_ref, own)
    out_ref[:, width + qwidth :] = turned(mix_ref, own)


def pack_mixer(cols, kv_head, *shards):
    own, qwidth = shards[0].shape
    zat, xat, dat, width = cols
    body = lambda *refs: pack_mixer_kernel(cols, *refs)
    whole = lambda shape: pl.BlockSpec(shape, lambda i: (0, 0))
    shape = (own, width + qwidth + xat - zat)
    return pl.pallas_call(
        body,
        grid=(1,),
        in_specs=[pl.BlockSpec(memory_space=pltpu.SMEM)] + [whole(shard.shape) for shard in shards],
        out_specs=whole(shape),
        out_shape=jax.ShapeDtypeStruct(shape, BF16),
        compiler_params=pltpu.CompilerParams(vmem_limit_bytes=60 * MIB),
        cost_estimate=pl.CostEstimate(flops=10**7, bytes_accessed=10**6, transcendentals=0),
        name="pack_mixer",
    )(kv_head, *shards)


def pack_ffn_kernel(gate_ref, up_ref, down_ref, out_ref):
    own, hidden = gate_ref.shape
    out_ref[:, :hidden] = gate_ref[...]
    out_ref[:, hidden : 2 * hidden] = up_ref[...]
    out_ref[:, 2 * hidden :] = turned(down_ref, own)


def pack_ffn(gate, up, down):
    own, hidden = gate.shape
    whole = lambda shape: pl.BlockSpec(shape, lambda i: (0, 0))
    shape = (own, 3 * hidden)
    return pl.pallas_call(
        pack_ffn_kernel,
        grid=(1,),
        in_specs=[whole(gate.shape), whole(up.shape), whole(down.shape)],
        out_specs=whole(shape),
        out_shape=jax.ShapeDtypeStruct(shape, BF16),
        compiler_params=pltpu.CompilerParams(vmem_limit_bytes=60 * MIB),
        cost_estimate=pl.CostEstimate(flops=10**7, bytes_accessed=10**6, transcendentals=0),
        name="pack_ffn",
    )(gate, up, down)


def piece_at(rank_ref, refs, shift):
    if shift == 0:
        return refs[0][...]
    below, above = refs[2 * shift - 1][...], refs[2 * shift][...]
    return jnp.where(rank_ref[0] >= shift, below, above)


def norm_kernel(parts, rank_ref, *refs):
    gain_ref, out_ref = refs[2 * parts - 1], refs[2 * parts]
    rows = refs[0].shape[0]
    gain = gain_ref[...]
    for shift in range(parts):
        values = piece_at(rank_ref, refs, shift).astype(F32)
        spot = lax.rem(rank_ref[0] + (parts - shift), parts) * rows
        out_ref[pl.ds(pl.multiple_of(spot, rows), rows), :] = (values * rms_scale(values) * gain).astype(BF16)


def norm_rows(rank, parts, pieces, gain):
    rows, model = pieces[0].shape
    body = lambda *refs: norm_kernel(parts, *refs)
    whole = lambda shape: pl.BlockSpec(shape, lambda i: (0, 0))
    return pl.pallas_call(
        body,
        grid=(1,),
        in_specs=[pl.BlockSpec(memory_space=pltpu.SMEM)]
        + [whole((rows, model))] * len(pieces)
        + [whole((1, model))],
        out_specs=whole((parts * rows, model)),
        out_shape=jax.ShapeDtypeStruct((parts * rows, model), BF16),
        compiler_params=pltpu.CompilerParams(vmem_limit_bytes=60 * MIB),
        cost_estimate=pl.CostEstimate(flops=10**7, bytes_accessed=5 * 10**6, transcendentals=0),
        name="norm_rows",
    )(rank, *pieces, gain)


def branch_back_kernel(parts, rank_ref, *refs):
    count = 2 * parts - 1
    out_w_ref, am_ref, gain_ref, gatt_ref, gmix_ref, gow_ref, inner_ref, ggain_ref, sum_ref = refs[count:]
    rows = refs[0].shape[0]
    qwidth = gatt_ref.shape[1]
    sum_ref[...] = jnp.zeros_like(sum_ref)
    total = jnp.zeros((1, gmix_ref.shape[1]), F32)
    ones = jnp.ones((16, gmix_ref.shape[1]), BF16)
    for shift in range(parts):
        grads = piece_at(rank_ref, refs, shift)
        spot = pl.multiple_of(lax.rem(rank_ref[0] + (parts - shift), parts) * rows, rows)
        here = pl.ds(spot, rows)
        both = am_ref[here, :]
        grad_am = mm(grads, out_w_ref[...])
        gatt_ref[here, :] = grad_am[:, :qwidth].astype(BF16)
        grad_mixed = grad_am[:, qwidth:]
        gmix_ref[here, :] = grad_mixed
        product = grad_mixed * both[:, qwidth:].astype(F32)
        total = total + jnp.sum(product, axis=0, keepdims=True)
        high = product.astype(BF16)
        rest = (product - high.astype(F32)).astype(BF16)
        inner_ref[:, here] = (mm_nt(ones, high) + mm_nt(ones, rest))[:8]
        sum_ref[...] += mm_tn(grads, both)
    gow_ref[...] = sum_ref[...].astype(BF16)
    ggain_ref[...] = jnp.broadcast_to(total / gain_ref[...], ggain_ref.shape)


def branch_back(rank, parts, pieces, out_w, att_mixed, gain):
    rows, model = pieces[0].shape
    length, width = att_mixed.shape
    channels = gain.shape[1]
    body = lambda *refs: branch_back_kernel(parts, *refs)
    whole = lambda shape: pl.BlockSpec(shape, lambda i: (0, 0))
    shapes = [
        ((length, width - channels), BF16),
        ((length, channels), F32),
        ((model, width), BF16),
        ((8, length), F32),
        ((8, channels), F32),
    ]
    return pl.pallas_call(
        body,
        grid=(1,),
        in_specs=[pl.BlockSpec(memory_space=pltpu.SMEM)]
        + [whole((rows, model))] * len(pieces)
        + [whole((model, width)), whole((length, width)), whole((1, channels))],
        out_specs=[whole(shape) for shape, _ in shapes],
        out_shape=[jax.ShapeDtypeStruct(shape, dtype) for shape, dtype in shapes],
        scratch_shapes=[pltpu.VMEM((model, width), F32)],
        compiler_params=pltpu.CompilerParams(vmem_limit_bytes=32 * MIB),
        cost_estimate=pl.CostEstimate(flops=2 * 10**9, bytes_accessed=10**7, transcendentals=0),
        name="branch_back",
    )(rank, *pieces, out_w, att_mixed, gain)


def wgrad_kernel(step, own, core_ref, rows_ref, gq_ref, gkv_ref, grest_ref, gow_ref, theirs_ref, ours_ref):
    turn = pl.program_id(0)
    first = core_ref[0] == 0
    sources = []
    for ref in (gq_ref, gkv_ref, grest_ref, gow_ref):
        sources += [(ref, lane) for lane in range(0, ref.shape[1], LANES)]
    for index in range(len(sources) // step):

        @pl.when(turn == index)
        def _(index=index):
            lanes = sources[index * step : (index + 1) * step]
            at = 0
            while at < step:
                ref, lane = lanes[at]
                count = 1
                while at + count < step and lanes[at + count][0] is ref:
                    count += 1
                span = slice(lane, lane + count * LANES)
                to = slice(at * LANES, (at + count) * LANES)
                value = ref[:, span].astype(F32) if ref is gow_ref else mm_tn(rows_ref[...], ref[:, span])
                for chip in range(value.shape[0] // (2 * own)):
                    even = value[2 * chip * own : (2 * chip + 1) * own]
                    odd = value[(2 * chip + 1) * own : (2 * chip + 2) * own]
                    rows = slice(chip * own, (chip + 1) * own)
                    ours_ref[rows, to] = jnp.where(first, even, odd).astype(BF16)
                    theirs_ref[rows, to] = jnp.where(first, odd, even).astype(BF16)
                at += count


def mixer_wgrad(core, own, rows_one, grad_q, grad_kv, grad_rest, grad_out_w):
    length, model = rows_one.shape
    width = grad_q.shape[1] + grad_kv.shape[1] + grad_rest.shape[1] + grad_out_w.shape[1]
    step = 3
    whole = lambda shape: pl.BlockSpec(shape, lambda i: (0, 0))
    args = (rows_one, grad_q, grad_kv, grad_rest, grad_out_w)
    return pl.pallas_call(
        lambda *refs: wgrad_kernel(step, own, *refs),
        grid=(width // (step * LANES),),
        in_specs=[pl.BlockSpec(memory_space=pltpu.SMEM)] + [whole(arg.shape) for arg in args],
        out_specs=[pl.BlockSpec((model // 2, step * LANES), lambda i: (0, i))] * 2,
        out_shape=[jax.ShapeDtypeStruct((model // 2, width), BF16)] * 2,
        compiler_params=pltpu.CompilerParams(vmem_limit_bytes=32 * MIB),
        cost_estimate=pl.CostEstimate(flops=3 * 10**9, bytes_accessed=10**7, transcendentals=0),
        name="mixer_wgrad",
    )(core, *args)


def back_proj_kernel(zat, rank_ref, gq_ref, gkv_ref, grest_ref, w_ref, rows_ref, gain_ref, two_ref, *refs):
    turn = pl.program_id(0)
    outs, share_ref = refs[:-1], refs[-1]
    qwidth = gq_ref.shape[1]
    term = mm_nt(gq_ref[...], w_ref[:, :qwidth]) + mm_nt(gkv_ref[...], w_ref[:, qwidth:zat])
    term = term + mm_nt(grest_ref[...], w_ref[:, zat:])
    share = jnp.sum(term * rows_ref[...].astype(F32), axis=0, keepdims=True) / gain_ref[...]

    @pl.when(turn == 0)
    def _():
        share_ref[...] = jnp.zeros_like(share_ref)
        share_ref[1:2, :] = two_ref[0:1, :]

    share_ref[0:1, :] += share
    for index in range(len(outs)):

        @pl.when(turn == index)
        def _(index=index):
            outs[index][...] = term.astype(outs[index].dtype)


def back_proj(rank, parts, zat, width, grad_q, grad_kv, grad_rest, mixer_w, rows_one, gain, gain_two):
    length, model = rows_one.shape
    rows = length // parts
    at = lambda s, rank_ref: (lax.rem(rank_ref[0] + s, parts), 0)
    fixed = lambda s, rank_ref: (0, 0)
    spec = pltpu.PrefetchScalarGridSpec(
        num_scalar_prefetch=1,
        grid=(parts,),
        in_specs=[
            pl.BlockSpec((rows, grad_q.shape[1]), at),
            pl.BlockSpec((rows, grad_kv.shape[1]), at),
            pl.BlockSpec((rows, grad_rest.shape[1]), at),
            pl.BlockSpec((model, width), fixed),
            pl.BlockSpec((rows, model), at),
            pl.BlockSpec((1, model), fixed),
            pl.BlockSpec(gain_two.shape, fixed),
        ],
        out_specs=[pl.BlockSpec((rows, model), fixed)] * parts + [pl.BlockSpec((8, model), fixed)],
    )
    return pl.pallas_call(
        lambda *refs: back_proj_kernel(zat, *refs),
        grid_spec=spec,
        out_shape=[jax.ShapeDtypeStruct((rows, model), F32)]
        + [jax.ShapeDtypeStruct((rows, model), BF16)] * (parts - 1)
        + [jax.ShapeDtypeStruct((8, model), F32)],
        compiler_params=pltpu.CompilerParams(vmem_limit_bytes=32 * MIB),
        cost_estimate=pl.CostEstimate(flops=3 * 10**9, bytes_accessed=10**7, transcendentals=0),
        name="back_proj",
    )(rank, grad_q, grad_kv, grad_rest, mixer_w, rows_one, gain, gain_two)


def ffn_kernel(middle_ref, cot_ref, gain_ref, w_ref, out_ref, gmid_ref, glow_ref, ggain_ref, gw_ref, low_ref, sum_ref, gsum_ref):
    step = pl.program_id(0)
    hidden = w_ref.shape[1] // 3

    @pl.when(step == 0)
    def _():
        middle = middle_ref[...]
        low_ref[...] = (middle * rms_scale(middle) * gain_ref[...]).astype(BF16)
        sum_ref[...] = jnp.zeros_like(sum_ref)
        gsum_ref[...] = jnp.zeros_like(gsum_ref)

    low = low_ref[...]
    cot = cot_ref[...]
    gate_pre = mm(low, w_ref[:, :hidden])
    up_pre = mm(low, w_ref[:, hidden : 2 * hidden])
    sig = sigmoid(gate_pre)
    silu_gate = gate_pre * sig
    act = (silu_gate * up_pre).astype(BF16)
    sum_ref[...] += mm_nt(act, w_ref[:, 2 * hidden :])
    gw_ref[:, 2 * hidden :] = mm_tn(cot, act).astype(BF16)
    grad_hidden = mm(cot, w_ref[:, 2 * hidden :])
    grad_gate = (grad_hidden * up_pre * sig * (1.0 + gate_pre * (1.0 - sig))).astype(BF16)
    grad_up = (grad_hidden * silu_gate).astype(BF16)
    gw_ref[:, :hidden] = mm_tn(low, grad_gate).astype(BF16)
    gw_ref[:, hidden : 2 * hidden] = mm_tn(low, grad_up).astype(BF16)
    gsum_ref[...] += mm_nt(grad_gate, w_ref[:, :hidden]) + mm_nt(grad_up, w_ref[:, hidden : 2 * hidden])

    @pl.when(step == pl.num_programs(0) - 1)
    def _():
        middle = middle_ref[...]
        out_ref[...] = (middle + sum_ref[...]).astype(BF16)
        scale = rms_scale(middle)
        normed = middle * scale
        grad_two = gsum_ref[...]
        ggain_ref[...] = jnp.broadcast_to(jnp.sum(grad_two * normed, axis=0, keepdims=True), ggain_ref.shape)
        grad_middle = cot_ref[...].astype(F32) + norm_back(grad_two * gain_ref[...], normed, scale)
        gmid_ref[...] = grad_middle
        glow_ref[...] = grad_middle.astype(BF16)


def ffn_both(middle, cotangent, gain, ffn_w, parts):
    rows, model = middle.shape
    piece = ffn_w.shape[1] // parts
    rowspec = pl.BlockSpec((rows, model), lambda s: (0, 0))
    wspec = pl.BlockSpec((model, piece), lambda s: (0, s))
    return pl.pallas_call(
        ffn_kernel,
        grid=(parts,),
        in_specs=[rowspec, rowspec, pl.BlockSpec((1, model), lambda s: (0, 0)), wspec],
        out_specs=[rowspec, rowspec, rowspec, pl.BlockSpec((8, model), lambda s: (0, 0)), wspec],
        out_shape=[
            jax.ShapeDtypeStruct((rows, model), BF16),
            jax.ShapeDtypeStruct((rows, model), F32),
            jax.ShapeDtypeStruct((rows, model), BF16),
            jax.ShapeDtypeStruct((8, model), F32),
            jax.ShapeDtypeStruct(ffn_w.shape, BF16),
        ],
        scratch_shapes=[
            pltpu.VMEM((rows, model), BF16),
            pltpu.VMEM((rows, model), F32),
            pltpu.VMEM((rows, model), F32),
        ],
        compiler_params=pltpu.CompilerParams(vmem_limit_bytes=60 * MIB),
        cost_estimate=pl.CostEstimate(flops=10**10, bytes_accessed=3 * 10**7, transcendentals=10**6),
        name="ffn_both",
    )(middle, cotangent, gain, ffn_w)


def lane_rows(values, rows):
    padded = jnp.pad(values, (0, rows - values.shape[0]))
    return jnp.broadcast_to(padded[:, None], (rows, LANES))


def shifted(values, axis, size, shift):
    return lax.ppermute(values, axis, [(i, (i + shift) % size) for i in range(size)])


def sent(values, pairs):
    return lax.ppermute(values, "tensor", pairs)


def after(values, *earlier):
    return lax.optimization_barrier((values, earlier))[0]


def first_phase(values, parts):
    up = [(i, i + 1) for i in range(parts - 1)]
    return sent(values, up), sent(values, [(j, i) for i, j in up])


def second_phase(values, firsts, parts):
    first_up, first_down = firsts
    if parts == 4:
        below = [first_up, sent(first_up, [(1, 2), (2, 3)]), sent(first_up, [(1, 3)])]
        above = [first_down, sent(first_down, [(2, 1), (1, 0)]), sent(first_down, [(2, 0)])]
    else:
        up = lambda shift: [(i, i + shift) for i in range(parts - shift)]
        below = [first_up] + [sent(values, up(shift)) for shift in range(2, parts)]
        above = [first_down] + [sent(values, [(j, i) for i, j in up(shift)]) for shift in range(2, parts)]
    pieces = [values]
    for shift in range(1, parts):
        pieces += [below[shift - 1], above[parts - shift - 1]]
    return pieces


def sum_first(terms, rank, parts):
    if parts != 4:
        return [shifted(terms[shift].astype(BF16), "tensor", parts, shift) for shift in range(1, parts)]
    far = jnp.where(rank == 0, terms[3], terms[1])
    return [
        sent(terms[2].astype(BF16), [(0, 1), (3, 2)]),
        sent(terms[2].astype(BF16), [(1, 2), (2, 1)]),
        sent(far.astype(BF16), [(0, 2), (3, 1)]),
    ]


def sum_second(terms, firsts, rank, parts):
    if parts != 4:
        return firsts
    near, cross = firsts[0].astype(F32), firsts[1].astype(F32) + firsts[2].astype(F32)
    up = terms[1].astype(F32) + jnp.where(rank == 1, near, cross)
    down = terms[3].astype(F32) + jnp.where(rank == 1, cross, near)
    return [
        sent(up.astype(BF16), [(0, 1), (1, 2), (2, 3)]),
        sent(down.astype(BF16), [(3, 2), (2, 1), (1, 0)]),
    ]


def sum_last(terms, seconds):
    total = terms[0].astype(F32)
    for second in seconds:
        total = total + second.astype(F32)
    return total


def chip_total(theirs, ours, earlier):
    size = lax.axis_size("dp")
    theirs = after(lax.ppermute(theirs, "dp", [(i, i ^ 1) for i in range(size)]), earlier)
    return (ours.astype(F32) + theirs.astype(F32)).astype(BF16)


def sum_over_chips(values):
    size = lax.axis_size("dp")
    groups = [list(range(core, size, 2)) for core in range(2)]
    return lax.psum_scatter(values, "dp", scatter_dimension=0, axis_index_groups=groups, tiled=True)


def rows_of(values, rank, shift, parts):
    rows = values.shape[0] // parts
    return lax.dynamic_slice(values, (lax.rem(rank + shift, parts) * rows, 0), (rows, values.shape[1]))


def group_total(values, parts):
    total = values.astype(F32)
    for shift in range(1, parts):
        total = total + shifted(values, "tensor", parts, shift).astype(F32)
    return total


def butterfly(values, axis, size, step):
    while step < size:
        values = values + lax.ppermute(values, axis, [(i, i ^ step) for i in range(size)])
        step *= 2
    return values


def local(
    x_in,
    cotangent,
    segments,
    norm_one,
    w_query,
    w_keyval,
    w_attn_out,
    w_zgate,
    w_xin,
    w_bcin,
    w_dtin,
    conv_x,
    conv_bc,
    bias_x,
    bias_bc,
    dt_bias,
    a_log,
    d_skip,
    ssm_gain,
    w_mix_out,
    norm_two,
    w_gate,
    w_up,
    w_down,
):
    parts = lax.axis_size("tensor")
    rank = lax.axis_index("tensor")
    own = w_query.shape[0]
    length = segments.shape[1]
    qwidth = w_query.shape[1]
    channels = w_zgate.shape[1]
    heads = w_dtin.shape[1]
    hidden_own = w_gate.shape[1]
    width_ssm = MH * PD
    kv_head = (rank * (qwidth // HD)) // (QH // KVH)
    zat = 2 * qwidth
    xat = zat + channels
    bat = xat + channels
    dat = bat + 2 * NS
    width = dat + LANES
    cols = (zat, xat, dat, width)

    mixer_own = pack_mixer(
        cols,
        kv_head.astype(jnp.int32)[None],
        w_query,
        w_keyval,
        w_zgate,
        w_xin,
        w_bcin,
        w_dtin,
        norm_one[None, :],
        norm_two[None, :],
        w_attn_out,
        w_mix_out,
    )
    mixer_w = lax.all_gather(mixer_own, "dp", axis=0, tiled=True)
    proj_w = mixer_w[:, :width]
    out_w = mixer_w[:, width:]
    gain_one = mixer_w[:, dat + HD].astype(F32)[None, :]
    gain_two = mixer_w[:, dat + HD + 1].astype(F32)[None, :]
    ffn_own = pack_ffn(w_gate, w_up, w_down)
    ffn_first, x_first = first_phase(ffn_own, parts), first_phase(x_in, parts)
    x_pieces = after(second_phase(x_in, x_first, parts), gain_one, gain_two)
    ffn_pieces = second_phase(ffn_own, after(ffn_first, x_pieces), parts)

    seg = segments[0]
    start = jnp.sum((seg[None, :] < seg[:, None]).astype(jnp.int32), axis=1)
    start_col = jnp.broadcast_to(start[:, None], (length, LANES))
    start_row = jnp.broadcast_to(start[None, :], (8, length))
    cosine, sine = rope_tables(length)
    taps = jnp.pad(jnp.concatenate([conv_x, conv_bc], axis=1), ((0, 8 - KW), (0, 0)))
    bias = jnp.concatenate([bias_x, bias_bc])[None, :]
    params = (taps, bias, lane_rows(dt_bias, 8), lane_rows(jnp.exp(a_log), 8), jnp.repeat(d_skip, PD)[None, :])

    residual = x_in.astype(F32)
    scale_one = rms_scale(residual)
    normed_one = residual * scale_one
    rank_arg = rank.astype(jnp.int32)[None]
    rows_one = norm_rows(rank_arg, parts, x_pieces, gain_one)
    proj = mm(rows_one, proj_w)
    y, gated, states, squares = scan_forward(cols, proj, start_col, start_row, params)
    ffn_pieces = after(ffn_pieces, squares)
    ffn_own = jnp.concatenate(
        ffn_pieces[:1]
        + [jnp.where(rank >= k, ffn_pieces[2 * k - 1], ffn_pieces[2 * k]) for k in range(1, parts)],
        axis=1,
    )
    ffn_w = lax.all_gather(ffn_own, "dp", axis=0, tiled=True)
    attended, lse, low_q, low_kv = attn_forward(proj, cosine, sine, start_col)
    scale_ssm = lax.rsqrt(group_total(squares[:1], parts) / width_ssm + EPSILON)
    mixed = (gated * scale_ssm[0][:, None] * ssm_gain[None, :]).astype(BF16)
    att_mixed = jnp.concatenate([attended, mixed], axis=1)
    terms = [mm_nt(rows_of(att_mixed, rank, shift, parts), out_w) for shift in range(parts)]
    middle = residual + sum_last(terms, sum_second(terms, sum_first(terms, rank, parts), rank, parts))
    block_out, grad_middle, grad_low, grad_gain_two, grad_ffn_w = ffn_both(middle, cotangent, gain_two, ffn_w, parts)

    branch_pieces = second_phase(grad_low, first_phase(grad_low, parts), parts)
    grad_ffn_own = lax.psum_scatter(grad_ffn_w, "dp", scatter_dimension=0, tiled=True)
    piece = grad_ffn_own.shape[1] // parts
    ffn_terms = [grad_ffn_own[:, k * piece : (k + 1) * piece] for k in range(parts)]
    ffn_terms = ffn_terms[:1] + ffn_terms[:0:-1]

    grad_att, grad_mixed, grad_out_w, inner, grad_gain_ssm = branch_back(
        rank_arg, parts, branch_pieces, out_w, att_mixed, ssm_gain[None, :]
    )
    inner = group_total(inner[:1], parts) / width_ssm
    stats = jnp.concatenate([scale_ssm, inner, jnp.zeros((6, length), F32)], axis=0)
    grad_q, grad_kv = attn_backward(low_q, low_kv, lse, attended, grad_att, cosine, sine, start_col)
    grad_rest, conv_acc, head_acc, skip_acc = scan_backward(
        cols, proj, start_col, start_row, params, y, states, grad_mixed, stats, ssm_gain[None, :]
    )
    core = lax.rem(lax.axis_index("dp"), 2).astype(jnp.int32)[None]
    theirs, ours = mixer_wgrad(core, own, rows_one, grad_q, grad_kv, grad_rest, grad_out_w)
    *terms, norm_shares = back_proj(
        rank_arg, parts, zat, width, grad_q, grad_kv, after(grad_rest, theirs), mixer_w, rows_one, gain_one, grad_gain_two
    )

    model = x_in.shape[1]
    wide = lambda rows: jnp.pad(rows, ((0, 0), (0, model - rows.shape[1])))
    head_sums = jnp.sum(head_acc, axis=1)[None, :]
    small = jnp.concatenate(
        [
            wide(conv_acc),
            norm_shares[:2],
            wide(grad_gain_ssm[:1]),
            wide(skip_acc[:1]),
            wide(head_sums),
            jnp.zeros((3, model), F32),
        ],
        axis=0,
    )
    size = lax.axis_size("dp")
    small = small + lax.ppermute(small, "dp", [(i, i ^ 1) for i in range(size)])

    chip_share = chip_total(theirs, ours, small)
    small = butterfly(after(small, chip_share), "dp", size, 2)
    firsts = after(sum_first(terms, rank, parts), small, grad_ffn_own)
    seconds = sum_second(terms, firsts, rank, parts)
    grad_w = sum_over_chips(chip_share)
    seconds, ffn_firsts, grad_w = lax.optimization_barrier((seconds, sum_first(ffn_terms, rank, parts), grad_w))
    ffn_seconds = sum_second(ffn_terms, ffn_firsts, rank, parts)
    grad_one = sum_last(terms, seconds)
    grad_input = grad_middle + norm_back(grad_one * gain_one, normed_one, scale_one)

    grad_conv_x = small[:KW, :channels]
    grad_bias_x = small[KW, :channels]
    grad_ssm_gain = small[10, :channels]
    grad_d_skip = jnp.sum(small[11, :channels].reshape(heads, PD), axis=1)
    grad_dt_bias = small[12, :heads]
    grad_a_log = small[12, 8 : 8 + heads]

    place = lax.axis_index("dp") * own
    norm_parts = lax.dynamic_slice(small, (8, place), (2, own))
    conv_parts = small[: KW + 1, channels : channels + 2 * NS]
    small_rows = jnp.concatenate(
        [
            jnp.pad(norm_parts, ((0, 0), (0, LANES - own))),
            conv_parts[:, :NS],
            conv_parts[:, NS:],
            jnp.zeros((own - 2 * KW - 4, LANES), F32),
        ],
        axis=0,
    )
    keyval = jnp.zeros((own, 2 * KVH * HD), BF16)
    keyval = lax.dynamic_update_slice(keyval, grad_w[:, qwidth : qwidth + HD], (0, kv_head * HD))
    keyval = lax.dynamic_update_slice(keyval, grad_w[:, qwidth + HD : zat], (0, (KVH + kv_head) * HD))
    shared = group_total(jnp.concatenate([keyval, grad_w[:, bat:dat], small_rows.astype(BF16)], axis=1), parts)
    grad_ffn = sum_last(ffn_terms, ffn_seconds)
    grad_w = grad_w.astype(F32)
    small_rows = shared[:, 2 * KVH * HD + 2 * NS :]
    grad_norm_one, grad_norm_two = small_rows[0, :own], small_rows[1, :own]
    conv_parts = jnp.concatenate([small_rows[2 : KW + 3], small_rows[KW + 3 : 2 * KW + 4]], axis=1)
    grad_conv_bc, grad_bias_bc = conv_parts[:KW], conv_parts[KW]

    return (
        block_out,
        grad_input,
        grad_norm_one,
        grad_w[:, :qwidth],
        shared[:, : 2 * KVH * HD],
        grad_w[:, width : width + qwidth].T,
        grad_w[:, zat:xat],
        grad_w[:, xat:bat],
        shared[:, 2 * KVH * HD : 2 * KVH * HD + 2 * NS],
        grad_w[:, dat : dat + heads],
        grad_conv_x,
        grad_conv_bc,
        grad_bias_x,
        grad_bias_bc,
        grad_dt_bias,
        grad_a_log,
        grad_d_skip,
        grad_ssm_gain,
        grad_w[:, width + qwidth :].T,
        grad_norm_two,
        grad_ffn[:, :hidden_own],
        grad_ffn[:, hidden_own : 2 * hidden_own],
        grad_ffn[:, 2 * hidden_own :].T,
    )


def solution(mesh):
    return jax.shard_map(
        local,
        mesh=mesh,
        in_specs=(
            P(("dp", "tensor"), None),
            P(("dp", "tensor"), None),
            P("dp", None),
            P("dp"),
            P("dp", "tensor"),
            P("dp", None),
            P("tensor", "dp"),
            P("dp", "tensor"),
            P("dp", "tensor"),
            P("dp", None),
            P("dp", "tensor"),
            P(None, "tensor"),
            P(),
            P("tensor"),
            P(),
            P("tensor"),
            P("tensor"),
            P("tensor"),
            P("tensor"),
            P("tensor", "dp"),
            P("dp"),
            P("dp", "tensor"),
            P("dp", "tensor"),
            P("tensor", "dp"),
        ),
        out_specs=(
            P(("dp", "tensor"), None),
            P(("dp", "tensor"), None),
            P("dp"),
            P("dp", "tensor"),
            P("dp", None),
            P("tensor", "dp"),
            P("dp", "tensor"),
            P("dp", "tensor"),
            P("dp", None),
            P("dp", "tensor"),
            P(None, "tensor"),
            P(),
            P("tensor"),
            P(),
            P("tensor"),
            P("tensor"),
            P("tensor"),
            P("tensor"),
            P("tensor", "dp"),
            P("dp"),
            P("dp", "tensor"),
            P("dp", "tensor"),
            P("tensor", "dp"),
        ),
        check_vma=False,
    )
```
